32 devices in a mesh: section: 2 (over x), head: 4 (over z), frame: 4 (over y, core).
Axes of the slice: x: 2, y: 2, z: 4, core: 2. Of those that a mesh axis runs over, the one named last changes fastest.
Arguments:
- inputs: bfloat16 [2, 2048, 1024], P(None, 'frame'), may hold values from -6 to 6
- lengths: int32 [2, 4], replicated, may hold values from 1 to 2045, as said below
- text: bfloat16 [2, 4, 64, 1024], P(None, None, 'frame'), may hold values from -6 to 6
- cotangent: float32 [2, 2048, 1024], P(None, 'frame'), may hold values from -6 to 6
- first_gain: float32 [2, 1024], P('section'), may hold values from 0.25 to 1.75
- first_shift: float32 [2, 1024], P('section'), may hold values from -2 to 2
- query_weight: bfloat16 [2, 1024, 1024], P('section', None, 'head'), may hold values from -0.1875 to 0.1875
- key_weight: bfloat16 [2, 1024, 1024], P('section', None, 'head'), may hold values from -0.1875 to 0.1875
- value_weight: bfloat16 [2, 1024, 1024], P('section', None, 'head'), may hold values from -0.1875 to 0.1875
- output_weight: bfloat16 [2, 1024, 1024], P('section', 'head'), may hold values from -4 to 4
- second_gain: float32 [2, 1024], P('section'), may hold values from 0.25 to 1.75
- second_shift: float32 [2, 1024], P('section'), may hold values from -2 to 2
- cross_query: bfloat16 [2, 1024, 1024], P('section', None, 'head'), may hold values from -0.1875 to 0.1875
- cross_key: bfloat16 [2, 1024, 1024], P('section', None, 'head'), may hold values from -0.1875 to 0.1875
- cross_value: bfloat16 [2, 1024, 1024], P('section', None, 'head'), may hold values from -0.1875 to 0.1875
- cross_output: bfloat16 [2, 1024, 1024], P('section', 'head'), may hold values from -0.75 to 0.75
- third_gain: float32 [2, 1024], P('section'), may hold values from 0.25 to 1.75
- third_shift: float32 [2, 1024], P('section'), may hold values from -2 to 2
- expand_weight: bfloat16 [2, 1024, 4096], P('section', None, 'head'), may hold values from -0.1875 to 0.1875
- reduce_weight: bfloat16 [2, 4096, 1024], P('section', 'head'), may hold values from -0.09375 to 0.09375
Outputs:
- layer_outputs: float32 [2, 2, 2048, 1024], P('section', None, 'frame')
- input_grads: float32 [2, 2, 2048, 1024], P('section', None, 'frame')
- text_grad: float32 [2, 4, 64, 1024], P(None, None, 'frame')
- first_gain_grad: float32 [2, 1024], P('section', 'frame')
- first_shift_grad: float32 [2, 1024], P('section', 'frame')
- query_weight_grad: float32 [2, 1024, 1024], P('section', 'frame', 'head')
- key_weight_grad: float32 [2, 1024, 1024], P('section', 'frame', 'head')
- value_weight_grad: float32 [2, 1024, 1024], P('section', 'frame', 'head')
- output_weight_grad: float32 [2, 1024, 1024], P('section', ('head', 'frame'))
- second_gain_grad: float32 [2, 1024], P('section', 'frame')
- second_shift_grad: float32 [2, 1024], P('section', 'frame')
- cross_query_grad: float32 [2, 1024, 1024], P('section', 'frame', 'head')
- cross_key_grad: float32 [2, 1024, 1024], P('section', 'frame', 'head')
- cross_value_grad: float32 [2, 1024, 1024], P('section', 'frame', 'head')
- cross_output_grad: float32 [2, 1024, 1024], P('section', ('head', 'frame'))
- third_gain_grad: float32 [2, 1024], P('section', 'frame')
- third_shift_grad: float32 [2, 1024], P('section', 'frame')
- expand_weight_grad: float32 [2, 1024, 4096], P('section', 'frame', 'head')
- reduce_weight_grad: float32 [2, 4096, 1024], P('section', ('head', 'frame'))
The draws below stay inside these ranges and needn't reach their ends.
Inputs may be any that keep to these rules, and one draw needn't show every extreme that they name: Row m lists the lengths of the 4 items packed in order into micro-batch m; they sum to 2048. In every row one item, in a slot drawn from the seed, is longer than 1536; the other items together are shorter than 512. In one micro-batch, drawn from the seed, the other items have length 1 each.
All inputs are finite; a program needn't handle non-finite values.
Results may differ from the reference program's by a relative error of at most 0.025.
Values may be sent and summed in bfloat16 or wider, within the bound.
A program may use at most 320 MiB of HBM per device.

```python
import math
import jax
import jax.numpy as jnp
from jax import lax

D = 1024
H = 16
HEAD = 64
FF = 4096
TEXT = 64
ITEMS = 4
MICRO = 2
LAYERS = 2
ROWS = 2048
RDEV = 512


def draw_lengths(key, part):
    key = jax.random.fold_in(key, 7)
    key_fill, key_slot, key_row = jax.random.split(key, 3)
    filler = jax.random.randint(key_fill, (MICRO, ITEMS), 1, RDEV // ITEMS + 1)
    chosen = jax.random.randint(key_slot, (MICRO, 1), 0, ITEMS)
    row_pick = jax.random.randint(key_row, (), 0, MICRO)
    short_row = (jnp.arange(MICRO) == row_pick)[:, None]
    filler = jnp.where(short_row, 1, filler)
    picked = jnp.arange(ITEMS)[None, :] == chosen
    others = jnp.sum(jnp.where(picked, 0, filler), axis=1, keepdims=True)
    return jnp.where(picked, ROWS - others, filler).astype(jnp.int32)


def steps_of(rng, shape, cuts, least, high):
    def one(axis_at, blocks):
        steps = jax.random.uniform(jax.random.fold_in(jax.random.fold_in(rng, 6), axis_at), (blocks,), jnp.float32, least / len(cuts), high / len(cuts))
        return jnp.repeat(jnp.exp(steps), shape[axis_at] // blocks).reshape((-1,) + (1,) * (len(shape) - axis_at - 1))

    level = one(*cuts[0])
    for cut in cuts[1:]:
        level = level * one(*cut)
    return level


def bell_draw(own_key, extent, width, limit, cuts=(), kind=jnp.bfloat16):
    values = jax.random.normal(own_key, extent, jnp.float32) * width
    if len(cuts) > 0:
        values = steps_of(own_key, extent, cuts, -0.22, 0.18) * values
    return jnp.clip(values, min=-limit, max=limit).astype(kind)


def setup_inputs(seed: int = 0) -> dict:
    seeds = jax.random.split(jax.random.key(seed), 21)
    return {
        "inputs": bell_draw(seeds[0], (MICRO, ROWS, D), 1.0, 6.0, ((1, 4),)),
        "lengths": draw_lengths(jax.random.fold_in(seeds[20], 71), 0),
        "text": bell_draw(seeds[2], (MICRO, ITEMS, TEXT, D), 1.0, 6.0, ((2, 4),)),
        "cotangent": bell_draw(seeds[3], (MICRO, ROWS, D), 1.0, 6.0, ((1, 4),), jnp.float32),
        "first_gain": jnp.clip(1.0 + 0.15 * jax.random.normal(seeds[4], (LAYERS, D), jnp.float32), 0.25, 1.75),
        "first_shift": bell_draw(seeds[5], (LAYERS, D), 0.3, 2.0, ((0, 2),), jnp.float32),
        "query_weight": bell_draw(seeds[6], (LAYERS, D, D), D ** -0.5, 0.1875, ((0, 2), (2, 4))),
        "key_weight": bell_draw(seeds[7], (LAYERS, D, D), D ** -0.5, 0.1875, ((0, 2), (2, 4))),
        "value_weight": bell_draw(seeds[8], (LAYERS, D, D), D ** -0.5, 0.1875, ((0, 2), (2, 4))),
        "output_weight": bell_draw(seeds[9], (LAYERS, D, D), 2 ** -0.5, 4.0, ((0, 2), (1, 4))),
        "second_gain": jnp.clip(1.0 + 0.15 * jax.random.normal(seeds[10], (LAYERS, D), jnp.float32), 0.25, 1.75),
        "second_shift": bell_draw(seeds[11], (LAYERS, D), 0.3, 2.0, ((0, 2),), jnp.float32),
        "cross_query": bell_draw(seeds[12], (LAYERS, D, D), D ** -0.5, 0.1875, ((0, 2), (2, 4))),
        "cross_key": bell_draw(seeds[13], (LAYERS, D, D), D ** -0.5, 0.1875, ((0, 2), (2, 4))),
        "cross_value": bell_draw(seeds[14], (LAYERS, D, D), D ** -0.5, 0.1875, ((0, 2), (2, 4))),
        "cross_output": bell_draw(seeds[15], (LAYERS, D, D), TEXT ** -0.5, 0.75, ((0, 2), (1, 4))),
        "third_gain": jnp.clip(1.0 + 0.15 * jax.random.normal(seeds[16], (LAYERS, D), jnp.float32), 0.25, 1.75),
        "third_shift": bell_draw(seeds[17], (LAYERS, D), 0.3, 2.0, ((0, 2),), jnp.float32),
        "expand_weight": bell_draw(seeds[18], (LAYERS, D, FF), D ** -0.5, 0.1875, ((0, 2), (2, 4))),
        "reduce_weight": bell_draw(seeds[19], (LAYERS, FF, D), FF ** -0.5, 0.09375, ((0, 2), (1, 4))),
    }


@jax.custom_vjp
def low(v):
    return lax.optimization_barrier(v.astype(jnp.bfloat16)).astype(jnp.float32)

@jax.custom_vjp
def low_back(v):
    return v

def low_keep(v):
    return (low(v), None)

def low_pass(kept, grad):
    return (grad,)

def back_keep(v):
    return (v, None)

def back_low(kept, grad):
    return (low(grad),)
low.defvjp(low_keep, low_pass)
low_back.defvjp(back_keep, back_low)
masked_score = -1e+30
highest = lax.Precision.HIGHEST

def product(left_side, right_side):
    return jnp.dot(left_side, right_side, precision=highest)

def layer_norm(signal, gain_vec, shift_vec):
    average = lax.optimization_barrier(jnp.mean(signal, axis=-1, keepdims=True))
    centered = signal - average
    variance = lax.optimization_barrier(jnp.mean(centered * centered, axis=-1, keepdims=True))
    return centered * lax.rsqrt(variance + 1e-05) * gain_vec + shift_vec

def segments(item_lengths, positions):
    item_ends = jnp.cumsum(item_lengths).astype(jnp.int32)
    return lax.optimization_barrier(jnp.sum((positions[:, None] >= item_ends[None, :]).astype(jnp.int32), axis=1))

def attend(query, key_rows, value_rows, query_seg, query_pos, key_seg, key_pos, causal):
    row_count = query.shape[0]
    block = math.gcd(row_count, 512)
    blocks = row_count // block
    scale = HEAD ** (-0.5)

    def one_block(pieces):
        query_block, seg_block, pos_block = pieces
        logits = jnp.einsum('qhd,khd->hqk', query_block, key_rows, precision=highest) * scale
        allowed = seg_block[:, None] == key_seg[None, :]
        if causal:
            allowed = allowed & (key_pos[None, :] <= pos_block[:, None])
        logits = jnp.where(allowed[None], logits, masked_score)
        logits = low_back(logits)
        weights_block = low(jax.nn.softmax(logits, axis=-1))
        return jnp.einsum('hqk,khd->qhd', weights_block, value_rows, precision=highest)
    result = lax.map(jax.checkpoint(one_block), (query.reshape(blocks, block, H, HEAD), query_seg.reshape(blocks, block), query_pos.reshape(blocks, block)))
    return result.reshape(row_count, H * HEAD)

def layer(signal, text_rows, seg_rows, weight_set):
    first_gain, first_shift, query_weight, key_weight, value_weight, output_weight, second_gain, second_shift, cross_query, cross_key, cross_value, cross_output, third_gain, third_shift, expand_weight, reduce_weight = weight_set
    positions = jnp.arange(ROWS, dtype=jnp.int32)
    first_normed = low(layer_norm(signal, first_gain, first_shift))
    query = low_back(low(product(first_normed, query_weight))).reshape(ROWS, H, HEAD)
    key_rows = low_back(low(product(first_normed, key_weight))).reshape(ROWS, H, HEAD)
    value_rows = low_back(low(product(first_normed, value_weight))).reshape(ROWS, H, HEAD)
    attended = low_back(low(attend(query, key_rows, value_rows, seg_rows, positions, seg_rows, positions, True)))
    middle = signal + low_back(product(attended, output_weight))
    second_normed = low(layer_norm(middle, second_gain, second_shift))
    cross_queries = low_back(low(product(second_normed, cross_query))).reshape(ROWS, H, HEAD)
    cross_keys = low_back(low(product(text_rows, cross_key))).reshape(ITEMS * TEXT, H, HEAD)
    cross_values = low_back(low(product(text_rows, cross_value))).reshape(ITEMS * TEXT, H, HEAD)
    text_item = jnp.arange(ITEMS * TEXT, dtype=jnp.int32) // TEXT
    cross_att = low_back(low(attend(cross_queries, cross_keys, cross_values, seg_rows, positions, text_item, text_item, False)))
    latter = middle + low_back(product(cross_att, cross_output))
    third_normed = low(layer_norm(latter, third_gain, third_shift))
    hidden_pre = low_back(product(third_normed, expand_weight))
    hidden_act = low(jax.nn.gelu(hidden_pre, approximate=False))
    return latter + low_back(product(hidden_act, reduce_weight))

def reference(inputs, lengths, text, cotangent, first_gain, first_shift, query_weight, key_weight, value_weight, output_weight, second_gain, second_shift, cross_query, cross_key, cross_value, cross_output, third_gain, third_shift, expand_weight, reduce_weight):
    weight_args = (first_gain, first_shift, query_weight, key_weight, value_weight, output_weight, second_gain, second_shift, cross_query, cross_key, cross_value, cross_output, third_gain, third_shift, expand_weight, reduce_weight)
    params = tuple((array_in.astype(jnp.float32) for array_in in weight_args))
    text_float = text.astype(jnp.float32)
    start = inputs.astype(jnp.float32)
    probe = jnp.zeros((LAYERS,) + start.shape, jnp.float32)
    positions = jnp.arange(ROWS, dtype=jnp.int32)

    def forward(start_in, text_in, probe_in, param_in):
        current = [start_in[index] for index in range(MICRO)]
        stacked_out = []
        for layer_index in range(LAYERS):
            layer_weights = tuple((array_in[layer_index] for array_in in param_in))
            produced = []
            for batch_index in range(MICRO):
                seg_rows = segments(lengths[batch_index], positions)
                text_rows = text_in[batch_index].reshape(ITEMS * TEXT, D)
                entering = current[batch_index] + probe_in[layer_index, batch_index]
                produced.append(layer(entering, text_rows, seg_rows, layer_weights))
            stacked_out.append(jnp.stack(produced))
            current = [low_back(low(rows_out)) for rows_out in produced]
        return jnp.stack(stacked_out)
    layer_outputs, pullback = jax.vjp(forward, start, text_float, probe, params)
    cotangent_all = jnp.concatenate([jnp.zeros((LAYERS - 1,) + cotangent.shape, jnp.float32), cotangent.astype(jnp.float32)[None]], axis=0)
    start_grad, text_grad, input_grads, param_grads = pullback(cotangent_all)
    return (layer_outputs, input_grads, text_grad, param_grads[0], param_grads[1], param_grads[2], param_grads[3], param_grads[4], param_grads[5], param_grads[6], param_grads[7], param_grads[8], param_grads[9], param_grads[10], param_grads[11], param_grads[12], param_grads[13], param_grads[14], param_grads[15])
```

```python
import functools

import jax
import jax.numpy as jnp
from jax import lax
from jax.experimental import pallas as pl
from jax.experimental.pallas import tpu as pltpu
from jax.sharding import PartitionSpec as P

HEAD = 64
TEXT = 64
ITEMS = 4

masked_score = -1e30
inv_sqrt_two = 0.7071067811865476
inv_sqrt_tau = 0.3989422804014327
MESH_IDS = pl.DeviceIdType.MESH
LAG = 2
VMEM_BYTES = 56 * 1024 * 1024
EPS = 1e-05


def chunking(rows):
    return max(1, min(16, rows // 16))


def norm_parts(v):
    average = jnp.mean(v, axis=-1, keepdims=True)
    centered = v - average
    inverse = lax.rsqrt(jnp.mean(centered * centered, axis=-1, keepdims=True) + EPS)
    return centered * inverse, inverse


def line_sum(rows, pieces, send, recv, across, held, sems, partial_rows, finish_rows):
    send_in, recv_in, send_across, recv_across, send_out, recv_out = sems
    place = lax.axis_index("head")
    step = rows // pieces
    is_end = (place == 0) | (place == 3)
    in_middle = jnp.logical_not(is_end)
    inner = jnp.where(place == 0, 1, 2)
    outer = jnp.where(place == 1, 0, 3)
    peer = 3 - place

    def spot(piece):
        return pl.ds(pl.multiple_of(piece * step, step), step)

    def inwards(piece):
        return pltpu.make_async_remote_copy(
            src_ref=send.at[spot(piece)],
            dst_ref=recv.at[spot(piece)],
            send_sem=send_in.at[piece],
            recv_sem=recv_in.at[piece],
            device_id={"head": inner},
            device_id_type=MESH_IDS,
        )

    def crossing(piece):
        return pltpu.make_async_remote_copy(
            src_ref=send.at[spot(piece)],
            dst_ref=across.at[spot(piece)],
            send_sem=send_across.at[piece],
            recv_sem=recv_across.at[piece],
            device_id={"head": peer},
            device_id_type=MESH_IDS,
        )

    def outwards(piece):
        return pltpu.make_async_remote_copy(
            src_ref=held.at[spot(piece)],
            dst_ref=held.at[spot(piece)],
            send_sem=send_out.at[piece],
            recv_sem=recv_out.at[piece],
            device_id={"head": outer},
            device_id_type=MESH_IDS,
        )

    barrier = pltpu.get_barrier_semaphore()

    @pl.when(is_end)
    def _():
        pl.semaphore_signal(barrier, 1, device_id={"head": inner}, device_id_type=MESH_IDS)
        pl.semaphore_wait(barrier, 1)

    @pl.when(in_middle)
    def _():
        pl.semaphore_signal(barrier, 1, device_id={"head": outer}, device_id_type=MESH_IDS)
        pl.semaphore_signal(barrier, 1, device_id={"head": peer}, device_id_type=MESH_IDS)
        pl.semaphore_wait(barrier, 2)

    @pl.when(is_end)
    def _():
        def give(piece, carry):
            send[spot(piece), :] = partial_rows(spot(piece)).astype(jnp.bfloat16)
            inwards(piece).start()
            return carry

        lax.fori_loop(0, pieces, give, 0)

        def take(piece, carry):
            outwards(piece).wait_recv()
            finish_rows(spot(piece), piece)
            return carry

        lax.fori_loop(0, pieces, take, 0)

        def drain(piece, carry):
            inwards(piece).wait_send()
            return carry

        lax.fori_loop(0, pieces, drain, 0)

    @pl.when(in_middle)
    def _():
        def add(piece):
            part = partial_rows(spot(piece))
            inwards(piece).wait_recv()
            send[spot(piece), :] = (part + recv[spot(piece), :].astype(jnp.float32)).astype(jnp.bfloat16)
            crossing(piece).start()

        def settle(piece):
            crossing(piece).wait_recv()
            held[spot(piece), :] = (
                send[spot(piece), :].astype(jnp.float32) + across[spot(piece), :].astype(jnp.float32)
            ).astype(jnp.bfloat16)
            outwards(piece).start()
            finish_rows(spot(piece), piece)

        lag = min(LAG, pieces)

        def both(t, carry):
            @pl.when(t < pieces)
            def _():
                add(t)

            @pl.when(t >= lag)
            def _():
                settle(t - lag)

            return carry

        lax.fori_loop(0, pieces + lag, both, 0)

        def drain(piece, carry):
            crossing(piece).wait_send()
            outwards(piece).wait_send()
            return carry

        lax.fori_loop(0, pieces, drain, 0)


def product_rows(left, weight, transposed):
    def rows_of(where_rows):
        contract = ((1,), (1,)) if transposed else ((1,), (0,))
        return lax.dot_general(
            left[where_rows, :], weight[...], (contract, ((), ())), preferred_element_type=jnp.float32
        )

    return rows_of


def forward_sum_kernel(pieces, normed, flipped, rounded, left, weight, base, gain, shift, *rest):
    if normed:
        out, out_normed, *rest = rest
        if rounded:
            out_low, *rest = rest
    else:
        out, *rest = rest
    if flipped:
        turned, *rest = rest
        turned[...] = left[...].T
        left = turned
    send, recv, across, held, *sems = rest

    def finish_rows(where_rows, slot):
        value = base[where_rows, :].astype(jnp.float32) + held[where_rows, :].astype(jnp.float32)
        out[where_rows, :] = value
        if rounded:
            low = value.astype(jnp.bfloat16)
            out_low[where_rows, :] = low
            value = low.astype(jnp.float32)
        if normed:
            standard, _ = norm_parts(value)
            out_normed[where_rows, :] = (standard * gain[...] + shift[...]).astype(jnp.bfloat16)

    line_sum(left.shape[0], pieces, send, recv, across, held, sems, product_rows(left, weight, False), finish_rows)


def sum_scratch(rows, width, pieces):
    return [pltpu.VMEM((rows, width), jnp.bfloat16)] * 4 + [pltpu.SemaphoreType.DMA((pieces,))] * 6


def turned_scratch(left, flipped):
    return [pltpu.VMEM(left.shape[::-1], jnp.bfloat16)] if flipped else []


def forward_sum(left, weight, base, gain, shift, normed, flipped, rounded, collective_id):
    rows, width = base.shape
    pieces = chunking(rows)
    outs = [jax.ShapeDtypeStruct((rows, width), jnp.float32)]
    outs += [jax.ShapeDtypeStruct((rows, width), jnp.bfloat16)] * (normed + rounded)
    whole = pl.BlockSpec(memory_space=pltpu.VMEM)
    result = pl.pallas_call(
        functools.partial(forward_sum_kernel, pieces, normed, flipped, rounded),
        out_shape=outs,
        in_specs=[whole] * 5,
        out_specs=[whole] * len(outs),
        scratch_shapes=turned_scratch(left, flipped) + sum_scratch(rows, width, pieces),
        compiler_params=pltpu.CompilerParams(
            collective_id=collective_id, has_side_effects=True, vmem_limit_bytes=VMEM_BYTES
        ),
    )(left, weight, base, gain[None], shift[None])
    return result if normed else result[0]


def backward_sum_kernel(
    pieces, flipped, weight_flipped, left, weight, value, gain, upstream, out, out_low, gain_grad, shift_grad, *rest
):
    if flipped:
        turned, *rest = rest
        turned[...] = left[...].T
        left = turned
    send, recv, across, held, gain_parts, shift_parts, *sems = rest

    def finish_rows(where_rows, slot):
        grad = held[where_rows, :].astype(jnp.float32)
        standard, inverse = norm_parts(value[where_rows, :].astype(jnp.float32))
        scaled = grad * gain[...]
        through = inverse * (
            scaled
            - jnp.mean(scaled, axis=-1, keepdims=True)
            - standard * jnp.mean(scaled * standard, axis=-1, keepdims=True)
        )
        total = through + upstream[where_rows, :].astype(jnp.float32)
        out[where_rows, :] = total
        out_low[where_rows, :] = total.astype(jnp.bfloat16)
        gain_parts[slot] = jnp.sum(grad * standard, axis=0, keepdims=True)
        shift_parts[slot] = jnp.sum(grad, axis=0, keepdims=True)

    line_sum(left.shape[0], pieces, send, recv, across, held, sems, product_rows(left, weight, weight_flipped), finish_rows)
    gain_grad[...] = jnp.sum(gain_parts[...], axis=0)
    shift_grad[...] = jnp.sum(shift_parts[...], axis=0)


def backward_sum(left, weight, value, gain, upstream, flipped, weight_flipped, collective_id):
    rows, width = value.shape
    pieces = chunking(rows)
    whole = pl.BlockSpec(memory_space=pltpu.VMEM)
    vector = jax.ShapeDtypeStruct((1, width), jnp.float32)
    scratch = sum_scratch(rows, width, pieces)
    scratch[4:4] = [pltpu.VMEM((pieces, 1, width), jnp.float32)] * 2
    return pl.pallas_call(
        functools.partial(backward_sum_kernel, pieces, flipped, weight_flipped),
        out_shape=[
            jax.ShapeDtypeStruct((rows, width), jnp.float32),
            jax.ShapeDtypeStruct((rows, width), jnp.bfloat16),
            vector,
            vector,
        ],
        in_specs=[whole] * 5,
        out_specs=[whole] * 4,
        scratch_shapes=turned_scratch(left, flipped) + scratch,
        compiler_params=pltpu.CompilerParams(
            collective_id=collective_id, has_side_effects=True, vmem_limit_bytes=VMEM_BYTES
        ),
    )(left, weight, value, gain[None], upstream)


def block_of(rows):
    return 256 if rows % 256 == 0 else rows


def nt_product(left, right):
    return lax.dot_general(left, right, (((1,), (1,)), ((), ())), preferred_element_type=jnp.float32)


def plain_product(left, right):
    return jnp.dot(left, right, preferred_element_type=jnp.float32)


def greet_frames(frames):
    me = lax.axis_index("frame")
    barrier = pltpu.get_barrier_semaphore()
    for by in range(1, frames):
        pl.semaphore_signal(
            barrier, 1, device_id={"frame": lax.rem(me + by, frames)}, device_id_type=MESH_IDS
        )
    pl.semaphore_wait(barrier, frames - 1)


def masked_scores(keys, query_t, begins, start):
    reach, block = keys.shape[0], query_t.shape[1]
    scores = plain_product(keys, query_t)
    key_pos = lax.broadcasted_iota(jnp.int32, (reach, 1), 0)
    query_pos = start + lax.broadcasted_iota(jnp.int32, (1, block), 1)
    allowed = (key_pos <= query_pos) & (key_pos >= begins)
    return jnp.where(allowed, scores * HEAD ** (-0.5), masked_score)


def lane_span(index, width):
    return pl.ds(pl.multiple_of(index * width, width), width)


def exchange(frames, source, landing, send_sems, recv_sems):
    me = lax.axis_index("frame")

    def copy(by):
        other = lax.rem(me + by, frames)
        return pltpu.make_async_remote_copy(
            src_ref=source(other),
            dst_ref=landing(me),
            send_sem=send_sems.at[by - 1],
            recv_sem=recv_sems.at[by - 1],
            device_id={"frame": other},
            device_id_type=MESH_IDS,
        )

    return copy


def attention_kernel(frames, normed, weight, begins, heads_t, out, own, keys, mixed_t, *sems):
    send_heads, recv_heads, send_out, recv_out = sems
    me = lax.axis_index("frame")
    rows = normed.shape[0]
    total_rows = rows * frames
    block = block_of(rows)
    width = 3 * HEAD
    greet_frames(frames)
    to_heads = exchange(
        frames,
        lambda g: own.at[g],
        lambda f: heads_t.at[:, lane_span(f, rows)],
        send_heads,
        recv_heads,
    )
    for by in (2, 3, 1, 0):
        other = lax.rem(me + by, frames)
        piece = nt_product(weight[pl.ds(pl.multiple_of(other * width, width), width), :], normed[...])
        if by:
            own[other] = piece.astype(jnp.bfloat16)
            to_heads(by).start()
        else:
            heads_t[:, lane_span(me, rows)] = piece.astype(jnp.bfloat16)
    for by in (1, 2, 3):
        to_heads(by).wait()
    keys[...] = heads_t[HEAD : 2 * HEAD, :].T
    to_frames = exchange(
        frames,
        lambda g: mixed_t.at[g],
        lambda f: out.at[pl.ds(pl.multiple_of(f * HEAD, HEAD), HEAD), :],
        send_out,
        recv_out,
    )
    for target in range(frames):
        for start in range(target * rows, (target + 1) * rows, block):
            reach = start + block
            scores = masked_scores(keys[:reach, :], heads_t[:HEAD, start:reach], begins[:, start:reach], start)
            e = jnp.exp(scores - jnp.max(scores, axis=0, keepdims=True))
            total = jnp.sum(e, axis=0, keepdims=True)
            mixed = plain_product(heads_t[2 * HEAD :, :reach], e.astype(jnp.bfloat16))
            at = start - target * rows
            mixed_t[target, :, at : at + block] = (mixed * (1.0 / total)).astype(jnp.bfloat16)

        for by in range(1, frames):

            @pl.when(lax.rem(me + by, frames) == target)
            def _():
                to_frames(by).start()

    out[pl.ds(pl.multiple_of(me * HEAD, HEAD), HEAD), :] = mixed_t[me]
    for by in (1, 2, 3):
        to_frames(by).wait()


def attention(normed, weight, begins, collective_id):
    rows = normed.shape[0]
    frames = lax.axis_size("frame")
    whole = pl.BlockSpec(memory_space=pltpu.VMEM)
    dma = pltpu.SemaphoreType.DMA((frames - 1,))
    return pl.pallas_call(
        functools.partial(attention_kernel, frames),
        out_shape=[
            jax.ShapeDtypeStruct((3 * HEAD, rows * frames), jnp.bfloat16),
            jax.ShapeDtypeStruct((frames * HEAD, rows), jnp.bfloat16),
        ],
        in_specs=[whole] * 3,
        out_specs=[whole] * 2,
        scratch_shapes=[
            pltpu.VMEM((frames, 3 * HEAD, rows), jnp.bfloat16),
            pltpu.VMEM((rows * frames, HEAD), jnp.bfloat16),
            pltpu.VMEM((frames, HEAD, rows), jnp.bfloat16),
            dma,
            dma,
            dma,
            dma,
        ],
        compiler_params=pltpu.CompilerParams(
            collective_id=collective_id, has_side_effects=True, vmem_limit_bytes=VMEM_BYTES
        ),
    )(normed, weight, begins)


def attention_back_kernel(
    frames, heads_t, grad_low, weight, begins, out, own, grad_t, columns, key_sum, value_sum, grads_t, *sems
):
    send_heads, recv_heads, send_out, recv_out = sems
    me = lax.axis_index("frame")
    rows = grad_low.shape[0]
    block = block_of(rows)
    scale = HEAD ** (-0.5)
    width = 3 * HEAD
    greet_frames(frames)
    to_heads = exchange(
        frames,
        lambda g: own.at[g],
        lambda f: grad_t.at[:, lane_span(f, rows)],
        send_heads,
        recv_heads,
    )
    for by in (2, 3, 1, 0):
        other = lax.rem(me + by, frames)
        piece = nt_product(weight[pl.ds(pl.multiple_of(other * HEAD, HEAD), HEAD), :], grad_low[...])
        if by:
            own[other] = piece.astype(jnp.bfloat16)
            to_heads(by).start()
        else:
            grad_t[:, lane_span(me, rows)] = piece.astype(jnp.bfloat16)
    key_sum[...] = jnp.zeros_like(key_sum)
    value_sum[...] = jnp.zeros_like(value_sum)
    for part in range(3):
        columns[part] = heads_t[part * HEAD : (part + 1) * HEAD, :].T
    for by in (1, 2, 3):
        to_heads(by).wait()
    columns[3] = grad_t[...].T
    to_frames = exchange(
        frames,
        lambda g: grads_t.at[g],
        lambda f: out.at[pl.ds(pl.multiple_of(f * width, width), width), :],
        send_out,
        recv_out,
    )
    for target in reversed(range(frames)):
        for start in reversed(range(target * rows, (target + 1) * rows, block)):
            reach = start + block
            scores = masked_scores(
                columns[1, :reach, :], heads_t[:HEAD, start:reach], begins[:, start:reach], start
            )
            e = jnp.exp(scores - jnp.max(scores, axis=0, keepdims=True))
            p = e * (1.0 / jnp.sum(e, axis=0, keepdims=True))
            slope = plain_product(columns[2, :reach, :], grad_t[:, start:reach])
            weighted = p * slope
            ds = (weighted - p * jnp.sum(weighted, axis=0, keepdims=True)).astype(jnp.bfloat16)
            value_sum[:reach, :] += plain_product(p.astype(jnp.bfloat16), columns[3, start:reach, :])
            key_sum[:reach, :] += plain_product(ds, columns[0, start:reach, :])
            at = start - target * rows
            here = slice(at, at + block)
            grads_t[target, :HEAD, here] = (
                plain_product(heads_t[HEAD : 2 * HEAD, :reach], ds) * scale
            ).astype(jnp.bfloat16)
            grads_t[target, HEAD : 2 * HEAD, here] = (key_sum[start:reach, :] * scale).T.astype(jnp.bfloat16)
            grads_t[target, 2 * HEAD :, here] = value_sum[start:reach, :].T.astype(jnp.bfloat16)

        for by in range(1, frames):

            @pl.when(lax.rem(me + by, frames) == target)
            def _():
                to_frames(by).start()

    out[pl.ds(pl.multiple_of(me * width, width), width), :] = grads_t[me]
    for by in (1, 2, 3):
        to_frames(by).wait()


def attention_back(heads_t, grad_low, weight, begins, collective_id):
    rows = grad_low.shape[0]
    frames = lax.axis_size("frame")
    whole = pl.BlockSpec(memory_space=pltpu.VMEM)
    dma = pltpu.SemaphoreType.DMA((frames - 1,))
    total_rows = rows * frames
    return pl.pallas_call(
        functools.partial(attention_back_kernel, frames),
        out_shape=jax.ShapeDtypeStruct((frames * 3 * HEAD, rows), jnp.bfloat16),
        in_specs=[whole] * 4,
        out_specs=whole,
        scratch_shapes=[
            pltpu.VMEM((frames, HEAD, rows), jnp.bfloat16),
            pltpu.VMEM((HEAD, total_rows), jnp.bfloat16),
            pltpu.VMEM((4, total_rows, HEAD), jnp.bfloat16),
            pltpu.VMEM((total_rows, HEAD), jnp.float32),
            pltpu.VMEM((total_rows, HEAD), jnp.float32),
            pltpu.VMEM((frames, 3 * HEAD, rows), jnp.bfloat16),
            dma,
            dma,
            dma,
            dma,
        ],
        compiler_params=pltpu.CompilerParams(
            collective_id=collective_id, has_side_effects=True, vmem_limit_bytes=VMEM_BYTES
        ),
    )(heads_t, grad_low, weight, begins)


def matmul(left_side, right_side):
    return jnp.dot(left_side, right_side, preferred_element_type=jnp.float32)


def matmul_tn(left_side, right_side):
    return lax.dot_general(
        left_side, right_side, (((0,), (0,)), ((), ())), preferred_element_type=jnp.float32
    )


def matmul_nt(left_side, right_side):
    return lax.dot_general(
        left_side, right_side, (((1,), (1,)), ((), ())), preferred_element_type=jnp.float32
    )


def layer_norm(signal, gain_vec, shift_vec):
    average = jnp.mean(signal, axis=-1, keepdims=True)
    centered = signal - average
    variance = jnp.mean(centered * centered, axis=-1, keepdims=True)
    return centered * lax.rsqrt(variance + 1e-05) * gain_vec + shift_vec


def norm_back(signal, gain_vec, upstream):
    average = jnp.mean(signal, axis=-1, keepdims=True)
    centered = signal - average
    inverse = lax.rsqrt(jnp.mean(centered * centered, axis=-1, keepdims=True) + 1e-05)
    standard = centered * inverse
    scaled = upstream * gain_vec
    through = inverse * (
        scaled
        - jnp.mean(scaled, axis=-1, keepdims=True)
        - standard * jnp.mean(scaled * standard, axis=-1, keepdims=True)
    )
    return (through, jnp.sum(upstream * standard, axis=0), jnp.sum(upstream, axis=0))


def head_total(partial_sum):
    return lax.psum(partial_sum.astype(jnp.bfloat16), "head").astype(jnp.float32)


def swapped(x):
    return lax.ppermute(x, "section", [(0, 1), (1, 0)])


def across_frames(x, bit):
    return lax.ppermute(x, "frame", [(i, i ^ bit) for i in range(lax.axis_size("frame"))])


def split_heads(matrix):
    return matrix.reshape(matrix.shape[0], matrix.shape[1] // HEAD, HEAD)


def softmax_rows(query, key_rows, allowed):
    logits = jnp.einsum(
        "qhd,khd->hqk",
        split_heads(query),
        split_heads(key_rows),
        preferred_element_type=jnp.float32,
    ) * HEAD ** (-0.5)
    logits = jnp.where(allowed[None], logits, masked_score)
    exponent = jnp.exp(logits - jnp.max(logits, axis=-1, keepdims=True))
    return exponent / jnp.sum(exponent, axis=-1, keepdims=True)


def attend(query, key_rows, value_rows, allowed):
    weights_low = softmax_rows(query, key_rows, allowed).astype(jnp.bfloat16)
    result = jnp.einsum(
        "hqk,khd->qhd", weights_low, split_heads(value_rows), preferred_element_type=jnp.float32
    )
    return result.reshape(query.shape).astype(jnp.bfloat16)


def attend_back(query, key_rows, value_rows, allowed, grad_out):
    probabilities = softmax_rows(query, key_rows, allowed)
    weights_low = probabilities.astype(jnp.bfloat16)
    grad_heads = split_heads(grad_out)
    grad_prob = jnp.einsum(
        "qhd,khd->hqk", grad_heads, split_heads(value_rows), preferred_element_type=jnp.float32
    )
    centre = jnp.sum(probabilities * grad_prob, axis=-1, keepdims=True)
    grad_logit = (probabilities * (grad_prob - centre)).astype(jnp.bfloat16)
    scale = HEAD ** (-0.5)
    grad_query = (
        jnp.einsum(
            "hqk,khd->qhd", grad_logit, split_heads(key_rows), preferred_element_type=jnp.float32
        )
        * scale
    )
    grad_keys = (
        jnp.einsum(
            "hqk,qhd->khd", grad_logit, split_heads(query), preferred_element_type=jnp.float32
        )
        * scale
    )
    grad_values = jnp.einsum(
        "hqk,qhd->khd", weights_low, grad_heads, preferred_element_type=jnp.float32
    )
    return (
        grad_query.reshape(query.shape),
        grad_keys.reshape(key_rows.shape),
        grad_values.reshape(value_rows.shape),
    )


def add_and_norm(left, weight, base, gain, shift, normed, flipped, rounded, collective_id):
    if lax.axis_size("head") == 4:
        return forward_sum(left, weight, base, gain, shift, normed, flipped, rounded, collective_id)
    part = matmul_tn(left, weight) if flipped else matmul(left, weight)
    value = base.astype(jnp.float32) + head_total(part)
    if not normed:
        return value
    if not rounded:
        return value, layer_norm(value, gain, shift).astype(jnp.bfloat16)
    low = value.astype(jnp.bfloat16)
    return value, layer_norm(low.astype(jnp.float32), gain, shift).astype(jnp.bfloat16), low


def norm_and_back(left, weight, value, gain, upstream, flipped, weight_flipped, collective_id):
    if lax.axis_size("head") == 4:
        return backward_sum(
            left, weight, value, gain, upstream, flipped, weight_flipped, collective_id
        )
    left = left.T if flipped else left
    part = matmul_nt(left, weight) if weight_flipped else matmul(left, weight)
    through, gain_grad, shift_grad = norm_back(value.astype(jnp.float32), gain, head_total(part))
    through = through + upstream
    return through, through.astype(jnp.bfloat16), gain_grad[None], shift_grad[None]


def self_attention(normed, weight, masks):
    frames = lax.axis_size("frame")
    heads = weight.shape[0] // (3 * HEAD)
    if frames == heads:
        heads_t, attended_t = attention(normed, weight, masks["begins"], 1)
        return attended_t, heads_t
    rows = normed.shape[0]
    packed = matmul_nt(normed, weight).astype(jnp.bfloat16).reshape(rows, heads, 3, HEAD)
    query, keys, values = (packed[:, :, i].reshape(rows, heads * HEAD) for i in range(3))
    all_keys = lax.all_gather(keys, "frame", axis=0, tiled=True)
    all_values = lax.all_gather(values, "frame", axis=0, tiled=True)
    attended = attend(query, all_keys, all_values, masks["own"])
    return attended.T, (query, all_keys, all_values)


def self_attention_back(kept, grad_low, output_weight, masks):
    frames = lax.axis_size("frame")
    columns = output_weight.shape[0]
    heads = columns // HEAD
    if frames == heads:
        return attention_back(kept, grad_low, output_weight, masks["begins"], 2)
    query, keys, values = kept
    rows = query.shape[0]
    grad_out = matmul_nt(grad_low, output_weight).astype(jnp.bfloat16)
    grad_q, grad_k_all, grad_v_all = attend_back(query, keys, values, masks["own"], grad_out)
    grad_k, grad_v = (
        lax.psum_scatter(g.astype(jnp.bfloat16), "frame", scatter_dimension=0, tiled=True)
        for g in (grad_k_all, grad_v_all)
    )
    packed = jnp.stack(
        [g.reshape(rows, heads, HEAD) for g in (grad_q.astype(jnp.bfloat16), grad_k, grad_v)], axis=2
    )
    return packed.reshape(rows, heads * 3 * HEAD).T


def forward(entering, normed, vectors, next_vectors, weights, cross_keys, cross_values, masks):
    second_gain, second_shift, third_gain, third_shift = vectors[2:]
    heads_weight, output_weight, cross_query, cross_output, expand_weight, reduce_weight = weights
    attended_t, heads_kept = self_attention(normed, heads_weight, masks)
    middle, second_normed = add_and_norm(
        attended_t, output_weight, entering, second_gain, second_shift, True, True, False, 3
    )
    cross_queries = matmul(second_normed, cross_query).astype(jnp.bfloat16)
    cross_att = attend(cross_queries, cross_keys, cross_values, masks["cross"])
    latter, third_normed = add_and_norm(
        cross_att, cross_output, middle, third_gain, third_shift, True, False, False, 4
    )
    hidden_pre = matmul(third_normed, expand_weight)
    hidden_act = jax.nn.gelu(hidden_pre, approximate=False).astype(jnp.bfloat16)
    saved = (
        entering,
        normed,
        heads_kept,
        attended_t,
        middle,
        second_normed,
        cross_queries,
        cross_att,
        latter,
        third_normed,
        hidden_pre,
        hidden_act,
    )
    if next_vectors is None:
        result = add_and_norm(
            hidden_act, reduce_weight, latter, third_gain, third_shift, False, False, False, 5
        )
        return result, None, None, saved
    result, next_normed, result_low = add_and_norm(
        hidden_act, reduce_weight, latter, next_vectors[0], next_vectors[1], True, False, True, 6
    )
    return result, next_normed, result_low, saved


def frame_share(grad, axis):
    frames = lax.axis_size("frame")
    if frames != 4:
        return lax.psum_scatter(
            grad.astype(jnp.bfloat16), "frame", scatter_dimension=axis, tiled=True
        )
    me = lax.axis_index("frame")
    side, core = me // 2, me % 2
    share = grad.shape[axis] // 4

    def of_core(which):
        pieces = [
            lax.dynamic_slice_in_dim(grad, (2 * s + which) * share, share, axis) for s in range(2)
        ]
        return jnp.stack(pieces)

    mine = of_core(core).astype(jnp.float32)
    mine = mine + across_frames(of_core(1 - core).astype(jnp.bfloat16), 1).astype(jnp.float32)
    mine = mine.astype(jnp.bfloat16)
    kept = lax.dynamic_index_in_dim(mine, side, 0, keepdims=False).astype(jnp.float32)
    given = lax.dynamic_index_in_dim(mine, 1 - side, 0, keepdims=False)
    return (kept + across_frames(given, 2).astype(jnp.float32)).astype(jnp.bfloat16)


def backward(saved, upstream, grad_out, vectors, weights, cross_keys, cross_values, masks):
    first_gain, _, second_gain, _, third_gain, _ = vectors
    heads_weight, output_weight, cross_query, cross_output, expand_weight, reduce_weight = weights
    (
        entering,
        normed,
        heads_kept,
        attended_t,
        middle,
        second_normed,
        cross_queries,
        cross_att,
        latter,
        third_normed,
        hidden_pre,
        hidden_act,
    ) = saved
    grad_act = matmul_nt(grad_out, reduce_weight)
    slope = (
        0.5 * (1.0 + lax.erf(hidden_pre * inv_sqrt_two))
        + hidden_pre * jnp.exp(-0.5 * hidden_pre * hidden_pre) * inv_sqrt_tau
    )
    grad_pre = (grad_act * slope).astype(jnp.bfloat16)
    first_id = 7 if upstream.dtype == jnp.float32 else 10
    grad_latter, grad_cross, grad_third_gain, grad_third_shift = norm_and_back(
        grad_pre, expand_weight, latter, third_gain, upstream, False, True, first_id
    )
    grad_reduce = frame_share(matmul_tn(hidden_act, grad_out), 0)
    grad_expand = frame_share(matmul_tn(third_normed, grad_pre), 0)
    grad_cross_att = matmul_nt(grad_cross, cross_output).astype(jnp.bfloat16)
    grad_cq, grad_ck, grad_cv = attend_back(
        cross_queries, cross_keys, cross_values, masks["cross"], grad_cross_att
    )
    grad_text_rows = jnp.concatenate([grad_ck, grad_cv], axis=1)
    grad_text_rows = frame_share(grad_text_rows.reshape(ITEMS, TEXT, -1), 1)
    grad_cquery = grad_cq.astype(jnp.bfloat16)
    grad_middle, grad_self, grad_second_gain, grad_second_shift = norm_and_back(
        grad_cquery, cross_query, middle, second_gain, grad_latter, False, True, 8
    )
    grad_cross_output = frame_share(matmul_tn(cross_att, grad_cross), 0)
    grad_cross_query = frame_share(matmul_tn(second_normed, grad_cquery), 0)
    grad_heads_t = self_attention_back(heads_kept, grad_self, output_weight, masks)
    grad_output = frame_share(matmul(attended_t, grad_self), 0)
    grad_signal, grad_low, grad_first_gain, grad_first_shift = norm_and_back(
        grad_heads_t, heads_weight, entering, first_gain, grad_middle, True, False, 9
    )
    grad_heads = frame_share(matmul(grad_heads_t, normed), 1)
    vector_grads = jnp.concatenate(
        [
            grad_first_gain,
            grad_first_shift,
            grad_second_gain,
            grad_second_shift,
            grad_third_gain,
            grad_third_shift,
        ]
    )
    matrix_grads = (
        grad_heads,
        grad_output,
        grad_cross_query,
        grad_cross_output,
        grad_expand,
        grad_reduce,
    )
    return grad_signal, grad_low, vector_grads, matrix_grads, grad_text_rows


def per_device(
    inputs,
    lengths,
    text,
    cotangent,
    first_gain,
    first_shift,
    query_weight,
    key_weight,
    value_weight,
    output_weight,
    second_gain,
    second_shift,
    cross_query,
    cross_key,
    cross_value,
    cross_output,
    third_gain,
    third_shift,
    expand_weight,
    reduce_weight,
):
    section = lax.axis_index("section")
    at_zero = section == 0
    frame_count = lax.axis_size("frame")
    frame_index = lax.axis_index("frame")
    core = frame_index % 2
    micro_count, rows_dev, model_width = inputs.shape
    rows_all = rows_dev * frame_count
    text_rows_dev = text.shape[2]

    def keep(pair):
        return jnp.where(at_zero, pair[0], pair[1])

    def give(pair):
        return jnp.where(at_zero, pair[1], pair[0])

    def both_layers(weight):
        half = weight.shape[0] // 2
        mine = lax.dynamic_slice_in_dim(weight, core * half, half, 0)
        came = swapped(mine)
        sibling = across_frames(came, 1)
        other = jnp.concatenate(
            [jnp.where(core == 0, came, sibling), jnp.where(core == 0, sibling, came)], axis=0
        )
        return jnp.where(at_zero, weight, other), jnp.where(at_zero, other, weight)

    vector_args = jnp.concatenate(
        [first_gain, first_shift, second_gain, second_shift, third_gain, third_shift], axis=0
    )
    vectors = lax.all_gather(vector_args, "section")
    columns = query_weight.shape[2]
    heads_weight = jnp.stack(
        [
            w[0].T.reshape(columns // HEAD, HEAD, model_width)
            for w in (query_weight, key_weight, value_weight)
        ],
        axis=1,
    ).reshape(3 * columns, model_width)
    pairs = []
    previous = None
    for weight in (
        heads_weight,
        output_weight[0],
        cross_query[0],
        cross_output[0],
        expand_weight[0],
        reduce_weight[0],
    ):
        if previous is not None:
            weight, _ = lax.optimization_barrier((weight, previous))
        pairs.append(both_layers(weight))
        previous = pairs[-1][0][:8, :128]
    weights = list(zip(*pairs))

    text_full = lax.all_gather(text, "frame", axis=2, tiled=True)
    text_flat = text_full.reshape(micro_count * ITEMS * TEXT, model_width)
    text_heads = jnp.concatenate(
        [matmul(text_flat, cross_key[0]), matmul(text_flat, cross_value[0])], axis=1
    ).astype(jnp.bfloat16)
    text_heads = text_heads.reshape(micro_count, ITEMS * TEXT, -1)
    own_text = keep(text_heads)
    other_text = swapped(give(text_heads))
    cross_states = [
        jnp.where(at_zero, own_text, other_text),
        jnp.where(at_zero, other_text, own_text),
    ]
    cross_keys = [c[:, :columns] for c in cross_states]
    cross_values = [c[:, columns:] for c in cross_states]

    item_ends = jnp.cumsum(lax.dynamic_index_in_dim(lengths, section, 0, keepdims=False))
    all_positions = jnp.arange(rows_all, dtype=jnp.int32)
    passed = all_positions[:, None] >= item_ends[None, :]
    seg_all = jnp.sum(passed.astype(jnp.int32), axis=1)
    begins = jnp.max(jnp.where(passed, item_ends[None, :], 0), axis=1)
    own_start = frame_index * rows_dev
    own_positions = own_start + jnp.arange(rows_dev, dtype=jnp.int32)
    seg_own = lax.dynamic_slice_in_dim(seg_all, own_start, rows_dev)
    text_item = jnp.arange(ITEMS * TEXT, dtype=jnp.int32) // TEXT
    masks = {
        "own": (all_positions[None, :] <= own_positions[:, None])
        & (seg_own[:, None] == seg_all[None, :]),
        "begins": begins[None].astype(jnp.int32),
        "cross": seg_own[:, None] == text_item[None, :],
    }

    signal = lax.dynamic_index_in_dim(inputs, section, 0, keepdims=False)
    normed = layer_norm(signal.astype(jnp.float32), vectors[0][0], vectors[0][1])
    normed = normed.astype(jnp.bfloat16)
    results, saves = [], []
    for layer in range(2):
        result, normed, signal, saved = forward(
            signal,
            normed,
            vectors[layer],
            vectors[1] if layer == 0 else None,
            weights[layer],
            cross_keys[layer],
            cross_values[layer],
            masks,
        )
        results.append(result)
        saves.append(saved)

    upstream = lax.dynamic_index_in_dim(cotangent, section, 0, keepdims=False)
    grad_out = upstream.astype(jnp.bfloat16)
    in_grads, vector_grads, matrix_grads, text_grads = ([None] * 2 for _ in range(4))
    for layer in (1, 0):
        in_grads[layer], grad_low, vector_grads[layer], matrix_grads[layer], text_grads[layer] = (
            backward(
                saves[layer],
                upstream,
                grad_out,
                vectors[layer],
                weights[layer],
                cross_keys[layer],
                cross_values[layer],
                masks,
            )
        )
        grad_out = grad_low
        upstream = grad_low

    def both_micros(pair):
        own = keep(pair)
        other = swapped(give([p.astype(jnp.bfloat16) for p in pair])).astype(own.dtype)
        return jnp.stack([jnp.where(at_zero, own, other), jnp.where(at_zero, other, own)])

    layer_outputs = both_micros(results)
    input_grads = both_micros(in_grads)
    totals = [
        keep(pair).astype(jnp.float32) + swapped(give(pair)).astype(jnp.float32)
        for pair in zip(*matrix_grads)
    ]
    text_rows = both_micros(text_grads)
    text_rows = text_rows.reshape(micro_count * ITEMS * text_rows_dev, -1)
    key_part, value_part = text_rows[:, :columns], text_rows[:, columns:]
    text_local = text.reshape(-1, model_width)
    grad_cross_key, grad_cross_value = (
        frame_share(matmul_tn(text_local, part), 0).astype(jnp.float32)
        for part in (key_part, value_part)
    )
    text_part = matmul_nt(key_part, cross_key[0]) + matmul_nt(value_part, cross_value[0])
    text_grad = lax.psum(text_part.astype(jnp.bfloat16), ("section", "head")).astype(jnp.float32)
    text_grad = text_grad.reshape(text.shape)

    stacked = lax.psum_scatter(
        jnp.stack(vector_grads).astype(jnp.bfloat16), "frame", scatter_dimension=2, tiled=True
    )
    vector_total = keep(stacked).astype(jnp.float32) + swapped(give(stacked)).astype(jnp.float32)

    grad_heads, grad_o, grad_cq, grad_co, grad_e, grad_r = totals
    grad_heads = grad_heads.reshape(columns // HEAD, 3, HEAD, -1)
    grad_q, grad_k, grad_v = (grad_heads[:, i].reshape(columns, -1).T for i in range(3))
    ordered = (
        vector_total[0],
        vector_total[1],
        grad_q,
        grad_k,
        grad_v,
        grad_o,
        vector_total[2],
        vector_total[3],
        grad_cq,
        grad_cross_key,
        grad_cross_value,
        grad_co,
        vector_total[4],
        vector_total[5],
        grad_e,
        grad_r,
    )
    return (layer_outputs[None], input_grads[None], text_grad) + tuple(g[None] for g in ordered)


def solution(mesh):
    return jax.shard_map(
        per_device,
        mesh=mesh,
        in_specs=(
            P(None, "frame", None),
            P(),
            P(None, None, "frame", None),
            P(None, "frame", None),
            P("section", None),
            P("section", None),
            P("section", None, "head"),
            P("section", None, "head"),
            P("section", None, "head"),
            P("section", "head", None),
            P("section", None),
            P("section", None),
            P("section", None, "head"),
            P("section", None, "head"),
            P("section", None, "head"),
            P("section", "head", None),
            P("section", None),
            P("section", None),
            P("section", None, "head"),
            P("section", "head", None),
        ),
        out_specs=(
            P("section", None, "frame", None),
            P("section", None, "frame", None),
            P(None, None, "frame", None),
            P("section", "frame"),
            P("section", "frame"),
            P("section", "frame", "head"),
            P("section", "frame", "head"),
            P("section", "frame", "head"),
            P("section", ("head", "frame"), None),
            P("section", "frame"),
            P("section", "frame"),
            P("section", "frame", "head"),
            P("section", "frame", "head"),
            P("section", "frame", "head"),
            P("section", ("head", "frame"), None),
            P("section", "frame"),
            P("section", "frame"),
            P("section", "frame", "head"),
            P("section", ("head", "frame"), None),
        ),
        check_vma=False,
    )
```

```python
import jax
import jax.numpy as jnp
from jax import lax
from jax.experimental import pallas as pl
from jax.experimental.pallas import tpu as pltpu
from jax.sharding import PartitionSpec as P

HEAD = 64
TEXT = 64
ITEMS = 4

masked_score = -1e30
inv_sqrt_two = 0.7071067811865476
inv_sqrt_tau = 0.3989422804014327

MESH_IDS = pl.DeviceIdType.MESH
BUSY = pl.CostEstimate(flops=30_000_000_000, bytes_accessed=8_000_000, transcendentals=0)
LAG = 2
BLOCK = 128
VMEM_BYTES = 56 * 1024 * 1024
EPS = 1e-05


class Task:
    operands = ()
    outs = ()
    out_in_vmem = True
    scratch = ()
    greets = ()

    def bind(self, ins, outs, scratch):
        self.ins, self.out, self.room = ins, outs, scratch


def remote(source, landing, send_sem, recv_sem, target):
    return pltpu.make_async_remote_copy(
        src_ref=source,
        dst_ref=landing,
        send_sem=send_sem,
        recv_sem=recv_sem,
        device_id=target,
        device_id_type=MESH_IDS,
    )


def frame_partners():
    me = lax.axis_index("frame")
    return (me + 1 - 2 * lax.rem(me, 2), lax.rem(me + 2, 4), 3 - me)


def span(index, size):
    return pl.ds(pl.multiple_of(index * size, size), size)


class WeightTask(Task):
    out_in_vmem = False
    greets = ("section", "frame")

    def __init__(self, weight):
        self.operands = (weight,)
        self.outs = (jax.ShapeDtypeStruct(weight.shape, weight.dtype),)
        self.scratch = (pltpu.SemaphoreType.DMA((4,)),)
        self.half = weight.shape[0] // 2

    def copies(self):
        (sems,) = self.room
        core = lax.rem(lax.axis_index("frame"), 2)
        rows = span(core, self.half)
        other_section = {"section": 1 - lax.axis_index("section")}
        other_core = {"frame": frame_partners()[0]}
        over = remote(self.ins[0].at[rows], self.out[0].at[rows], sems.at[0], sems.at[1], other_section)
        on = remote(self.out[0].at[rows], self.out[0].at[rows], sems.at[2], sems.at[3], other_core)
        return over, on

    def begin(self):
        self.copies()[0].start()

    def steps(self):
        over, on = self.copies()

        def pass_on():
            over.wait_recv()
            on.start()

        def end():
            over.wait_send()
            on.wait()

        return [pass_on, end]


class ShareTask(Task):
    greets = ("frame",)

    def __init__(self, grad):
        rows, width = grad.shape
        self.share = rows // lax.axis_size("frame")
        self.operands = (grad,)
        self.outs = (jax.ShapeDtypeStruct((self.share, width), jnp.bfloat16),)
        self.scratch = (
            pltpu.VMEM((3, self.share, width), jnp.bfloat16),
            pltpu.VMEM((self.share, width), jnp.bfloat16),
            pltpu.SemaphoreType.DMA((3,)),
            pltpu.SemaphoreType.DMA((3,)),
            pltpu.SemaphoreType.DMA,
        )

    def copies(self):
        landing, own, send_sems, recv_sems, here = self.room
        me = lax.axis_index("frame")
        away = [
            remote(
                self.ins[0].at[span(partner, self.share)],
                landing.at[k],
                send_sems.at[k],
                recv_sems.at[k],
                {"frame": partner},
            )
            for k, partner in enumerate(frame_partners())
        ]
        return away, pltpu.make_async_copy(self.ins[0].at[span(me, self.share)], own, here)

    def begin(self):
        away, stay = self.copies()
        for copy in away[::-1]:
            copy.start()
        stay.start()

    def steps(self):
        away, stay = self.copies()

        def end():
            stay.wait()
            for copy in away:
                copy.wait()
            landing, own = self.room[:2]
            total = own[...].astype(jnp.float32)
            for k in range(3):
                total = total + landing[k].astype(jnp.float32)
            self.out[0][...] = total.astype(jnp.bfloat16)

        return [end]


class CrossTask(Task):
    greets = ("section",)

    def __init__(self, first, second, added):
        self.operands = (first, second)
        self.added = added
        self.out_in_vmem = added
        shape = first.shape
        if added:
            self.outs = (jax.ShapeDtypeStruct(shape, jnp.float32),)
            self.scratch = (pltpu.VMEM(shape, jnp.bfloat16),) * 2 + (pltpu.SemaphoreType.DMA((3,)),)
        else:
            self.outs = (jax.ShapeDtypeStruct(shape, first.dtype),)
            self.scratch = (pltpu.SemaphoreType.DMA((2,)),)

    def copies(self, given, kept):
        sems = self.room[-1]
        landing = self.room[0] if self.added else self.out[0]
        target = {"section": 1 - lax.axis_index("section")}
        copies = [remote(self.ins[given], landing, sems.at[0], sems.at[1], target)]
        if self.added:
            copies.append(pltpu.make_async_copy(self.ins[kept], self.room[1], sems.at[2]))
        return copies

    def begin(self):
        section = lax.axis_index("section")
        for which in (0, 1):

            @pl.when(section == which)
            def _():
                for copy in self.copies(1 - which, which):
                    copy.start()

    def steps(self):
        def end():
            for copy in self.copies(0, 1):
                copy.wait()
            if self.added:
                self.out[0][...] = self.room[0][...].astype(jnp.float32) + self.room[1][...].astype(
                    jnp.float32
                )

        return [end]


class TextTask(Task):
    out_in_vmem = False
    greets = ("section", "frame", "both")

    def __init__(self, states):
        micros, rows, width = states.shape
        self.operands = (states,)
        self.outs = (jax.ShapeDtypeStruct((2, 4, rows, width), states.dtype),)
        self.scratch = (pltpu.SemaphoreType.DMA((8,)), pltpu.SemaphoreType.DMA((8,)))

    def copies(self):
        send_sems, recv_sems = self.room
        section, me = lax.axis_index("section"), lax.axis_index("frame")
        landing = self.out[0].at[section, me]
        copies = []
        for far in (0, 1):
            micro = section if far == 0 else 1 - section
            for k, frame in enumerate((me,) + frame_partners()):
                slot = far * 4 + k
                source = self.ins[0].at[micro]
                if slot == 0:
                    copies.append(pltpu.make_async_copy(source, landing, send_sems.at[0]))
                    continue
                target = {"section": micro, "frame": frame}
                copies.append(remote(source, landing, send_sems.at[slot], recv_sems.at[slot], target))
        return copies

    def begin(self):
        for copy in self.copies():
            copy.start()

    def steps(self):
        def end():
            for copy in self.copies():
                copy.wait()

        return [end]


class TotalTask(Task):
    greets = ("section", "head")

    def __init__(self, part):
        rows, width = part.shape
        self.share = rows // 4
        self.operands = (part,)
        self.outs = (jax.ShapeDtypeStruct((rows, width), jnp.bfloat16),)
        piece = (self.share, width)
        self.scratch = (
            pltpu.VMEM((4,) + piece, jnp.bfloat16),
            pltpu.VMEM((2,) + piece, jnp.bfloat16),
            pltpu.SemaphoreType.DMA((4,)),
            pltpu.SemaphoreType.DMA((4,)),
            pltpu.SemaphoreType.DMA((2,)),
            pltpu.SemaphoreType.DMA((4,)),
            pltpu.SemaphoreType.DMA((4,)),
        )

    def partners(self):
        me = lax.axis_index("head")
        return [lax.rem(me + by, 4) for by in (1, 2, 3)]

    def spread(self):
        landing, _, send_sems, recv_sems = self.room[:4]
        me = lax.axis_index("head")
        away = [
            remote(
                self.ins[0].at[span(partner, self.share)],
                landing.at[by],
                send_sems.at[by],
                recv_sems.at[by],
                {"head": partner},
            )
            for by, partner in enumerate(self.partners(), 1)
        ]
        stay = pltpu.make_async_copy(self.ins[0].at[span(me, self.share)], landing.at[0], send_sems.at[0])
        return away + [stay]

    def over(self):
        sums, sems = self.room[1], self.room[4]
        target = {"section": 1 - lax.axis_index("section")}
        return remote(sums.at[0], sums.at[1], sems.at[0], sems.at[1], target)

    def gather(self):
        send_sems, recv_sems = self.room[5:]
        mine = self.out[0].at[span(lax.axis_index("head"), self.share)]
        return [
            remote(mine, mine, send_sems.at[by], recv_sems.at[by], {"head": partner})
            for by, partner in enumerate(self.partners(), 1)
        ]

    def begin(self):
        for copy in self.spread():
            copy.start()

    def steps(self):
        landing, sums = self.room[:2]

        def first():
            for copy in self.spread():
                copy.wait()
            total = landing[0].astype(jnp.float32)
            for by in (1, 2, 3):
                total = total + landing[by].astype(jnp.float32)
            sums[0] = total.astype(jnp.bfloat16)
            self.over().start()

        def second():
            self.over().wait()
            total = sums[0].astype(jnp.float32) + sums[1].astype(jnp.float32)
            self.out[0][span(lax.axis_index("head"), self.share), :] = total.astype(jnp.bfloat16)
            for copy in self.gather():
                copy.start()

        def third():
            for copy in self.gather():
                copy.wait()

        return [first, second, third]


class VectorTask(Task):
    greets = ("section", "frame")

    def __init__(self, grads):
        self.operands = (grads,)
        shape = grads.shape[1:]
        self.outs = (jax.ShapeDtypeStruct(shape, jnp.float32),)
        self.scratch = (
            pltpu.VMEM((4,) + grads.shape, jnp.float32),
            pltpu.VMEM((3,) + shape, jnp.float32),
            pltpu.SemaphoreType.DMA((4,)),
            pltpu.SemaphoreType.DMA((4,)),
            pltpu.SemaphoreType.DMA((2,)),
        )

    def spread(self):
        landing, _, send_sems, recv_sems, _ = self.room
        away = [
            remote(self.ins[0], landing.at[k], send_sems.at[k], recv_sems.at[k], {"frame": partner})
            for k, partner in enumerate(frame_partners(), 1)
        ]
        return away + [pltpu.make_async_copy(self.ins[0], landing.at[0], send_sems.at[0])]

    def over(self):
        sums, sems = self.room[1], self.room[4]
        target = {"section": 1 - lax.axis_index("section")}
        return remote(sums.at[0], sums.at[1], sems.at[0], sems.at[1], target)

    def begin(self):
        for copy in self.spread():
            copy.start()

    def steps(self):
        landing, sums = self.room[:2]
        section = lax.axis_index("section")

        def first():
            for copy in self.spread():
                copy.wait()
            total = [
                (landing[0, layer] + landing[1, layer]) + (landing[2, layer] + landing[3, layer])
                for layer in (0, 1)
            ]
            for which in (0, 1):

                @pl.when(section == which)
                def _():
                    sums[0] = total[1 - which]
                    sums[2] = total[which]

            self.over().start()

        def second():
            self.over().wait()
            self.out[0][...] = sums[2] + sums[1]

        return [first, second]


def greet(kinds):
    barrier = pltpu.get_barrier_semaphore()
    section, head, frame = (lax.axis_index(a) for a in ("section", "head", "frame"))
    targets = []
    if "frame" in kinds:
        targets += [{"frame": other} for other in frame_partners()]
    if "section" in kinds:
        targets.append({"section": 1 - section})
    if "both" in kinds:
        targets += [{"section": 1 - section, "frame": other} for other in frame_partners()]
    if "head" in kinds:
        targets += [{"head": lax.rem(head + by, 4)} for by in (1, 2, 3)]
    for target in targets:
        pl.semaphore_signal(barrier, 1, device_id=target, device_id_type=MESH_IDS)
    if "line" not in kinds or "head" in kinds:
        pl.semaphore_wait(barrier, len(targets))
        return

    for way in (-1, 1):
        other = head + way

        @pl.when((other >= 0) & (other < 4))
        def _():
            pl.semaphore_signal(barrier, 1, device_id={"head": other}, device_id_type=MESH_IDS)

    is_end = (head == 0) | (head == 3)

    @pl.when(is_end)
    def _():
        pl.semaphore_wait(barrier, len(targets) + 1)

    @pl.when(jnp.logical_not(is_end))
    def _():
        pl.semaphore_wait(barrier, len(targets) + 2)


def call(body, operands, outs, scratch, kinds, collective_id, tasks=(), picked=()):
    whole, anywhere = pl.BlockSpec(memory_space=pltpu.VMEM), pl.BlockSpec(memory_space=pl.ANY)
    in_specs, out_specs = [whole] * len(operands), [whole] * len(outs)
    operands, all_outs, scratch = list(operands), list(outs), list(scratch)
    n_plain, n_scratch = len(operands), len(scratch)
    for own, other, _ in picked:
        operands += [own, other]
        in_specs += [anywhere] * 2
        scratch.append(pltpu.VMEM(own.shape, own.dtype))
    if picked:
        scratch.append(pltpu.SemaphoreType.DMA((len(picked),)))
    counts = [(len(operands), len(outs), len(scratch))]
    kinds = set(kinds)
    for task in tasks:
        kinds |= set(task.greets)
        in_specs += [anywhere] * len(task.operands)
        out_specs += [whole if task.out_in_vmem else anywhere] * len(task.outs)
        operands += task.operands
        all_outs += task.outs
        scratch += task.scratch
        counts.append((len(task.operands), len(task.outs), len(task.scratch)))
    n_in, n_out = len(operands), len(all_outs)

    def kernel(*refs):
        groups = [list(refs[:n_in]), list(refs[n_in : n_in + n_out]), list(refs[n_in + n_out :])]
        bound = []
        for sizes in counts:
            bound.append([])
            for group, size in zip(groups, sizes):
                bound[-1].append(group[:size])
                del group[:size]
        for task, parts in zip(tasks, bound[1:]):
            task.bind(*parts)
        ins, main_outs, room = bound[0]
        section = lax.axis_index("section")

        def fetch(index, from_other):
            source = ins[n_plain + 2 * index + from_other]
            return pltpu.make_async_copy(source, room[n_scratch + index], room[-1].at[index])

        for index, (_, _, layer) in enumerate(picked):

            @pl.when(section == layer)
            def _():
                fetch(index, 0).start()

            @pl.when(section != layer)
            def _():
                fetch(index, 1).start()

        greet(kinds)
        for task in tasks:
            task.begin()
        for index in range(len(picked)):
            fetch(index, 0).wait()
        if body is not None:
            body(ins[:n_plain] + room[n_scratch : n_scratch + len(picked)], main_outs, room[:n_scratch])
        queues = [task.steps() for task in tasks]
        while any(queues):
            for queue in queues:
                if queue:
                    queue.pop(0)()

    results = pl.pallas_call(
        kernel,
        out_shape=all_outs,
        in_specs=in_specs,
        out_specs=out_specs,
        scratch_shapes=scratch,
        cost_estimate=BUSY,
        compiler_params=pltpu.CompilerParams(
            collective_id=collective_id, has_side_effects=True, vmem_limit_bytes=VMEM_BYTES
        ),
    )(*operands)
    results = list(results)
    main, results = results[: len(outs)], results[len(outs) :]
    carried = []
    for task in tasks:
        carried.append(results[: len(task.outs)])
        results = results[len(task.outs) :]
    return main, [c[0] for c in carried]


def chunking(rows):
    return max(1, min(16, rows // 16))


def nt_product(left, right):
    return lax.dot_general(left, right, (((1,), (1,)), ((), ())), preferred_element_type=jnp.float32)


def plain_product(left, right):
    return jnp.dot(left, right, preferred_element_type=jnp.float32)


def norm_parts(v):
    average = jnp.mean(v, axis=-1, keepdims=True)
    centered = v - average
    inverse = lax.rsqrt(jnp.mean(centered * centered, axis=-1, keepdims=True) + EPS)
    return centered * inverse, inverse


def line_scratch(rows, width):
    pieces = chunking(rows)
    return [pltpu.VMEM((rows, width), jnp.bfloat16)] * 4 + [pltpu.SemaphoreType.DMA((pieces,))] * 6


def line_sum(rows, room, partial_rows, finish_rows, prepare=None):
    send, recv, across, held, send_in, recv_in, send_across, recv_across, send_out, recv_out = room
    pieces = chunking(rows)
    place = lax.axis_index("head")
    step = rows // pieces
    per_block = max(1, BLOCK // step)
    is_end = (place == 0) | (place == 3)
    inner = {"head": jnp.where(place == 0, 1, 2)}
    outer = {"head": jnp.where(place == 1, 0, 3)}
    peer = {"head": 3 - place}

    def inwards(piece):
        at = span(piece, step)
        return remote(send.at[at], recv.at[at], send_in.at[piece], recv_in.at[piece], inner)

    def crossing(piece):
        at = span(piece, step)
        return remote(send.at[at], across.at[at], send_across.at[piece], recv_across.at[piece], peer)

    def outwards(piece):
        at = span(piece, step)
        return remote(held.at[at], held.at[at], send_out.at[piece], recv_out.at[piece], outer)

    def part_of(piece):
        if prepare is not None:

            @pl.when(lax.rem(piece, per_block) == 0)
            def _():
                prepare(lax.div(piece, per_block))

        return partial_rows(span(piece, step))

    @pl.when(is_end)
    def _():
        def give(piece, carry):
            send[span(piece, step), :] = part_of(piece).astype(jnp.bfloat16)
            inwards(piece).start()
            return carry

        lax.fori_loop(0, pieces, give, 0)

        def take(piece, carry):
            outwards(piece).wait_recv()
            finish_rows(span(piece, step), piece)
            return carry

        lax.fori_loop(0, pieces, take, 0)

        def drain(piece, carry):
            inwards(piece).wait_send()
            return carry

        lax.fori_loop(0, pieces, drain, 0)

    @pl.when(jnp.logical_not(is_end))
    def _():
        def add(piece):
            at = span(piece, step)
            part = part_of(piece)
            inwards(piece).wait_recv()
            send[at, :] = (part + recv[at, :].astype(jnp.float32)).astype(jnp.bfloat16)
            crossing(piece).start()

        def settle(piece):
            at = span(piece, step)
            crossing(piece).wait_recv()
            total = send[at, :].astype(jnp.float32) + across[at, :].astype(jnp.float32)
            held[at, :] = total.astype(jnp.bfloat16)
            outwards(piece).start()
            finish_rows(at, piece)

        lag = min(LAG, pieces)

        def both(t, carry):
            @pl.when(t < pieces)
            def _():
                add(t)

            @pl.when(t >= lag)
            def _():
                settle(t - lag)

            return carry

        lax.fori_loop(0, pieces + lag, both, 0)

        def drain(piece, carry):
            crossing(piece).wait_send()
            outwards(piece).wait_send()
            return carry

        lax.fori_loop(0, pieces, drain, 0)


def sum_forward(kind, layer, operands, weights, base, gain, shift, mode, collective_id, tasks):
    rows, width = base.shape
    wide = [jax.ShapeDtypeStruct((rows, width), jnp.float32)]
    low = jax.ShapeDtypeStruct((rows, width), jnp.bfloat16)
    outs = wide + [low] * {"norm": 1, "next": 2, "end": 0}[mode]
    n_main = len(outs)
    block = min(BLOCK, rows)
    scratch = line_scratch(rows, width)
    if kind == "self":
        columns = operands[0].shape[0]
        scratch.append(pltpu.VMEM((rows, columns), jnp.bfloat16))
    elif kind == "cross":
        columns = weights[0][0].shape[1]
        states = operands[1].shape[0]
        outs += [jax.ShapeDtypeStruct((rows, columns), jnp.bfloat16)] * 2
        scratch.append(pltpu.VMEM((columns, states), jnp.bfloat16))
    else:
        hidden = weights[0][0].shape[1]
        outs += [
            jax.ShapeDtypeStruct((rows, hidden), jnp.float32),
            jax.ShapeDtypeStruct((rows, hidden), jnp.bfloat16),
        ]

    def body(ins, outs, scratch):
        *parts, base, gain, shift = ins[: len(operands) + 3]
        matrices = ins[len(operands) + 3 :]
        room, extra = scratch[:10], scratch[10:]
        result = outs[0]
        prepare = None
        if kind == "self":
            (left,) = extra
            left[...] = parts[0][...].T
        elif kind == "cross":
            queries, left = outs[n_main:]
            normed, keys, values, seg = parts
            (values_t,) = extra
            values_t[...] = values[...].T

            def prepare(index):
                at = span(index, block)
                query = plain_product(normed[at, :], matrices[0][...]).astype(jnp.bfloat16)
                queries[at, :] = query
                query_t = query.T
                allowed = text_mask(states, seg[:, at])
                mixed = []
                for head in range(columns // HEAD):
                    cols = slice(head * HEAD, (head + 1) * HEAD)
                    scores = plain_product(keys[:, cols], query_t[cols, :]) * HEAD ** (-0.5)
                    scores = jnp.where(allowed, scores, masked_score)
                    e = jnp.exp(scores - jnp.max(scores, axis=0, keepdims=True))
                    total = jnp.sum(e, axis=0, keepdims=True)
                    value = plain_product(values_t[cols, :], e.astype(jnp.bfloat16))
                    mixed.append((value * (1.0 / total)).astype(jnp.bfloat16))
                left[at, :] = jnp.concatenate(mixed, axis=0).T

        else:
            before, left = outs[n_main:]
            (normed,) = parts

            def prepare(index):
                at = span(index, block)
                u = plain_product(normed[at, :], matrices[0][...])
                before[at, :] = u
                left[at, :] = (0.5 * u * (1.0 + lax.erf(u * inv_sqrt_two))).astype(jnp.bfloat16)

        def partial_rows(at):
            return plain_product(left[at, :], matrices[-1][...])

        def finish_rows(at, piece):
            value = base[at, :].astype(jnp.float32) + room[3][at, :].astype(jnp.float32)
            result[at, :] = value
            if mode == "next":
                rounded = value.astype(jnp.bfloat16)
                outs[2][at, :] = rounded
                value = rounded.astype(jnp.float32)
            if mode != "end":
                standard, _ = norm_parts(value)
                outs[1][at, :] = (standard * gain[...] + shift[...]).astype(jnp.bfloat16)

        line_sum(rows, room, partial_rows, finish_rows, prepare)

    return call(
        body, [*operands, base, gain[None], shift[None]], outs, scratch, ("line",), collective_id, tasks,
        [(*pair, layer) for pair in weights],
    )


def text_mask(states, seg):
    item = lax.rem(lax.div(lax.broadcasted_iota(jnp.int32, (states, 1), 0), TEXT // 4), ITEMS)
    return item == seg


def sum_backward(kind, layer, operands, weights, value, gain, upstream, collective_id, tasks, spare=None):
    rows, width = value.shape
    vector = jax.ShapeDtypeStruct((1, width), jnp.float32)
    low = jax.ShapeDtypeStruct((rows, width), jnp.bfloat16)
    outs = [jax.ShapeDtypeStruct((rows, width), jnp.float32), low, vector, vector]
    if spare is not None:
        outs.append(low)
    n_main = len(outs)
    block = min(BLOCK, rows)
    pieces = chunking(rows)
    scratch = line_scratch(rows, width)
    scratch += [pltpu.VMEM((pieces, 1, width), jnp.float32)] * 2
    scratch += [pltpu.SemaphoreType.DMA((pieces,))] * 2
    if kind == "self":
        columns = operands[0].shape[0]
        scratch.append(pltpu.VMEM((rows, columns), jnp.bfloat16))
    elif kind == "cross":
        columns = weights[0][0].shape[0]
        states = operands[2].shape[0]
        outs += [
            jax.ShapeDtypeStruct((rows, columns), jnp.bfloat16),
            jax.ShapeDtypeStruct((states, 2 * columns), jnp.bfloat16),
        ]
        scratch += [pltpu.VMEM((columns, states), jnp.bfloat16), pltpu.VMEM((states, 2 * columns), jnp.float32)]
    else:
        hidden = weights[0][0].shape[0]
        outs.append(jax.ShapeDtypeStruct((rows, hidden), jnp.bfloat16))

    def body(ins, outs, scratch):
        n_fixed = len(operands) + 3 + (spare is not None)
        *parts, value, gain, upstream = ins[: len(operands) + 3]
        matrices = ins[n_fixed:]
        room, (gain_parts, shift_parts, send_cross, recv_cross, *extra) = scratch[:10], scratch[10:]
        result, result_low, gain_grad, shift_grad = outs[:4]
        section = lax.axis_index("section")
        prepare = None
        if kind == "self":
            (left,) = extra
            left[...] = parts[0][...].T
        elif kind == "cross":
            left, state_grads = outs[n_main:]
            keys_t, sums = extra
            grad_low, queries, keys, values, seg = parts
            keys_t[...] = keys[...].T
            sums[...] = jnp.zeros_like(sums)

            def prepare(index):
                at = span(index, block)
                grad = nt_product(grad_low[at, :], matrices[0][...]).astype(jnp.bfloat16)
                query = queries[at, :]
                grad_t, query_t = grad.T, query.T
                allowed = text_mask(states, seg[:, at])
                query_grads = []
                for head in range(columns // HEAD):
                    cols = slice(head * HEAD, (head + 1) * HEAD)
                    more = slice(columns + head * HEAD, columns + (head + 1) * HEAD)
                    scores = plain_product(keys[:, cols], query_t[cols, :]) * HEAD ** (-0.5)
                    scores = jnp.where(allowed, scores, masked_score)
                    e = jnp.exp(scores - jnp.max(scores, axis=0, keepdims=True))
                    p = e * (1.0 / jnp.sum(e, axis=0, keepdims=True))
                    slope = plain_product(values[:, cols], grad_t[cols, :])
                    weighted = p * slope
                    ds = weighted - p * jnp.sum(weighted, axis=0, keepdims=True)
                    ds = ds.astype(jnp.bfloat16)
                    query_grads.append(
                        (plain_product(keys_t[cols, :], ds) * HEAD ** (-0.5)).astype(jnp.bfloat16)
                    )
                    sums[:, cols] += plain_product(ds, query[:, cols]) * HEAD ** (-0.5)
                    sums[:, more] += plain_product(p.astype(jnp.bfloat16), grad[:, cols])
                left[at, :] = jnp.concatenate(query_grads, axis=0).T

        else:
            (left,) = outs[n_main:]
            grad_out, before = parts

            def prepare(index):
                at = span(index, block)
                grad = nt_product(grad_out[at, :], matrices[0][...])
                u = before[at, :]
                slope = 0.5 * (1.0 + lax.erf(u * inv_sqrt_two)) + u * jnp.exp(-0.5 * u * u) * inv_sqrt_tau
                left[at, :] = (grad * slope).astype(jnp.bfloat16)

        def partial_rows(at):
            if kind == "self":
                return plain_product(left[at, :], matrices[-1][...])
            return nt_product(left[at, :], matrices[-1][...])

        def over(at, piece, source):
            target = {"section": 1 - section}
            return remote(source.at[at], outs[4].at[at], send_cross.at[piece], recv_cross.at[piece], target)

        def finish_rows(at, piece):
            grad = room[3][at, :].astype(jnp.float32)
            standard, inverse = norm_parts(value[at, :].astype(jnp.float32))
            scaled = grad * gain[...]
            through = inverse * (
                scaled
                - jnp.mean(scaled, axis=-1, keepdims=True)
                - standard * jnp.mean(scaled * standard, axis=-1, keepdims=True)
            )
            total = through + upstream[at, :].astype(jnp.float32)
            result[at, :] = total
            result_low[at, :] = total.astype(jnp.bfloat16)
            gain_parts[piece] = jnp.sum(grad * standard, axis=0, keepdims=True)
            shift_parts[piece] = jnp.sum(grad, axis=0, keepdims=True)
            if spare is not None:

                @pl.when(section == 0)
                def _():
                    over(at, piece, ins[len(operands) + 3]).start()

                @pl.when(section == 1)
                def _():
                    over(at, piece, result_low).start()

        line_sum(rows, room, partial_rows, finish_rows, prepare)
        gain_grad[...] = jnp.sum(gain_parts[...], axis=0)
        shift_grad[...] = jnp.sum(shift_parts[...], axis=0)
        if kind == "cross":
            state_grads[...] = sums[...].astype(jnp.bfloat16)
        if spare is not None:

            def drain(piece, carry):
                over(span(piece, rows // pieces), piece, result_low).wait()
                return carry

            lax.fori_loop(0, pieces, drain, 0)

    fixed = [*operands, value, gain[None], upstream]
    kinds = ("line",)
    if spare is not None:
        fixed.append(spare)
        kinds = ("line", "section")
    return call(
        body, fixed, outs, scratch, kinds, collective_id, tasks, [(*pair, layer) for pair in weights]
    )


def masked_scores(keys, query_t, begins, start):
    reach, block = keys.shape[0], query_t.shape[1]
    scores = plain_product(keys, query_t)
    key_pos = lax.broadcasted_iota(jnp.int32, (reach, 1), 0)
    query_pos = start + lax.broadcasted_iota(jnp.int32, (1, block), 1)
    allowed = (key_pos <= query_pos) & (key_pos >= begins)
    return jnp.where(allowed, scores * HEAD ** (-0.5), masked_score)


def to_frames(source, landing, sems):
    me = lax.axis_index("frame")
    send_sems, recv_sems = sems
    return [
        remote(source(other), landing(me), send_sems.at[k], recv_sems.at[k], {"frame": other})
        for k, other in enumerate(frame_partners())
    ]


def self_forward(normed, weight, begins, layer, collective_id, tasks):
    rows, frames, width = normed.shape[0], 4, 3 * HEAD
    dma = pltpu.SemaphoreType.DMA((frames - 1,))
    outs = [
        jax.ShapeDtypeStruct((width, rows * frames), jnp.bfloat16),
        jax.ShapeDtypeStruct((frames * HEAD, rows), jnp.bfloat16),
    ]
    scratch = [
        pltpu.VMEM((frames, width, rows), jnp.bfloat16),
        pltpu.VMEM((rows * frames, HEAD), jnp.bfloat16),
        pltpu.VMEM((frames, HEAD, rows), jnp.bfloat16),
        dma,
        dma,
        dma,
        dma,
    ]

    def body(ins, outs, scratch):
        normed, begins, weight = ins
        heads_t, out = outs
        own, keys, mixed_t, *sems = scratch
        me = lax.axis_index("frame")
        partners = frame_partners()
        block = min(2 * BLOCK, rows)
        arriving = to_frames(lambda g: own.at[g], lambda f: heads_t.at[:, span(f, rows)], sems[:2])
        leaving = to_frames(lambda g: mixed_t.at[g], lambda f: out.at[span(f, HEAD), :], sems[2:])

        def project(other):
            return nt_product(weight[span(other, width), :], normed[...]).astype(jnp.bfloat16)

        for k in (2, 1, 0):
            own[partners[k]] = project(partners[k])
            arriving[k].start()
        heads_t[:, span(me, rows)] = project(me)
        for copy in arriving:
            copy.wait()
        keys[...] = heads_t[HEAD : 2 * HEAD, :].T
        for target in range(frames):
            for start in range(target * rows, (target + 1) * rows, block):
                reach = start + block
                scores = masked_scores(
                    keys[:reach, :], heads_t[:HEAD, start:reach], begins[:, start:reach], start
                )
                e = jnp.exp(scores - jnp.max(scores, axis=0, keepdims=True))
                total = jnp.sum(e, axis=0, keepdims=True)
                mixed = plain_product(heads_t[2 * HEAD :, :reach], e.astype(jnp.bfloat16))
                at = start - target * rows
                mixed_t[target, :, at : at + block] = (mixed * (1.0 / total)).astype(jnp.bfloat16)

            for copy, other in zip(leaving, partners):

                @pl.when(other == target)
                def _():
                    copy.start()

        out[span(me, HEAD), :] = mixed_t[me]
        for copy in leaving:
            copy.wait()

    return call(
        body, [normed, begins], outs, scratch, ("frame",), collective_id, tasks, [(*weight, layer)]
    )


def self_backward(heads_t, grad_low, weight, begins, layer, collective_id, tasks):
    rows, frames, width = grad_low.shape[0], 4, 3 * HEAD
    all_rows = rows * frames
    dma = pltpu.SemaphoreType.DMA((frames - 1,))
    outs = [jax.ShapeDtypeStruct((frames * width, rows), jnp.bfloat16)]
    scratch = [
        pltpu.VMEM((frames, HEAD, rows), jnp.bfloat16),
        pltpu.VMEM((HEAD, all_rows), jnp.bfloat16),
        pltpu.VMEM((4, all_rows, HEAD), jnp.bfloat16),
        pltpu.VMEM((all_rows, HEAD), jnp.float32),
        pltpu.VMEM((all_rows, HEAD), jnp.float32),
        pltpu.VMEM((frames, width, rows), jnp.bfloat16),
        dma,
        dma,
        dma,
        dma,
    ]

    def body(ins, outs, scratch):
        heads_t, grad_low, begins, weight = ins
        (out,) = outs
        own, grad_t, columns, key_sum, value_sum, grads_t, *sems = scratch
        me = lax.axis_index("frame")
        partners = frame_partners()
        block = min(2 * BLOCK, rows)
        scale = HEAD ** (-0.5)
        arriving = to_frames(lambda g: own.at[g], lambda f: grad_t.at[:, span(f, rows)], sems[:2])
        leaving = to_frames(lambda g: grads_t.at[g], lambda f: out.at[span(f, width), :], sems[2:])

        def project(other):
            return nt_product(weight[span(other, HEAD), :], grad_low[...]).astype(jnp.bfloat16)

        for k in (2, 1, 0):
            own[partners[k]] = project(partners[k])
            arriving[k].start()
        grad_t[:, span(me, rows)] = project(me)
        key_sum[...] = jnp.zeros_like(key_sum)
        value_sum[...] = jnp.zeros_like(value_sum)
        for part in range(3):
            columns[part] = heads_t[part * HEAD : (part + 1) * HEAD, :].T
        for copy in arriving:
            copy.wait()
        columns[3] = grad_t[...].T
        for target in reversed(range(frames)):
            for start in reversed(range(target * rows, (target + 1) * rows, block)):
                reach = start + block
                scores = masked_scores(
                    columns[1, :reach, :], heads_t[:HEAD, start:reach], begins[:, start:reach], start
                )
                e = jnp.exp(scores - jnp.max(scores, axis=0, keepdims=True))
                p = e * (1.0 / jnp.sum(e, axis=0, keepdims=True))
                slope = plain_product(columns[2, :reach, :], grad_t[:, start:reach])
                weighted = p * slope
                ds = (weighted - p * jnp.sum(weighted, axis=0, keepdims=True)).astype(jnp.bfloat16)
                value_sum[:reach, :] += plain_product(p.astype(jnp.bfloat16), columns[3, start:reach, :])
                key_sum[:reach, :] += plain_product(ds, columns[0, start:reach, :])
                here = slice(start - target * rows, reach - target * rows)
                grads_t[target, :HEAD, here] = (
                    plain_product(heads_t[HEAD : 2 * HEAD, :reach], ds) * scale
                ).astype(jnp.bfloat16)
                grads_t[target, HEAD : 2 * HEAD, here] = (
                    (key_sum[start:reach, :] * scale).T.astype(jnp.bfloat16)
                )
                grads_t[target, 2 * HEAD :, here] = value_sum[start:reach, :].T.astype(jnp.bfloat16)

            for copy, other in zip(leaving, partners):

                @pl.when(other == target)
                def _():
                    copy.start()

        out[span(me, width), :] = grads_t[me]
        for copy in leaving:
            copy.wait()

    return call(
        body,
        [heads_t, grad_low, begins],
        outs,
        scratch,
        ("frame",),
        collective_id,
        tasks,
        [(*weight, layer)],
    )


def matmul(left_side, right_side):
    return jnp.dot(left_side, right_side, preferred_element_type=jnp.float32)


def matmul_tn(left_side, right_side):
    return lax.dot_general(
        left_side, right_side, (((0,), (0,)), ((), ())), preferred_element_type=jnp.float32
    )


def matmul_nt(left_side, right_side):
    return lax.dot_general(
        left_side, right_side, (((1,), (1,)), ((), ())), preferred_element_type=jnp.float32
    )


def layer_norm(signal, gain_vec, shift_vec):
    average = jnp.mean(signal, axis=-1, keepdims=True)
    centered = signal - average
    variance = jnp.mean(centered * centered, axis=-1, keepdims=True)
    return centered * lax.rsqrt(variance + 1e-05) * gain_vec + shift_vec


def norm_back(signal, gain_vec, upstream):
    average = jnp.mean(signal, axis=-1, keepdims=True)
    centered = signal - average
    inverse = lax.rsqrt(jnp.mean(centered * centered, axis=-1, keepdims=True) + 1e-05)
    standard = centered * inverse
    scaled = upstream * gain_vec
    through = inverse * (
        scaled
        - jnp.mean(scaled, axis=-1, keepdims=True)
        - standard * jnp.mean(scaled * standard, axis=-1, keepdims=True)
    )
    return (through, jnp.sum(upstream * standard, axis=0), jnp.sum(upstream, axis=0))


def head_total(partial_sum):
    return lax.psum(partial_sum.astype(jnp.bfloat16), "head").astype(jnp.float32)


def swapped(x):
    return lax.ppermute(x, "section", [(0, 1), (1, 0)])


def split_heads(matrix):
    return matrix.reshape(matrix.shape[0], matrix.shape[1] // HEAD, HEAD)


def softmax_rows(query, key_rows, allowed):
    logits = jnp.einsum(
        "qhd,khd->hqk",
        split_heads(query),
        split_heads(key_rows),
        preferred_element_type=jnp.float32,
    ) * HEAD ** (-0.5)
    logits = jnp.where(allowed[None], logits, masked_score)
    exponent = jnp.exp(logits - jnp.max(logits, axis=-1, keepdims=True))
    return exponent / jnp.sum(exponent, axis=-1, keepdims=True)


def attend(query, key_rows, value_rows, allowed):
    weights_low = softmax_rows(query, key_rows, allowed).astype(jnp.bfloat16)
    result = jnp.einsum(
        "hqk,khd->qhd", weights_low, split_heads(value_rows), preferred_element_type=jnp.float32
    )
    return result.reshape(query.shape).astype(jnp.bfloat16)


def attend_back(query, key_rows, value_rows, allowed, grad_out):
    probabilities = softmax_rows(query, key_rows, allowed)
    weights_low = probabilities.astype(jnp.bfloat16)
    grad_heads = split_heads(grad_out)
    grad_prob = jnp.einsum(
        "qhd,khd->hqk", grad_heads, split_heads(value_rows), preferred_element_type=jnp.float32
    )
    centre = jnp.sum(probabilities * grad_prob, axis=-1, keepdims=True)
    grad_logit = (probabilities * (grad_prob - centre)).astype(jnp.bfloat16)
    scale = HEAD ** (-0.5)
    grad_query = (
        jnp.einsum(
            "hqk,khd->qhd", grad_logit, split_heads(key_rows), preferred_element_type=jnp.float32
        )
        * scale
    )
    grad_keys = (
        jnp.einsum(
            "hqk,qhd->khd", grad_logit, split_heads(query), preferred_element_type=jnp.float32
        )
        * scale
    )
    grad_values = jnp.einsum(
        "hqk,qhd->khd", weights_low, grad_heads, preferred_element_type=jnp.float32
    )
    return (
        grad_query.reshape(query.shape),
        grad_keys.reshape(key_rows.shape),
        grad_values.reshape(value_rows.shape),
    )


def sum_rows(rows):
    return jnp.concatenate(rows, axis=0)


def on_four_frames(inputs, lengths, text, cotangent, vector_args, matrix_args):
    section = lax.axis_index("section")
    at_zero = section == 0
    frame_index = lax.axis_index("frame")
    micro_count, rows_dev, model_width = inputs.shape
    rows_all = rows_dev * 4
    (
        query_weight,
        key_weight,
        value_weight,
        output_weight,
        cross_query,
        cross_key,
        cross_value,
        cross_output,
        expand_weight,
        reduce_weight,
    ) = (w[0] for w in matrix_args)
    columns = query_weight.shape[1]
    heads = columns // HEAD

    def by_section(first, second):
        return jnp.where(at_zero, first, second)

    own_vectors = jnp.pad(jnp.concatenate(vector_args, axis=0), ((0, 2), (0, 0)))
    heads_weight = jnp.stack(
        [w.T.reshape(heads, HEAD, model_width) for w in (query_weight, key_weight, value_weight)], axis=1
    ).reshape(3 * columns, model_width)
    _, (other_heads, other_vectors) = call(
        None, [], [], [], (), 1, [WeightTask(heads_weight), CrossTask(own_vectors, own_vectors, False)]
    )
    vectors = [by_section(own_vectors, other_vectors), by_section(other_vectors, own_vectors)]
    heads_pair = (heads_weight, other_heads)
    text_local = text.reshape(-1, model_width)
    text_states = jnp.concatenate(
        [matmul(text_local, cross_key), matmul(text_local, cross_value)], axis=1
    ).astype(jnp.bfloat16)
    text_states = text_states.reshape(micro_count, -1, 2 * columns)

    item_ends = jnp.cumsum(lax.dynamic_index_in_dim(lengths, section, 0, keepdims=False))
    passed = jnp.arange(rows_all, dtype=jnp.int32)[None, :] >= item_ends[:, None]
    begins = jnp.max(jnp.where(passed, item_ends[:, None], 0), axis=0, keepdims=True).astype(jnp.int32)
    seg = jnp.sum(passed.astype(jnp.int32), axis=0, keepdims=True)
    seg = lax.dynamic_slice_in_dim(seg, frame_index * rows_dev, rows_dev, 1)

    entering = lax.dynamic_index_in_dim(inputs, section, 0, keepdims=False)
    normed = layer_norm(entering.astype(jnp.float32), vectors[0][0], vectors[0][1]).astype(jnp.bfloat16)
    saved, results = [], []
    for layer in range(2):
        gains = vectors[layer]
        first = layer == 0
        (heads_t, attended_t), carried = self_forward(
            normed,
            heads_pair,
            begins,
            layer,
            2 + layer,
            [
                WeightTask(output_weight),
                WeightTask(cross_query),
                WeightTask(cross_output),
                TextTask(text_states),
            ]
            if first
            else [],
        )
        if first:
            output_pair, query_pair, cross_pair = (
                (own, other) for own, other in zip((output_weight, cross_query, cross_output), carried)
            )
            states = carried[3].reshape(2, -1, 2 * columns)
        keys, values = states[layer, :, :columns], states[layer, :, columns:]
        (middle, second_normed), carried = sum_forward(
            "self",
            layer,
            [attended_t],
            [output_pair],
            entering,
            gains[2],
            gains[3],
            "norm",
            4 + layer,
            [WeightTask(expand_weight)] if first else [],
        )
        if first:
            expand_pair = (expand_weight, carried[0])
        (latter, third_normed, queries, cross_att), carried = sum_forward(
            "cross",
            layer,
            [second_normed, keys, values, seg],
            [query_pair, cross_pair],
            middle,
            gains[4],
            gains[5],
            "norm",
            6 + layer,
            [WeightTask(reduce_weight)] if first else [],
        )
        if first:
            reduce_pair = (reduce_weight, carried[0])
        after = vectors[1]
        (result, *lows, before, hidden), _ = sum_forward(
            "feed",
            layer,
            [third_normed],
            [expand_pair, reduce_pair],
            latter,
            after[0],
            after[1],
            "next" if first else "end",
            8 + layer,
            [],
        )
        saved.append(
            (
                entering,
                normed,
                heads_t,
                attended_t,
                middle,
                second_normed,
                queries,
                keys,
                values,
                cross_att,
                latter,
                third_normed,
                before,
                hidden,
            )
        )
        results.append(result)
        if first:
            normed, entering = lows

    upstream = lax.dynamic_index_in_dim(cotangent, section, 0, keepdims=False)
    grad_out = upstream.astype(jnp.bfloat16)
    in_grads, in_lows, vector_grads, shares = [None] * 2, [None] * 2, [None] * 2, [{}, {}]
    totals = {}

    def low_product(left, right):
        return matmul_tn(left, right).astype(jnp.bfloat16)

    for layer in (1, 0):
        last = layer == 0
        gains = vectors[layer]
        (
            entering,
            normed,
            heads_t,
            attended_t,
            middle,
            second_normed,
            queries,
            keys,
            values,
            cross_att,
            latter,
            third_normed,
            before,
            hidden,
        ) = saved[layer]
        mine, later = shares[layer], shares[1]

        def crossing(*names):
            return [CrossTask(mine[name], later[name], True) for name in names] if last else []

        tasks = [ShareTask(low_product(hidden, grad_out))]
        if not last:
            lows = (saved[1][0], results[1].astype(jnp.bfloat16))
            tasks.append(CrossTask(*lows, False))
        (grad_latter, grad_cross, third_gain_grad, third_shift_grad, grad_pre), carried = sum_backward(
            "feed",
            layer,
            [grad_out, before],
            [reduce_pair, expand_pair],
            latter,
            gains[4],
            upstream,
            10 + layer,
            tasks,
        )
        mine["reduce"] = carried[0]
        if not last:
            other_result = carried[1]

        tasks = [
            ShareTask(low_product(third_normed, grad_pre)),
            ShareTask(low_product(cross_att, grad_cross)),
        ]
        (grad_middle, grad_self, second_gain_grad, second_shift_grad, grad_queries, grad_states), carried = (
            sum_backward(
                "cross",
                layer,
                [grad_cross, queries, keys, values, seg],
                [cross_pair, query_pair],
                middle,
                gains[2],
                grad_latter,
                12 + layer,
                tasks + crossing("reduce"),
            )
        )
        mine["expand"], mine["cross_output"] = carried[:2]
        if last:
            totals["reduce"] = carried[2]

        tasks = [
            ShareTask(low_product(second_normed, grad_queries)),
            ShareTask(grad_states),
            ShareTask(matmul(attended_t, grad_self).astype(jnp.bfloat16)),
        ]
        (grad_heads_t,), carried = self_backward(
            heads_t,
            grad_self,
            output_pair,
            begins,
            layer,
            14 + layer,
            tasks + crossing("expand", "cross_output"),
        )
        mine["cross_query"], mine["states"], mine["output"] = carried[:3]
        if last:
            totals["expand"], totals["cross_output"] = carried[3:]

        grad_heads = lax.dot_general(
            normed, grad_heads_t, (((0,), (1,)), ((), ())), preferred_element_type=jnp.float32
        ).astype(jnp.bfloat16)
        tasks = [ShareTask(grad_heads)] + crossing("cross_query", "output")
        if last:
            tasks.append(CrossTask(mine["states"], later["states"], False))
        (in_grads[layer], in_lows[layer], first_gain_grad, first_shift_grad, *other_grad), carried = (
            sum_backward(
                "self",
                layer,
                [grad_heads_t],
                [heads_pair],
                entering,
                gains[0],
                grad_middle,
                16 + layer,
                tasks,
                in_lows[1] if last else None,
            )
        )
        mine["heads"] = carried[0]
        if last:
            totals["cross_query"], totals["output"], other_states = carried[1:]
        vector_grads[layer] = sum_rows(
            [
                first_gain_grad,
                first_shift_grad,
                second_gain_grad,
                second_shift_grad,
                third_gain_grad,
                third_shift_grad,
                jnp.zeros((2, model_width), jnp.float32),
            ]
        )
        grad_out = upstream = in_lows[layer]

    own_states = by_section(shares[0]["states"], shares[1]["states"])
    text_rows = sum_rows([by_section(own_states, other_states), by_section(other_states, own_states)])
    key_part, value_part = text_rows[:, :columns], text_rows[:, columns:]
    text_part = matmul_nt(key_part, cross_key) + matmul_nt(value_part, cross_value)
    _, (heads_total, text_grad, vector_total, cross_grads) = call(
        None,
        [],
        [],
        [],
        (),
        18,
        [
            CrossTask(shares[0]["heads"], shares[1]["heads"], True),
            TotalTask(text_part.astype(jnp.bfloat16)),
            VectorTask(jnp.stack(vector_grads)),
            ShareTask(low_product(text_local, text_rows)),
        ],
    )
    text_grad = text_grad.astype(jnp.float32).reshape(text.shape)
    vector_total = lax.dynamic_slice_in_dim(
        vector_total, frame_index * (model_width // 4), model_width // 4, 1
    )
    grad_query, grad_key, grad_value = (
        heads_total.reshape(-1, heads, 3, HEAD)[:, :, i].reshape(-1, columns) for i in range(3)
    )
    cross_grads = cross_grads.astype(jnp.float32)

    def both_micros(pair, other):
        own = by_section(*pair)
        other = other.astype(own.dtype)
        return jnp.where(at_zero, jnp.stack([own, other]), jnp.stack([other, own]))

    ordered = (
        vector_total[0],
        vector_total[1],
        grad_query,
        grad_key,
        grad_value,
        totals["output"],
        vector_total[2],
        vector_total[3],
        totals["cross_query"],
        cross_grads[:, :columns],
        cross_grads[:, columns:],
        totals["cross_output"],
        vector_total[4],
        vector_total[5],
        totals["expand"],
        totals["reduce"],
    )
    layer_outputs = both_micros(results, other_result)
    input_grads = both_micros(in_grads, other_grad[0])
    return (layer_outputs[None], input_grads[None], text_grad) + tuple(g[None] for g in ordered)


def self_attention(query, key_rows, value_rows, masks):
    all_keys = lax.all_gather(key_rows, "frame", axis=0, tiled=True)
    all_values = lax.all_gather(value_rows, "frame", axis=0, tiled=True)
    return attend(query, all_keys, all_values, masks["own"]), (query, all_keys, all_values)


def self_attention_back(kept, grad_out, masks):
    query, keys, values = kept
    grad_q, grad_k_all, grad_v_all = attend_back(query, keys, values, masks["own"], grad_out)
    grad_k, grad_v = (
        lax.psum_scatter(g.astype(jnp.bfloat16), "frame", scatter_dimension=0, tiled=True)
        for g in (grad_k_all, grad_v_all)
    )
    return grad_q.astype(jnp.bfloat16), grad_k, grad_v


def forward(entering, vectors, weights, cross_keys, cross_values, masks):
    first_gain, first_shift, second_gain, second_shift, third_gain, third_shift = vectors
    (
        query_weight,
        key_weight,
        value_weight,
        output_weight,
        cross_query,
        cross_output,
        expand_weight,
        reduce_weight,
    ) = weights
    signal = entering.astype(jnp.float32)
    first_normed = layer_norm(signal, first_gain, first_shift).astype(jnp.bfloat16)
    query = matmul(first_normed, query_weight).astype(jnp.bfloat16)
    key_rows = matmul(first_normed, key_weight).astype(jnp.bfloat16)
    value_rows = matmul(first_normed, value_weight).astype(jnp.bfloat16)
    attended, heads_kept = self_attention(query, key_rows, value_rows, masks)
    middle = signal + head_total(matmul(attended, output_weight))
    second_normed = layer_norm(middle, second_gain, second_shift).astype(jnp.bfloat16)
    cross_queries = matmul(second_normed, cross_query).astype(jnp.bfloat16)
    cross_att = attend(cross_queries, cross_keys, cross_values, masks["cross"])
    latter = middle + head_total(matmul(cross_att, cross_output))
    third_normed = layer_norm(latter, third_gain, third_shift).astype(jnp.bfloat16)
    hidden_pre = matmul(third_normed, expand_weight)
    hidden_act = jax.nn.gelu(hidden_pre, approximate=False).astype(jnp.bfloat16)
    result = latter + head_total(matmul(hidden_act, reduce_weight))
    saved = (
        signal,
        first_normed,
        heads_kept,
        attended,
        middle,
        second_normed,
        cross_queries,
        cross_att,
        latter,
        third_normed,
        hidden_pre,
        hidden_act,
    )
    return (result, saved)


def backward(saved, upstream, vectors, weights, cross_keys, cross_values, masks):
    first_gain, first_shift, second_gain, second_shift, third_gain, third_shift = vectors
    (
        query_weight,
        key_weight,
        value_weight,
        output_weight,
        cross_query,
        cross_output,
        expand_weight,
        reduce_weight,
    ) = weights
    (
        signal,
        first_normed,
        heads_kept,
        attended,
        middle,
        second_normed,
        cross_queries,
        cross_att,
        latter,
        third_normed,
        hidden_pre,
        hidden_act,
    ) = saved
    grad_out = upstream.astype(jnp.bfloat16)
    grad_reduce = matmul_tn(hidden_act, grad_out)
    grad_act = matmul_nt(grad_out, reduce_weight)
    slope = (
        0.5 * (1.0 + lax.erf(hidden_pre * inv_sqrt_two))
        + hidden_pre * jnp.exp(-0.5 * hidden_pre * hidden_pre) * inv_sqrt_tau
    )
    grad_pre = (grad_act * slope).astype(jnp.bfloat16)
    grad_expand = matmul_tn(third_normed, grad_pre)
    grad_third = head_total(matmul_nt(grad_pre, expand_weight))
    grad_latter, grad_third_gain, grad_third_shift = norm_back(latter, third_gain, grad_third)
    grad_latter = grad_latter + upstream
    grad_cross = grad_latter.astype(jnp.bfloat16)
    grad_cross_output = matmul_tn(cross_att, grad_cross)
    grad_cross_att = matmul_nt(grad_cross, cross_output).astype(jnp.bfloat16)
    grad_cq, grad_ck, grad_cv = attend_back(
        cross_queries, cross_keys, cross_values, masks["cross"], grad_cross_att
    )
    grad_text_rows = jnp.concatenate([grad_ck, grad_cv], axis=1).astype(jnp.bfloat16)
    grad_text_rows = lax.psum_scatter(
        grad_text_rows.reshape(ITEMS, TEXT, -1), "frame", scatter_dimension=1, tiled=True
    )
    grad_cquery = grad_cq.astype(jnp.bfloat16)
    grad_cross_query = matmul_tn(second_normed, grad_cquery)
    grad_second = head_total(matmul_nt(grad_cquery, cross_query))
    grad_middle, grad_second_gain, grad_second_shift = norm_back(middle, second_gain, grad_second)
    grad_middle = grad_middle + grad_latter
    grad_self = grad_middle.astype(jnp.bfloat16)
    grad_output = matmul_tn(attended, grad_self)
    grad_att = matmul_nt(grad_self, output_weight).astype(jnp.bfloat16)
    grad_query_low, grad_key_low, grad_value_low = self_attention_back(heads_kept, grad_att, masks)
    grad_query = matmul_tn(first_normed, grad_query_low)
    grad_key = matmul_tn(first_normed, grad_key_low)
    grad_value = matmul_tn(first_normed, grad_value_low)
    grad_first = head_total(
        matmul_nt(grad_query_low, query_weight)
        + matmul_nt(grad_key_low, key_weight)
        + matmul_nt(grad_value_low, value_weight)
    )
    grad_signal, grad_first_gain, grad_first_shift = norm_back(signal, first_gain, grad_first)
    grad_signal = grad_signal + grad_middle
    vector_grads = (
        grad_first_gain,
        grad_first_shift,
        grad_second_gain,
        grad_second_shift,
        grad_third_gain,
        grad_third_shift,
    )
    matrix_grads = (
        grad_query,
        grad_key,
        grad_value,
        grad_output,
        grad_cross_query,
        grad_cross_output,
        grad_expand,
        grad_reduce,
    )
    matrix_grads = tuple(
        lax.psum_scatter(g.astype(jnp.bfloat16), "frame", scatter_dimension=0, tiled=True)
        for g in matrix_grads
    )
    return grad_signal, vector_grads, matrix_grads, grad_text_rows


def per_device(
    inputs,
    lengths,
    text,
    cotangent,
    first_gain,
    first_shift,
    query_weight,
    key_weight,
    value_weight,
    output_weight,
    second_gain,
    second_shift,
    cross_query,
    cross_key,
    cross_value,
    cross_output,
    third_gain,
    third_shift,
    expand_weight,
    reduce_weight,
):
    head_count, frame_count = lax.axis_size("head"), lax.axis_size("frame")
    local_heads = query_weight.shape[2] // HEAD
    if head_count == 4 and frame_count == 4 and local_heads == 4:
        return on_four_frames(
            inputs,
            lengths,
            text,
            cotangent,
            (first_gain, first_shift, second_gain, second_shift, third_gain, third_shift),
            (
                query_weight,
                key_weight,
                value_weight,
                output_weight,
                cross_query,
                cross_key,
                cross_value,
                cross_output,
                expand_weight,
                reduce_weight,
            ),
        )
    section = lax.axis_index("section")
    at_zero = section == 0
    frame_index = lax.axis_index("frame")
    micro_count, rows_dev, model_width = inputs.shape
    rows_all = rows_dev * frame_count
    text_rows_dev = text.shape[2]

    def keep(pair):
        return jnp.where(at_zero, pair[0], pair[1])

    def give(pair):
        return jnp.where(at_zero, pair[1], pair[0])

    vector_args = jnp.concatenate(
        [first_gain, first_shift, second_gain, second_shift, third_gain, third_shift], axis=0
    )
    vectors = lax.all_gather(vector_args, "section")
    matrix_args = (
        query_weight,
        key_weight,
        value_weight,
        output_weight,
        cross_query,
        cross_output,
        expand_weight,
        reduce_weight,
    )
    matrices = [lax.all_gather(w[0], "section") for w in matrix_args]
    weights = [tuple(w[layer] for w in matrices) for layer in range(2)]

    text_full = lax.all_gather(text, "frame", axis=2, tiled=True)
    text_flat = text_full.reshape(micro_count * ITEMS * TEXT, model_width)
    text_heads = jnp.concatenate(
        [matmul(text_flat, cross_key[0]), matmul(text_flat, cross_value[0])], axis=1
    ).astype(jnp.bfloat16)
    text_heads = text_heads.reshape(micro_count, ITEMS * TEXT, -1)
    own_text = keep(text_heads)
    other_text = swapped(give(text_heads))
    columns = cross_key.shape[2]
    cross_states = [
        jnp.where(at_zero, own_text, other_text),
        jnp.where(at_zero, other_text, own_text),
    ]
    cross_keys = [c[:, :columns] for c in cross_states]
    cross_values = [c[:, columns:] for c in cross_states]

    item_ends = jnp.cumsum(lax.dynamic_index_in_dim(lengths, section, 0, keepdims=False))
    all_positions = jnp.arange(rows_all, dtype=jnp.int32)
    seg_all = jnp.sum((all_positions[:, None] >= item_ends[None, :]).astype(jnp.int32), axis=1)
    own_start = frame_index * rows_dev
    own_positions = own_start + jnp.arange(rows_dev, dtype=jnp.int32)
    seg_own = lax.dynamic_slice_in_dim(seg_all, own_start, rows_dev)
    text_item = jnp.arange(ITEMS * TEXT, dtype=jnp.int32) // TEXT
    masks = {
        "own": (all_positions[None, :] <= own_positions[:, None])
        & (seg_own[:, None] == seg_all[None, :]),
        "cross": seg_own[:, None] == text_item[None, :],
    }

    signal = lax.dynamic_index_in_dim(inputs, section, 0, keepdims=False)
    results, saves = [], []
    for layer in range(2):
        result, saved = forward(
            signal, vectors[layer], weights[layer], cross_keys[layer], cross_values[layer], masks
        )
        results.append(result)
        saves.append(saved)
        signal = result.astype(jnp.bfloat16)

    upstream = lax.dynamic_index_in_dim(cotangent, section, 0, keepdims=False)
    in_grads, vector_grads, matrix_grads, text_grads = [None] * 2, [None] * 2, [None] * 2, [None] * 2
    for layer in (1, 0):
        grad_signal, vector_grads[layer], matrix_grads[layer], text_grads[layer] = backward(
            saves[layer],
            upstream,
            vectors[layer],
            weights[layer],
            cross_keys[layer],
            cross_values[layer],
            masks,
        )
        in_grads[layer] = grad_signal
        upstream = grad_signal.astype(jnp.bfloat16).astype(jnp.float32)

    def both_micros(pair):
        own = keep(pair)
        other = swapped(give([p.astype(jnp.bfloat16) for p in pair])).astype(own.dtype)
        return jnp.stack([jnp.where(at_zero, own, other), jnp.where(at_zero, other, own)])

    layer_outputs = both_micros(results)
    input_grads = both_micros(in_grads)
    totals = [
        keep(pair).astype(jnp.float32) + swapped(give(pair)).astype(jnp.float32)
        for pair in zip(*matrix_grads)
    ]
    text_rows = both_micros(text_grads)
    text_rows = text_rows.reshape(micro_count * ITEMS * text_rows_dev, -1)
    key_part, value_part = text_rows[:, :columns], text_rows[:, columns:]
    text_local = text.reshape(-1, model_width)
    grad_cross_key, grad_cross_value = (
        lax.psum_scatter(
            matmul_tn(text_local, part).astype(jnp.bfloat16),
            "frame",
            scatter_dimension=0,
            tiled=True,
        ).astype(jnp.float32)
        for part in (key_part, value_part)
    )
    text_part = matmul_nt(key_part, cross_key[0]) + matmul_nt(value_part, cross_value[0])
    text_grad = lax.psum(text_part.astype(jnp.bfloat16), ("section", "head")).astype(jnp.float32)
    text_grad = text_grad.reshape(text.shape)

    stacked = jnp.stack([jnp.stack(v) for v in vector_grads])
    stacked = lax.psum_scatter(
        stacked.astype(jnp.bfloat16), "frame", scatter_dimension=2, tiled=True
    )
    vector_total = keep(stacked).astype(jnp.float32) + swapped(give(stacked)).astype(jnp.float32)

    grad_q, grad_k, grad_v, grad_o, grad_cq, grad_co, grad_e, grad_r = totals
    ordered = (
        vector_total[0],
        vector_total[1],
        grad_q,
        grad_k,
        grad_v,
        grad_o,
        vector_total[2],
        vector_total[3],
        grad_cq,
        grad_cross_key,
        grad_cross_value,
        grad_co,
        vector_total[4],
        vector_total[5],
        grad_e,
        grad_r,
    )
    return (layer_outputs[None], input_grads[None], text_grad) + tuple(g[None] for g in ordered)


def solution(mesh):
    return jax.shard_map(
        per_device,
        mesh=mesh,
        in_specs=(
            P(None, "frame", None),
            P(),
            P(None, None, "frame", None),
            P(None, "frame", None),
            P("section", None),
            P("section", None),
            P("section", None, "head"),
            P("section", None, "head"),
            P("section", None, "head"),
            P("section", "head", None),
            P("section", None),
            P("section", None),
            P("section", None, "head"),
            P("section", None, "head"),
            P("section", None, "head"),
            P("section", "head", None),
            P("section", None),
            P("section", None),
            P("section", None, "head"),
            P("section", "head", None),
        ),
        out_specs=(
            P("section", None, "frame", None),
            P("section", None, "frame", None),
            P(None, None, "frame", None),
            P("section", "frame"),
            P("section", "frame"),
            P("section", "frame", "head"),
            P("section", "frame", "head"),
            P("section", "frame", "head"),
            P("section", ("head", "frame"), None),
            P("section", "frame"),
            P("section", "frame"),
            P("section", "frame", "head"),
            P("section", "frame", "head"),
            P("section", "frame", "head"),
            P("section", ("head", "frame"), None),
            P("section", "frame"),
            P("section", "frame"),
            P("section", "frame", "head"),
            P("section", ("head", "frame"), None),
        ),
        check_vma=False,
    )
```

```python
import jax
import jax.numpy as jnp
from jax import lax
from jax.experimental import pallas as pl
from jax.experimental.pallas import tpu as pltpu
from jax.sharding import PartitionSpec as P

HEAD = 64
TEXT = 64
ITEMS = 4

masked_score = -1e30
inv_sqrt_two = 0.7071067811865476
inv_sqrt_tau = 0.3989422804014327

MESH_IDS = pl.DeviceIdType.MESH
BUSY = pl.CostEstimate(flops=30_000_000_000, bytes_accessed=8_000_000, transcendentals=0)
LAG = 2
BLOCK = 128
VMEM_BYTES = 56 * 1024 * 1024
EPS = 1e-05
SECTION, LINE, FRAME = "section", "head", "frame"
BOTH, LINE_ONLY, BY_SECTION = "both", "line", "one"
NORM, NEXT, END = range(3)


class Task:
    operands = ()
    outs = ()
    out_in_vmem = True
    scratch = ()
    greets = ()

    def bind(self, ins, outs, scratch):
        self.ins, self.out, self.room = ins, outs, scratch


def remote(source, landing, send_sem, recv_sem, target):
    return pltpu.make_async_remote_copy(
        src_ref=source,
        dst_ref=landing,
        send_sem=send_sem,
        recv_sem=recv_sem,
        device_id=target,
        device_id_type=MESH_IDS,
    )


def frame_partners():
    me = lax.axis_index(FRAME)
    return (me + 1 - 2 * lax.rem(me, 2), lax.rem(me + 2, 4), 3 - me)


def span(index, size):
    return pl.ds(pl.multiple_of(index * size, size), size)


class WeightTask(Task):
    out_in_vmem = False
    greets = (SECTION, FRAME)

    def __init__(self, weight):
        self.operands = (weight,)
        self.outs = (jax.ShapeDtypeStruct(weight.shape, weight.dtype),)
        self.scratch = (pltpu.SemaphoreType.DMA((4,)),)
        self.half = weight.shape[0] // 2

    def copies(self):
        (sems,) = self.room
        core = lax.rem(lax.axis_index(FRAME), 2)
        rows = span(core, self.half)
        other_section = {SECTION: 1 - lax.axis_index(SECTION)}
        other_core = {FRAME: frame_partners()[0]}
        over = remote(self.ins[0].at[rows], self.out[0].at[rows], sems.at[0], sems.at[1], other_section)
        on = remote(self.out[0].at[rows], self.out[0].at[rows], sems.at[2], sems.at[3], other_core)
        return over, on

    def begin(self):
        self.copies()[0].start()

    def steps(self):
        over, on = self.copies()

        def pass_on():
            over.wait_recv()
            on.start()

        def end():
            over.wait_send()
            on.wait()

        return [pass_on, end]


class ShareTask(Task):
    greets = (FRAME,)

    def __init__(self, grad):
        rows, width = grad.shape
        self.share = rows // lax.axis_size(FRAME)
        self.operands = (grad,)
        self.outs = (jax.ShapeDtypeStruct((self.share, width), jnp.bfloat16),)
        self.scratch = (
            pltpu.VMEM((3, self.share, width), jnp.bfloat16),
            pltpu.VMEM((self.share, width), jnp.bfloat16),
            pltpu.SemaphoreType.DMA((3,)),
            pltpu.SemaphoreType.DMA((3,)),
            pltpu.SemaphoreType.DMA,
        )

    def copies(self):
        landing, own, send_sems, recv_sems, here = self.room
        me = lax.axis_index(FRAME)
        away = [
            remote(
                self.ins[0].at[span(partner, self.share)],
                landing.at[k],
                send_sems.at[k],
                recv_sems.at[k],
                {FRAME: partner},
            )
            for k, partner in enumerate(frame_partners())
        ]
        return away, pltpu.make_async_copy(self.ins[0].at[span(me, self.share)], own, here)

    def begin(self):
        away, stay = self.copies()
        for copy in away[::-1]:
            copy.start()
        stay.start()

    def steps(self):
        away, stay = self.copies()

        def end():
            stay.wait()
            for copy in away:
                copy.wait()
            landing, own = self.room[:2]
            total = own[...].astype(jnp.float32)
            for k in range(3):
                total = total + landing[k].astype(jnp.float32)
            self.out[0][...] = total.astype(jnp.bfloat16)

        return [end]


class CrossTask(Task):
    greets = (SECTION,)

    def __init__(self, first, second, added):
        self.operands = (first, second)
        self.added = added
        self.out_in_vmem = added
        shape = first.shape
        if added:
            self.outs = (jax.ShapeDtypeStruct(shape, jnp.float32),)
            self.scratch = (pltpu.VMEM(shape, jnp.bfloat16),) * 2 + (pltpu.SemaphoreType.DMA((3,)),)
        else:
            self.outs = (jax.ShapeDtypeStruct(shape, first.dtype),)
            self.scratch = (pltpu.SemaphoreType.DMA((2,)),)

    def copies(self, given, kept):
        sems = self.room[-1]
        landing = self.room[0] if self.added else self.out[0]
        target = {SECTION: 1 - lax.axis_index(SECTION)}
        copies = [remote(self.ins[given], landing, sems.at[0], sems.at[1], target)]
        if self.added:
            copies.append(pltpu.make_async_copy(self.ins[kept], self.room[1], sems.at[2]))
        return copies

    def begin(self):
        section = lax.axis_index(SECTION)
        for which in (0, 1):

            @pl.when(section == which)
            def _():
                for copy in self.copies(1 - which, which):
                    copy.start()

    def steps(self):
        def end():
            for copy in self.copies(0, 1):
                copy.wait()
            if self.added:
                self.out[0][...] = self.room[0][...].astype(jnp.float32) + self.room[1][...].astype(
                    jnp.float32
                )

        return [end]


class TextTask(Task):
    out_in_vmem = False
    greets = (SECTION, FRAME, BOTH)

    def __init__(self, states):
        micros, rows, width = states.shape
        self.operands = (states,)
        self.outs = (jax.ShapeDtypeStruct((2, 4, rows, width), states.dtype),)
        self.scratch = (pltpu.SemaphoreType.DMA((8,)), pltpu.SemaphoreType.DMA((8,)))

    def copies(self):
        send_sems, recv_sems = self.room
        section, me = lax.axis_index(SECTION), lax.axis_index(FRAME)
        landing = self.out[0].at[section, me]
        copies = []
        for far in (0, 1):
            micro = section if far == 0 else 1 - section
            for k, frame in enumerate((me,) + frame_partners()):
                slot = far * 4 + k
                source = self.ins[0].at[micro]
                if slot == 0:
                    copies.append(pltpu.make_async_copy(source, landing, send_sems.at[0]))
                    continue
                target = {SECTION: micro, FRAME: frame}
                copies.append(remote(source, landing, send_sems.at[slot], recv_sems.at[slot], target))
        return copies

    def begin(self):
        for copy in self.copies():
            copy.start()

    def steps(self):
        def end():
            for copy in self.copies():
                copy.wait()

        return [end]


class TotalTask(Task):
    greets = (SECTION, LINE)

    def __init__(self, part):
        rows, width = part.shape
        self.share = rows // 4
        self.operands = (part,)
        self.outs = (jax.ShapeDtypeStruct((rows, width), jnp.bfloat16),)
        piece = (self.share, width)
        self.scratch = (
            pltpu.VMEM((4,) + piece, jnp.bfloat16),
            pltpu.VMEM((2,) + piece, jnp.bfloat16),
            pltpu.SemaphoreType.DMA((4,)),
            pltpu.SemaphoreType.DMA((4,)),
            pltpu.SemaphoreType.DMA((2,)),
            pltpu.SemaphoreType.DMA((4,)),
            pltpu.SemaphoreType.DMA((4,)),
        )

    def partners(self):
        me = lax.axis_index(LINE)
        return [lax.rem(me + by, 4) for by in (1, 2, 3)]

    def spread(self):
        landing, _, send_sems, recv_sems = self.room[:4]
        me = lax.axis_index(LINE)
        away = [
            remote(
                self.ins[0].at[span(partner, self.share)],
                landing.at[by],
                send_sems.at[by],
                recv_sems.at[by],
                {LINE: partner},
            )
            for by, partner in enumerate(self.partners(), 1)
        ]
        stay = pltpu.make_async_copy(self.ins[0].at[span(me, self.share)], landing.at[0], send_sems.at[0])
        return away + [stay]

    def over(self):
        sums, sems = self.room[1], self.room[4]
        target = {SECTION: 1 - lax.axis_index(SECTION)}
        return remote(sums.at[0], sums.at[1], sems.at[0], sems.at[1], target)

    def gather(self):
        send_sems, recv_sems = self.room[5:]
        mine = self.out[0].at[span(lax.axis_index(LINE), self.share)]
        return [
            remote(mine, mine, send_sems.at[by], recv_sems.at[by], {LINE: partner})
            for by, partner in enumerate(self.partners(), 1)
        ]

    def begin(self):
        for copy in self.spread():
            copy.start()

    def steps(self):
        landing, sums = self.room[:2]

        def first():
            for copy in self.spread():
                copy.wait()
            total = landing[0].astype(jnp.float32)
            for by in (1, 2, 3):
                total = total + landing[by].astype(jnp.float32)
            sums[0] = total.astype(jnp.bfloat16)
            self.over().start()

        def second():
            self.over().wait()
            total = sums[0].astype(jnp.float32) + sums[1].astype(jnp.float32)
            self.out[0][span(lax.axis_index(LINE), self.share), :] = total.astype(jnp.bfloat16)
            for copy in self.gather():
                copy.start()

        def third():
            for copy in self.gather():
                copy.wait()

        return [first, second, third]


class VectorTask(Task):
    greets = (SECTION, FRAME)

    def __init__(self, grads):
        self.operands = (grads,)
        shape = grads.shape[1:]
        self.outs = (jax.ShapeDtypeStruct(shape, jnp.float32),)
        self.scratch = (
            pltpu.VMEM((4,) + grads.shape, jnp.float32),
            pltpu.VMEM((3,) + shape, jnp.float32),
            pltpu.SemaphoreType.DMA((4,)),
            pltpu.SemaphoreType.DMA((4,)),
            pltpu.SemaphoreType.DMA((2,)),
        )

    def spread(self):
        landing, _, send_sems, recv_sems, _ = self.room
        away = [
            remote(self.ins[0], landing.at[k], send_sems.at[k], recv_sems.at[k], {FRAME: partner})
            for k, partner in enumerate(frame_partners(), 1)
        ]
        return away + [pltpu.make_async_copy(self.ins[0], landing.at[0], send_sems.at[0])]

    def over(self):
        sums, sems = self.room[1], self.room[4]
        target = {SECTION: 1 - lax.axis_index(SECTION)}
        return remote(sums.at[0], sums.at[1], sems.at[0], sems.at[1], target)

    def begin(self):
        for copy in self.spread():
            copy.start()

    def steps(self):
        landing, sums = self.room[:2]
        section = lax.axis_index(SECTION)

        def first():
            for copy in self.spread():
                copy.wait()
            total = [
                (landing[0, layer] + landing[1, layer]) + (landing[2, layer] + landing[3, layer])
                for layer in (0, 1)
            ]
            for which in (0, 1):

                @pl.when(section == which)
                def _():
                    sums[0] = total[1 - which]
                    sums[2] = total[which]

            self.over().start()

        def second():
            self.over().wait()
            self.out[0][...] = sums[2] + sums[1]

        return [first, second]


def greet(kinds):
    barrier = pltpu.get_barrier_semaphore()
    section, head, frame = (lax.axis_index(a) for a in (SECTION, LINE, FRAME))
    targets = []
    if FRAME in kinds:
        targets += [{FRAME: other} for other in frame_partners()]
    if SECTION in kinds:
        targets.append({SECTION: 1 - section})
    if BOTH in kinds:
        targets += [{SECTION: 1 - section, FRAME: other} for other in frame_partners()]
    if LINE in kinds:
        targets += [{LINE: lax.rem(head + by, 4)} for by in (1, 2, 3)]
    for target in targets:
        pl.semaphore_signal(barrier, 1, device_id=target, device_id_type=MESH_IDS)
    if LINE_ONLY not in kinds or LINE in kinds:
        pl.semaphore_wait(barrier, len(targets))
        return

    for way in (-1, 1):
        other = head + way

        @pl.when((other >= 0) & (other < 4))
        def _():
            pl.semaphore_signal(barrier, 1, device_id={LINE: other}, device_id_type=MESH_IDS)

    is_end = (head == 0) | (head == 3)

    @pl.when(is_end)
    def _():
        pl.semaphore_wait(barrier, len(targets) + 1)

    @pl.when(jnp.logical_not(is_end))
    def _():
        pl.semaphore_wait(barrier, len(targets) + 2)


def call(body, operands, outs, scratch, kinds, collective_id, tasks=(), in_vmem=True, end=None):
    whole, anywhere = pl.BlockSpec(memory_space=pltpu.VMEM), pl.BlockSpec(memory_space=pl.ANY)
    place = whole if in_vmem else anywhere
    in_specs, out_specs = [place] * len(operands), [place] * len(outs)
    operands, all_outs, scratch = list(operands), list(outs), list(scratch)
    counts = [(len(operands), len(outs), len(scratch))]
    kinds = set(kinds)
    for task in tasks:
        kinds |= set(task.greets)
        in_specs += [anywhere] * len(task.operands)
        out_specs += [whole if task.out_in_vmem else anywhere] * len(task.outs)
        operands += task.operands
        all_outs += task.outs
        scratch += task.scratch
        counts.append((len(task.operands), len(task.outs), len(task.scratch)))
    n_in, n_out = len(operands), len(all_outs)

    def kernel(*refs):
        groups = [list(refs[:n_in]), list(refs[n_in : n_in + n_out]), list(refs[n_in + n_out :])]
        bound = []
        for sizes in counts:
            bound.append([])
            for group, size in zip(groups, sizes):
                bound[-1].append(group[:size])
                del group[:size]
        for task, parts in zip(tasks, bound[1:]):
            task.bind(*parts)

        def meet():
            greet(kinds)

        def ride():
            for task in tasks:
                task.begin()

        if body is None:
            meet()
            ride()
        else:
            body(*bound[0], meet, ride)
        queues = [task.steps() for task in tasks]
        while any(queues):
            for queue in queues:
                if queue:
                    queue.pop(0)()
        if end is not None:
            end()

    results = pl.pallas_call(
        kernel,
        out_shape=all_outs,
        in_specs=in_specs,
        out_specs=out_specs,
        scratch_shapes=scratch,
        compiler_params=pltpu.CompilerParams(
            collective_id=collective_id, has_side_effects=True, vmem_limit_bytes=VMEM_BYTES
        ),
    )(*operands)
    results = list(results)
    main, results = results[: len(outs)], results[len(outs) :]
    return main, results


def chunking(rows):
    return max(1, min(16, rows // 16))


def nt_product(left, right):
    return lax.dot_general(left, right, (((1,), (1,)), ((), ())), preferred_element_type=jnp.float32)


def plain_product(left, right):
    return jnp.dot(left, right, preferred_element_type=jnp.float32)


def norm_parts(v):
    average = jnp.mean(v, axis=-1, keepdims=True)
    centered = v - average
    inverse = lax.rsqrt(jnp.mean(centered * centered, axis=-1, keepdims=True) + EPS)
    return centered * inverse, inverse


class Held:
    def __init__(self, shape, dtype, sources=(), choose=None, stage=0, kept=False):
        self.shape, self.dtype = tuple(shape), dtype
        self.sources, self.choose, self.stage, self.kept = sources, choose, stage, kept
        self.ref = self.far = self.sem = None

    def copy_in(self, index=0):
        source = self.far[index]
        if self.choose == BY_SECTION:
            source = source.at[lax.axis_index(SECTION)]
        return pltpu.make_async_copy(source, self.ref, self.sem)

    def start_in(self):
        if not isinstance(self.choose, int):
            self.copy_in().start()
            return
        section = lax.axis_index(SECTION)

        @pl.when(section == self.choose)
        def _():
            self.copy_in(0).start()

        @pl.when(section != self.choose)
        def _():
            self.copy_in(1).start()

    def write(self, at, value):
        self.ref[at, :] = value
        if self.kept:
            pltpu.make_async_copy(self.ref.at[at], self.far[0].at[at], self.sem).start()

    def drain(self):
        pltpu.make_async_copy(self.ref, self.far[0], self.sem).wait()


class Build:
    def __init__(self):
        self.helds, self.rooms, self.extras = [], [], []

    def add(self, held):
        self.helds.append(held)
        return held

    def arg(self, array, stage, choose=None):
        shape = array.shape[1:] if choose == BY_SECTION else array.shape
        return self.add(Held(shape, array.dtype, (array,), choose, stage))

    def pick(self, pair, layer, stage):
        return self.add(Held(pair[0].shape, pair[0].dtype, tuple(pair), layer, stage))

    def out(self, shape, dtype):
        return self.add(Held(shape, dtype, kept=True))

    def temp(self, shape, dtype):
        return self.add(Held(shape, dtype))

    def extra(self, scratch):
        self.extras.append(scratch)
        return len(self.extras) - 1


class Stage:
    def __init__(self, rows, width):
        self.rows, self.width = rows, width
        self.begin = self.prepare = self.partial = self.finish = None
        self.ends = []


def line_chain(stages, need):
    place = lax.axis_index(LINE)
    rows = stages[0].rows
    pieces = chunking(rows)
    step = rows // pieces
    per_block = max(1, min(BLOCK, rows) // step)
    lag = max(0, min(LAG, pieces - per_block))
    is_end = (place == 0) | (place == 3)
    inner = {LINE: jnp.where(place == 0, 1, 2)}
    outer = {LINE: jnp.where(place == 1, 0, 3)}
    peer = {LINE: 3 - place}

    def inwards(stage, piece):
        send, recv, _, _, send_sems, recv_sems = stage.room[:6]
        at = span(piece, step)
        return remote(send.at[at], recv.at[at], send_sems.at[piece], recv_sems.at[piece], inner)

    def crossing(stage, piece):
        send, _, across = stage.room[:3]
        send_sems, recv_sems = stage.room[6:8]
        at = span(piece, step)
        return remote(send.at[at], across.at[at], send_sems.at[piece], recv_sems.at[piece], peer)

    def outwards(stage, piece):
        held = stage.room[3]
        send_sems, recv_sems = stage.room[8:]
        at = span(piece, step)
        return remote(held.at[at], held.at[at], send_sems.at[piece], recv_sems.at[piece], outer)

    def open_stage(index):
        need(index)
        if stages[index].begin is not None:
            stages[index].begin()

    def loop(first, last, step_of):
        def one(piece, carry):
            step_of(piece)
            return carry

        lax.fori_loop(first, last, one, 0)

    @pl.when(is_end)
    def _():
        def give(stage, piece):
            at = span(piece, step)
            stage.room[0][at, :] = stage.partial(at).astype(jnp.bfloat16)
            inwards(stage, piece).start()

        def take(stage, piece):
            outwards(stage, piece).wait_recv()
            stage.finish(span(piece, step), piece)

        for index, stage in enumerate(stages):
            open_stage(index)

            def block_step(block):
                low, high = block * per_block, (block + 1) * per_block
                if index:
                    loop(low, high, lambda piece: take(stages[index - 1], piece))
                if stage.prepare is not None:
                    stage.prepare(block)
                loop(low, high, lambda piece: give(stage, piece))

            loop(0, pieces // per_block, block_step)
        loop(0, pieces, lambda piece: take(stages[-1], piece))
        for stage in stages:
            loop(0, pieces, lambda piece: inwards(stage, piece).wait_send())

    @pl.when(jnp.logical_not(is_end))
    def _():
        def add(stage, piece):
            if stage.prepare is not None:

                @pl.when(lax.rem(piece, per_block) == 0)
                def _():
                    stage.prepare(lax.div(piece, per_block))

            at = span(piece, step)
            send, recv = stage.room[:2]
            part = stage.partial(at)
            inwards(stage, piece).wait_recv()
            send[at, :] = (part + recv[at, :].astype(jnp.float32)).astype(jnp.bfloat16)
            crossing(stage, piece).start()

        def settle(stage, piece):
            at = span(piece, step)
            send, _, across, held = stage.room[:4]
            crossing(stage, piece).wait_recv()
            total = send[at, :].astype(jnp.float32) + across[at, :].astype(jnp.float32)
            held[at, :] = total.astype(jnp.bfloat16)
            outwards(stage, piece).start()
            stage.finish(at, piece)

        for index, stage in enumerate(stages):
            open_stage(index)

            def both(piece):
                add(stage, piece)

                @pl.when(piece >= lag)
                def _():
                    settle(stage, piece - lag)

                if index and lag:

                    @pl.when(piece < lag)
                    def _():
                        settle(stages[index - 1], pieces - lag + piece)

            loop(0, pieces, both)
        loop(pieces - lag, pieces, lambda piece: settle(stages[-1], piece))

        def drain(stage, piece):
            crossing(stage, piece).wait_send()
            outwards(stage, piece).wait_send()

        for stage in stages:
            loop(0, pieces, lambda piece: drain(stage, piece))

    for stage in stages:
        for end in stage.ends:
            end()


def run_build(build, body, kinds, collective_id, tasks):
    operands, outs, scratch = [], [], []
    for held in build.helds:
        operands += held.sources
        if held.kept:
            outs.append(jax.ShapeDtypeStruct(held.shape, held.dtype))
        scratch.append(pltpu.VMEM(held.shape, held.dtype))
    n_held = len(scratch)
    scratch += build.extras
    scratch.append(pltpu.SemaphoreType.DMA((n_held,)))
    reads = sorted((held for held in build.helds if held.sources), key=lambda held: held.stage)

    def need(stage):
        for held in reads:
            if held.stage == stage:
                held.copy_in().wait()

    def run(ins, outs, scratch, meet, ride):
        ins, outs = list(ins), list(outs)
        sems = scratch[-1]
        for index, held in enumerate(build.helds):
            held.ref, held.sem = scratch[index], sems.at[index]
            held.far = [ins.pop(0) for _ in held.sources]
            if held.kept:
                held.far = [outs.pop(0)]
        build.bound = scratch[n_held:-1]
        for held in reads:
            held.start_in()
        body(need, meet, ride)

    def end():
        for held in build.helds:
            if held.kept:
                held.drain()

    return call(run, operands, outs, scratch, kinds, collective_id, tasks, in_vmem=False, end=end)


def run_chain(build, stages, collective_id, tasks, kinds=(LINE_ONLY,)):
    slots = []
    for stage in stages:
        pieces = chunking(stage.rows)
        room = [pltpu.VMEM((stage.rows, stage.width), jnp.bfloat16)] * 4
        room += [pltpu.SemaphoreType.DMA((pieces,))] * 6
        slots.append([build.extra(scratch) for scratch in room])

    def body(need, meet, ride):
        for stage, places in zip(stages, slots):
            stage.room = [build.bound[place] for place in places]
        meet()
        ride()
        line_chain(stages, need)

    return run_build(build, body, kinds, collective_id, tasks)


def residual_norm(build, index, stage, base, gain, shift, mode):
    shape = (stage.rows, stage.width)
    result = build.out(shape, jnp.float32)
    normed = build.out(shape, jnp.bfloat16) if mode != END else None
    low = build.out(shape, jnp.bfloat16) if mode != NORM else None
    if mode != END:
        gain, shift = build.arg(gain[None], index), build.arg(shift[None], index)

    def finish(at, piece):
        value = base.ref[at, :].astype(jnp.float32) + stage.room[3][at, :].astype(jnp.float32)
        result.write(at, value)
        if low is not None:
            rounded = value.astype(jnp.bfloat16)
            low.write(at, rounded)
            value = rounded.astype(jnp.float32)
        if normed is not None:
            standard, _ = norm_parts(value)
            normed.write(at, (standard * gain.ref[...] + shift.ref[...]).astype(jnp.bfloat16))

    stage.finish = finish
    return result, normed, low


def self_out_stage(build, index, layer, attended_t, weight, base):
    rows, width = base.shape
    stage = Stage(rows, width)
    flipped, matrix = build.arg(attended_t, index), build.pick(weight, layer, index)
    left = build.temp(attended_t.shape[::-1], jnp.bfloat16)

    def begin():
        left.ref[...] = flipped.ref[...].T

    stage.begin = begin
    stage.partial = lambda at: plain_product(left.ref[at, :], matrix.ref[...])
    return stage


def text_mask(states, seg):
    item = lax.rem(lax.div(lax.broadcasted_iota(jnp.int32, (states, 1), 0), TEXT // 4), ITEMS)
    return item == seg


def cross_stage(build, index, layer, normed, states, seg, into, out_of):
    rows, width = normed.shape
    stage = Stage(rows, width)
    columns, block = into[0].shape[1], min(BLOCK, rows)
    states, seg = build.arg(states, index), build.arg(seg, index)
    into, out_of = build.pick(into, layer, index), build.pick(out_of, layer, index)
    queries = build.out((rows, columns), jnp.bfloat16)
    left = build.out((rows, columns), jnp.bfloat16)
    values_t = build.temp((columns, states.shape[0]), jnp.bfloat16)

    def begin():
        values_t.ref[...] = states.ref[:, columns:].T

    def prepare(number):
        at = span(number, block)
        query = plain_product(normed.ref[at, :], into.ref[...]).astype(jnp.bfloat16)
        queries.write(at, query)
        query_t = query.T
        allowed = text_mask(states.shape[0], seg.ref[:, at])
        mixed = []
        for head in range(columns // HEAD):
            cols = slice(head * HEAD, (head + 1) * HEAD)
            scores = plain_product(states.ref[:, cols], query_t[cols, :]) * HEAD ** (-0.5)
            scores = jnp.where(allowed, scores, masked_score)
            e = jnp.exp(scores - jnp.max(scores, axis=0, keepdims=True))
            total = jnp.sum(e, axis=0, keepdims=True)
            value = plain_product(values_t.ref[cols, :], e.astype(jnp.bfloat16))
            mixed.append((value * (1.0 / total)).astype(jnp.bfloat16))
        left.write(at, jnp.concatenate(mixed, axis=0).T)

    stage.begin, stage.prepare = begin, prepare
    stage.partial = lambda at: plain_product(left.ref[at, :], out_of.ref[...])
    return stage


def feed_stage(build, index, layer, normed, into, out_of):
    rows, width = normed.shape
    stage = Stage(rows, width)
    hidden, block = into[0].shape[1], min(BLOCK, rows)
    into, out_of = build.pick(into, layer, index), build.pick(out_of, layer, index)
    before = build.out((rows, hidden), jnp.float32)
    left = build.out((rows, hidden), jnp.bfloat16)

    def prepare(number):
        at = span(number, block)
        u = plain_product(normed.ref[at, :], into.ref[...])
        before.write(at, u)
        left.write(at, (0.5 * u * (1.0 + lax.erf(u * inv_sqrt_two))).astype(jnp.bfloat16))

    stage.prepare = prepare
    stage.partial = lambda at: plain_product(left.ref[at, :], out_of.ref[...])
    return stage


def norm_backward(build, index, stage, value, gain, upstream, kept, spare=None):
    shape = (stage.rows, stage.width)
    pieces = chunking(stage.rows)
    vector = (1, stage.width)
    by_section = BY_SECTION if value.ndim == 3 else None
    value, gain = build.arg(value, index, by_section), build.arg(gain[None], index)
    result = (build.out if kept else build.temp)(shape, jnp.float32)
    low = build.out(shape, jnp.bfloat16)
    gain_grad, shift_grad = build.out(vector, jnp.float32), build.out(vector, jnp.float32)
    parts = build.extra(pltpu.VMEM((2, pieces, 1, stage.width), jnp.float32))
    if spare is not None:
        spare = build.arg(spare, index)
        other = build.out(shape, jnp.bfloat16)
        sems = build.extra(pltpu.SemaphoreType.DMA((2, pieces)))

    def over(at, piece, source):
        target = {SECTION: 1 - lax.axis_index(SECTION)}
        pair = build.bound[sems]
        return remote(source.ref.at[at], other.ref.at[at], pair.at[0, piece], pair.at[1, piece], target)

    def finish(at, piece):
        grad = stage.room[3][at, :].astype(jnp.float32)
        standard, inverse = norm_parts(value.ref[at, :].astype(jnp.float32))
        scaled = grad * gain.ref[...]
        through = inverse * (
            scaled
            - jnp.mean(scaled, axis=-1, keepdims=True)
            - standard * jnp.mean(scaled * standard, axis=-1, keepdims=True)
        )
        total = through + upstream.ref[at, :].astype(jnp.float32)
        result.write(at, total)
        low.write(at, total.astype(jnp.bfloat16))
        build.bound[parts][0, piece] = jnp.sum(grad * standard, axis=0, keepdims=True)
        build.bound[parts][1, piece] = jnp.sum(grad, axis=0, keepdims=True)
        if spare is not None:
            section = lax.axis_index(SECTION)

            @pl.when(section == 0)
            def _():
                over(at, piece, spare).start()

            @pl.when(section == 1)
            def _():
                over(at, piece, low).start()

    def end():
        whole = slice(0, 1)
        gain_grad.write(whole, jnp.sum(build.bound[parts][0], axis=0))
        shift_grad.write(whole, jnp.sum(build.bound[parts][1], axis=0))
        if spare is not None:
            step = stage.rows // pieces

            def one(piece, carry):
                at = span(piece, step)
                over(at, piece, low).wait()
                pltpu.make_async_copy(other.ref.at[at], other.far[0].at[at], other.sem).start()
                return carry

            lax.fori_loop(0, pieces, one, 0)

    stage.finish = finish
    stage.ends.append(end)
    return result, low


def feed_back_stage(build, index, layer, grad_out, before, out_of, into):
    rows, width = grad_out.shape
    stage = Stage(rows, width)
    hidden, block = out_of[0].shape[0], min(BLOCK, rows)
    before = build.arg(before, index)
    out_of, into = build.pick(out_of, layer, index), build.pick(into, layer, index)
    left = build.out((rows, hidden), jnp.bfloat16)

    def prepare(number):
        at = span(number, block)
        grad = nt_product(grad_out.ref[at, :].astype(jnp.bfloat16), out_of.ref[...])
        u = before.ref[at, :]
        slope = 0.5 * (1.0 + lax.erf(u * inv_sqrt_two)) + u * jnp.exp(-0.5 * u * u) * inv_sqrt_tau
        left.write(at, (grad * slope).astype(jnp.bfloat16))

    stage.prepare = prepare
    stage.partial = lambda at: nt_product(left.ref[at, :], into.ref[...])
    return stage


def cross_back_stage(build, index, layer, grad_low, queries, states, seg, out_of, into):
    rows, width = grad_low.shape
    stage = Stage(rows, width)
    columns, block = out_of[0].shape[0], min(BLOCK, rows)
    queries, states, seg = (build.arg(array, index) for array in (queries, states, seg))
    out_of, into = build.pick(out_of, layer, index), build.pick(into, layer, index)
    left = build.out((rows, columns), jnp.bfloat16)
    state_grads = build.out(states.shape, jnp.bfloat16)
    keys_t = build.temp((columns, states.shape[0]), jnp.bfloat16)
    sums = build.temp(states.shape, jnp.float32)
    scale = HEAD ** (-0.5)

    def begin():
        keys_t.ref[...] = states.ref[:, :columns].T
        sums.ref[...] = jnp.zeros(sums.shape, jnp.float32)

    def prepare(number):
        at = span(number, block)
        grad = nt_product(grad_low.ref[at, :], out_of.ref[...]).astype(jnp.bfloat16)
        query = queries.ref[at, :]
        grad_t, query_t = grad.T, query.T
        allowed = text_mask(states.shape[0], seg.ref[:, at])
        query_grads = []
        for head in range(columns // HEAD):
            cols = slice(head * HEAD, (head + 1) * HEAD)
            more = slice(columns + head * HEAD, columns + (head + 1) * HEAD)
            scores = plain_product(states.ref[:, cols], query_t[cols, :]) * scale
            scores = jnp.where(allowed, scores, masked_score)
            e = jnp.exp(scores - jnp.max(scores, axis=0, keepdims=True))
            p = e * (1.0 / jnp.sum(e, axis=0, keepdims=True))
            slope = plain_product(states.ref[:, more], grad_t[cols, :])
            weighted = p * slope
            ds = (weighted - p * jnp.sum(weighted, axis=0, keepdims=True)).astype(jnp.bfloat16)
            query_grads.append((plain_product(keys_t.ref[cols, :], ds) * scale).astype(jnp.bfloat16))
            sums.ref[:, cols] += plain_product(ds, query[:, cols]) * scale
            sums.ref[:, more] += plain_product(p.astype(jnp.bfloat16), grad[:, cols])
        left.write(at, jnp.concatenate(query_grads, axis=0).T)

    def end():
        state_grads.write(slice(0, states.shape[0]), sums.ref[...].astype(jnp.bfloat16))

    stage.begin, stage.prepare = begin, prepare
    stage.partial = lambda at: nt_product(left.ref[at, :], into.ref[...])
    stage.ends.append(end)
    return stage


def self_in_stage(build, index, layer, grads_t, weight, width):
    columns, rows = grads_t.shape
    stage = Stage(rows, width)
    flipped, matrix = build.arg(grads_t, index), build.pick(weight, layer, index)
    left = build.temp((rows, columns), jnp.bfloat16)

    def begin():
        left.ref[...] = flipped.ref[...].T

    stage.begin = begin
    stage.partial = lambda at: plain_product(left.ref[at, :], matrix.ref[...])
    return stage


def forward_chain(
    layer, attended_t, entering, states, seg, gains, weights, collective_id, tasks
):
    output, query, cross, *more = weights
    build = Build()
    base = build.arg(entering, 0, BY_SECTION if entering.ndim == 3 else None)
    first = self_out_stage(build, 0, layer, attended_t, output, base)
    middle, second_normed, _ = residual_norm(build, 0, first, base, gains[2], gains[3], NORM)
    second = cross_stage(build, 1, layer, second_normed, states, seg, query, cross)
    latter, third_normed, _ = residual_norm(build, 1, second, middle, gains[4], gains[5], NORM)
    stages = [first, second]
    if more:
        stages.append(feed_stage(build, 2, layer, third_normed, *more))
        residual_norm(build, 2, stages[2], latter, None, None, END)
    return run_chain(build, stages, collective_id, tasks)


def feed_chain(layer, normed, latter, weights, after, collective_id):
    build = Build()
    normed, latter = build.arg(normed, 0), build.arg(latter, 0)
    stage = feed_stage(build, 0, layer, normed, *weights[3:])
    residual_norm(build, 0, stage, latter, after[0], after[1], NEXT)
    return run_chain(build, [stage], collective_id, [])


def backward_chain(
    layer, upstream, before, latter, queries, states, seg, middle, gains, weights, collective_id, tasks
):
    _, query, cross, expand, reduce = weights
    build = Build()
    arriving = build.arg(upstream, 0, BY_SECTION if upstream.ndim == 3 else None)
    first = feed_back_stage(build, 0, layer, arriving, before, reduce, expand)
    grad_latter, grad_cross = norm_backward(build, 0, first, latter, gains[4], arriving, False)
    second = cross_back_stage(build, 1, layer, grad_cross, queries, states, seg, cross, query)
    norm_backward(build, 1, second, middle, gains[2], grad_latter, True)
    return run_chain(build, [first, second], collective_id, tasks)


def last_chain(layer, grads_t, entering, gain, upstream, weight, spare, collective_id, tasks):
    build = Build()
    upstream = build.arg(upstream, 0)
    stage = self_in_stage(build, 0, layer, grads_t, weight, upstream.shape[1])
    norm_backward(build, 0, stage, entering, gain, upstream, True, spare)
    kinds = (LINE_ONLY,) if spare is None else (LINE_ONLY, SECTION)
    return run_chain(build, [stage], collective_id, tasks, kinds)


def masked_scores(keys, query_t, begins, start):
    reach, block = keys.shape[0], query_t.shape[1]
    scores = plain_product(keys, query_t)
    key_pos = lax.broadcasted_iota(jnp.int32, (reach, 1), 0)
    query_pos = start + lax.broadcasted_iota(jnp.int32, (1, block), 1)
    allowed = (key_pos <= query_pos) & (key_pos >= begins)
    return jnp.where(allowed, scores * HEAD ** (-0.5), masked_score)


def to_frames(source, landing, sems):
    me = lax.axis_index(FRAME)
    return [
        remote(source(other), landing(me), sems.at[0, k], sems.at[1, k], {FRAME: other})
        for k, other in enumerate(frame_partners())
    ]


def self_forward(normed, weight, begins, layer, collective_id, tasks):
    rows, frames, width = normed.shape[0], 4, 3 * HEAD
    all_rows = rows * frames
    build = Build()
    normed, begins, weight = build.arg(normed, 0), build.arg(begins, 1), build.pick(weight, layer, 0)
    heads_t = build.out((width, all_rows), jnp.bfloat16)
    out = build.out((frames * HEAD, rows), jnp.bfloat16)
    own = build.temp((frames, width, rows), jnp.bfloat16)
    keys = build.temp((all_rows, HEAD), jnp.bfloat16)
    mixed_t = build.temp((frames, HEAD, rows), jnp.bfloat16)
    sems = [build.extra(pltpu.SemaphoreType.DMA((2, frames - 1))) for _ in range(2)]

    def body(need, meet, ride):
        me = lax.axis_index(FRAME)
        partners = frame_partners()
        block = min(2 * BLOCK, rows)
        arriving = to_frames(
            lambda g: own.ref.at[g], lambda f: heads_t.ref.at[:, span(f, rows)], build.bound[sems[0]]
        )
        leaving = to_frames(
            lambda g: mixed_t.ref.at[g], lambda f: out.ref.at[span(f, HEAD), :], build.bound[sems[1]]
        )

        def project(other):
            return nt_product(weight.ref[span(other, width), :], normed.ref[...]).astype(jnp.bfloat16)

        meet()
        need(0)
        for k in (2, 1, 0):
            own.ref[partners[k]] = project(partners[k])
            arriving[k].start()
        ride()
        heads_t.ref[:, span(me, rows)] = project(me)
        need(1)
        for copy in arriving:
            copy.wait()
        pltpu.make_async_copy(heads_t.ref, heads_t.far[0], heads_t.sem).start()
        keys.ref[...] = heads_t.ref[HEAD : 2 * HEAD, :].T
        for target in range(frames):
            for start in range(target * rows, (target + 1) * rows, block):
                reach = start + block
                scores = masked_scores(
                    keys.ref[:reach, :], heads_t.ref[:HEAD, start:reach], begins.ref[:, start:reach], start
                )
                e = jnp.exp(scores - jnp.max(scores, axis=0, keepdims=True))
                total = jnp.sum(e, axis=0, keepdims=True)
                mixed = plain_product(heads_t.ref[2 * HEAD :, :reach], e.astype(jnp.bfloat16))
                at = start - target * rows
                mixed_t.ref[target, :, at : at + block] = (mixed * (1.0 / total)).astype(jnp.bfloat16)

            for copy, other in zip(leaving, partners):

                @pl.when(other == target)
                def _():
                    copy.start()

        out.ref[span(me, HEAD), :] = mixed_t.ref[me]
        for copy in leaving:
            copy.wait()
        pltpu.make_async_copy(out.ref, out.far[0], out.sem).start()

    return run_build(build, body, (FRAME,), collective_id, tasks)


def self_backward(heads_t, grad_low, weight, begins, layer, collective_id, tasks):
    rows, frames, width = grad_low.shape[0], 4, 3 * HEAD
    all_rows = rows * frames
    build = Build()
    heads_t, begins = build.arg(heads_t, 1), build.arg(begins, 1)
    grad_low, weight = build.arg(grad_low, 0), build.pick(weight, layer, 0)
    out = build.out((frames * width, rows), jnp.bfloat16)
    own = build.temp((frames, HEAD, rows), jnp.bfloat16)
    grad_t = build.temp((HEAD, all_rows), jnp.bfloat16)
    columns = build.temp((4, all_rows, HEAD), jnp.bfloat16)
    key_sum, value_sum = (build.temp((all_rows, HEAD), jnp.float32) for _ in range(2))
    grads_t = build.temp((frames, width, rows), jnp.bfloat16)
    sems = [build.extra(pltpu.SemaphoreType.DMA((2, frames - 1))) for _ in range(2)]

    def body(need, meet, ride):
        me = lax.axis_index(FRAME)
        partners = frame_partners()
        block = min(2 * BLOCK, rows)
        scale = HEAD ** (-0.5)
        arriving = to_frames(
            lambda g: own.ref.at[g], lambda f: grad_t.ref.at[:, span(f, rows)], build.bound[sems[0]]
        )
        leaving = to_frames(
            lambda g: grads_t.ref.at[g], lambda f: out.ref.at[span(f, width), :], build.bound[sems[1]]
        )

        def project(other):
            return nt_product(weight.ref[span(other, HEAD), :], grad_low.ref[...]).astype(jnp.bfloat16)

        meet()
        need(0)
        for k in (2, 1, 0):
            own.ref[partners[k]] = project(partners[k])
            arriving[k].start()
        ride()
        grad_t.ref[:, span(me, rows)] = project(me)
        key_sum.ref[...] = jnp.zeros(key_sum.shape, jnp.float32)
        value_sum.ref[...] = jnp.zeros(key_sum.shape, jnp.float32)
        need(1)
        for part in range(3):
            columns.ref[part] = heads_t.ref[part * HEAD : (part + 1) * HEAD, :].T
        for copy in arriving:
            copy.wait()
        columns.ref[3] = grad_t.ref[...].T
        for target in reversed(range(frames)):
            for start in reversed(range(target * rows, (target + 1) * rows, block)):
                reach = start + block
                scores = masked_scores(
                    columns.ref[1, :reach, :],
                    heads_t.ref[:HEAD, start:reach],
                    begins.ref[:, start:reach],
                    start,
                )
                e = jnp.exp(scores - jnp.max(scores, axis=0, keepdims=True))
                p = e * (1.0 / jnp.sum(e, axis=0, keepdims=True))
                slope = plain_product(columns.ref[2, :reach, :], grad_t.ref[:, start:reach])
                weighted = p * slope
                ds = (weighted - p * jnp.sum(weighted, axis=0, keepdims=True)).astype(jnp.bfloat16)
                value_sum.ref[:reach, :] += plain_product(
                    p.astype(jnp.bfloat16), columns.ref[3, start:reach, :]
                )
                key_sum.ref[:reach, :] += plain_product(ds, columns.ref[0, start:reach, :])
                here = slice(start - target * rows, reach - target * rows)
                query_grad = plain_product(heads_t.ref[HEAD : 2 * HEAD, :reach], ds) * scale
                grads_t.ref[target, :HEAD, here] = query_grad.astype(jnp.bfloat16)
                key_grad = key_sum.ref[start:reach, :] * scale
                grads_t.ref[target, HEAD : 2 * HEAD, here] = key_grad.T.astype(jnp.bfloat16)
                grads_t.ref[target, 2 * HEAD :, here] = value_sum.ref[start:reach, :].T.astype(jnp.bfloat16)

            for copy, other in zip(leaving, partners):

                @pl.when(other == target)
                def _():
                    copy.start()

        out.ref[span(me, width), :] = grads_t.ref[me]
        for copy in leaving:
            copy.wait()
        pltpu.make_async_copy(out.ref, out.far[0], out.sem).start()

    return run_build(build, body, (FRAME,), collective_id, tasks)


def matmul(left_side, right_side):
    return jnp.dot(left_side, right_side, preferred_element_type=jnp.float32)


def matmul_tn(left_side, right_side):
    return lax.dot_general(
        left_side, right_side, (((0,), (0,)), ((), ())), preferred_element_type=jnp.float32
    )


def matmul_nt(left_side, right_side):
    return lax.dot_general(
        left_side, right_side, (((1,), (1,)), ((), ())), preferred_element_type=jnp.float32
    )


def layer_norm(signal, gain_vec, shift_vec):
    average = jnp.mean(signal, axis=-1, keepdims=True)
    centered = signal - average
    variance = jnp.mean(centered * centered, axis=-1, keepdims=True)
    return centered * lax.rsqrt(variance + 1e-05) * gain_vec + shift_vec


def norm_back(signal, gain_vec, upstream):
    average = jnp.mean(signal, axis=-1, keepdims=True)
    centered = signal - average
    inverse = lax.rsqrt(jnp.mean(centered * centered, axis=-1, keepdims=True) + 1e-05)
    standard = centered * inverse
    scaled = upstream * gain_vec
    through = inverse * (
        scaled
        - jnp.mean(scaled, axis=-1, keepdims=True)
        - standard * jnp.mean(scaled * standard, axis=-1, keepdims=True)
    )
    return (through, jnp.sum(upstream * standard, axis=0), jnp.sum(upstream, axis=0))


def head_total(partial_sum):
    return lax.psum(partial_sum.astype(jnp.bfloat16), LINE).astype(jnp.float32)


def swapped(x):
    return lax.ppermute(x, SECTION, [(0, 1), (1, 0)])


def split_heads(matrix):
    return matrix.reshape(matrix.shape[0], matrix.shape[1] // HEAD, HEAD)


def softmax_rows(query, key_rows, allowed):
    logits = jnp.einsum(
        "qhd,khd->hqk",
        split_heads(query),
        split_heads(key_rows),
        preferred_element_type=jnp.float32,
    ) * HEAD ** (-0.5)
    logits = jnp.where(allowed[None], logits, masked_score)
    exponent = jnp.exp(logits - jnp.max(logits, axis=-1, keepdims=True))
    return exponent / jnp.sum(exponent, axis=-1, keepdims=True)


def attend(query, key_rows, value_rows, allowed):
    weights_low = softmax_rows(query, key_rows, allowed).astype(jnp.bfloat16)
    result = jnp.einsum(
        "hqk,khd->qhd", weights_low, split_heads(value_rows), preferred_element_type=jnp.float32
    )
    return result.reshape(query.shape).astype(jnp.bfloat16)


def attend_back(query, key_rows, value_rows, allowed, grad_out):
    probabilities = softmax_rows(query, key_rows, allowed)
    weights_low = probabilities.astype(jnp.bfloat16)
    grad_heads = split_heads(grad_out)
    grad_prob = jnp.einsum(
        "qhd,khd->hqk", grad_heads, split_heads(value_rows), preferred_element_type=jnp.float32
    )
    centre = jnp.sum(probabilities * grad_prob, axis=-1, keepdims=True)
    grad_logit = (probabilities * (grad_prob - centre)).astype(jnp.bfloat16)
    scale = HEAD ** (-0.5)
    grad_query = (
        jnp.einsum(
            "hqk,khd->qhd", grad_logit, split_heads(key_rows), preferred_element_type=jnp.float32
        )
        * scale
    )
    grad_keys = (
        jnp.einsum(
            "hqk,qhd->khd", grad_logit, split_heads(query), preferred_element_type=jnp.float32
        )
        * scale
    )
    grad_values = jnp.einsum(
        "hqk,qhd->khd", weights_low, grad_heads, preferred_element_type=jnp.float32
    )
    return (
        grad_query.reshape(query.shape),
        grad_keys.reshape(key_rows.shape),
        grad_values.reshape(value_rows.shape),
    )


def sum_rows(rows):
    return jnp.concatenate(rows, axis=0)


def on_four_frames(inputs, lengths, text, cotangent, vector_args, matrix_args):
    section = lax.axis_index(SECTION)
    at_zero = section == 0
    frame_index = lax.axis_index(FRAME)
    micro_count, rows_dev, model_width = inputs.shape
    rows_all = rows_dev * 4
    (
        query_weight,
        key_weight,
        value_weight,
        output_weight,
        cross_query,
        cross_key,
        cross_value,
        cross_output,
        expand_weight,
        reduce_weight,
    ) = (w[0] for w in matrix_args)
    columns = query_weight.shape[1]
    heads = columns // HEAD

    def by_section(first, second):
        return jnp.where(at_zero, first, second)

    own_vectors = jnp.pad(jnp.concatenate(vector_args, axis=0), ((0, 2), (0, 0)))
    heads_weight = jnp.stack(
        [w.T.reshape(heads, HEAD, model_width) for w in (query_weight, key_weight, value_weight)], axis=1
    ).reshape(3 * columns, model_width)
    _, (other_heads, other_vectors) = call(
        None, [], [], [], (), 1, [WeightTask(heads_weight), CrossTask(own_vectors, own_vectors, False)]
    )
    vectors = [by_section(own_vectors, other_vectors), by_section(other_vectors, own_vectors)]
    heads_pair = (heads_weight, other_heads)
    text_local = text.reshape(-1, model_width)
    text_states = jnp.concatenate(
        [matmul(text_local, cross_key), matmul(text_local, cross_value)], axis=1
    ).astype(jnp.bfloat16)
    text_states = text_states.reshape(micro_count, -1, 2 * columns)

    item_ends = jnp.cumsum(lax.dynamic_index_in_dim(lengths, section, 0, keepdims=False))
    passed = jnp.arange(rows_all, dtype=jnp.int32)[None, :] >= item_ends[:, None]
    begins = jnp.max(jnp.where(passed, item_ends[:, None], 0), axis=0, keepdims=True).astype(jnp.int32)
    seg = jnp.sum(passed.astype(jnp.int32), axis=0, keepdims=True)
    seg = lax.dynamic_slice_in_dim(seg, frame_index * rows_dev, rows_dev, 1)

    entering = inputs
    normed = layer_norm(
        lax.dynamic_index_in_dim(inputs, section, 0, keepdims=False).astype(jnp.float32),
        vectors[0][0],
        vectors[0][1],
    ).astype(jnp.bfloat16)
    saved, results = [], []
    for layer in range(2):
        gains, first = vectors[layer], layer == 0
        tasks = []
        if first:
            tasks = [WeightTask(w) for w in (output_weight, cross_query, cross_output)]
            tasks.append(TextTask(text_states))
        (heads_t, attended_t), carried = self_forward(
            normed, heads_pair, begins, layer, 2 + layer, tasks
        )
        tasks = []
        if first:
            weights = list(zip((output_weight, cross_query, cross_output), carried))
            states = carried[3].reshape(2, -1, 2 * columns)
            (middle, second_normed, queries, cross_att, latter, third_normed), carried = forward_chain(
                layer,
                attended_t,
                entering,
                states[layer],
                seg,
                gains,
                weights,
                4,
                [WeightTask(expand_weight), WeightTask(reduce_weight)],
            )
            weights += list(zip((expand_weight, reduce_weight), carried))
            (before, hidden, result, next_normed, result_low), _ = feed_chain(
                layer, third_normed, latter, weights, vectors[1], 5
            )
        else:
            outs, _ = forward_chain(
                layer, attended_t, entering, states[layer], seg, gains, weights, 6, []
            )
            (middle, second_normed, queries, cross_att, latter, third_normed) = outs[:6]
            before, hidden, result, result_low = outs[6:]
        saved.append(
            (
                entering,
                normed,
                heads_t,
                attended_t,
                middle,
                second_normed,
                latter,
                third_normed,
                queries,
                cross_att,
                before,
                hidden,
            )
        )
        results.append(result)
        if first:
            normed, entering = next_normed, result_low

    upstream = cotangent
    in_grads, in_lows, vector_grads, shares = [None] * 2, [None] * 2, [None] * 2, [{}, {}]
    totals = {}

    def low_product(left, right):
        return matmul_tn(left, right).astype(jnp.bfloat16)

    def crossing(*names):
        return [CrossTask(shares[0][name], shares[1][name], True) for name in names]

    def shared(layer, names, arrays):
        for name, array in zip(names, arrays):
            shares[layer][name] = array

    held_back = {}
    for layer in (1, 0):
        last = layer == 0
        gains = vectors[layer]
        (
            entering,
            normed,
            heads_t,
            attended_t,
            middle,
            second_normed,
            latter,
            third_normed,
            queries,
            cross_att,
            before,
            hidden,
        ) = saved[layer]
        if last:
            grad_out = in_lows[1]
        else:
            grad_out = lax.dynamic_index_in_dim(cotangent, section, 0, keepdims=False)
            grad_out = grad_out.astype(jnp.bfloat16)
        tasks = [ShareTask(low_product(hidden, grad_out))]
        if last:
            tasks += [ShareTask(grad) for grad in held_back.values()]
        else:
            tasks.append(CrossTask(saved[1][0], result_low, False))
        (
            grad_pre,
            grad_cross,
            third_gain_grad,
            third_shift_grad,
            grad_queries,
            grad_states,
            grad_middle,
            grad_self,
            second_gain_grad,
            second_shift_grad,
        ), carried = backward_chain(
            layer,
            upstream,
            before,
            latter,
            queries,
            states[layer],
            seg,
            middle,
            gains,
            weights,
            8 + layer,
            tasks,
        )
        shares[layer]["reduce"] = carried[0]
        if last:
            shared(1, held_back, carried[1:])
        else:
            other_result = carried[1]

        expand_grad = low_product(third_normed, grad_pre)
        tasks = [ShareTask(grad_states)]
        if last:
            tasks += [ShareTask(expand_grad)] + crossing("reduce")
        (grad_heads_t,), carried = self_backward(
            heads_t, grad_self, weights[0], begins, layer, 10 + layer, tasks
        )
        shares[layer]["states"] = carried[0]
        if last:
            shares[0]["expand"], totals["reduce"] = carried[1:]

        grads = {
            "cross_output": low_product(cross_att, grad_cross),
            "cross_query": low_product(second_normed, grad_queries),
            "output": matmul(attended_t, grad_self).astype(jnp.bfloat16),
            "heads": lax.dot_general(
                normed, grad_heads_t, (((0,), (1,)), ((), ())), preferred_element_type=jnp.float32
            ).astype(jnp.bfloat16),
        }
        if last:
            tasks = [ShareTask(grad) for grad in grads.values()] + crossing("expand")
            tasks.append(CrossTask(shares[0]["states"], shares[1]["states"], False))
        else:
            held_back = grads
            tasks = [ShareTask(expand_grad)]
        (in_grads[layer], in_lows[layer], first_gain_grad, first_shift_grad, *other_grad), carried = (
            last_chain(
                layer,
                grad_heads_t,
                entering,
                gains[0],
                grad_middle,
                heads_pair,
                in_lows[1] if last else None,
                12 + layer,
                tasks,
            )
        )
        if last:
            shared(0, grads, carried)
            totals["expand"], other_states = carried[len(grads) :]
        else:
            shares[1]["expand"] = carried[0]
        vector_grads[layer] = sum_rows(
            [
                first_gain_grad,
                first_shift_grad,
                second_gain_grad,
                second_shift_grad,
                third_gain_grad,
                third_shift_grad,
                jnp.zeros((2, model_width), jnp.float32),
            ]
        )
        upstream = in_lows[layer]

    own_states = by_section(shares[0]["states"], shares[1]["states"])
    text_rows = sum_rows([by_section(own_states, other_states), by_section(other_states, own_states)])
    key_part, value_part = text_rows[:, :columns], text_rows[:, columns:]
    text_part = matmul_nt(key_part, cross_key) + matmul_nt(value_part, cross_value)
    names = ("heads", "output", "cross_query", "cross_output")
    _, (text_grad, vector_total, cross_grads, *carried) = call(
        None,
        [],
        [],
        [],
        (),
        18,
        [
            TotalTask(text_part.astype(jnp.bfloat16)),
            VectorTask(jnp.stack(vector_grads)),
            ShareTask(low_product(text_local, text_rows)),
        ]
        + crossing(*names),
    )
    totals.update(zip(names, carried))
    text_grad = text_grad.astype(jnp.float32).reshape(text.shape)
    vector_total = lax.dynamic_slice_in_dim(
        vector_total, frame_index * (model_width // 4), model_width // 4, 1
    )
    grad_query, grad_key, grad_value = (
        totals["heads"].reshape(-1, heads, 3, HEAD)[:, :, i].reshape(-1, columns) for i in range(3)
    )
    cross_grads = cross_grads.astype(jnp.float32)

    def both_micros(pair, other):
        own = by_section(*pair)
        other = other.astype(own.dtype)
        return jnp.where(at_zero, jnp.stack([own, other]), jnp.stack([other, own]))

    ordered = (
        vector_total[0],
        vector_total[1],
        grad_query,
        grad_key,
        grad_value,
        totals["output"],
        vector_total[2],
        vector_total[3],
        totals["cross_query"],
        cross_grads[:, :columns],
        cross_grads[:, columns:],
        totals["cross_output"],
        vector_total[4],
        vector_total[5],
        totals["expand"],
        totals["reduce"],
    )
    layer_outputs = both_micros(results, other_result)
    input_grads = both_micros(in_grads, other_grad[0])
    return (layer_outputs[None], input_grads[None], text_grad) + tuple(g[None] for g in ordered)


def self_attention(query, key_rows, value_rows, masks):
    all_keys = lax.all_gather(key_rows, FRAME, axis=0, tiled=True)
    all_values = lax.all_gather(value_rows, FRAME, axis=0, tiled=True)
    return attend(query, all_keys, all_values, masks["own"]), (query, all_keys, all_values)


def self_attention_back(kept, grad_out, masks):
    query, keys, values = kept
    grad_q, grad_k_all, grad_v_all = attend_back(query, keys, values, masks["own"], grad_out)
    grad_k, grad_v = (
        lax.psum_scatter(g.astype(jnp.bfloat16), FRAME, scatter_dimension=0, tiled=True)
        for g in (grad_k_all, grad_v_all)
    )
    return grad_q.astype(jnp.bfloat16), grad_k, grad_v


def forward(entering, vectors, weights, cross_keys, cross_values, masks):
    first_gain, first_shift, second_gain, second_shift, third_gain, third_shift = vectors
    (
        query_weight,
        key_weight,
        value_weight,
        output_weight,
        cross_query,
        cross_output,
        expand_weight,
        reduce_weight,
    ) = weights
    signal = entering.astype(jnp.float32)
    first_normed = layer_norm(signal, first_gain, first_shift).astype(jnp.bfloat16)
    query = matmul(first_normed, query_weight).astype(jnp.bfloat16)
    key_rows = matmul(first_normed, key_weight).astype(jnp.bfloat16)
    value_rows = matmul(first_normed, value_weight).astype(jnp.bfloat16)
    attended, heads_kept = self_attention(query, key_rows, value_rows, masks)
    middle = signal + head_total(matmul(attended, output_weight))
    second_normed = layer_norm(middle, second_gain, second_shift).astype(jnp.bfloat16)
    cross_queries = matmul(second_normed, cross_query).astype(jnp.bfloat16)
    cross_att = attend(cross_queries, cross_keys, cross_values, masks["cross"])
    latter = middle + head_total(matmul(cross_att, cross_output))
    third_normed = layer_norm(latter, third_gain, third_shift).astype(jnp.bfloat16)
    hidden_pre = matmul(third_normed, expand_weight)
    hidden_act = jax.nn.gelu(hidden_pre, approximate=False).astype(jnp.bfloat16)
    result = latter + head_total(matmul(hidden_act, reduce_weight))
    saved = (
        signal,
        first_normed,
        heads_kept,
        attended,
        middle,
        second_normed,
        cross_queries,
        cross_att,
        latter,
        third_normed,
        hidden_pre,
        hidden_act,
    )
    return (result, saved)


def backward(saved, upstream, vectors, weights, cross_keys, cross_values, masks):
    first_gain, first_shift, second_gain, second_shift, third_gain, third_shift = vectors
    (
        query_weight,
        key_weight,
        value_weight,
        output_weight,
        cross_query,
        cross_output,
        expand_weight,
        reduce_weight,
    ) = weights
    (
        signal,
        first_normed,
        heads_kept,
        attended,
        middle,
        second_normed,
        cross_queries,
        cross_att,
        latter,
        third_normed,
        hidden_pre,
        hidden_act,
    ) = saved
    grad_out = upstream.astype(jnp.bfloat16)
    grad_reduce = matmul_tn(hidden_act, grad_out)
    grad_act = matmul_nt(grad_out, reduce_weight)
    slope = (
        0.5 * (1.0 + lax.erf(hidden_pre * inv_sqrt_two))
        + hidden_pre * jnp.exp(-0.5 * hidden_pre * hidden_pre) * inv_sqrt_tau
    )
    grad_pre = (grad_act * slope).astype(jnp.bfloat16)
    grad_expand = matmul_tn(third_normed, grad_pre)
    grad_third = head_total(matmul_nt(grad_pre, expand_weight))
    grad_latter, grad_third_gain, grad_third_shift = norm_back(latter, third_gain, grad_third)
    grad_latter = grad_latter + upstream
    grad_cross = grad_latter.astype(jnp.bfloat16)
    grad_cross_output = matmul_tn(cross_att, grad_cross)
    grad_cross_att = matmul_nt(grad_cross, cross_output).astype(jnp.bfloat16)
    grad_cq, grad_ck, grad_cv = attend_back(
        cross_queries, cross_keys, cross_values, masks["cross"], grad_cross_att
    )
    grad_text_rows = jnp.concatenate([grad_ck, grad_cv], axis=1).astype(jnp.bfloat16)
    grad_text_rows = lax.psum_scatter(
        grad_text_rows.reshape(ITEMS, TEXT, -1), FRAME, scatter_dimension=1, tiled=True
    )
    grad_cquery = grad_cq.astype(jnp.bfloat16)
    grad_cross_query = matmul_tn(second_normed, grad_cquery)
    grad_second = head_total(matmul_nt(grad_cquery, cross_query))
    grad_middle, grad_second_gain, grad_second_shift = norm_back(middle, second_gain, grad_second)
    grad_middle = grad_middle + grad_latter
    grad_self = grad_middle.astype(jnp.bfloat16)
    grad_output = matmul_tn(attended, grad_self)
    grad_att = matmul_nt(grad_self, output_weight).astype(jnp.bfloat16)
    grad_query_low, grad_key_low, grad_value_low = self_attention_back(heads_kept, grad_att, masks)
    grad_query = matmul_tn(first_normed, grad_query_low)
    grad_key = matmul_tn(first_normed, grad_key_low)
    grad_value = matmul_tn(first_normed, grad_value_low)
    grad_first = head_total(
        matmul_nt(grad_query_low, query_weight)
        + matmul_nt(grad_key_low, key_weight)
        + matmul_nt(grad_value_low, value_weight)
    )
    grad_signal, grad_first_gain, grad_first_shift = norm_back(signal, first_gain, grad_first)
    grad_signal = grad_signal + grad_middle
    vector_grads = (
        grad_first_gain,
        grad_first_shift,
        grad_second_gain,
        grad_second_shift,
        grad_third_gain,
        grad_third_shift,
    )
    matrix_grads = (
        grad_query,
        grad_key,
        grad_value,
        grad_output,
        grad_cross_query,
        grad_cross_output,
        grad_expand,
        grad_reduce,
    )
    matrix_grads = tuple(
        lax.psum_scatter(g.astype(jnp.bfloat16), FRAME, scatter_dimension=0, tiled=True)
        for g in matrix_grads
    )
    return grad_signal, vector_grads, matrix_grads, grad_text_rows


def per_device(
    inputs,
    lengths,
    text,
    cotangent,
    first_gain,
    first_shift,
    query_weight,
    key_weight,
    value_weight,
    output_weight,
    second_gain,
    second_shift,
    cross_query,
    cross_key,
    cross_value,
    cross_output,
    third_gain,
    third_shift,
    expand_weight,
    reduce_weight,
):
    head_count, frame_count = lax.axis_size(LINE), lax.axis_size(FRAME)
    local_heads = query_weight.shape[2] // HEAD
    if head_count == 4 and frame_count == 4 and local_heads == 4:
        return on_four_frames(
            inputs,
            lengths,
            text,
            cotangent,
            (first_gain, first_shift, second_gain, second_shift, third_gain, third_shift),
            (
                query_weight,
                key_weight,
                value_weight,
                output_weight,
                cross_query,
                cross_key,
                cross_value,
                cross_output,
                expand_weight,
                reduce_weight,
            ),
        )
    section = lax.axis_index(SECTION)
    at_zero = section == 0
    frame_index = lax.axis_index(FRAME)
    micro_count, rows_dev, model_width = inputs.shape
    rows_all = rows_dev * frame_count
    text_rows_dev = text.shape[2]

    def keep(pair):
        return jnp.where(at_zero, pair[0], pair[1])

    def give(pair):
        return jnp.where(at_zero, pair[1], pair[0])

    vector_args = jnp.concatenate(
        [first_gain, first_shift, second_gain, second_shift, third_gain, third_shift], axis=0
    )
    vectors = lax.all_gather(vector_args, SECTION)
    matrix_args = (
        query_weight,
        key_weight,
        value_weight,
        output_weight,
        cross_query,
        cross_output,
        expand_weight,
        reduce_weight,
    )
    matrices = [lax.all_gather(w[0], SECTION) for w in matrix_args]
    weights = [tuple(w[layer] for w in matrices) for layer in range(2)]

    text_full = lax.all_gather(text, FRAME, axis=2, tiled=True)
    text_flat = text_full.reshape(micro_count * ITEMS * TEXT, model_width)
    text_heads = jnp.concatenate(
        [matmul(text_flat, cross_key[0]), matmul(text_flat, cross_value[0])], axis=1
    ).astype(jnp.bfloat16)
    text_heads = text_heads.reshape(micro_count, ITEMS * TEXT, -1)
    own_text = keep(text_heads)
    other_text = swapped(give(text_heads))
    columns = cross_key.shape[2]
    cross_states = [
        jnp.where(at_zero, own_text, other_text),
        jnp.where(at_zero, other_text, own_text),
    ]
    cross_keys = [c[:, :columns] for c in cross_states]
    cross_values = [c[:, columns:] for c in cross_states]

    item_ends = jnp.cumsum(lax.dynamic_index_in_dim(lengths, section, 0, keepdims=False))
    all_positions = jnp.arange(rows_all, dtype=jnp.int32)
    seg_all = jnp.sum((all_positions[:, None] >= item_ends[None, :]).astype(jnp.int32), axis=1)
    own_start = frame_index * rows_dev
    own_positions = own_start + jnp.arange(rows_dev, dtype=jnp.int32)
    seg_own = lax.dynamic_slice_in_dim(seg_all, own_start, rows_dev)
    text_item = jnp.arange(ITEMS * TEXT, dtype=jnp.int32) // TEXT
    masks = {
        "own": (all_positions[None, :] <= own_positions[:, None])
        & (seg_own[:, None] == seg_all[None, :]),
        "cross": seg_own[:, None] == text_item[None, :],
    }

    signal = lax.dynamic_index_in_dim(inputs, section, 0, keepdims=False)
    results, saves = [], []
    for layer in range(2):
        result, saved = forward(
            signal, vectors[layer], weights[layer], cross_keys[layer], cross_values[layer], masks
        )
        results.append(result)
        saves.append(saved)
        signal = result.astype(jnp.bfloat16)

    upstream = lax.dynamic_index_in_dim(cotangent, section, 0, keepdims=False)
    in_grads, vector_grads, matrix_grads, text_grads = [None] * 2, [None] * 2, [None] * 2, [None] * 2
    for layer in (1, 0):
        grad_signal, vector_grads[layer], matrix_grads[layer], text_grads[layer] = backward(
            saves[layer],
            upstream,
            vectors[layer],
            weights[layer],
            cross_keys[layer],
            cross_values[layer],
            masks,
        )
        in_grads[layer] = grad_signal
        upstream = grad_signal.astype(jnp.bfloat16).astype(jnp.float32)

    def both_micros(pair):
        own = keep(pair)
        other = swapped(give([p.astype(jnp.bfloat16) for p in pair])).astype(own.dtype)
        return jnp.stack([jnp.where(at_zero, own, other), jnp.where(at_zero, other, own)])

    layer_outputs = both_micros(results)
    input_grads = both_micros(in_grads)
    totals = [
        keep(pair).astype(jnp.float32) + swapped(give(pair)).astype(jnp.float32)
        for pair in zip(*matrix_grads)
    ]
    text_rows = both_micros(text_grads)
    text_rows = text_rows.reshape(micro_count * ITEMS * text_rows_dev, -1)
    key_part, value_part = text_rows[:, :columns], text_rows[:, columns:]
    text_local = text.reshape(-1, model_width)
    grad_cross_key, grad_cross_value = (
        lax.psum_scatter(
            matmul_tn(text_local, part).astype(jnp.bfloat16),
            FRAME,
            scatter_dimension=0,
            tiled=True,
        ).astype(jnp.float32)
        for part in (key_part, value_part)
    )
    text_part = matmul_nt(key_part, cross_key[0]) + matmul_nt(value_part, cross_value[0])
    text_grad = lax.psum(text_part.astype(jnp.bfloat16), (SECTION, LINE)).astype(jnp.float32)
    text_grad = text_grad.reshape(text.shape)

    stacked = jnp.stack([jnp.stack(v) for v in vector_grads])
    stacked = lax.psum_scatter(
        stacked.astype(jnp.bfloat16), FRAME, scatter_dimension=2, tiled=True
    )
    vector_total = keep(stacked).astype(jnp.float32) + swapped(give(stacked)).astype(jnp.float32)

    grad_q, grad_k, grad_v, grad_o, grad_cq, grad_co, grad_e, grad_r = totals
    ordered = (
        vector_total[0],
        vector_total[1],
        grad_q,
        grad_k,
        grad_v,
        grad_o,
        vector_total[2],
        vector_total[3],
        grad_cq,
        grad_cross_key,
        grad_cross_value,
        grad_co,
        vector_total[4],
        vector_total[5],
        grad_e,
        grad_r,
    )
    return (layer_outputs[None], input_grads[None], text_grad) + tuple(g[None] for g in ordered)


def solution(mesh):
    return jax.shard_map(
        per_device,
        mesh=mesh,
        in_specs=(
            P(None, FRAME, None),
            P(),
            P(None, None, FRAME, None),
            P(None, FRAME, None),
            P(SECTION, None),
            P(SECTION, None),
            P(SECTION, None, LINE),
            P(SECTION, None, LINE),
            P(SECTION, None, LINE),
            P(SECTION, LINE, None),
            P(SECTION, None),
            P(SECTION, None),
            P(SECTION, None, LINE),
            P(SECTION, None, LINE),
            P(SECTION, None, LINE),
            P(SECTION, LINE, None),
            P(SECTION, None),
            P(SECTION, None),
            P(SECTION, None, LINE),
            P(SECTION, LINE, None),
        ),
        out_specs=(
            P(SECTION, None, FRAME, None),
            P(SECTION, None, FRAME, None),
            P(None, None, FRAME, None),
            P(SECTION, FRAME),
            P(SECTION, FRAME),
            P(SECTION, FRAME, LINE),
            P(SECTION, FRAME, LINE),
            P(SECTION, FRAME, LINE),
            P(SECTION, (LINE, FRAME), None),
            P(SECTION, FRAME),
            P(SECTION, FRAME),
            P(SECTION, FRAME, LINE),
            P(SECTION, FRAME, LINE),
            P(SECTION, FRAME, LINE),
            P(SECTION, (LINE, FRAME), None),
            P(SECTION, FRAME),
            P(SECTION, FRAME),
            P(SECTION, FRAME, LINE),
            P(SECTION, (LINE, FRAME), None),
        ),
        check_vma=False,
    )
```

```python
import jax
import jax.numpy as jnp
from jax import lax
from jax.experimental import pallas as pl
from jax.experimental.pallas import tpu as pltpu
from jax.sharding import PartitionSpec as P

HEAD = 64
TEXT = 64
ITEMS = 4

masked_score = -1e30
inv_sqrt_two = 0.7071067811865476
inv_sqrt_tau = 0.3989422804014327

MESH_IDS = pl.DeviceIdType.MESH
BUSY = pl.CostEstimate(flops=30_000_000_000, bytes_accessed=8_000_000, transcendentals=0)
LAG = 3
BLOCK = 128
VMEM_BYTES = 56 * 1024 * 1024
EPS = 1e-05
SECTION, LINE, FRAME = "section", "head", "frame"
BOTH, LINE_ONLY, BY_SECTION = "both", "line", "one"
NORM, NEXT, END = range(3)


class Task:
    operands = ()
    outs = ()
    out_in_vmem = True
    scratch = ()
    greets = ()
    late = False

    def middle(self):
        pass

    def bind(self, ins, outs, scratch):
        self.ins, self.out, self.room = ins, outs, scratch


def remote(source, landing, send_sem, recv_sem, target):
    return pltpu.make_async_remote_copy(
        src_ref=source,
        dst_ref=landing,
        send_sem=send_sem,
        recv_sem=recv_sem,
        device_id=target,
        device_id_type=MESH_IDS,
    )


def frame_partners():
    me = lax.axis_index(FRAME)
    return (me + 1 - 2 * lax.rem(me, 2), lax.rem(me + 2, 4), 3 - me)


def span(index, size):
    return pl.ds(pl.multiple_of(index * size, size), size)


class WeightTask(Task):
    out_in_vmem = False
    greets = (SECTION, FRAME)

    def __init__(self, weight):
        self.operands = (weight,)
        self.outs = (jax.ShapeDtypeStruct(weight.shape, weight.dtype),)
        self.scratch = (pltpu.SemaphoreType.DMA((4,)),)
        self.half = weight.shape[0] // 2

    def copies(self):
        (sems,) = self.room
        core = lax.rem(lax.axis_index(FRAME), 2)
        rows = span(core, self.half)
        other_section = {SECTION: 1 - lax.axis_index(SECTION)}
        other_core = {FRAME: frame_partners()[0]}
        over = remote(self.ins[0].at[rows], self.out[0].at[rows], sems.at[0], sems.at[1], other_section)
        on = remote(self.out[0].at[rows], self.out[0].at[rows], sems.at[2], sems.at[3], other_core)
        return over, on

    def begin(self):
        self.copies()[0].start()

    def steps(self):
        over, on = self.copies()

        def pass_on():
            over.wait_recv()
            on.start()

        def end():
            over.wait_send()
            on.wait()

        return [pass_on, end]


class ShareTask(Task):
    greets = (FRAME,)

    def __init__(self, grad):
        rows, width = grad.shape
        self.share = rows // 4
        self.operands = (grad,) if isinstance(grad, jax.Array) else ()
        piece = (self.share, width)
        self.outs = (jax.ShapeDtypeStruct(piece, jnp.bfloat16),)
        self.scratch = (
            pltpu.VMEM((2,) + piece, jnp.bfloat16),
            pltpu.VMEM((2,) + piece, jnp.bfloat16),
            pltpu.VMEM((2,) + piece, jnp.bfloat16),
            pltpu.SemaphoreType.DMA((3,)),
            pltpu.SemaphoreType.DMA((3,)),
            pltpu.SemaphoreType.DMA((2,)),
        )

    def within(self):
        own, landing, _, send_sems, recv_sems, here = self.room
        me = lax.axis_index(FRAME)
        other = frame_partners()[0]
        side = lax.div(me, 2)
        copies = []
        for k, to_side in enumerate((1 - side, side)):
            given = 2 * to_side + lax.rem(other, 2)
            kept = 2 * to_side + lax.rem(me, 2)
            copies.append(
                remote(
                    self.ins[0].at[span(given, self.share)],
                    landing.at[k],
                    send_sems.at[k],
                    recv_sems.at[k],
                    {FRAME: other},
                )
            )
            copies.append(
                pltpu.make_async_copy(self.ins[0].at[span(kept, self.share)], own.at[k], here.at[k])
            )
        return copies

    def over(self):
        crossing, send_sems, recv_sems = self.room[2:5]
        target = {FRAME: frame_partners()[1]}
        return remote(crossing.at[0], crossing.at[1], send_sems.at[2], recv_sems.at[2], target)

    def chip_sum(self, k):
        own, landing = self.room[:2]
        return own[k].astype(jnp.float32) + landing[k].astype(jnp.float32)

    def begin(self):
        for copy in self.within():
            copy.start()

    def middle(self):
        for copy in self.within():
            copy.wait()
        self.room[2][0] = self.chip_sum(0).astype(jnp.bfloat16)
        self.over().start()

    def steps(self):
        def end():
            self.over().wait()
            total = self.chip_sum(1) + self.room[2][1].astype(jnp.float32)
            self.out[0][...] = total.astype(jnp.bfloat16)

        return [end]


class BothTask(Task):
    out_in_vmem = False
    greets = (SECTION,)

    def __init__(self, first, second):
        self.operands = (first, second)
        self.outs = (jax.ShapeDtypeStruct((2,) + first.shape, first.dtype),)
        self.scratch = (pltpu.SemaphoreType.DMA((3,)),)

    def copies(self, given, kept):
        (sems,) = self.room
        section = lax.axis_index(SECTION)
        place = self.out[0].at[section]
        over = remote(self.ins[given], place, sems.at[0], sems.at[1], {SECTION: 1 - section})
        return over, pltpu.make_async_copy(self.ins[kept], place, sems.at[2])

    def begin(self):
        section = lax.axis_index(SECTION)
        for which in (0, 1):

            @pl.when(section == which)
            def _():
                for copy in self.copies(1 - which, which):
                    copy.start()

    def steps(self):
        def end():
            for copy in self.copies(0, 1):
                copy.wait()

        return [end]


class CrossTask(Task):
    greets = (SECTION,)

    def __init__(self, first, second, added):
        self.operands = (first, second)
        self.added = added
        self.out_in_vmem = added
        shape = first.shape
        if added:
            self.outs = (jax.ShapeDtypeStruct(shape, jnp.float32),)
            self.scratch = (pltpu.VMEM(shape, jnp.bfloat16),) * 2 + (pltpu.SemaphoreType.DMA((3,)),)
        else:
            self.outs = (jax.ShapeDtypeStruct(shape, first.dtype),)
            self.scratch = (pltpu.SemaphoreType.DMA((2,)),)

    def copies(self, given, kept):
        sems = self.room[-1]
        landing = self.room[0] if self.added else self.out[0]
        target = {SECTION: 1 - lax.axis_index(SECTION)}
        copies = [remote(self.ins[given], landing, sems.at[0], sems.at[1], target)]
        if self.added:
            copies.append(pltpu.make_async_copy(self.ins[kept], self.room[1], sems.at[2]))
        return copies

    def begin(self):
        section = lax.axis_index(SECTION)
        for which in (0, 1):

            @pl.when(section == which)
            def _():
                for copy in self.copies(1 - which, which):
                    copy.start()

    def steps(self):
        def end():
            for copy in self.copies(0, 1):
                copy.wait()
            if self.added:
                self.out[0][...] = self.room[0][...].astype(jnp.float32) + self.room[1][...].astype(
                    jnp.float32
                )

        return [end]


class TextTask(Task):
    out_in_vmem = False
    greets = (SECTION, FRAME, BOTH)

    def __init__(self, states):
        micros, rows, width = states.shape
        self.operands = (states,)
        self.outs = (jax.ShapeDtypeStruct((2, 4, rows, width), states.dtype),)
        self.scratch = (pltpu.SemaphoreType.DMA((8,)), pltpu.SemaphoreType.DMA((8,)))

    def copies(self):
        send_sems, recv_sems = self.room
        section, me = lax.axis_index(SECTION), lax.axis_index(FRAME)
        landing = self.out[0].at[section, me]
        copies = []
        for far in (0, 1):
            micro = section if far == 0 else 1 - section
            for k, frame in enumerate((me,) + frame_partners()):
                slot = far * 4 + k
                source = self.ins[0].at[micro]
                if slot == 0:
                    copies.append(pltpu.make_async_copy(source, landing, send_sems.at[0]))
                    continue
                target = {SECTION: micro, FRAME: frame}
                copies.append(remote(source, landing, send_sems.at[slot], recv_sems.at[slot], target))
        return copies

    def begin(self):
        for copy in self.copies():
            copy.start()

    def steps(self):
        def end():
            for copy in self.copies():
                copy.wait()

        return [end]


class TotalTask(Task):
    greets = (SECTION, LINE)

    def __init__(self, part):
        rows, width = part.shape
        self.share = rows // 4
        self.operands = (part,)
        self.outs = (jax.ShapeDtypeStruct((rows, width), jnp.bfloat16),)
        piece = (self.share, width)
        self.scratch = (
            pltpu.VMEM((4,) + piece, jnp.bfloat16),
            pltpu.VMEM((2,) + piece, jnp.bfloat16),
            pltpu.SemaphoreType.DMA((4,)),
            pltpu.SemaphoreType.DMA((4,)),
            pltpu.SemaphoreType.DMA((2,)),
            pltpu.SemaphoreType.DMA((4,)),
            pltpu.SemaphoreType.DMA((4,)),
        )

    def partners(self):
        me = lax.axis_index(LINE)
        return [lax.rem(me + by, 4) for by in (1, 2, 3)]

    def spread(self):
        landing, _, send_sems, recv_sems = self.room[:4]
        me = lax.axis_index(LINE)
        away = [
            remote(
                self.ins[0].at[span(partner, self.share)],
                landing.at[by],
                send_sems.at[by],
                recv_sems.at[by],
                {LINE: partner},
            )
            for by, partner in enumerate(self.partners(), 1)
        ]
        stay = pltpu.make_async_copy(self.ins[0].at[span(me, self.share)], landing.at[0], send_sems.at[0])
        return away + [stay]

    def over(self):
        sums, sems = self.room[1], self.room[4]
        target = {SECTION: 1 - lax.axis_index(SECTION)}
        return remote(sums.at[0], sums.at[1], sems.at[0], sems.at[1], target)

    def gather(self):
        send_sems, recv_sems = self.room[5:]
        mine = self.out[0].at[span(lax.axis_index(LINE), self.share)]
        return [
            remote(mine, mine, send_sems.at[by], recv_sems.at[by], {LINE: partner})
            for by, partner in enumerate(self.partners(), 1)
        ]

    def begin(self):
        for copy in self.spread():
            copy.start()

    def steps(self):
        landing, sums = self.room[:2]

        def first():
            for copy in self.spread():
                copy.wait()
            total = landing[0].astype(jnp.float32)
            for by in (1, 2, 3):
                total = total + landing[by].astype(jnp.float32)
            sums[0] = total.astype(jnp.bfloat16)
            self.over().start()

        def second():
            self.over().wait()
            total = sums[0].astype(jnp.float32) + sums[1].astype(jnp.float32)
            self.out[0][span(lax.axis_index(LINE), self.share), :] = total.astype(jnp.bfloat16)
            for copy in self.gather():
                copy.start()

        def third():
            for copy in self.gather():
                copy.wait()

        return [first, second, third]


class VectorTask(Task):
    greets = (SECTION, FRAME)

    def __init__(self, grads):
        self.operands = (grads,)
        shape = grads.shape[1:]
        self.outs = (jax.ShapeDtypeStruct(shape, jnp.float32),)
        self.scratch = (
            pltpu.VMEM((4,) + grads.shape, jnp.float32),
            pltpu.VMEM((3,) + shape, jnp.float32),
            pltpu.SemaphoreType.DMA((4,)),
            pltpu.SemaphoreType.DMA((4,)),
            pltpu.SemaphoreType.DMA((2,)),
        )

    def spread(self):
        landing, _, send_sems, recv_sems, _ = self.room
        away = [
            remote(self.ins[0], landing.at[k], send_sems.at[k], recv_sems.at[k], {FRAME: partner})
            for k, partner in enumerate(frame_partners(), 1)
        ]
        return away + [pltpu.make_async_copy(self.ins[0], landing.at[0], send_sems.at[0])]

    def over(self):
        sums, sems = self.room[1], self.room[4]
        target = {SECTION: 1 - lax.axis_index(SECTION)}
        return remote(sums.at[0], sums.at[1], sems.at[0], sems.at[1], target)

    def begin(self):
        for copy in self.spread():
            copy.start()

    def steps(self):
        landing, sums = self.room[:2]
        section = lax.axis_index(SECTION)

        def first():
            for copy in self.spread():
                copy.wait()
            total = [
                (landing[0, layer] + landing[1, layer]) + (landing[2, layer] + landing[3, layer])
                for layer in (0, 1)
            ]
            for which in (0, 1):

                @pl.when(section == which)
                def _():
                    sums[0] = total[1 - which]
                    sums[2] = total[which]

            self.over().start()

        def second():
            self.over().wait()
            self.out[0][...] = sums[2] + sums[1]

        return [first, second]


def greet(kinds):
    barrier = pltpu.get_barrier_semaphore()
    section, head, frame = (lax.axis_index(a) for a in (SECTION, LINE, FRAME))
    targets = []
    if FRAME in kinds:
        targets += [{FRAME: other} for other in frame_partners()]
    if SECTION in kinds:
        targets.append({SECTION: 1 - section})
    if BOTH in kinds:
        targets += [{SECTION: 1 - section, FRAME: other} for other in frame_partners()]
    if LINE in kinds:
        targets += [{LINE: lax.rem(head + by, 4)} for by in (1, 2, 3)]
    for target in targets:
        pl.semaphore_signal(barrier, 1, device_id=target, device_id_type=MESH_IDS)
    if LINE_ONLY not in kinds or LINE in kinds:
        pl.semaphore_wait(barrier, len(targets))
        return

    for way in (-1, 1):
        other = head + way

        @pl.when((other >= 0) & (other < 4))
        def _():
            pl.semaphore_signal(barrier, 1, device_id={LINE: other}, device_id_type=MESH_IDS)

    is_end = (head == 0) | (head == 3)

    @pl.when(is_end)
    def _():
        pl.semaphore_wait(barrier, len(targets) + 1)

    @pl.when(jnp.logical_not(is_end))
    def _():
        pl.semaphore_wait(barrier, len(targets) + 2)


def call(body, operands, outs, scratch, kinds, collective_id, tasks=(), in_vmem=True, end=None):
    whole, anywhere = pl.BlockSpec(memory_space=pltpu.VMEM), pl.BlockSpec(memory_space=pl.ANY)
    place = whole if in_vmem else anywhere
    in_specs, out_specs = [place] * len(operands), [place] * len(outs)
    operands, all_outs, scratch = list(operands), list(outs), list(scratch)
    counts = [(len(operands), len(outs), len(scratch))]
    kinds = set(kinds)
    for task in tasks:
        kinds |= set(task.greets)
        in_specs += [anywhere] * len(task.operands)
        out_specs += [whole if task.out_in_vmem else anywhere] * len(task.outs)
        operands += task.operands
        all_outs += task.outs
        scratch += task.scratch
        counts.append((len(task.operands), len(task.outs), len(task.scratch)))
    n_in, n_out = len(operands), len(all_outs)

    def kernel(*refs):
        groups = [list(refs[:n_in]), list(refs[n_in : n_in + n_out]), list(refs[n_in + n_out :])]
        bound = []
        for sizes in counts:
            bound.append([])
            for group, size in zip(groups, sizes):
                bound[-1].append(group[:size])
                del group[:size]
        for task, parts in zip(tasks, bound[1:]):
            task.bind(*parts)

        def meet():
            greet(kinds)

        def ride():
            for task in tasks:
                if not task.late:
                    task.begin()

        def middle():
            for task in tasks:
                if not task.late:
                    task.middle()

        if body is None:
            meet()
            ride()
            middle()
        else:
            body(*bound[0], meet, ride, middle)
        queues = [task.steps() for task in tasks]
        while any(queues):
            for queue in queues:
                if queue:
                    queue.pop(0)()
        if end is not None:
            end()

    results = pl.pallas_call(
        kernel,
        out_shape=all_outs,
        in_specs=in_specs,
        out_specs=out_specs,
        scratch_shapes=scratch,
        compiler_params=pltpu.CompilerParams(
            collective_id=collective_id, has_side_effects=True, vmem_limit_bytes=VMEM_BYTES
        ),
    )(*operands)
    results = list(results)
    main, results = results[: len(outs)], results[len(outs) :]
    return main, results


def chunking(rows):
    return max(1, min(16, rows // 16))


def nt_product(left, right):
    return lax.dot_general(left, right, (((1,), (1,)), ((), ())), preferred_element_type=jnp.float32)


def plain_product(left, right):
    return jnp.dot(left, right, preferred_element_type=jnp.float32)


def norm_parts(v):
    average = jnp.mean(v, axis=-1, keepdims=True)
    centered = v - average
    inverse = lax.rsqrt(jnp.mean(centered * centered, axis=-1, keepdims=True) + EPS)
    return centered * inverse, inverse


class Held:
    def __init__(self, shape, dtype, sources=(), choose=None, stage=0, kept=False):
        self.shape, self.dtype = tuple(shape), dtype
        self.sources, self.choose, self.stage, self.kept = sources, choose, stage, kept
        self.ref = self.far = self.sem = None

    def copy_in(self, index=0):
        source = self.far[index]
        if self.choose == BY_SECTION:
            source = source.at[lax.axis_index(SECTION)]
        return pltpu.make_async_copy(source, self.ref, self.sem)

    def start_in(self):
        if not isinstance(self.choose, int):
            self.copy_in().start()
            return
        section = lax.axis_index(SECTION)

        @pl.when(section == self.choose)
        def _():
            self.copy_in(0).start()

        @pl.when(section != self.choose)
        def _():
            self.copy_in(1).start()

    def write(self, at, value):
        self.ref[at, :] = value
        if self.kept:
            pltpu.make_async_copy(self.ref.at[at], self.far[0].at[at], self.sem).start()

    def flush(self):
        pltpu.make_async_copy(self.ref, self.far[0], self.sem).start()

    def drain(self):
        pltpu.make_async_copy(self.ref, self.far[0], self.sem).wait()


class Build:
    def __init__(self):
        self.helds, self.rooms, self.extras = [], [], []

    def add(self, held):
        self.helds.append(held)
        return held

    def arg(self, array, stage, choose=None):
        shape = array.shape[1:] if choose == BY_SECTION else array.shape
        return self.add(Held(shape, array.dtype, (array,), choose, stage))

    def pick(self, pair, layer, stage):
        return self.add(Held(pair[0].shape, pair[0].dtype, tuple(pair), layer, stage))

    def out(self, shape, dtype):
        return self.add(Held(shape, dtype, kept=True))

    def temp(self, shape, dtype):
        return self.add(Held(shape, dtype))

    def extra(self, scratch):
        self.extras.append(scratch)
        return len(self.extras) - 1


class Stage:
    def __init__(self, rows, width):
        self.rows, self.width = rows, width
        self.begin = self.prepare = self.finish = None
        self.ends = []


class Chore:
    def __init__(self, build, stage, left, right, flipped=False):
        self.stage, self.left, self.right, self.flipped = stage, left, right, flipped
        columns = left.shape[0] if flipped else left.shape[1]
        self.units = columns // BLOCK
        self.product = build.temp((columns, right.shape[1]), jnp.bfloat16)
        self.task = ShareTask(self.product)
        self.task.late = True

    def unit(self, number):
        at = span(number, BLOCK)
        right = self.right.ref[...].astype(jnp.bfloat16)
        if self.flipped:
            product = plain_product(self.left.ref[at, :], right)
        else:
            product = lax.dot_general(
                self.left.ref[:, at], right, (((0,), (0,)), ((), ())), preferred_element_type=jnp.float32
            )
        self.product.ref[at, :] = product.astype(jnp.bfloat16)

    def run(self, piece):
        @pl.when(piece < self.units)
        def _():
            self.unit(piece)

        @pl.when(piece == self.units)
        def _():
            self.task.ins = [self.product.ref]
            self.task.begin()

        @pl.when(piece == self.units + 5)
        def _():
            self.task.middle()


def line_chain(stages, need, part, middle, chores):
    place = lax.axis_index(LINE)
    rows = stages[0].rows
    pieces = chunking(rows)
    step = rows // pieces
    per_block = max(1, min(BLOCK, rows) // step)
    lag = max(0, min(LAG, pieces - per_block))
    is_end = (place == 0) | (place == 3)
    inner = {LINE: jnp.where(place == 0, 1, 2)}
    outer = {LINE: jnp.where(place == 1, 0, 3)}
    peer = {LINE: 3 - place}

    def inwards(stage, piece):
        send, recv, _, _, send_sems, recv_sems = stage.room[:6]
        at = span(piece, step)
        return remote(send.at[at], recv.at[at], send_sems.at[piece], recv_sems.at[piece], inner)

    def crossing(stage, piece):
        send, _, across = stage.room[:3]
        send_sems, recv_sems = stage.room[6:8]
        at = span(piece, step)
        return remote(send.at[at], across.at[at], send_sems.at[piece], recv_sems.at[piece], peer)

    def outwards(stage, piece):
        held = stage.room[3]
        send_sems, recv_sems = stage.room[8:]
        at = span(piece, step)
        return remote(held.at[at], held.at[at], send_sems.at[piece], recv_sems.at[piece], outer)

    def open_stage(index):
        need(index)
        if stages[index].begin is not None:
            stages[index].begin()

    def loop(first, last, step_of):
        def one(piece, carry):
            step_of(piece)
            return carry

        lax.fori_loop(first, last, one, 0)

    def chore(stage, piece):
        for one in chores:
            if stages[one.stage] is stage:
                one.run(piece)

    @pl.when(is_end)
    def _():
        def give(stage, piece):
            inwards(stage, piece).start()
            chore(stage, piece)

        def take(stage, piece):
            outwards(stage, piece).wait_recv()
            stage.finish(span(piece, step), piece)

        for index, stage in enumerate(stages):
            open_stage(index)

            def block_step(block):
                low, high = block * per_block, (block + 1) * per_block
                if index:
                    loop(low, high, lambda piece: take(stages[index - 1], piece))
                stage.room[0][span(block, per_block * step), :] = stage.prepare(block).astype(jnp.bfloat16)
                loop(low, high, lambda piece: give(stage, piece))
                if index == 0:

                    @pl.when(block == 1)
                    def _():
                        middle()

            loop(0, pieces // per_block, block_step)
        loop(0, pieces, lambda piece: take(stages[-1], piece))
        for stage in stages:
            loop(0, pieces, lambda piece: inwards(stage, piece).wait_send())

    @pl.when(jnp.logical_not(is_end))
    def _():
        def add(stage, piece):
            @pl.when(lax.rem(piece, per_block) == 0)
            def _():
                part[...] = stage.prepare(lax.div(piece, per_block))

            at = span(piece, step)
            send, recv = stage.room[:2]
            inwards(stage, piece).wait_recv()
            own = part[span(lax.rem(piece, per_block), step), :]
            send[at, :] = (own + recv[at, :].astype(jnp.float32)).astype(jnp.bfloat16)
            crossing(stage, piece).start()
            chore(stage, piece)
            if stage is stages[0]:

                @pl.when(piece == 2 * per_block - 1)
                def _():
                    middle()

        def settle(stage, piece):
            at = span(piece, step)
            send, _, across, held = stage.room[:4]
            crossing(stage, piece).wait_recv()
            total = send[at, :].astype(jnp.float32) + across[at, :].astype(jnp.float32)
            held[at, :] = total.astype(jnp.bfloat16)
            outwards(stage, piece).start()
            stage.finish(at, piece)

        for index, stage in enumerate(stages):
            open_stage(index)

            def both(piece):
                add(stage, piece)

                @pl.when(piece >= lag)
                def _():
                    settle(stage, piece - lag)

                if index and lag:

                    @pl.when(piece < lag)
                    def _():
                        settle(stages[index - 1], pieces - lag + piece)

            loop(0, pieces, both)
        loop(pieces - lag, pieces, lambda piece: settle(stages[-1], piece))

        def drain(stage, piece):
            crossing(stage, piece).wait_send()
            outwards(stage, piece).wait_send()

        for stage in stages:
            loop(0, pieces, lambda piece: drain(stage, piece))

    for stage in stages:
        for end in stage.ends:
            end()


def run_build(build, body, kinds, collective_id, tasks):
    operands, outs, scratch = [], [], []
    for held in build.helds:
        operands += held.sources
        if held.kept:
            outs.append(jax.ShapeDtypeStruct(held.shape, held.dtype))
        scratch.append(pltpu.VMEM(held.shape, held.dtype))
    n_held = len(scratch)
    scratch += build.extras
    scratch.append(pltpu.SemaphoreType.DMA((n_held,)))
    reads = sorted((held for held in build.helds if held.sources), key=lambda held: held.stage)

    def need(stage):
        for held in reads:
            if held.stage == stage:
                held.copy_in().wait()

    def run(ins, outs, scratch, meet, ride, middle):
        ins, outs = list(ins), list(outs)
        sems = scratch[-1]
        for index, held in enumerate(build.helds):
            held.ref, held.sem = scratch[index], sems.at[index]
            held.far = [ins.pop(0) for _ in held.sources]
            if held.kept:
                held.far = [outs.pop(0)]
        build.bound = scratch[n_held:-1]
        for held in reads:
            held.start_in()
        body(need, meet, ride, middle)

    def end():
        for held in build.helds:
            if held.kept:
                held.drain()

    return call(run, operands, outs, scratch, kinds, collective_id, tasks, in_vmem=False, end=end)


def run_chain(build, stages, collective_id, tasks, kinds=(LINE_ONLY,), chores=()):
    slots = []
    for stage in stages:
        pieces = chunking(stage.rows)
        room = [pltpu.VMEM((stage.rows, stage.width), jnp.bfloat16)] * 4
        room += [pltpu.SemaphoreType.DMA((pieces,))] * 6
        slots.append([build.extra(scratch) for scratch in room])
    part = build.extra(pltpu.VMEM((min(BLOCK, stages[0].rows), stages[0].width), jnp.float32))

    def body(need, meet, ride, middle):
        for stage, places in zip(stages, slots):
            stage.room = [build.bound[place] for place in places]
        meet()
        ride()
        line_chain(stages, need, build.bound[part], middle, chores)

    tasks = list(tasks) + [one.task for one in chores]
    return run_build(build, body, kinds, collective_id, tasks)


def residual_norm(build, index, stage, base, gain, shift, mode):
    shape = (stage.rows, stage.width)
    result = build.temp(shape, jnp.float32) if mode == NORM else None
    normed = build.out(shape, jnp.bfloat16) if mode != END else None
    low = build.out(shape, jnp.bfloat16)
    if mode != END:
        gain, shift = build.arg(gain[None], index), build.arg(shift[None], index)

    def finish(at, piece):
        value = base.ref[at, :].astype(jnp.float32) + stage.room[3][at, :].astype(jnp.float32)
        rounded = value.astype(jnp.bfloat16)
        low.write(at, rounded)
        if mode == NORM:
            result.write(at, value)
        if mode == NEXT:
            value = rounded.astype(jnp.float32)
        if mode != END:
            standard, _ = norm_parts(value)
            normed.write(at, (standard * gain.ref[...] + shift.ref[...]).astype(jnp.bfloat16))

    stage.finish = finish
    return result, normed


def self_out_stage(build, index, layer, attended_t, weight, base):
    rows, width = base.shape
    stage = Stage(rows, width)
    flipped, matrix = build.arg(attended_t, index), build.pick(weight, layer, index)
    left = build.temp(attended_t.shape[::-1], jnp.bfloat16)

    def begin():
        left.ref[...] = flipped.ref[...].T

    def prepare(number):
        return plain_product(left.ref[span(number, min(BLOCK, rows)), :], matrix.ref[...])

    stage.begin, stage.prepare = begin, prepare
    return stage


def text_mask(states, seg):
    item = lax.rem(lax.div(lax.broadcasted_iota(jnp.int32, (states, 1), 0), TEXT // 4), ITEMS)
    return item == seg


def cross_stage(build, index, layer, normed, states, seg, into, out_of):
    rows, width = normed.shape
    stage = Stage(rows, width)
    columns, block = into[0].shape[1], min(BLOCK, rows)
    states, seg = build.arg(states, index), build.arg(seg, index)
    into, out_of = build.pick(into, layer, index), build.pick(out_of, layer, index)
    queries = build.out((rows, columns), jnp.bfloat16)
    left = build.out((rows, columns), jnp.bfloat16)
    values_t = build.temp((columns, states.shape[0]), jnp.bfloat16)

    def begin():
        values_t.ref[...] = states.ref[:, columns:].T

    def prepare(number):
        at = span(number, block)
        query = plain_product(normed.ref[at, :], into.ref[...]).astype(jnp.bfloat16)
        queries.write(at, query)
        query_t = query.T
        allowed = text_mask(states.shape[0], seg.ref[:, at])
        mixed = []
        for head in range(columns // HEAD):
            cols = slice(head * HEAD, (head + 1) * HEAD)
            scores = plain_product(states.ref[:, cols], query_t[cols, :]) * HEAD ** (-0.5)
            scores = jnp.where(allowed, scores, masked_score)
            e = jnp.exp(scores - jnp.max(scores, axis=0, keepdims=True))
            total = jnp.sum(e, axis=0, keepdims=True)
            value = plain_product(values_t.ref[cols, :], e.astype(jnp.bfloat16))
            mixed.append((value * (1.0 / total)).astype(jnp.bfloat16))
        mixed = jnp.concatenate(mixed, axis=0).T
        left.write(at, mixed)
        return plain_product(mixed, out_of.ref[...])

    stage.begin, stage.prepare = begin, prepare
    return stage


def feed_stage(build, index, layer, normed, into, out_of):
    rows, width = normed.shape
    stage = Stage(rows, width)
    hidden, block = into[0].shape[1], min(BLOCK, rows)
    into, out_of = build.pick(into, layer, index), build.pick(out_of, layer, index)
    before = build.out((rows, hidden), jnp.bfloat16)
    left = build.out((rows, hidden), jnp.bfloat16)

    def prepare(number):
        at = span(number, block)
        u = plain_product(normed.ref[at, :], into.ref[...])
        before.write(at, u.astype(jnp.bfloat16))
        active = (0.5 * u * (1.0 + lax.erf(u * inv_sqrt_two))).astype(jnp.bfloat16)
        left.write(at, active)
        return plain_product(active, out_of.ref[...])

    stage.prepare = prepare
    return stage


def norm_backward(build, index, stage, value, gain, upstream, feeds, spare=None):
    shape = (stage.rows, stage.width)
    pieces = chunking(stage.rows)
    vector = (1, stage.width)
    by_section = BY_SECTION if value.ndim == 3 else None
    value, gain = build.arg(value, index, by_section), build.arg(gain[None], index)
    result = build.temp(shape, jnp.float32) if feeds else None
    low = build.out(shape, jnp.bfloat16)
    gain_grad, shift_grad = build.out(vector, jnp.float32), build.out(vector, jnp.float32)
    parts = build.extra(pltpu.VMEM((2, pieces, 1, stage.width), jnp.float32))
    if spare is not None:
        spare = build.arg(spare, index)
        both = build.out((2,) + shape, jnp.bfloat16)
        sems = build.extra(pltpu.SemaphoreType.DMA((2, pieces)))

    def over(at, piece, source):
        target = {SECTION: 1 - lax.axis_index(SECTION)}
        pair = build.bound[sems]
        landing = both.ref.at[lax.axis_index(SECTION), at]
        return remote(source.ref.at[at], landing, pair.at[0, piece], pair.at[1, piece], target)

    def finish(at, piece):
        grad = stage.room[3][at, :].astype(jnp.float32)
        standard, inverse = norm_parts(value.ref[at, :].astype(jnp.float32))
        scaled = grad * gain.ref[...]
        through = inverse * (
            scaled
            - jnp.mean(scaled, axis=-1, keepdims=True)
            - standard * jnp.mean(scaled * standard, axis=-1, keepdims=True)
        )
        total = through + upstream.ref[at, :].astype(jnp.float32)
        if feeds:
            result.write(at, total)
        low.write(at, total.astype(jnp.bfloat16))
        build.bound[parts][0, piece] = jnp.sum(grad * standard, axis=0, keepdims=True)
        build.bound[parts][1, piece] = jnp.sum(grad, axis=0, keepdims=True)
        if spare is not None:
            section = lax.axis_index(SECTION)

            @pl.when(section == 0)
            def _():
                both.ref[0, at, :] = low.ref[at, :]
                over(at, piece, spare).start()

            @pl.when(section == 1)
            def _():
                both.ref[1, at, :] = spare.ref[at, :]
                over(at, piece, low).start()

    def end():
        whole = slice(0, 1)
        gain_grad.write(whole, jnp.sum(build.bound[parts][0], axis=0))
        shift_grad.write(whole, jnp.sum(build.bound[parts][1], axis=0))
        if spare is not None:
            step = stage.rows // pieces

            def one(piece, carry):
                over(span(piece, step), piece, low).wait()
                return carry

            lax.fori_loop(0, pieces, one, 0)
            both.flush()

    stage.finish = finish
    stage.ends.append(end)
    return result, low


def feed_back_stage(build, index, layer, grad_out, before, out_of, into):
    rows, width = grad_out.shape
    stage = Stage(rows, width)
    hidden, block = out_of[0].shape[0], min(BLOCK, rows)
    before = build.arg(before, index)
    out_of, into = build.pick(out_of, layer, index), build.pick(into, layer, index)
    left = build.out((rows, hidden), jnp.bfloat16)

    def prepare(number):
        at = span(number, block)
        grad = nt_product(grad_out.ref[at, :].astype(jnp.bfloat16), out_of.ref[...])
        u = before.ref[at, :].astype(jnp.float32)
        slope = 0.5 * (1.0 + lax.erf(u * inv_sqrt_two)) + u * jnp.exp(-0.5 * u * u) * inv_sqrt_tau
        grad = (grad * slope).astype(jnp.bfloat16)
        left.write(at, grad)
        return nt_product(grad, into.ref[...])

    stage.prepare, stage.left = prepare, left
    return stage


def cross_back_stage(build, index, layer, grad_low, queries, states, seg, out_of, into):
    rows, width = grad_low.shape
    stage = Stage(rows, width)
    columns, block = out_of[0].shape[0], min(BLOCK, rows)
    queries, states, seg = (build.arg(array, index) for array in (queries, states, seg))
    out_of, into = build.pick(out_of, layer, index), build.pick(into, layer, index)
    left = build.out((rows, columns), jnp.bfloat16)
    state_grads = build.out(states.shape, jnp.bfloat16)
    keys_t = build.temp((columns, states.shape[0]), jnp.bfloat16)
    sums = build.temp(states.shape, jnp.float32)
    scale = HEAD ** (-0.5)

    def begin():
        keys_t.ref[...] = states.ref[:, :columns].T
        sums.ref[...] = jnp.zeros(sums.shape, jnp.float32)

    def prepare(number):
        at = span(number, block)
        grad = nt_product(grad_low.ref[at, :], out_of.ref[...]).astype(jnp.bfloat16)
        query = queries.ref[at, :]
        grad_t, query_t = grad.T, query.T
        allowed = text_mask(states.shape[0], seg.ref[:, at])
        query_grads = []
        for head in range(columns // HEAD):
            cols = slice(head * HEAD, (head + 1) * HEAD)
            more = slice(columns + head * HEAD, columns + (head + 1) * HEAD)
            scores = plain_product(states.ref[:, cols], query_t[cols, :]) * scale
            scores = jnp.where(allowed, scores, masked_score)
            e = jnp.exp(scores - jnp.max(scores, axis=0, keepdims=True))
            p = e * (1.0 / jnp.sum(e, axis=0, keepdims=True))
            slope = plain_product(states.ref[:, more], grad_t[cols, :])
            weighted = p * slope
            ds = (weighted - p * jnp.sum(weighted, axis=0, keepdims=True)).astype(jnp.bfloat16)
            query_grads.append((plain_product(keys_t.ref[cols, :], ds) * scale).astype(jnp.bfloat16))
            sums.ref[:, cols] += plain_product(ds, query[:, cols]) * scale
            sums.ref[:, more] += plain_product(p.astype(jnp.bfloat16), grad[:, cols])
        query_grads = jnp.concatenate(query_grads, axis=0).T
        left.write(at, query_grads)
        return nt_product(query_grads, into.ref[...])

    def end():
        state_grads.write(slice(0, states.shape[0]), sums.ref[...].astype(jnp.bfloat16))

    stage.begin, stage.prepare = begin, prepare
    stage.ends.append(end)
    return stage


def self_in_stage(build, index, layer, grads_t, weight, width):
    columns, rows = grads_t.shape
    stage = Stage(rows, width)
    flipped, matrix = build.arg(grads_t, index), build.pick(weight, layer, index)
    left = build.temp((rows, columns), jnp.bfloat16)

    def begin():
        left.ref[...] = flipped.ref[...].T

    def prepare(number):
        return plain_product(left.ref[span(number, min(BLOCK, rows)), :], matrix.ref[...])

    stage.begin, stage.prepare = begin, prepare
    stage.left = left
    return stage


def forward_chain(
    layer, attended_t, entering, states, seg, gains, weights, collective_id, tasks
):
    output, query, cross, *more = weights
    build = Build()
    base = build.arg(entering, 0, BY_SECTION if entering.ndim == 3 else None)
    first = self_out_stage(build, 0, layer, attended_t, output, base)
    middle, second_normed = residual_norm(build, 0, first, base, gains[2], gains[3], NORM)
    second = cross_stage(build, 1, layer, second_normed, states, seg, query, cross)
    latter, third_normed = residual_norm(build, 1, second, middle, gains[4], gains[5], NORM)
    stages = [first, second]
    if more:
        stages.append(feed_stage(build, 2, layer, third_normed, *more))
        residual_norm(build, 2, stages[2], latter, None, None, END)
    return run_chain(build, stages, collective_id, tasks)


def feed_chain(layer, normed, latter, weights, after, collective_id):
    build = Build()
    normed, latter = build.arg(normed, 0), build.arg(latter, 0)
    stage = feed_stage(build, 0, layer, normed, *weights[3:])
    residual_norm(build, 0, stage, latter, after[0], after[1], NEXT)
    return run_chain(build, [stage], collective_id, [])


def backward_chain(
    layer,
    upstream,
    before,
    hidden,
    third_normed,
    latter,
    queries,
    states,
    seg,
    middle,
    gains,
    weights,
    collective_id,
    tasks,
):
    _, query, cross, expand, reduce = weights
    build = Build()
    arriving = build.arg(upstream, 0, BY_SECTION if upstream.ndim == 3 else None)
    first = feed_back_stage(build, 0, layer, arriving, before, reduce, expand)
    grad_latter, grad_cross = norm_backward(build, 0, first, latter, gains[4], arriving, True)
    second = cross_back_stage(build, 1, layer, grad_cross, queries, states, seg, cross, query)
    norm_backward(build, 1, second, middle, gains[2], grad_latter, False)
    chores = [
        Chore(build, 0, build.arg(hidden, 0), arriving),
        Chore(build, 1, build.arg(third_normed, 1), first.left),
    ]
    return run_chain(build, [first, second], collective_id, tasks, chores=chores)


def last_chain(layer, grads_t, entering, gain, upstream, weight, spare, products, collective_id, tasks):
    build = Build()
    residual = build.arg(upstream, 0)
    stage = self_in_stage(build, 0, layer, grads_t, weight, upstream.shape[1])
    norm_backward(build, 0, stage, entering, gain, residual, False, spare)
    chores = []
    for left, right in products:
        flipped = left.shape[0] != upstream.shape[0]
        if right is None:
            right = stage.left
        else:
            right = residual if right is upstream else build.arg(right, 0)
        chores.append(Chore(build, 0, build.arg(left, 0), right, flipped))
    kinds = (LINE_ONLY,) if spare is None else (LINE_ONLY, SECTION)
    return run_chain(build, [stage], collective_id, tasks, kinds, chores)


def masked_scores(keys, query_t, begins, start):
    reach, block = keys.shape[0], query_t.shape[1]
    scores = plain_product(keys, query_t)
    key_pos = lax.broadcasted_iota(jnp.int32, (reach, 1), 0)
    query_pos = start + lax.broadcasted_iota(jnp.int32, (1, block), 1)
    allowed = (key_pos <= query_pos) & (key_pos >= begins)
    return jnp.where(allowed, scores * HEAD ** (-0.5), masked_score)


def to_frames(source, landing, sems):
    me = lax.axis_index(FRAME)
    return [
        remote(source(other), landing(me), sems.at[0, k], sems.at[1, k], {FRAME: other})
        for k, other in enumerate(frame_partners())
    ]


def self_forward(normed, weight, begins, layer, collective_id, tasks):
    rows, frames, width = normed.shape[0], 4, 3 * HEAD
    all_rows = rows * frames
    build = Build()
    normed, begins, weight = build.arg(normed, 0), build.arg(begins, 1), build.pick(weight, layer, 0)
    heads_t = build.out((width, all_rows), jnp.bfloat16)
    out = build.out((frames * HEAD, rows), jnp.bfloat16)
    own = build.temp((frames, width, rows), jnp.bfloat16)
    keys = build.temp((all_rows, HEAD), jnp.bfloat16)
    mixed_t = build.temp((frames, HEAD, rows), jnp.bfloat16)
    sems = [build.extra(pltpu.SemaphoreType.DMA((2, frames - 1))) for _ in range(2)]

    def body(need, meet, ride, middle):
        me = lax.axis_index(FRAME)
        partners = frame_partners()
        block = min(2 * BLOCK, rows)
        arriving = to_frames(
            lambda g: own.ref.at[g], lambda f: heads_t.ref.at[:, span(f, rows)], build.bound[sems[0]]
        )
        leaving = to_frames(
            lambda g: mixed_t.ref.at[g], lambda f: out.ref.at[span(f, HEAD), :], build.bound[sems[1]]
        )

        def project(other):
            return nt_product(weight.ref[span(other, width), :], normed.ref[...]).astype(jnp.bfloat16)

        meet()
        need(0)
        for k in (2, 1, 0):
            own.ref[partners[k]] = project(partners[k])
            arriving[k].start()
        ride()
        heads_t.ref[:, span(me, rows)] = project(me)
        need(1)
        for copy in arriving:
            copy.wait()
        pltpu.make_async_copy(heads_t.ref, heads_t.far[0], heads_t.sem).start()
        keys.ref[...] = heads_t.ref[HEAD : 2 * HEAD, :].T
        for target in range(frames):
            for start in range(target * rows, (target + 1) * rows, block):
                reach = start + block
                scores = masked_scores(
                    keys.ref[:reach, :], heads_t.ref[:HEAD, start:reach], begins.ref[:, start:reach], start
                )
                e = jnp.exp(scores - jnp.max(scores, axis=0, keepdims=True))
                total = jnp.sum(e, axis=0, keepdims=True)
                mixed = plain_product(heads_t.ref[2 * HEAD :, :reach], e.astype(jnp.bfloat16))
                at = start - target * rows
                mixed_t.ref[target, :, at : at + block] = (mixed * (1.0 / total)).astype(jnp.bfloat16)

            for copy, other in zip(leaving, partners):

                @pl.when(other == target)
                def _():
                    copy.start()

        out.ref[span(me, HEAD), :] = mixed_t.ref[me]
        for copy in leaving:
            copy.wait()
        pltpu.make_async_copy(out.ref, out.far[0], out.sem).start()

    return run_build(build, body, (FRAME,), collective_id, tasks)


def self_backward(heads_t, grad_low, weight, begins, layer, collective_id, tasks):
    rows, frames, width = grad_low.shape[0], 4, 3 * HEAD
    all_rows = rows * frames
    build = Build()
    heads_t, begins = build.arg(heads_t, 1), build.arg(begins, 1)
    grad_low, weight = build.arg(grad_low, 0), build.pick(weight, layer, 0)
    out = build.out((frames * width, rows), jnp.bfloat16)
    own = build.temp((frames, HEAD, rows), jnp.bfloat16)
    grad_t = build.temp((HEAD, all_rows), jnp.bfloat16)
    columns = build.temp((4, all_rows, HEAD), jnp.bfloat16)
    key_sum, value_sum = (build.temp((all_rows, HEAD), jnp.float32) for _ in range(2))
    grads_t = build.temp((frames, width, rows), jnp.bfloat16)
    sems = [build.extra(pltpu.SemaphoreType.DMA((2, frames - 1))) for _ in range(2)]

    def body(need, meet, ride, middle):
        me = lax.axis_index(FRAME)
        partners = frame_partners()
        block = min(2 * BLOCK, rows)
        scale = HEAD ** (-0.5)
        arriving = to_frames(
            lambda g: own.ref.at[g], lambda f: grad_t.ref.at[:, span(f, rows)], build.bound[sems[0]]
        )
        leaving = to_frames(
            lambda g: grads_t.ref.at[g], lambda f: out.ref.at[span(f, width), :], build.bound[sems[1]]
        )

        def project(other):
            return nt_product(weight.ref[span(other, HEAD), :], grad_low.ref[...]).astype(jnp.bfloat16)

        meet()
        need(0)
        for k in (2, 1, 0):
            own.ref[partners[k]] = project(partners[k])
            arriving[k].start()
        ride()
        grad_t.ref[:, span(me, rows)] = project(me)
        key_sum.ref[...] = jnp.zeros(key_sum.shape, jnp.float32)
        value_sum.ref[...] = jnp.zeros(key_sum.shape, jnp.float32)
        need(1)
        for part in range(3):
            columns.ref[part] = heads_t.ref[part * HEAD : (part + 1) * HEAD, :].T
        for copy in arriving:
            copy.wait()
        columns.ref[3] = grad_t.ref[...].T
        middle()
        for target in reversed(range(frames)):
            for start in reversed(range(target * rows, (target + 1) * rows, block)):
                reach = start + block
                scores = masked_scores(
                    columns.ref[1, :reach, :],
                    heads_t.ref[:HEAD, start:reach],
                    begins.ref[:, start:reach],
                    start,
                )
                e = jnp.exp(scores - jnp.max(scores, axis=0, keepdims=True))
                p = e * (1.0 / jnp.sum(e, axis=0, keepdims=True))
                slope = plain_product(columns.ref[2, :reach, :], grad_t.ref[:, start:reach])
                weighted = p * slope
                ds = (weighted - p * jnp.sum(weighted, axis=0, keepdims=True)).astype(jnp.bfloat16)
                value_sum.ref[:reach, :] += plain_product(
                    p.astype(jnp.bfloat16), columns.ref[3, start:reach, :]
                )
                key_sum.ref[:reach, :] += plain_product(ds, columns.ref[0, start:reach, :])
                here = slice(start - target * rows, reach - target * rows)
                query_grad = plain_product(heads_t.ref[HEAD : 2 * HEAD, :reach], ds) * scale
                grads_t.ref[target, :HEAD, here] = query_grad.astype(jnp.bfloat16)
                key_grad = key_sum.ref[start:reach, :] * scale
                grads_t.ref[target, HEAD : 2 * HEAD, here] = key_grad.T.astype(jnp.bfloat16)
                grads_t.ref[target, 2 * HEAD :, here] = value_sum.ref[start:reach, :].T.astype(jnp.bfloat16)

            for copy, other in zip(leaving, partners):

                @pl.when(other == target)
                def _():
                    copy.start()

        out.ref[span(me, width), :] = grads_t.ref[me]
        for copy in leaving:
            copy.wait()
        pltpu.make_async_copy(out.ref, out.far[0], out.sem).start()

    return run_build(build, body, (FRAME,), collective_id, tasks)


def matmul(left_side, right_side):
    return jnp.dot(left_side, right_side, preferred_element_type=jnp.float32)


def matmul_tn(left_side, right_side):
    return lax.dot_general(
        left_side, right_side, (((0,), (0,)), ((), ())), preferred_element_type=jnp.float32
    )


def matmul_nt(left_side, right_side):
    return lax.dot_general(
        left_side, right_side, (((1,), (1,)), ((), ())), preferred_element_type=jnp.float32
    )


def layer_norm(signal, gain_vec, shift_vec):
    average = jnp.mean(signal, axis=-1, keepdims=True)
    centered = signal - average
    variance = jnp.mean(centered * centered, axis=-1, keepdims=True)
    return centered * lax.rsqrt(variance + 1e-05) * gain_vec + shift_vec


def norm_back(signal, gain_vec, upstream):
    average = jnp.mean(signal, axis=-1, keepdims=True)
    centered = signal - average
    inverse = lax.rsqrt(jnp.mean(centered * centered, axis=-1, keepdims=True) + 1e-05)
    standard = centered * inverse
    scaled = upstream * gain_vec
    through = inverse * (
        scaled
        - jnp.mean(scaled, axis=-1, keepdims=True)
        - standard * jnp.mean(scaled * standard, axis=-1, keepdims=True)
    )
    return (through, jnp.sum(upstream * standard, axis=0), jnp.sum(upstream, axis=0))


def head_total(partial_sum):
    return lax.psum(partial_sum.astype(jnp.bfloat16), LINE).astype(jnp.float32)


def swapped(x):
    return lax.ppermute(x, SECTION, [(0, 1), (1, 0)])


def split_heads(matrix):
    return matrix.reshape(matrix.shape[0], matrix.shape[1] // HEAD, HEAD)


def softmax_rows(query, key_rows, allowed):
    logits = jnp.einsum(
        "qhd,khd->hqk",
        split_heads(query),
        split_heads(key_rows),
        preferred_element_type=jnp.float32,
    ) * HEAD ** (-0.5)
    logits = jnp.where(allowed[None], logits, masked_score)
    exponent = jnp.exp(logits - jnp.max(logits, axis=-1, keepdims=True))
    return exponent / jnp.sum(exponent, axis=-1, keepdims=True)


def attend(query, key_rows, value_rows, allowed):
    weights_low = softmax_rows(query, key_rows, allowed).astype(jnp.bfloat16)
    result = jnp.einsum(
        "hqk,khd->qhd", weights_low, split_heads(value_rows), preferred_element_type=jnp.float32
    )
    return result.reshape(query.shape).astype(jnp.bfloat16)


def attend_back(query, key_rows, value_rows, allowed, grad_out):
    probabilities = softmax_rows(query, key_rows, allowed)
    weights_low = probabilities.astype(jnp.bfloat16)
    grad_heads = split_heads(grad_out)
    grad_prob = jnp.einsum(
        "qhd,khd->hqk", grad_heads, split_heads(value_rows), preferred_element_type=jnp.float32
    )
    centre = jnp.sum(probabilities * grad_prob, axis=-1, keepdims=True)
    grad_logit = (probabilities * (grad_prob - centre)).astype(jnp.bfloat16)
    scale = HEAD ** (-0.5)
    grad_query = (
        jnp.einsum(
            "hqk,khd->qhd", grad_logit, split_heads(key_rows), preferred_element_type=jnp.float32
        )
        * scale
    )
    grad_keys = (
        jnp.einsum(
            "hqk,qhd->khd", grad_logit, split_heads(query), preferred_element_type=jnp.float32
        )
        * scale
    )
    grad_values = jnp.einsum(
        "hqk,qhd->khd", weights_low, grad_heads, preferred_element_type=jnp.float32
    )
    return (
        grad_query.reshape(query.shape),
        grad_keys.reshape(key_rows.shape),
        grad_values.reshape(value_rows.shape),
    )


def sum_rows(rows):
    return jnp.concatenate(rows, axis=0)


def on_four_frames(inputs, lengths, text, cotangent, vector_args, matrix_args):
    section = lax.axis_index(SECTION)
    at_zero = section == 0
    frame_index = lax.axis_index(FRAME)
    micro_count, rows_dev, model_width = inputs.shape
    rows_all = rows_dev * 4
    (
        query_weight,
        key_weight,
        value_weight,
        output_weight,
        cross_query,
        cross_key,
        cross_value,
        cross_output,
        expand_weight,
        reduce_weight,
    ) = (w[0] for w in matrix_args)
    columns = query_weight.shape[1]
    heads = columns // HEAD

    def by_section(first, second):
        return jnp.where(at_zero, first, second)

    own_vectors = jnp.pad(jnp.concatenate(vector_args, axis=0), ((0, 2), (0, 0)))
    heads_weight = jnp.stack(
        [w.T.reshape(heads, HEAD, model_width) for w in (query_weight, key_weight, value_weight)], axis=1
    ).reshape(3 * columns, model_width)
    _, (other_heads, other_vectors) = call(
        None, [], [], [], (), 1, [WeightTask(heads_weight), CrossTask(own_vectors, own_vectors, False)]
    )
    vectors = [by_section(own_vectors, other_vectors), by_section(other_vectors, own_vectors)]
    heads_pair = (heads_weight, other_heads)
    text_local = text.reshape(-1, model_width)
    text_states = jnp.concatenate(
        [matmul(text_local, cross_key), matmul(text_local, cross_value)], axis=1
    ).astype(jnp.bfloat16)
    text_states = text_states.reshape(micro_count, -1, 2 * columns)

    item_ends = jnp.cumsum(lax.dynamic_index_in_dim(lengths, section, 0, keepdims=False))
    passed = jnp.arange(rows_all, dtype=jnp.int32)[None, :] >= item_ends[:, None]
    begins = jnp.max(jnp.where(passed, item_ends[:, None], 0), axis=0, keepdims=True).astype(jnp.int32)
    seg = jnp.sum(passed.astype(jnp.int32), axis=0, keepdims=True)
    seg = lax.dynamic_slice_in_dim(seg, frame_index * rows_dev, rows_dev, 1)

    entering = inputs
    normed = layer_norm(
        lax.dynamic_index_in_dim(inputs, section, 0, keepdims=False).astype(jnp.float32),
        vectors[0][0],
        vectors[0][1],
    ).astype(jnp.bfloat16)
    saved = []
    for layer in range(2):
        gains, first = vectors[layer], layer == 0
        tasks = []
        if first:
            tasks = [WeightTask(w) for w in (output_weight, cross_query, cross_output)]
            tasks.append(TextTask(text_states))
        (heads_t, attended_t), carried = self_forward(
            normed, heads_pair, begins, layer, 2 + layer, tasks
        )
        tasks = []
        if first:
            weights = list(zip((output_weight, cross_query, cross_output), carried))
            states = carried[3].reshape(2, -1, 2 * columns)
            (second_normed, middle, queries, cross_att, third_normed, latter), carried = forward_chain(
                layer,
                attended_t,
                entering,
                states[layer],
                seg,
                gains,
                weights,
                4,
                [WeightTask(expand_weight), WeightTask(reduce_weight)],
            )
            weights += list(zip((expand_weight, reduce_weight), carried))
            (before, hidden, next_normed, result_low), _ = feed_chain(
                layer, third_normed, latter, weights, vectors[1], 5
            )
        else:
            outs, _ = forward_chain(
                layer, attended_t, entering, states[layer], seg, gains, weights, 6, []
            )
            second_normed, middle, queries, cross_att, third_normed, latter = outs[:6]
            before, hidden, result_low = outs[6:]
        saved.append(
            (
                entering,
                normed,
                heads_t,
                attended_t,
                middle,
                second_normed,
                latter,
                third_normed,
                queries,
                cross_att,
                before,
                hidden,
            )
        )
        if first:
            normed, entering = next_normed, result_low

    upstream = cotangent
    in_lows, vector_grads, shares = [None] * 2, [None] * 2, [{}, {}]
    totals = {}

    def low_product(left, right):
        return matmul_tn(left, right).astype(jnp.bfloat16)

    def crossing(*names):
        return [CrossTask(shares[0][name], shares[1][name], True) for name in names]

    for layer in (1, 0):
        last = layer == 0
        gains = vectors[layer]
        (
            entering,
            normed,
            heads_t,
            attended_t,
            middle,
            second_normed,
            latter,
            third_normed,
            queries,
            cross_att,
            before,
            hidden,
        ) = saved[layer]
        tasks = [] if last else [BothTask(saved[1][0], result_low)]
        (
            grad_pre,
            grad_cross,
            third_gain_grad,
            third_shift_grad,
            grad_queries,
            grad_states,
            grad_self,
            second_gain_grad,
            second_shift_grad,
        ), carried = backward_chain(
            layer,
            upstream,
            before,
            hidden,
            third_normed,
            latter,
            queries,
            states[layer],
            seg,
            middle,
            gains,
            weights,
            8 + layer,
            tasks,
        )
        shares[layer]["reduce"], shares[layer]["expand"] = carried[-2:]
        if not last:
            layer_outputs = carried[0]

        tasks = [ShareTask(grad_states)] + (crossing("reduce", "expand") if last else [])
        (grad_heads_t,), carried = self_backward(
            heads_t, grad_self, weights[0], begins, layer, 10 + layer, tasks
        )
        shares[layer]["states"] = carried[0]
        if last:
            totals["reduce"], totals["expand"] = carried[1:]

        tasks = [CrossTask(shares[0]["states"], shares[1]["states"], False)] if last else []
        (in_lows[layer], first_gain_grad, first_shift_grad, *both_grads), carried = last_chain(
            layer,
            grad_heads_t,
            entering,
            gains[0],
            grad_self,
            heads_pair,
            in_lows[1] if last else None,
            [(cross_att, grad_cross), (attended_t, grad_self), (second_normed, grad_queries), (normed, None)],
            12 + layer,
            tasks,
        )
        names = ("cross_output", "output", "cross_query", "heads")
        shares[layer].update(zip(names, carried[-4:]))
        if last:
            other_states = carried[0]
        vector_grads[layer] = sum_rows(
            [
                first_gain_grad,
                first_shift_grad,
                second_gain_grad,
                second_shift_grad,
                third_gain_grad,
                third_shift_grad,
                jnp.zeros((2, model_width), jnp.float32),
            ]
        )
        upstream = in_lows[layer]

    own_states = by_section(shares[0]["states"], shares[1]["states"])
    text_rows = sum_rows([by_section(own_states, other_states), by_section(other_states, own_states)])
    key_part, value_part = text_rows[:, :columns], text_rows[:, columns:]
    text_part = matmul_nt(key_part, cross_key) + matmul_nt(value_part, cross_value)
    _, (text_grad, vector_total, cross_grads, *carried) = call(
        None,
        [],
        [],
        [],
        (),
        18,
        [
            TotalTask(text_part.astype(jnp.bfloat16)),
            VectorTask(jnp.stack(vector_grads)),
            ShareTask(low_product(text_local, text_rows)),
        ]
        + crossing(*names),
    )
    totals.update(zip(names, carried))
    text_grad = text_grad.astype(jnp.float32).reshape(text.shape)
    vector_total = lax.dynamic_slice_in_dim(
        vector_total, frame_index * (model_width // 4), model_width // 4, 1
    )
    grad_query, grad_key, grad_value = (
        totals["heads"].reshape(-1, heads, 3, HEAD)[:, :, i].reshape(-1, columns) for i in range(3)
    )
    cross_grads = cross_grads.astype(jnp.float32)

    ordered = (
        vector_total[0],
        vector_total[1],
        grad_query,
        grad_key,
        grad_value,
        totals["output"],
        vector_total[2],
        vector_total[3],
        totals["cross_query"],
        cross_grads[:, :columns],
        cross_grads[:, columns:],
        totals["cross_output"],
        vector_total[4],
        vector_total[5],
        totals["expand"],
        totals["reduce"],
    )
    layer_outputs, input_grads = (a.astype(jnp.float32) for a in (layer_outputs, both_grads[0]))
    return (layer_outputs[None], input_grads[None], text_grad) + tuple(g[None] for g in ordered)


def self_attention(query, key_rows, value_rows, masks):
    all_keys = lax.all_gather(key_rows, FRAME, axis=0, tiled=True)
    all_values = lax.all_gather(value_rows, FRAME, axis=0, tiled=True)
    return attend(query, all_keys, all_values, masks["own"]), (query, all_keys, all_values)


def self_attention_back(kept, grad_out, masks):
    query, keys, values = kept
    grad_q, grad_k_all, grad_v_all = attend_back(query, keys, values, masks["own"], grad_out)
    grad_k, grad_v = (
        lax.psum_scatter(g.astype(jnp.bfloat16), FRAME, scatter_dimension=0, tiled=True)
        for g in (grad_k_all, grad_v_all)
    )
    return grad_q.astype(jnp.bfloat16), grad_k, grad_v


def forward(entering, vectors, weights, cross_keys, cross_values, masks):
    first_gain, first_shift, second_gain, second_shift, third_gain, third_shift = vectors
    (
        query_weight,
        key_weight,
        value_weight,
        output_weight,
        cross_query,
        cross_output,
        expand_weight,
        reduce_weight,
    ) = weights
    signal = entering.astype(jnp.float32)
    first_normed = layer_norm(signal, first_gain, first_shift).astype(jnp.bfloat16)
    query = matmul(first_normed, query_weight).astype(jnp.bfloat16)
    key_rows = matmul(first_normed, key_weight).astype(jnp.bfloat16)
    value_rows = matmul(first_normed, value_weight).astype(jnp.bfloat16)
    attended, heads_kept = self_attention(query, key_rows, value_rows, masks)
    middle = signal + head_total(matmul(attended, output_weight))
    second_normed = layer_norm(middle, second_gain, second_shift).astype(jnp.bfloat16)
    cross_queries = matmul(second_normed, cross_query).astype(jnp.bfloat16)
    cross_att = attend(cross_queries, cross_keys, cross_values, masks["cross"])
    latter = middle + head_total(matmul(cross_att, cross_output))
    third_normed = layer_norm(latter, third_gain, third_shift).astype(jnp.bfloat16)
    hidden_pre = matmul(third_normed, expand_weight)
    hidden_act = jax.nn.gelu(hidden_pre, approximate=False).astype(jnp.bfloat16)
    result = latter + head_total(matmul(hidden_act, reduce_weight))
    saved = (
        signal,
        first_normed,
        heads_kept,
        attended,
        middle,
        second_normed,
        cross_queries,
        cross_att,
        latter,
        third_normed,
        hidden_pre,
        hidden_act,
    )
    return (result, saved)


def backward(saved, upstream, vectors, weights, cross_keys, cross_values, masks):
    first_gain, first_shift, second_gain, second_shift, third_gain, third_shift = vectors
    (
        query_weight,
        key_weight,
        value_weight,
        output_weight,
        cross_query,
        cross_output,
        expand_weight,
        reduce_weight,
    ) = weights
    (
        signal,
        first_normed,
        heads_kept,
        attended,
        middle,
        second_normed,
        cross_queries,
        cross_att,
        latter,
        third_normed,
        hidden_pre,
        hidden_act,
    ) = saved
    grad_out = upstream.astype(jnp.bfloat16)
    grad_reduce = matmul_tn(hidden_act, grad_out)
    grad_act = matmul_nt(grad_out, reduce_weight)
    slope = (
        0.5 * (1.0 + lax.erf(hidden_pre * inv_sqrt_two))
        + hidden_pre * jnp.exp(-0.5 * hidden_pre * hidden_pre) * inv_sqrt_tau
    )
    grad_pre = (grad_act * slope).astype(jnp.bfloat16)
    grad_expand = matmul_tn(third_normed, grad_pre)
    grad_third = head_total(matmul_nt(grad_pre, expand_weight))
    grad_latter, grad_third_gain, grad_third_shift = norm_back(latter, third_gain, grad_third)
    grad_latter = grad_latter + upstream
    grad_cross = grad_latter.astype(jnp.bfloat16)
    grad_cross_output = matmul_tn(cross_att, grad_cross)
    grad_cross_att = matmul_nt(grad_cross, cross_output).astype(jnp.bfloat16)
    grad_cq, grad_ck, grad_cv = attend_back(
        cross_queries, cross_keys, cross_values, masks["cross"], grad_cross_att
    )
    grad_text_rows = jnp.concatenate([grad_ck, grad_cv], axis=1).astype(jnp.bfloat16)
    grad_text_rows = lax.psum_scatter(
        grad_text_rows.reshape(ITEMS, TEXT, -1), FRAME, scatter_dimension=1, tiled=True
    )
    grad_cquery = grad_cq.astype(jnp.bfloat16)
    grad_cross_query = matmul_tn(second_normed, grad_cquery)
    grad_second = head_total(matmul_nt(grad_cquery, cross_query))
    grad_middle, grad_second_gain, grad_second_shift = norm_back(middle, second_gain, grad_second)
    grad_middle = grad_middle + grad_latter
    grad_self = grad_middle.astype(jnp.bfloat16)
    grad_output = matmul_tn(attended, grad_self)
    grad_att = matmul_nt(grad_self, output_weight).astype(jnp.bfloat16)
    grad_query_low, grad_key_low, grad_value_low = self_attention_back(heads_kept, grad_att, masks)
    grad_query = matmul_tn(first_normed, grad_query_low)
    grad_key = matmul_tn(first_normed, grad_key_low)
    grad_value = matmul_tn(first_normed, grad_value_low)
    grad_first = head_total(
        matmul_nt(grad_query_low, query_weight)
        + matmul_nt(grad_key_low, key_weight)
        + matmul_nt(grad_value_low, value_weight)
    )
    grad_signal, grad_first_gain, grad_first_shift = norm_back(signal, first_gain, grad_first)
    grad_signal = grad_signal + grad_middle
    vector_grads = (
        grad_first_gain,
        grad_first_shift,
        grad_second_gain,
        grad_second_shift,
        grad_third_gain,
        grad_third_shift,
    )
    matrix_grads = (
        grad_query,
        grad_key,
        grad_value,
        grad_output,
        grad_cross_query,
        grad_cross_output,
        grad_expand,
        grad_reduce,
    )
    matrix_grads = tuple(
        lax.psum_scatter(g.astype(jnp.bfloat16), FRAME, scatter_dimension=0, tiled=True)
        for g in matrix_grads
    )
    return grad_signal, vector_grads, matrix_grads, grad_text_rows


def per_device(
    inputs,
    lengths,
    text,
    cotangent,
    first_gain,
    first_shift,
    query_weight,
    key_weight,
    value_weight,
    output_weight,
    second_gain,
    second_shift,
    cross_query,
    cross_key,
    cross_value,
    cross_output,
    third_gain,
    third_shift,
    expand_weight,
    reduce_weight,
):
    head_count, frame_count = lax.axis_size(LINE), lax.axis_size(FRAME)
    local_heads = query_weight.shape[2] // HEAD
    if head_count == 4 and frame_count == 4 and local_heads == 4:
        return on_four_frames(
            inputs,
            lengths,
            text,
            cotangent,
            (first_gain, first_shift, second_gain, second_shift, third_gain, third_shift),
            (
                query_weight,
                key_weight,
                value_weight,
                output_weight,
                cross_query,
                cross_key,
                cross_value,
                cross_output,
                expand_weight,
                reduce_weight,
            ),
        )
    section = lax.axis_index(SECTION)
    at_zero = section == 0
    frame_index = lax.axis_index(FRAME)
    micro_count, rows_dev, model_width = inputs.shape
    rows_all = rows_dev * frame_count
    text_rows_dev = text.shape[2]

    def keep(pair):
        return jnp.where(at_zero, pair[0], pair[1])

    def give(pair):
        return jnp.where(at_zero, pair[1], pair[0])

    vector_args = jnp.concatenate(
        [first_gain, first_shift, second_gain, second_shift, third_gain, third_shift], axis=0
    )
    vectors = lax.all_gather(vector_args, SECTION)
    matrix_args = (
        query_weight,
        key_weight,
        value_weight,
        output_weight,
        cross_query,
        cross_output,
        expand_weight,
        reduce_weight,
    )
    matrices = [lax.all_gather(w[0], SECTION) for w in matrix_args]
    weights = [tuple(w[layer] for w in matrices) for layer in range(2)]

    text_full = lax.all_gather(text, FRAME, axis=2, tiled=True)
    text_flat = text_full.reshape(micro_count * ITEMS * TEXT, model_width)
    text_heads = jnp.concatenate(
        [matmul(text_flat, cross_key[0]), matmul(text_flat, cross_value[0])], axis=1
    ).astype(jnp.bfloat16)
    text_heads = text_heads.reshape(micro_count, ITEMS * TEXT, -1)
    own_text = keep(text_heads)
    other_text = swapped(give(text_heads))
    columns = cross_key.shape[2]
    cross_states = [
        jnp.where(at_zero, own_text, other_text),
        jnp.where(at_zero, other_text, own_text),
    ]
    cross_keys = [c[:, :columns] for c in cross_states]
    cross_values = [c[:, columns:] for c in cross_states]

    item_ends = jnp.cumsum(lax.dynamic_index_in_dim(lengths, section, 0, keepdims=False))
    all_positions = jnp.arange(rows_all, dtype=jnp.int32)
    seg_all = jnp.sum((all_positions[:, None] >= item_ends[None, :]).astype(jnp.int32), axis=1)
    own_start = frame_index * rows_dev
    own_positions = own_start + jnp.arange(rows_dev, dtype=jnp.int32)
    seg_own = lax.dynamic_slice_in_dim(seg_all, own_start, rows_dev)
    text_item = jnp.arange(ITEMS * TEXT, dtype=jnp.int32) // TEXT
    masks = {
        "own": (all_positions[None, :] <= own_positions[:, None])
        & (seg_own[:, None] == seg_all[None, :]),
        "cross": seg_own[:, None] == text_item[None, :],
    }

    signal = lax.dynamic_index_in_dim(inputs, section, 0, keepdims=False)
    results, saves = [], []
    for layer in range(2):
        result, saved = forward(
            signal, vectors[layer], weights[layer], cross_keys[layer], cross_values[layer], masks
        )
        results.append(result)
        saves.append(saved)
        signal = result.astype(jnp.bfloat16)

    upstream = lax.dynamic_index_in_dim(cotangent, section, 0, keepdims=False)
    in_grads, vector_grads, matrix_grads, text_grads = [None] * 2, [None] * 2, [None] * 2, [None] * 2
    for layer in (1, 0):
        grad_signal, vector_grads[layer], matrix_grads[layer], text_grads[layer] = backward(
            saves[layer],
            upstream,
            vectors[layer],
            weights[layer],
            cross_keys[layer],
            cross_values[layer],
            masks,
        )
        in_grads[layer] = grad_signal
        upstream = grad_signal.astype(jnp.bfloat16).astype(jnp.float32)

    def both_micros(pair):
        own = keep(pair)
        other = swapped(give([p.astype(jnp.bfloat16) for p in pair])).astype(own.dtype)
        return jnp.stack([jnp.where(at_zero, own, other), jnp.where(at_zero, other, own)])

    layer_outputs = both_micros(results)
    input_grads = both_micros(in_grads)
    totals = [
        keep(pair).astype(jnp.float32) + swapped(give(pair)).astype(jnp.float32)
        for pair in zip(*matrix_grads)
    ]
    text_rows = both_micros(text_grads)
    text_rows = text_rows.reshape(micro_count * ITEMS * text_rows_dev, -1)
    key_part, value_part = text_rows[:, :columns], text_rows[:, columns:]
    text_local = text.reshape(-1, model_width)
    grad_cross_key, grad_cross_value = (
        lax.psum_scatter(
            matmul_tn(text_local, part).astype(jnp.bfloat16),
            FRAME,
            scatter_dimension=0,
            tiled=True,
        ).astype(jnp.float32)
        for part in (key_part, value_part)
    )
    text_part = matmul_nt(key_part, cross_key[0]) + matmul_nt(value_part, cross_value[0])
    text_grad = lax.psum(text_part.astype(jnp.bfloat16), (SECTION, LINE)).astype(jnp.float32)
    text_grad = text_grad.reshape(text.shape)

    stacked = jnp.stack([jnp.stack(v) for v in vector_grads])
    stacked = lax.psum_scatter(
        stacked.astype(jnp.bfloat16), FRAME, scatter_dimension=2, tiled=True
    )
    vector_total = keep(stacked).astype(jnp.float32) + swapped(give(stacked)).astype(jnp.float32)

    grad_q, grad_k, grad_v, grad_o, grad_cq, grad_co, grad_e, grad_r = totals
    ordered = (
        vector_total[0],
        vector_total[1],
        grad_q,
        grad_k,
        grad_v,
        grad_o,
        vector_total[2],
        vector_total[3],
        grad_cq,
        grad_cross_key,
        grad_cross_value,
        grad_co,
        vector_total[4],
        vector_total[5],
        grad_e,
        grad_r,
    )
    return (layer_outputs[None], input_grads[None], text_grad) + tuple(g[None] for g in ordered)


def solution(mesh):
    return jax.shard_map(
        per_device,
        mesh=mesh,
        in_specs=(
            P(None, FRAME, None),
            P(),
            P(None, None, FRAME, None),
            P(None, FRAME, None),
            P(SECTION, None),
            P(SECTION, None),
            P(SECTION, None, LINE),
            P(SECTION, None, LINE),
            P(SECTION, None, LINE),
            P(SECTION, LINE, None),
            P(SECTION, None),
            P(SECTION, None),
            P(SECTION, None, LINE),
            P(SECTION, None, LINE),
            P(SECTION, None, LINE),
            P(SECTION, LINE, None),
            P(SECTION, None),
            P(SECTION, None),
            P(SECTION, None, LINE),
            P(SECTION, LINE, None),
        ),
        out_specs=(
            P(SECTION, None, FRAME, None),
            P(SECTION, None, FRAME, None),
            P(None, None, FRAME, None),
            P(SECTION, FRAME),
            P(SECTION, FRAME),
            P(SECTION, FRAME, LINE),
            P(SECTION, FRAME, LINE),
            P(SECTION, FRAME, LINE),
            P(SECTION, (LINE, FRAME), None),
            P(SECTION, FRAME),
            P(SECTION, FRAME),
            P(SECTION, FRAME, LINE),
            P(SECTION, FRAME, LINE),
            P(SECTION, FRAME, LINE),
            P(SECTION, (LINE, FRAME), None),
            P(SECTION, FRAME),
            P(SECTION, FRAME),
            P(SECTION, FRAME, LINE),
            P(SECTION, (LINE, FRAME), None),
        ),
        check_vma=False,
    )
```

```python
import jax
import jax.numpy as jnp
from jax import lax
from jax.experimental import pallas as pl
from jax.experimental.pallas import tpu as pltpu
from jax.sharding import PartitionSpec as P

HEAD = 64
TEXT = 64
ITEMS = 4

masked_score = -1e30
inv_sqrt_two = 0.7071067811865476
inv_sqrt_tau = 0.3989422804014327

MESH_IDS = pl.DeviceIdType.MESH
BUSY = pl.CostEstimate(flops=30_000_000_000, bytes_accessed=8_000_000, transcendentals=0)
LAG = 3
BLOCK = 128
VMEM_BYTES = 60 * 1024 * 1024
EPS = 1e-05
SECTION, LINE, FRAME = "section", "head", "frame"
BOTH, LINE_ONLY, BY_SECTION = "both", "line", "one"
NORM, NEXT, END = range(3)


class Task:
    operands = ()
    outs = ()
    out_in_vmem = True
    scratch = ()
    greets = ()
    late = False
    hooked = 0

    def middle(self):
        pass

    def bind(self, ins, outs, scratch):
        self.ins, self.out, self.room = ins, outs, scratch


def remote(source, landing, send_sem, recv_sem, target):
    return pltpu.make_async_remote_copy(
        src_ref=source,
        dst_ref=landing,
        send_sem=send_sem,
        recv_sem=recv_sem,
        device_id=target,
        device_id_type=MESH_IDS,
    )


def frame_partners():
    me = lax.axis_index(FRAME)
    return (me + 1 - 2 * lax.rem(me, 2), lax.rem(me + 2, 4), 3 - me)


def span(index, size):
    return pl.ds(pl.multiple_of(index * size, size), size)


class WeightTask(Task):
    out_in_vmem = False
    greets = (SECTION, FRAME)

    def __init__(self, weight, layer=None, quarter=None):
        self.layer = layer
        self.operands = (weight,) if quarter is None else (weight, quarter)
        self.outs = (jax.ShapeDtypeStruct(weight.shape, weight.dtype),)
        self.scratch = (pltpu.SemaphoreType.DMA((10,)),)
        if layer is not None:
            self.scratch += (pltpu.VMEM((2,) + weight.shape, weight.dtype),)
        self.quarter = weight.shape[0] // 4

    @property
    def ref(self):
        other = jnp.where(lax.axis_index(SECTION) == self.layer, 0, 1)
        return self.room[1].at[other]

    def arrived(self, at):
        return self.out[0].at[at] if self.layer is None else self.room[1].at[1, at]

    def over(self):
        sems, at = self.room[0], span(lax.axis_index(FRAME), self.quarter)
        target = {SECTION: 1 - lax.axis_index(SECTION)}
        return remote(self.ins[0].at[at], self.arrived(at), sems.at[0], sems.at[1], target)

    def along(self):
        sems, at = self.room[0], span(lax.axis_index(FRAME), self.quarter)
        target = {FRAME: frame_partners()[1]}
        source = self.ins[1] if len(self.ins) > 1 else self.arrived(at)
        return remote(source, self.arrived(at), sems.at[2], sems.at[3], target)

    def settle(self):
        at = span(lax.axis_index(FRAME), self.quarter)
        return pltpu.make_async_copy(self.ins[1], self.arrived(at), self.room[0].at[0])

    def within(self):
        sems, partners = self.room[0], frame_partners()
        copies = []
        for k, whose in enumerate((lax.axis_index(FRAME), partners[1])):
            at = span(whose, self.quarter)
            copies.append(
                remote(
                    self.arrived(at),
                    self.arrived(at),
                    sems.at[4 + 2 * k],
                    sems.at[5 + 2 * k],
                    {FRAME: partners[0]},
                )
            )
        return copies

    def begin(self):
        if len(self.ins) > 1:
            self.settle().start()
            self.along().start()
        else:
            self.over().start()
        if self.layer is not None:
            pltpu.make_async_copy(self.ins[0], self.room[1].at[0], self.room[0].at[8]).start()

    def first_hop(self):
        self.over().wait_recv()
        self.along().start()

    def second_hop(self):
        if len(self.ins) > 1:
            self.settle().wait()
        self.along().wait_recv()
        for copy in self.within():
            copy.start()

    def arrive(self):
        for copy in self.within():
            copy.wait_recv()
        if self.layer is not None:
            sems = self.room[0]
            pltpu.make_async_copy(self.ins[0], self.room[1].at[0], sems.at[8]).wait()
            pltpu.make_async_copy(self.room[1].at[1], self.out[0], sems.at[9]).start()

    def sent(self):
        over = [] if len(self.ins) > 1 else [self.over()]
        for copy in over + [self.along()] + self.within():
            copy.wait_send()
        if self.layer is not None:
            pltpu.make_async_copy(self.room[1].at[1], self.out[0], self.room[0].at[9]).wait()

    def steps(self):
        if self.layer is not None:
            return [self.sent]
        return [self.first_hop, self.second_hop][self.hooked :] + [self.arrive, self.sent]


class QuarterTask(Task):
    out_in_vmem = False
    greets = (SECTION,)

    def __init__(self, weight):
        self.quarter = weight.shape[0] // 4
        self.operands = (weight,)
        self.outs = (jax.ShapeDtypeStruct((self.quarter, weight.shape[1]), weight.dtype),)
        self.scratch = (pltpu.SemaphoreType.DMA((2,)),)

    def over(self):
        sems, at = self.room[0], span(lax.axis_index(FRAME), self.quarter)
        target = {SECTION: 1 - lax.axis_index(SECTION)}
        return remote(self.ins[0].at[at], self.out[0], sems.at[0], sems.at[1], target)

    def begin(self):
        self.over().start()

    def steps(self):
        return [lambda: self.over().wait()]


class ShareTask(Task):
    greets = (FRAME,)

    def __init__(self, grad):
        rows, width = grad.shape
        self.share = rows // 4
        self.far = isinstance(grad, jax.Array)
        self.operands = (grad,) if self.far else ()
        piece = (self.share, width)
        self.outs = (jax.ShapeDtypeStruct(piece, jnp.bfloat16),)
        self.scratch = (
            pltpu.VMEM((2,) + piece, jnp.bfloat16),
            pltpu.VMEM((2,) + piece, jnp.bfloat16),
            pltpu.SemaphoreType.DMA((3,)),
            pltpu.SemaphoreType.DMA((3,)),
        )
        if self.far:
            self.scratch += (pltpu.VMEM((2,) + piece, jnp.bfloat16), pltpu.SemaphoreType.DMA((2,)))

    def within(self):
        landing, _, send_sems, recv_sems, *here = self.room
        me = lax.axis_index(FRAME)
        other = frame_partners()[0]
        side = lax.div(me, 2)
        copies = []
        for k, to_side in enumerate((1 - side, side)):
            given = 2 * to_side + lax.rem(other, 2)
            kept = 2 * to_side + lax.rem(me, 2)
            copies.append(
                remote(
                    self.ins[0].at[span(given, self.share)],
                    landing.at[k],
                    send_sems.at[k],
                    recv_sems.at[k],
                    {FRAME: other},
                )
            )
            if self.far:
                own, sems = here
                source = self.ins[0].at[span(kept, self.share)]
                copies.append(pltpu.make_async_copy(source, own.at[k], sems.at[k]))
        return copies

    def over(self):
        crossing, send_sems, recv_sems = self.room[1:4]
        target = {FRAME: frame_partners()[1]}
        return remote(crossing.at[0], crossing.at[1], send_sems.at[2], recv_sems.at[2], target)

    def chip_sum(self, k):
        me = lax.axis_index(FRAME)
        if self.far:
            own = self.room[4][k]
        else:
            side = lax.div(me, 2) if k else 1 - lax.div(me, 2)
            own = self.ins[0][span(2 * side + lax.rem(me, 2), self.share), :]
        return own.astype(jnp.float32) + self.room[0][k].astype(jnp.float32)

    def begin(self):
        for copy in self.within():
            copy.start()

    def middle(self):
        for copy in self.within():
            copy.wait()
        self.room[1][0] = self.chip_sum(0).astype(jnp.bfloat16)
        self.over().start()

    def steps(self):
        def end():
            self.over().wait()
            total = self.chip_sum(1) + self.room[1][1].astype(jnp.float32)
            self.out[0][...] = total.astype(jnp.bfloat16)

        return [end]


class BothTask(Task):
    out_in_vmem = False
    greets = (SECTION,)

    def __init__(self, first, second):
        self.operands = (first, second)
        self.outs = (jax.ShapeDtypeStruct((2,) + first.shape, first.dtype),)
        self.scratch = (pltpu.SemaphoreType.DMA((3,)),)

    def copies(self, given, kept):
        (sems,) = self.room
        section = lax.axis_index(SECTION)
        place = self.out[0].at[section]
        over = remote(self.ins[given], place, sems.at[0], sems.at[1], {SECTION: 1 - section})
        return over, pltpu.make_async_copy(self.ins[kept], place, sems.at[2])

    def begin(self):
        section = lax.axis_index(SECTION)
        for which in (0, 1):

            @pl.when(section == which)
            def _():
                for copy in self.copies(1 - which, which):
                    copy.start()

    def steps(self):
        def end():
            for copy in self.copies(0, 1):
                copy.wait()

        return [end]


class CrossTask(Task):
    greets = (SECTION,)

    def __init__(self, first, second, added):
        self.operands = (first, second)
        self.added = added
        self.out_in_vmem = added
        shape = first.shape
        if added:
            self.outs = (jax.ShapeDtypeStruct(shape, jnp.float32),)
            self.scratch = (pltpu.VMEM(shape, jnp.bfloat16),) * 2 + (pltpu.SemaphoreType.DMA((3,)),)
        else:
            self.outs = (jax.ShapeDtypeStruct(shape, first.dtype),)
            self.scratch = (pltpu.SemaphoreType.DMA((2,)),)

    def copies(self, given, kept):
        sems = self.room[-1]
        landing = self.room[0] if self.added else self.out[0]
        target = {SECTION: 1 - lax.axis_index(SECTION)}
        copies = [remote(self.ins[given], landing, sems.at[0], sems.at[1], target)]
        if self.added:
            copies.append(pltpu.make_async_copy(self.ins[kept], self.room[1], sems.at[2]))
        return copies

    def begin(self):
        section = lax.axis_index(SECTION)
        for which in (0, 1):

            @pl.when(section == which)
            def _():
                for copy in self.copies(1 - which, which):
                    copy.start()

    def steps(self):
        def end():
            for copy in self.copies(0, 1):
                copy.wait()
            if self.added:
                self.out[0][...] = self.room[0][...].astype(jnp.float32) + self.room[1][...].astype(
                    jnp.float32
                )

        return [lambda: None, lambda: None, end]


class TextTask(Task):
    out_in_vmem = False
    greets = (SECTION, FRAME)

    def __init__(self, states):
        micros, rows, width = states.shape
        self.operands = (states,)
        self.outs = (jax.ShapeDtypeStruct((2, 4, rows, width), states.dtype),)
        self.scratch = (pltpu.SemaphoreType.DMA((3,)),) + (pltpu.SemaphoreType.DMA((2, 3)),) * 2

    def place(self, layer):
        return self.out[0].at[layer, lax.axis_index(FRAME)]

    def over(self):
        sems, section = self.room[0], lax.axis_index(SECTION)
        source = self.ins[0].at[1 - section]
        return remote(source, self.place(section), sems.at[0], sems.at[1], {SECTION: 1 - section})

    def stay(self):
        section = lax.axis_index(SECTION)
        return pltpu.make_async_copy(self.ins[0].at[section], self.place(section), self.room[0].at[2])

    def spread(self, far):
        section = lax.axis_index(SECTION)
        layer = 1 - section if far else section
        source = self.place(layer) if far else self.ins[0].at[section]
        pair = self.room[1 + far]
        return [
            remote(source, self.place(layer), pair.at[0, k], pair.at[1, k], {FRAME: other})
            for k, other in enumerate(frame_partners())
        ]

    def begin(self):
        for copy in [self.over(), self.stay()] + self.spread(0):
            copy.start()

    def steps(self):
        def first():
            self.over().wait_recv()
            for copy in self.spread(1):
                copy.start()

        def second():
            self.over().wait_send()
            self.stay().wait()
            for copy in self.spread(0) + self.spread(1):
                copy.wait()

        return [first, second]


class TotalTask(Task):
    greets = (SECTION, LINE)

    def __init__(self, part):
        rows, width = part.shape
        self.share = rows // 4
        self.operands = (part,)
        self.outs = (jax.ShapeDtypeStruct((rows, width), jnp.bfloat16),)
        piece = (self.share, width)
        self.scratch = (
            pltpu.VMEM((4,) + piece, jnp.bfloat16),
            pltpu.VMEM((2,) + piece, jnp.bfloat16),
            pltpu.SemaphoreType.DMA((4,)),
            pltpu.SemaphoreType.DMA((4,)),
            pltpu.SemaphoreType.DMA((2,)),
            pltpu.SemaphoreType.DMA((4,)),
            pltpu.SemaphoreType.DMA((4,)),
        )

    def partners(self):
        me = lax.axis_index(LINE)
        return [lax.rem(me + by, 4) for by in (1, 2, 3)]

    def spread(self):
        landing, _, send_sems, recv_sems = self.room[:4]
        me = lax.axis_index(LINE)
        away = [
            remote(
                self.ins[0].at[span(partner, self.share)],
                landing.at[by],
                send_sems.at[by],
                recv_sems.at[by],
                {LINE: partner},
            )
            for by, partner in enumerate(self.partners(), 1)
        ]
        stay = pltpu.make_async_copy(self.ins[0].at[span(me, self.share)], landing.at[0], send_sems.at[0])
        return away + [stay]

    def over(self):
        sums, sems = self.room[1], self.room[4]
        target = {SECTION: 1 - lax.axis_index(SECTION)}
        return remote(sums.at[0], sums.at[1], sems.at[0], sems.at[1], target)

    def gather(self):
        send_sems, recv_sems = self.room[5:]
        mine = self.out[0].at[span(lax.axis_index(LINE), self.share)]
        return [
            remote(mine, mine, send_sems.at[by], recv_sems.at[by], {LINE: partner})
            for by, partner in enumerate(self.partners(), 1)
        ]

    def begin(self):
        for copy in self.spread():
            copy.start()

    def steps(self):
        landing, sums = self.room[:2]

        def first():
            for copy in self.spread():
                copy.wait()
            total = landing[0].astype(jnp.float32)
            for by in (1, 2, 3):
                total = total + landing[by].astype(jnp.float32)
            sums[0] = total.astype(jnp.bfloat16)
            self.over().start()

        def second():
            self.over().wait()
            total = sums[0].astype(jnp.float32) + sums[1].astype(jnp.float32)
            self.out[0][span(lax.axis_index(LINE), self.share), :] = total.astype(jnp.bfloat16)
            for copy in self.gather():
                copy.start()

        def third():
            for copy in self.gather():
                copy.wait()

        return [first, second, third]


class VectorTask(Task):
    greets = (SECTION, FRAME)

    def __init__(self, grads):
        self.operands = (grads,)
        shape = grads.shape[1:]
        self.outs = (jax.ShapeDtypeStruct(shape, jnp.float32),)
        self.scratch = (
            pltpu.VMEM((4,) + grads.shape, jnp.float32),
            pltpu.VMEM((3,) + shape, jnp.float32),
            pltpu.SemaphoreType.DMA((4,)),
            pltpu.SemaphoreType.DMA((4,)),
            pltpu.SemaphoreType.DMA((2,)),
        )

    def spread(self):
        landing, _, send_sems, recv_sems, _ = self.room
        away = [
            remote(self.ins[0], landing.at[k], send_sems.at[k], recv_sems.at[k], {FRAME: partner})
            for k, partner in enumerate(frame_partners(), 1)
        ]
        return away + [pltpu.make_async_copy(self.ins[0], landing.at[0], send_sems.at[0])]

    def over(self):
        sums, sems = self.room[1], self.room[4]
        target = {SECTION: 1 - lax.axis_index(SECTION)}
        return remote(sums.at[0], sums.at[1], sems.at[0], sems.at[1], target)

    def begin(self):
        for copy in self.spread():
            copy.start()

    def steps(self):
        landing, sums = self.room[:2]
        section = lax.axis_index(SECTION)

        def first():
            for copy in self.spread():
                copy.wait()
            total = [
                (landing[0, layer] + landing[1, layer]) + (landing[2, layer] + landing[3, layer])
                for layer in (0, 1)
            ]
            for which in (0, 1):

                @pl.when(section == which)
                def _():
                    sums[0] = total[1 - which]
                    sums[2] = total[which]

            self.over().start()

        def second():
            self.over().wait()
            self.out[0][...] = sums[2] + sums[1]

        return [first, second]


def greet(kinds):
    barrier = pltpu.get_barrier_semaphore()
    section, head, frame = (lax.axis_index(a) for a in (SECTION, LINE, FRAME))
    targets = []
    if FRAME in kinds:
        targets += [{FRAME: other} for other in frame_partners()]
    if SECTION in kinds:
        targets.append({SECTION: 1 - section})
    if BOTH in kinds:
        targets += [{SECTION: 1 - section, FRAME: other} for other in frame_partners()]
    if LINE in kinds:
        targets += [{LINE: lax.rem(head + by, 4)} for by in (1, 2, 3)]
    for target in targets:
        pl.semaphore_signal(barrier, 1, device_id=target, device_id_type=MESH_IDS)
    if LINE_ONLY not in kinds or LINE in kinds:
        return lambda: pl.semaphore_wait(barrier, len(targets))

    for way in (-1, 1):
        other = head + way

        @pl.when((other >= 0) & (other < 4))
        def _():
            pl.semaphore_signal(barrier, 1, device_id={LINE: other}, device_id_type=MESH_IDS)

    is_end = (head == 0) | (head == 3)

    def wait():
        @pl.when(is_end)
        def _():
            pl.semaphore_wait(barrier, len(targets) + 1)

        @pl.when(jnp.logical_not(is_end))
        def _():
            pl.semaphore_wait(barrier, len(targets) + 2)

    return wait


def call(body, operands, outs, scratch, kinds, collective_id, tasks=(), in_vmem=True, end=None):
    whole, anywhere = pl.BlockSpec(memory_space=pltpu.VMEM), pl.BlockSpec(memory_space=pl.ANY)
    place = whole if in_vmem else anywhere
    in_specs, out_specs = [place] * len(operands), [place] * len(outs)
    operands, all_outs, scratch = list(operands), list(outs), list(scratch)
    counts = [(len(operands), len(outs), len(scratch))]
    kinds = set(kinds)
    for task in tasks:
        kinds |= set(task.greets)
        in_specs += [anywhere] * len(task.operands)
        out_specs += [whole if task.out_in_vmem else anywhere] * len(task.outs)
        operands += task.operands
        all_outs += task.outs
        scratch += task.scratch
        counts.append((len(task.operands), len(task.outs), len(task.scratch)))
    n_in, n_out = len(operands), len(all_outs)

    def kernel(*refs):
        groups = [list(refs[:n_in]), list(refs[n_in : n_in + n_out]), list(refs[n_in + n_out :])]
        bound = []
        for sizes in counts:
            bound.append([])
            for group, size in zip(groups, sizes):
                bound[-1].append(group[:size])
                del group[:size]
        for task, parts in zip(tasks, bound[1:]):
            task.bind(*parts)

        meet = greet(kinds)

        def ride():
            for task in tasks:
                if not task.late:
                    task.begin()

        def middle():
            for task in tasks:
                if not task.late:
                    task.middle()

        if body is None:
            meet()
            ride()
            middle()
        else:
            body(*bound[0], meet, ride, middle)
        queues = [task.steps() for task in tasks]
        while any(queues):
            for queue in queues:
                if queue:
                    queue.pop(0)()
        if end is not None:
            end()

    results = pl.pallas_call(
        kernel,
        out_shape=all_outs,
        in_specs=in_specs,
        out_specs=out_specs,
        scratch_shapes=scratch,
        compiler_params=pltpu.CompilerParams(
            collective_id=collective_id, has_side_effects=True, vmem_limit_bytes=VMEM_BYTES
        ),
    )(*operands)
    results = list(results)
    main, results = results[: len(outs)], results[len(outs) :]
    return main, results


def chunking(rows):
    return max(1, min(16, rows // 16))


def nt_product(left, right):
    return lax.dot_general(left, right, (((1,), (1,)), ((), ())), preferred_element_type=jnp.float32)


def plain_product(left, right):
    return jnp.dot(left, right, preferred_element_type=jnp.float32)


def norm_parts(v):
    average = jnp.mean(v, axis=-1, keepdims=True)
    centered = v - average
    inverse = lax.rsqrt(jnp.mean(centered * centered, axis=-1, keepdims=True) + EPS)
    return centered * inverse, inverse


class Held:
    def __init__(self, shape, dtype, sources=(), choose=None, stage=0, kept=False):
        self.shape, self.dtype = tuple(shape), dtype
        self.sources, self.choose, self.stage, self.kept = sources, choose, stage, kept
        self.ref = self.far = self.sem = None

    def copy_in(self, index=0):
        source = self.far[index]
        if self.choose == BY_SECTION:
            source = source.at[lax.axis_index(SECTION)]
        return pltpu.make_async_copy(source, self.ref, self.sem)

    def start_in(self):
        if not isinstance(self.choose, int):
            self.copy_in().start()
            return
        section = lax.axis_index(SECTION)

        @pl.when(section == self.choose)
        def _():
            self.copy_in(0).start()

        @pl.when(section != self.choose)
        def _():
            self.copy_in(1).start()

    def write(self, at, value):
        self.ref[at, :] = value
        if self.kept:
            pltpu.make_async_copy(self.ref.at[at], self.far[0].at[at], self.sem).start()

    def flush(self):
        pltpu.make_async_copy(self.ref, self.far[0], self.sem).start()

    def drain(self):
        pltpu.make_async_copy(self.ref, self.far[0], self.sem).wait()


class Build:
    def __init__(self):
        self.helds, self.rooms, self.extras = [], [], []

    def add(self, held):
        self.helds.append(held)
        return held

    def arg(self, array, stage, choose=None):
        shape = array.shape[1:] if choose == BY_SECTION else array.shape
        return self.add(Held(shape, array.dtype, (array,), choose, stage))

    def pick(self, pair, layer, stage):
        return self.add(Held(pair[0].shape, pair[0].dtype, tuple(pair), layer, stage))

    def out(self, shape, dtype):
        return self.add(Held(shape, dtype, kept=True))

    def temp(self, shape, dtype):
        return self.add(Held(shape, dtype))

    def extra(self, scratch):
        self.extras.append(scratch)
        return len(self.extras) - 1


class Stage:
    def __init__(self, rows, width):
        self.rows, self.width = rows, width
        self.begin = self.prepare = self.finish = None
        self.ends = []


class Chore:
    def __init__(self, build, stage, piece, each, left, right, flipped=False):
        self.start, self.each = (stage, piece), each
        self.left, self.right, self.flipped = left, right, flipped
        columns = left.shape[0] if flipped else left.shape[1]
        self.units = columns // BLOCK
        self.product = build.temp((columns, right.shape[1]), jnp.bfloat16)
        self.task = ShareTask(self.product)
        self.task.late = True

    def unit(self, number):
        at = span(number, BLOCK)
        right = self.right.ref[...].astype(jnp.bfloat16)
        if self.flipped:
            product = plain_product(self.left.ref[at, :], right)
        else:
            product = lax.dot_general(
                self.left.ref[:, at], right, (((0,), (0,)), ((), ())), preferred_element_type=jnp.float32
            )
        self.product.ref[at, :] = product.astype(jnp.bfloat16)

    def run(self, stage, pieces, piece):
        shift = (stage - self.start[0]) * pieces - self.start[1]
        steps = -(-self.units // self.each)

        def at_step(first, last, what):
            if shift >= last or shift + pieces <= first:
                return
            now = piece + shift

            @pl.when((now >= first) & (now < last))
            def _():
                what(now)

        def make(now):
            for more in range(self.each):
                self.unit(now * self.each + more)

        def begin(now):
            self.task.ins = [self.product.ref]
            self.task.begin()

        at_step(0, steps, make)
        at_step(steps, steps + 1, begin)
        at_step(steps + 5, steps + 6, lambda now: self.task.middle())


def line_chain(stages, need, part, set_out, middle, chores, hooks):
    place = lax.axis_index(LINE)
    rows = stages[0].rows
    pieces = chunking(rows)
    step = rows // pieces
    per_block = max(1, min(BLOCK, rows) // step)
    lag = max(0, min(LAG, pieces - per_block))
    is_end = (place == 0) | (place == 3)
    inner = {LINE: jnp.where(place == 0, 1, 2)}
    outer = {LINE: jnp.where(place == 1, 0, 3)}
    peer = {LINE: 3 - place}

    def inwards(stage, piece):
        send, held, _, send_sems, recv_sems = stage.room[:5]
        at = span(piece, step)
        return remote(send.at[at], held.at[at], send_sems.at[piece], recv_sems.at[piece], inner)

    def crossing(stage, piece):
        send, _, across = stage.room[:3]
        send_sems, recv_sems = stage.room[5:7]
        at = span(piece, step)
        return remote(send.at[at], across.at[at], send_sems.at[piece], recv_sems.at[piece], peer)

    def outwards(stage, piece):
        held = stage.room[1]
        send_sems, recv_sems = stage.room[7:]
        at = span(piece, step)
        return remote(held.at[at], held.at[at], send_sems.at[piece], recv_sems.at[piece], outer)

    def hook(stage, piece, at_end):
        for run, *spots in hooks:
            index, when = spots[0 if at_end else 1]
            if stages[index] is stage:

                @pl.when(piece == when)
                def _():
                    run()

    def open_stage(index):
        need(index)
        if stages[index].begin is not None:
            stages[index].begin()

    def loop(first, last, step_of):
        def one(piece, carry):
            step_of(piece)
            return carry

        lax.fori_loop(first, last, one, 0)

    def chore(stage, piece):
        for one in chores:
            one.run(stages.index(stage), pieces, piece)

    @pl.when(is_end)
    def _():
        def give(stage, piece):
            inwards(stage, piece).start()
            chore(stage, piece)
            hook(stage, piece, True)

        def take(stage, piece):
            outwards(stage, piece).wait_recv()
            stage.finish(span(piece, step), piece)

        for index, stage in enumerate(stages):
            open_stage(index)

            def block_step(block):
                low, high = block * per_block, (block + 1) * per_block
                if index:
                    loop(low, high, lambda piece: take(stages[index - 1], piece))
                stage.room[0][span(block, per_block * step), :] = stage.prepare(block).astype(jnp.bfloat16)
                if index == 0:
                    pl.when(block == 0)(set_out)
                loop(low, high, lambda piece: give(stage, piece))
                if index == 0:

                    @pl.when(block == 1)
                    def _():
                        middle()

            loop(0, pieces // per_block, block_step)
        loop(0, pieces, lambda piece: take(stages[-1], piece))
        for stage in stages:
            loop(0, pieces, lambda piece: inwards(stage, piece).wait_send())

    @pl.when(jnp.logical_not(is_end))
    def _():
        def add(stage, piece):
            @pl.when(lax.rem(piece, per_block) == 0)
            def _():
                part[...] = stage.prepare(lax.div(piece, per_block))

            if stage is stages[0]:
                pl.when(piece == 0)(set_out)
            at = span(piece, step)
            send, held = stage.room[:2]
            inwards(stage, piece).wait_recv()
            own = part[span(lax.rem(piece, per_block), step), :]
            send[at, :] = (own + held[at, :].astype(jnp.float32)).astype(jnp.bfloat16)
            crossing(stage, piece).start()
            chore(stage, piece)
            hook(stage, piece, False)
            if stage is stages[0]:

                @pl.when(piece == 2 * per_block - 1)
                def _():
                    middle()

        def settle(stage, piece):
            at = span(piece, step)
            send, held, across = stage.room[:3]
            crossing(stage, piece).wait_recv()
            total = send[at, :].astype(jnp.float32) + across[at, :].astype(jnp.float32)
            held[at, :] = total.astype(jnp.bfloat16)
            outwards(stage, piece).start()
            stage.finish(at, piece)

        for index, stage in enumerate(stages):
            open_stage(index)

            def both(piece):
                add(stage, piece)

                @pl.when(piece >= lag)
                def _():
                    settle(stage, piece - lag)

                if index and lag:

                    @pl.when(piece < lag)
                    def _():
                        settle(stages[index - 1], pieces - lag + piece)

            loop(0, pieces, both)
        loop(pieces - lag, pieces, lambda piece: settle(stages[-1], piece))

        def drain(stage, piece):
            crossing(stage, piece).wait_send()
            outwards(stage, piece).wait_send()

        for stage in stages:
            loop(0, pieces, lambda piece: drain(stage, piece))

    for stage in stages:
        for end in stage.ends:
            end()


def run_build(build, body, kinds, collective_id, tasks):
    operands, outs, scratch = [], [], []
    for held in build.helds:
        operands += held.sources
        if held.kept:
            outs.append(jax.ShapeDtypeStruct(held.shape, held.dtype))
        scratch.append(pltpu.VMEM(held.shape, held.dtype))
    n_held = len(scratch)
    scratch += build.extras
    scratch.append(pltpu.SemaphoreType.DMA((n_held,)))
    reads = sorted((held for held in build.helds if held.sources), key=lambda held: held.stage)

    def need(stage):
        for held in reads:
            if held.stage == stage:
                held.copy_in().wait()

    def run(ins, outs, scratch, meet, ride, middle):
        ins, outs = list(ins), list(outs)
        sems = scratch[-1]
        for index, held in enumerate(build.helds):
            held.ref, held.sem = scratch[index], sems.at[index]
            held.far = [ins.pop(0) for _ in held.sources]
            if held.kept:
                held.far = [outs.pop(0)]
        build.bound = scratch[n_held:-1]
        for held in reads:
            held.start_in()
        body(need, meet, ride, middle)

    def end():
        for held in build.helds:
            if held.kept:
                held.drain()

    return call(run, operands, outs, scratch, kinds, collective_id, tasks, in_vmem=False, end=end)


def run_chain(build, stages, collective_id, tasks, kinds=(LINE_ONLY,), chores=(), hooks=()):
    slots = []
    for stage in stages:
        pieces = chunking(stage.rows)
        room = [pltpu.VMEM((stage.rows, stage.width), jnp.bfloat16)] * 3
        room += [pltpu.SemaphoreType.DMA((pieces,))] * 6
        slots.append([build.extra(scratch) for scratch in room])
    part = build.extra(pltpu.VMEM((min(BLOCK, stages[0].rows), stages[0].width), jnp.float32))

    def body(need, meet, ride, middle):
        for stage, places in zip(stages, slots):
            stage.room = [build.bound[place] for place in places]
        def set_out():
            meet()
            ride()

        line_chain(stages, need, build.bound[part], set_out, middle, chores, hooks)

    tasks = list(tasks) + [one.task for one in chores]
    return run_build(build, body, kinds, collective_id, tasks)


def residual_norm(build, index, stage, base, gain, shift, mode):
    shape = (stage.rows, stage.width)
    result = build.temp(shape, jnp.float32) if mode == NORM else None
    normed = build.out(shape, jnp.bfloat16) if mode != END else None
    low = build.out(shape, jnp.bfloat16)
    if mode != END:
        gain, shift = build.arg(gain[None], index), build.arg(shift[None], index)

    def finish(at, piece):
        value = base.ref[at, :].astype(jnp.float32) + stage.room[1][at, :].astype(jnp.float32)
        rounded = value.astype(jnp.bfloat16)
        low.write(at, rounded)
        if mode == NORM:
            result.write(at, value)
        if mode == NEXT:
            value = rounded.astype(jnp.float32)
        if mode != END:
            standard, _ = norm_parts(value)
            normed.write(at, (standard * gain.ref[...] + shift.ref[...]).astype(jnp.bfloat16))

    stage.finish = finish
    return result, normed


def self_out_stage(build, index, layer, attended_t, weight, base):
    rows, width = base.shape
    stage = Stage(rows, width)
    flipped, matrix = build.arg(attended_t, index), build.pick(weight, layer, index)
    left = build.temp(attended_t.shape[::-1], jnp.bfloat16)

    def begin():
        left.ref[...] = flipped.ref[...].T

    def prepare(number):
        return plain_product(left.ref[span(number, min(BLOCK, rows)), :], matrix.ref[...])

    stage.begin, stage.prepare = begin, prepare
    return stage


def text_mask(states, seg):
    item = lax.rem(lax.div(lax.broadcasted_iota(jnp.int32, (states, 1), 0), TEXT // 4), ITEMS)
    return item == seg


def cross_stage(build, index, layer, normed, states, seg, into, out_of):
    rows, width = normed.shape
    stage = Stage(rows, width)
    states, seg = build.arg(states, index), build.arg(seg, index)
    columns, block = states.shape[1] // 2, min(BLOCK, rows)
    if not isinstance(into, WeightTask):
        into, out_of = build.pick(into, layer, index), build.pick(out_of, layer, index)
    queries = build.out((rows, columns), jnp.bfloat16)
    left = build.out((rows, columns), jnp.bfloat16)
    values_t = build.temp((columns, states.shape[0]), jnp.bfloat16)

    def begin():
        values_t.ref[...] = states.ref[:, columns:].T

    def prepare(number):
        at = span(number, block)
        query = plain_product(normed.ref[at, :], into.ref[...]).astype(jnp.bfloat16)
        queries.write(at, query)
        query_t = query.T
        allowed = text_mask(states.shape[0], seg.ref[:, at])
        mixed = []
        for head in range(columns // HEAD):
            cols = slice(head * HEAD, (head + 1) * HEAD)
            scores = plain_product(states.ref[:, cols], query_t[cols, :]) * HEAD ** (-0.5)
            scores = jnp.where(allowed, scores, masked_score)
            e = jnp.exp(scores - jnp.max(scores, axis=0, keepdims=True))
            total = jnp.sum(e, axis=0, keepdims=True)
            value = plain_product(values_t.ref[cols, :], e.astype(jnp.bfloat16))
            mixed.append((value * (1.0 / total)).astype(jnp.bfloat16))
        mixed = jnp.concatenate(mixed, axis=0).T
        left.write(at, mixed)
        return plain_product(mixed, out_of.ref[...])

    stage.begin, stage.prepare = begin, prepare
    return stage


def feed_stage(build, index, layer, normed, into, out_of):
    rows, width = normed.shape
    stage = Stage(rows, width)
    block = min(BLOCK, rows)
    if isinstance(into, WeightTask):
        hidden = into.operands[0].shape[1]
    else:
        hidden = into[0].shape[1]
        into, out_of = build.pick(into, layer, index), build.pick(out_of, layer, index)
    before = build.out((rows, hidden), jnp.bfloat16)
    left = build.out((rows, hidden), jnp.bfloat16)

    def prepare(number):
        at = span(number, block)
        u = plain_product(normed.ref[at, :], into.ref[...])
        before.write(at, u.astype(jnp.bfloat16))
        active = (0.5 * u * (1.0 + lax.erf(u * inv_sqrt_two))).astype(jnp.bfloat16)
        left.write(at, active)
        return plain_product(active, out_of.ref[...])

    stage.prepare = prepare
    return stage


def norm_backward(build, index, stage, value, gain, upstream, feeds, spare=None):
    shape = (stage.rows, stage.width)
    pieces = chunking(stage.rows)
    vector = (1, stage.width)
    by_section = BY_SECTION if value.ndim == 3 else None
    value, gain = build.arg(value, index, by_section), build.arg(gain[None], index)
    result = build.temp(shape, jnp.float32) if feeds else None
    low = build.out(shape, jnp.bfloat16)
    gain_grad, shift_grad = build.out(vector, jnp.float32), build.out(vector, jnp.float32)
    parts = build.extra(pltpu.VMEM((2, pieces, 1, stage.width), jnp.float32))
    if spare is not None:
        spare = build.arg(spare, index)
        both = build.out((2,) + shape, jnp.bfloat16)
        sems = build.extra(pltpu.SemaphoreType.DMA((2, pieces)))

    def over(at, piece, source):
        target = {SECTION: 1 - lax.axis_index(SECTION)}
        pair = build.bound[sems]
        landing = both.ref.at[lax.axis_index(SECTION), at]
        return remote(source.ref.at[at], landing, pair.at[0, piece], pair.at[1, piece], target)

    def finish(at, piece):
        grad = stage.room[1][at, :].astype(jnp.float32)
        standard, inverse = norm_parts(value.ref[at, :].astype(jnp.float32))
        scaled = grad * gain.ref[...]
        through = inverse * (
            scaled
            - jnp.mean(scaled, axis=-1, keepdims=True)
            - standard * jnp.mean(scaled * standard, axis=-1, keepdims=True)
        )
        total = through + upstream.ref[at, :].astype(jnp.float32)
        if feeds:
            result.write(at, total)
        low.write(at, total.astype(jnp.bfloat16))
        build.bound[parts][0, piece] = jnp.sum(grad * standard, axis=0, keepdims=True)
        build.bound[parts][1, piece] = jnp.sum(grad, axis=0, keepdims=True)
        if spare is not None:
            section = lax.axis_index(SECTION)

            @pl.when(section == 0)
            def _():
                both.ref[0, at, :] = low.ref[at, :]
                over(at, piece, spare).start()

            @pl.when(section == 1)
            def _():
                both.ref[1, at, :] = spare.ref[at, :]
                over(at, piece, low).start()

    def end():
        whole = slice(0, 1)
        gain_grad.write(whole, jnp.sum(build.bound[parts][0], axis=0))
        shift_grad.write(whole, jnp.sum(build.bound[parts][1], axis=0))
        if spare is not None:
            step = stage.rows // pieces

            def one(piece, carry):
                over(span(piece, step), piece, low).wait()
                return carry

            lax.fori_loop(0, pieces, one, 0)
            both.flush()

    stage.finish = finish
    stage.ends.append(end)
    return result, low


def feed_back_stage(build, index, layer, grad_out, before, out_of, into):
    rows, width = grad_out.shape
    stage = Stage(rows, width)
    hidden, block = out_of[0].shape[0], min(BLOCK, rows)
    before = build.arg(before, index)
    out_of, into = build.pick(out_of, layer, index), build.pick(into, layer, index)
    left = build.out((rows, hidden), jnp.bfloat16)

    def prepare(number):
        at = span(number, block)
        grad = nt_product(grad_out.ref[at, :].astype(jnp.bfloat16), out_of.ref[...])
        u = before.ref[at, :].astype(jnp.float32)
        slope = 0.5 * (1.0 + lax.erf(u * inv_sqrt_two)) + u * jnp.exp(-0.5 * u * u) * inv_sqrt_tau
        grad = (grad * slope).astype(jnp.bfloat16)
        left.write(at, grad)
        return nt_product(grad, into.ref[...])

    stage.prepare, stage.left = prepare, left
    return stage


def cross_back_stage(build, index, layer, grad_low, queries, states, seg, out_of, into):
    rows, width = grad_low.shape
    stage = Stage(rows, width)
    columns, block = out_of[0].shape[0], min(BLOCK, rows)
    queries, states, seg = (build.arg(array, index) for array in (queries, states, seg))
    out_of, into = build.pick(out_of, layer, index), build.pick(into, layer, index)
    left = build.out((rows, columns), jnp.bfloat16)
    state_grads = build.out(states.shape, jnp.bfloat16)
    keys_t = build.temp((columns, states.shape[0]), jnp.bfloat16)
    sums = build.temp(states.shape, jnp.float32)
    scale = HEAD ** (-0.5)

    def begin():
        keys_t.ref[...] = states.ref[:, :columns].T
        sums.ref[...] = jnp.zeros(sums.shape, jnp.float32)

    def prepare(number):
        at = span(number, block)
        grad = nt_product(grad_low.ref[at, :], out_of.ref[...]).astype(jnp.bfloat16)
        query = queries.ref[at, :]
        grad_t, query_t = grad.T, query.T
        allowed = text_mask(states.shape[0], seg.ref[:, at])
        query_grads = []
        for head in range(columns // HEAD):
            cols = slice(head * HEAD, (head + 1) * HEAD)
            more = slice(columns + head * HEAD, columns + (head + 1) * HEAD)
            scores = plain_product(states.ref[:, cols], query_t[cols, :]) * scale
            scores = jnp.where(allowed, scores, masked_score)
            e = jnp.exp(scores - jnp.max(scores, axis=0, keepdims=True))
            p = e * (1.0 / jnp.sum(e, axis=0, keepdims=True))
            slope = plain_product(states.ref[:, more], grad_t[cols, :])
            weighted = p * slope
            ds = (weighted - p * jnp.sum(weighted, axis=0, keepdims=True)).astype(jnp.bfloat16)
            query_grads.append((plain_product(keys_t.ref[cols, :], ds) * scale).astype(jnp.bfloat16))
            sums.ref[:, cols] += plain_product(ds, query[:, cols]) * scale
            sums.ref[:, more] += plain_product(p.astype(jnp.bfloat16), grad[:, cols])
        query_grads = jnp.concatenate(query_grads, axis=0).T
        left.write(at, query_grads)
        return nt_product(query_grads, into.ref[...])

    def end():
        state_grads.write(slice(0, states.shape[0]), sums.ref[...].astype(jnp.bfloat16))

    stage.begin, stage.prepare = begin, prepare
    stage.ends.append(end)
    return stage


def self_in_stage(build, index, layer, grads_t, weights, width):
    columns, rows = grads_t.shape
    stage = Stage(rows, width)
    part = columns // 3
    flipped = build.arg(grads_t, index)
    matrices = [build.pick(weight, layer, index) for weight in weights]
    left = build.temp((rows, columns), jnp.bfloat16)

    def begin():
        for number in range(3):
            heads = [
                flipped.ref[(3 * head + number) * HEAD : (3 * head + number + 1) * HEAD, :]
                for head in range(part // HEAD)
            ]
            left.ref[:, number * part : (number + 1) * part] = jnp.concatenate(heads, axis=0).T

    def prepare(number):
        at = span(number, min(BLOCK, rows))
        total = jnp.zeros((min(BLOCK, rows), width), jnp.float32)
        for number, matrix in enumerate(matrices):
            total = total + nt_product(left.ref[at, number * part : (number + 1) * part], matrix.ref[...])
        return total

    stage.begin, stage.prepare = begin, prepare
    stage.left = left
    return stage


def forward_chain(
    layer, attended_t, entering, states, seg, gains, after, weights, collective_id, tasks, late
):
    output, query, cross, expand, reduce = weights
    build = Build()
    base = build.arg(entering, 0, BY_SECTION if entering.ndim == 3 else None)
    first = self_out_stage(build, 0, layer, attended_t, output, base)
    middle, second_normed = residual_norm(build, 0, first, base, gains[2], gains[3], NORM)
    second = cross_stage(build, 1, layer, second_normed, states, seg, query, cross)
    latter, third_normed = residual_norm(build, 1, second, middle, gains[4], gains[5], NORM)
    third = feed_stage(build, 2, layer, third_normed, expand, reduce)
    mode = END if after is None else NEXT
    residual_norm(build, 2, third, latter, *((None, None) if after is None else after[:2]), mode)
    hooks = []
    if isinstance(expand, WeightTask):
        hooks = [
            (expand.second_hop, (1, 4), (0, 15)),
            (reduce.first_hop, (1, 0), (0, 10)),
            (reduce.second_hop, (1, 15), (1, 8)),
        ]
        for one in late:
            hooks += [(one.first_hop, (2, 0), (1, 8)), (one.second_hop, (2, 10), (2, 4))]
        start_second = second.begin

        def begin_second():
            query.second_hop()
            cross.second_hop()
            query.arrive()
            cross.arrive()
            start_second()

        def begin_third():
            expand.arrive()
            reduce.arrive()

        second.begin, third.begin = begin_second, begin_third
    return run_chain(build, [first, second, third], collective_id, tasks, hooks=hooks)


def add_backward(build, index, layer, arriving, saved, states, seg, gains, weights):
    _, query, cross, expand, reduce = weights
    middle, latter, third_normed, queries, before, hidden = saved
    first = feed_back_stage(build, index, layer, arriving, before, reduce, expand)
    grad_latter, grad_cross = norm_backward(build, index, first, latter, gains[4], arriving, True)
    second = cross_back_stage(build, index + 1, layer, grad_cross, queries, states, seg, cross, query)
    norm_backward(build, index + 1, second, middle, gains[2], grad_latter, False)
    first_piece, each = (12, 2) if index else (0, 1)
    chores = [
        Chore(build, index, first_piece, each, build.arg(hidden, index), arriving),
        Chore(build, index + 1, 0, each, build.arg(third_normed, index + 1), first.left),
    ]
    return [first, second], chores


def add_last(build, layer, grads_t, entering, gain, upstream, weights, spare, products):
    residual = build.arg(upstream, 0)
    stage = self_in_stage(build, 0, layer, grads_t, weights, upstream.shape[1])
    _, low = norm_backward(build, 0, stage, entering, gain, residual, False, spare)
    chores = []
    for left, right in products:
        flipped = left.shape[0] != upstream.shape[0]
        if right is None:
            right = stage.left
        else:
            right = residual if right is upstream else build.arg(right, 0)
        chores.append(Chore(build, 0, 0, 1, build.arg(left, 0), right, flipped))
    return stage, low, chores


def backward_chain(layer, upstream, saved, states, seg, gains, weights, collective_id, tasks):
    build = Build()
    arriving = build.arg(upstream, 0, BY_SECTION)
    stages, chores = add_backward(build, 0, layer, arriving, saved, states, seg, gains, weights)
    return run_chain(build, stages, collective_id, tasks, chores=chores)


def last_chain(layer, *rest, spare, products, collective_id, tasks):
    build = Build()
    stage, _, chores = add_last(build, layer, *rest, spare, products)
    return run_chain(build, [stage], collective_id, tasks, (LINE_ONLY, SECTION), chores)


def between_chain(layer, last, products, backward, collective_id, tasks):
    build = Build()
    stage, low, chores = add_last(build, layer, *last, None, products)
    stages, more = add_backward(build, 1, layer - 1, low, *backward)
    return run_chain(build, [stage] + stages, collective_id, tasks, chores=chores + more)


def masked_scores(keys, query_t, begins, start):
    reach, block = keys.shape[0], query_t.shape[1]
    scores = plain_product(keys, query_t)
    key_pos = lax.broadcasted_iota(jnp.int32, (reach, 1), 0)
    query_pos = start + lax.broadcasted_iota(jnp.int32, (1, block), 1)
    allowed = (key_pos <= query_pos) & (key_pos >= begins)
    return jnp.where(allowed, scores * HEAD ** (-0.5), masked_score)


def to_frames(source, landing, sems):
    me = lax.axis_index(FRAME)
    return [
        remote(source(other), landing(me), sems.at[0, k], sems.at[1, k], {FRAME: other})
        for k, other in enumerate(frame_partners())
    ]


def turned_parts(normed, matrices, own, at):
    for part, matrix in enumerate(matrices):
        turned = plain_product(normed, matrix.ref[...]).astype(jnp.bfloat16).T
        for head in range(4):
            rows = slice(part * HEAD, (part + 1) * HEAD)
            own.ref[at + (head, rows)] = turned[head * HEAD : (head + 1) * HEAD, :]


def self_forward(normed, weights, begins, layer, collective_id, tasks, early):
    first = int(normed.ndim == 3)
    rows, frames, width = normed.shape[-2], 4, 3 * HEAD
    all_rows = rows * frames
    build = Build()
    normed, begins = build.arg(normed, 0), build.arg(begins, 1)
    if first:
        matrices = [build.arg(weight, 0) for weight in weights]
    else:
        matrices = [build.pick(weight, layer, 0) for weight in weights]
    heads_t = build.out((width, all_rows), jnp.bfloat16)
    out = build.out((frames * HEAD, rows), jnp.bfloat16)
    own = build.temp((1 + first, frames, width, rows), jnp.bfloat16)
    keys = build.temp((all_rows, HEAD), jnp.bfloat16)
    mixed_t = build.temp((frames, HEAD, rows), jnp.bfloat16)
    sems = [build.extra(pltpu.SemaphoreType.DMA((2, frames - 1))) for _ in range(2)]
    over_sems = build.extra(pltpu.SemaphoreType.DMA((2, frames)))

    def body(need, meet, ride, middle):
        me, section = lax.axis_index(FRAME), lax.axis_index(SECTION)
        partners = frame_partners()
        block = min(2 * BLOCK, rows)
        landing = heads_t.ref.at[:, span(me, rows)]
        arriving = to_frames(lambda g: own.ref.at[0, g], lambda f: landing, build.bound[sems[0]])
        leaving = to_frames(
            lambda g: mixed_t.ref.at[g], lambda f: out.ref.at[span(f, HEAD), :], build.bound[sems[1]]
        )
        pair = build.bound[over_sems]
        over = [
            remote(own.ref.at[first, g], landing, pair.at[0, k], pair.at[1, k], {SECTION: 1, FRAME: g})
            for k, g in enumerate((me,) + partners)
        ]

        need(0)
        if first:

            @pl.when(section == 0)
            def _():
                turned_parts(normed.ref[1], matrices, own, (1,))
                meet()
                for copy in over:
                    copy.start()
                turned_parts(normed.ref[0], matrices, own, (0,))
                for copy in arriving[::-1]:
                    copy.start()
                heads_t.ref[:, span(me, rows)] = own.ref[0, me]

            @pl.when(section == 1)
            def _():
                meet()

        else:
            turned_parts(normed.ref[...], matrices, own, (0,))
            meet()
            for copy in arriving[::-1]:
                copy.start()
            heads_t.ref[:, span(me, rows)] = own.ref[0, me]
        ride()
        need(1)
        if first:

            @pl.when(section == 0)
            def _():
                for copy in arriving + over:
                    copy.wait_send()
                for copy in arriving:
                    copy.wait_recv()

            @pl.when(section == 1)
            def _():
                for copy in over:
                    copy.wait_recv()

        else:
            for copy in arriving:
                copy.wait()
        heads_t.flush()
        keys.ref[...] = heads_t.ref[HEAD : 2 * HEAD, :].T
        for target in range(frames):
            if target == frames - 1:
                for task in early:
                    task.first_hop()
            for start in range(target * rows, (target + 1) * rows, block):
                reach = start + block
                scores = masked_scores(
                    keys.ref[:reach, :], heads_t.ref[:HEAD, start:reach], begins.ref[:, start:reach], start
                )
                e = jnp.exp(scores - jnp.max(scores, axis=0, keepdims=True))
                total = jnp.sum(e, axis=0, keepdims=True)
                mixed = plain_product(heads_t.ref[2 * HEAD :, :reach], e.astype(jnp.bfloat16))
                at = start - target * rows
                mixed_t.ref[target, :, at : at + block] = (mixed * (1.0 / total)).astype(jnp.bfloat16)

            for copy, other in zip(leaving, partners):

                @pl.when(other == target)
                def _():
                    copy.start()

        out.ref[span(me, HEAD), :] = mixed_t.ref[me]
        for copy in leaving:
            copy.wait()
        out.flush()

    kinds = (FRAME, SECTION, BOTH) if first else (FRAME,)
    return run_build(build, body, kinds, collective_id, tasks)


def self_backward(heads_t, grad_low, weight, begins, layer, collective_id, tasks):
    rows, frames, width = grad_low.shape[0], 4, 3 * HEAD
    all_rows = rows * frames
    build = Build()
    heads_t, begins = build.arg(heads_t, 1), build.arg(begins, 1)
    grad_low, weight = build.arg(grad_low, 0), build.pick(weight, layer, 0)
    out = build.out((frames * width, rows), jnp.bfloat16)
    own = build.temp((frames, HEAD, rows), jnp.bfloat16)
    grad_t = build.temp((HEAD, all_rows), jnp.bfloat16)
    columns = build.temp((4, all_rows, HEAD), jnp.bfloat16)
    key_sum, value_sum = (build.temp((all_rows, HEAD), jnp.float32) for _ in range(2))
    grads_t = build.temp((frames, width, rows), jnp.bfloat16)
    sems = [build.extra(pltpu.SemaphoreType.DMA((2, frames - 1))) for _ in range(2)]

    def body(need, meet, ride, middle):
        me = lax.axis_index(FRAME)
        partners = frame_partners()
        block = min(2 * BLOCK, rows)
        scale = HEAD ** (-0.5)
        arriving = to_frames(
            lambda g: own.ref.at[g], lambda f: grad_t.ref.at[:, span(f, rows)], build.bound[sems[0]]
        )
        leaving = to_frames(
            lambda g: grads_t.ref.at[g], lambda f: out.ref.at[span(f, width), :], build.bound[sems[1]]
        )

        def project(other):
            return nt_product(weight.ref[span(other, HEAD), :], grad_low.ref[...]).astype(jnp.bfloat16)

        need(0)
        own.ref[partners[2]] = project(partners[2])
        own.ref[partners[1]] = project(partners[1])
        meet()
        arriving[2].start()
        arriving[1].start()
        own.ref[partners[0]] = project(partners[0])
        arriving[0].start()
        ride()
        grad_t.ref[:, span(me, rows)] = project(me)
        key_sum.ref[...] = jnp.zeros(key_sum.shape, jnp.float32)
        value_sum.ref[...] = jnp.zeros(key_sum.shape, jnp.float32)
        need(1)
        for part in range(3):
            columns.ref[part] = heads_t.ref[part * HEAD : (part + 1) * HEAD, :].T
        for copy in arriving:
            copy.wait()
        columns.ref[3] = grad_t.ref[...].T
        middle()
        for target in reversed(range(frames)):
            for start in reversed(range(target * rows, (target + 1) * rows, block)):
                reach = start + block
                scores = masked_scores(
                    columns.ref[1, :reach, :],
                    heads_t.ref[:HEAD, start:reach],
                    begins.ref[:, start:reach],
                    start,
                )
                e = jnp.exp(scores - jnp.max(scores, axis=0, keepdims=True))
                p = e * (1.0 / jnp.sum(e, axis=0, keepdims=True))
                slope = plain_product(columns.ref[2, :reach, :], grad_t.ref[:, start:reach])
                weighted = p * slope
                ds = (weighted - p * jnp.sum(weighted, axis=0, keepdims=True)).astype(jnp.bfloat16)
                value_sum.ref[:reach, :] += plain_product(
                    p.astype(jnp.bfloat16), columns.ref[3, start:reach, :]
                )
                key_sum.ref[:reach, :] += plain_product(ds, columns.ref[0, start:reach, :])
                here = slice(start - target * rows, reach - target * rows)
                query_grad = plain_product(heads_t.ref[HEAD : 2 * HEAD, :reach], ds) * scale
                grads_t.ref[target, :HEAD, here] = query_grad.astype(jnp.bfloat16)
                key_grad = key_sum.ref[start:reach, :] * scale
                grads_t.ref[target, HEAD : 2 * HEAD, here] = key_grad.T.astype(jnp.bfloat16)
                grads_t.ref[target, 2 * HEAD :, here] = value_sum.ref[start:reach, :].T.astype(jnp.bfloat16)

            for copy, other in zip(leaving, partners):

                @pl.when(other == target)
                def _():
                    copy.start()

        out.ref[span(me, width), :] = grads_t.ref[me]
        for copy in leaving:
            copy.wait()
        out.flush()

    return run_build(build, body, (FRAME,), collective_id, tasks)


def matmul(left_side, right_side):
    return jnp.dot(left_side, right_side, preferred_element_type=jnp.float32)


def matmul_tn(left_side, right_side):
    return lax.dot_general(
        left_side, right_side, (((0,), (0,)), ((), ())), preferred_element_type=jnp.float32
    )


def matmul_nt(left_side, right_side):
    return lax.dot_general(
        left_side, right_side, (((1,), (1,)), ((), ())), preferred_element_type=jnp.float32
    )


def layer_norm(signal, gain_vec, shift_vec):
    average = jnp.mean(signal, axis=-1, keepdims=True)
    centered = signal - average
    variance = jnp.mean(centered * centered, axis=-1, keepdims=True)
    return centered * lax.rsqrt(variance + 1e-05) * gain_vec + shift_vec


def norm_back(signal, gain_vec, upstream):
    average = jnp.mean(signal, axis=-1, keepdims=True)
    centered = signal - average
    inverse = lax.rsqrt(jnp.mean(centered * centered, axis=-1, keepdims=True) + 1e-05)
    standard = centered * inverse
    scaled = upstream * gain_vec
    through = inverse * (
        scaled
        - jnp.mean(scaled, axis=-1, keepdims=True)
        - standard * jnp.mean(scaled * standard, axis=-1, keepdims=True)
    )
    return (through, jnp.sum(upstream * standard, axis=0), jnp.sum(upstream, axis=0))


def head_total(partial_sum):
    return lax.psum(partial_sum.astype(jnp.bfloat16), LINE).astype(jnp.float32)


def swapped(x):
    return lax.ppermute(x, SECTION, [(0, 1), (1, 0)])


def split_heads(matrix):
    return matrix.reshape(matrix.shape[0], matrix.shape[1] // HEAD, HEAD)


def softmax_rows(query, key_rows, allowed):
    logits = jnp.einsum(
        "qhd,khd->hqk",
        split_heads(query),
        split_heads(key_rows),
        preferred_element_type=jnp.float32,
    ) * HEAD ** (-0.5)
    logits = jnp.where(allowed[None], logits, masked_score)
    exponent = jnp.exp(logits - jnp.max(logits, axis=-1, keepdims=True))
    return exponent / jnp.sum(exponent, axis=-1, keepdims=True)


def attend(query, key_rows, value_rows, allowed):
    weights_low = softmax_rows(query, key_rows, allowed).astype(jnp.bfloat16)
    result = jnp.einsum(
        "hqk,khd->qhd", weights_low, split_heads(value_rows), preferred_element_type=jnp.float32
    )
    return result.reshape(query.shape).astype(jnp.bfloat16)


def attend_back(query, key_rows, value_rows, allowed, grad_out):
    probabilities = softmax_rows(query, key_rows, allowed)
    weights_low = probabilities.astype(jnp.bfloat16)
    grad_heads = split_heads(grad_out)
    grad_prob = jnp.einsum(
        "qhd,khd->hqk", grad_heads, split_heads(value_rows), preferred_element_type=jnp.float32
    )
    centre = jnp.sum(probabilities * grad_prob, axis=-1, keepdims=True)
    grad_logit = (probabilities * (grad_prob - centre)).astype(jnp.bfloat16)
    scale = HEAD ** (-0.5)
    grad_query = (
        jnp.einsum(
            "hqk,khd->qhd", grad_logit, split_heads(key_rows), preferred_element_type=jnp.float32
        )
        * scale
    )
    grad_keys = (
        jnp.einsum(
            "hqk,qhd->khd", grad_logit, split_heads(query), preferred_element_type=jnp.float32
        )
        * scale
    )
    grad_values = jnp.einsum(
        "hqk,qhd->khd", weights_low, grad_heads, preferred_element_type=jnp.float32
    )
    return (
        grad_query.reshape(query.shape),
        grad_keys.reshape(key_rows.shape),
        grad_values.reshape(value_rows.shape),
    )


def sum_rows(rows):
    return jnp.concatenate(rows, axis=0)


def on_four_frames(inputs, lengths, text, cotangent, vector_args, matrix_args):
    section = lax.axis_index(SECTION)
    at_zero = section == 0
    frame_index = lax.axis_index(FRAME)
    micro_count, rows_dev, model_width = inputs.shape
    rows_all = rows_dev * 4
    (
        query_weight,
        key_weight,
        value_weight,
        output_weight,
        cross_query,
        cross_key,
        cross_value,
        cross_output,
        expand_weight,
        reduce_weight,
    ) = (w[0] for w in matrix_args)
    columns = query_weight.shape[1]

    def by_section(first, second):
        return jnp.where(at_zero, first, second)

    own_vectors = jnp.pad(jnp.concatenate(vector_args, axis=0), ((0, 2), (0, 0)))
    self_weights = (query_weight, key_weight, value_weight)
    normed = layer_norm(inputs.astype(jnp.float32), own_vectors[0], own_vectors[1]).astype(jnp.bfloat16)
    text_local = text.reshape(-1, model_width)
    text_states = jnp.concatenate(
        [matmul(text_local, cross_key), matmul(text_local, cross_value)], axis=1
    ).astype(jnp.bfloat16)
    text_states = text_states.reshape(micro_count, -1, 2 * columns)

    item_ends = jnp.cumsum(lax.dynamic_index_in_dim(lengths, section, 0, keepdims=False))
    passed = jnp.arange(rows_all, dtype=jnp.int32)[None, :] >= item_ends[:, None]
    begins = jnp.max(jnp.where(passed, item_ends[:, None], 0), axis=0, keepdims=True).astype(jnp.int32)
    seg = jnp.sum(passed.astype(jnp.int32), axis=0, keepdims=True)
    seg = lax.dynamic_slice_in_dim(seg, frame_index * rows_dev, rows_dev, 1)

    entering = inputs
    saved = []
    for layer in range(2):
        first = layer == 0
        tasks = []
        if first:
            early = [WeightTask(output_weight)]
            early[0].hooked = 1
            tasks = early + [CrossTask(own_vectors, own_vectors, False), TextTask(text_states)]
            tasks += [QuarterTask(w) for w in (cross_query, cross_output, expand_weight)]
        (heads_t, attended_t), carried = self_forward(
            normed,
            self_weights if first else self_pairs,
            begins,
            layer,
            2 + layer,
            tasks,
            early if first else [],
        )
        if first:
            vectors = [by_section(own_vectors, carried[1]), by_section(carried[1], own_vectors)]
            normed = layer_norm(
                lax.dynamic_index_in_dim(inputs, section, 0, keepdims=False).astype(jnp.float32),
                vectors[0][0],
                vectors[0][1],
            ).astype(jnp.bfloat16)
        gains = vectors[layer]
        tasks = []
        if first:
            states = carried[2].reshape(2, -1, 2 * columns)
            others = (cross_query, cross_output, expand_weight, reduce_weight)
            coming = [WeightTask(w, 0, q) for w, q in zip(others, carried[3:] + [None])]
            late = [WeightTask(w) for w in self_weights]
            for task in late:
                task.hooked = 2
            weights = [(output_weight, carried[0])]
            tasks = coming + late
        outs, carried = forward_chain(
            layer,
            attended_t,
            entering,
            states[layer],
            seg,
            gains,
            vectors[1] if first else None,
            weights + coming if first else weights,
            4 + layer,
            tasks,
            late if first else [],
        )
        second_normed, middle, queries, cross_att, third_normed, latter, before, hidden = outs[:8]
        if first:
            weights += list(zip(others, carried))
            self_pairs = list(zip(self_weights, carried[4:]))
        saved.append(
            (
                entering,
                normed,
                heads_t,
                attended_t,
                middle,
                second_normed,
                latter,
                third_normed,
                queries,
                cross_att,
                before,
                hidden,
            )
        )
        if first:
            normed, entering = outs[8:]
        else:
            (result_low,) = outs[8:]

    vector_grads, shares = [None] * 2, [{}, {}]
    totals = {}

    def low_product(left, right):
        return matmul_tn(left, right).astype(jnp.bfloat16)

    def crossing(*names):
        return [CrossTask(shares[0][name], shares[1][name], True) for name in names]

    def unpack(outs):
        names = ("grad_pre", "grad_cross", "gain5", "shift5", "queries", "states", "grad_self", "gain3", "shift3")
        return dict(zip(names, outs))

    def for_backward(layer):
        return saved[layer][4], *saved[layer][6:9], *saved[layer][10:]

    def products(layer, outs):
        attended_t, second_normed, cross_att = saved[layer][3], saved[layer][5], saved[layer][9]
        return [
            (cross_att, outs["grad_cross"]),
            (attended_t, outs["grad_self"]),
            (second_normed, outs["queries"]),
            (saved[layer][1], None),
        ]

    def vector_rows(outs, first):
        rows = first + [outs[name] for name in ("gain3", "shift3", "gain5", "shift5")]
        return sum_rows(rows + [jnp.zeros((2, model_width), jnp.float32)])

    names = ("cross_output", "output", "cross_query", "heads")
    outs, carried = backward_chain(
        1,
        cotangent,
        for_backward(1),
        states[1],
        seg,
        vectors[1],
        weights,
        8,
        [BothTask(saved[1][0], result_low)],
    )
    later = unpack(outs)
    layer_outputs, shares[1]["reduce"], shares[1]["expand"] = carried
    (grad_heads_t,), (shares[1]["states"],) = self_backward(
        saved[1][2], later["grad_self"], weights[0], begins, 1, 9, [ShareTask(later["states"])]
    )
    outs, carried = between_chain(
        1,
        (grad_heads_t, saved[1][0], vectors[1][0], later["grad_self"], self_pairs),
        products(1, later),
        (for_backward(0), states[0], seg, vectors[0], weights),
        10,
        [],
    )
    later_low, first_vectors = outs[0], list(outs[1:3])
    vector_grads[1] = vector_rows(later, first_vectors)
    sooner = unpack(outs[3:])
    shares[1].update(zip(names, carried))
    shares[0]["reduce"], shares[0]["expand"] = carried[4:]
    (grad_heads_t,), carried = self_backward(
        saved[0][2],
        sooner["grad_self"],
        weights[0],
        begins,
        0,
        11,
        [ShareTask(sooner["states"])] + crossing("reduce", "expand"),
    )
    shares[0]["states"], totals["reduce"], totals["expand"] = carried
    outs, carried = last_chain(
        0,
        grad_heads_t,
        saved[0][0],
        vectors[0][0],
        sooner["grad_self"],
        self_pairs,
        spare=later_low,
        products=products(0, sooner),
        collective_id=12,
        tasks=[CrossTask(shares[0]["states"], shares[1]["states"], False)],
    )
    both_grads = outs[3]
    vector_grads[0] = vector_rows(sooner, list(outs[1:3]))
    other_states = carried[0]
    shares[0].update(zip(names, carried[1:]))

    own_states = by_section(shares[0]["states"], shares[1]["states"])
    text_rows = sum_rows([by_section(own_states, other_states), by_section(other_states, own_states)])
    key_part, value_part = text_rows[:, :columns], text_rows[:, columns:]
    text_part = matmul_nt(key_part, cross_key) + matmul_nt(value_part, cross_value)
    _, (text_grad, vector_total, cross_grads, *carried) = call(
        None,
        [],
        [],
        [],
        (),
        18,
        [
            TotalTask(text_part.astype(jnp.bfloat16)),
            VectorTask(jnp.stack(vector_grads)),
            ShareTask(low_product(text_local, text_rows)),
        ]
        + crossing(*names),
    )
    totals.update(zip(names, carried))
    text_grad = text_grad.astype(jnp.float32).reshape(text.shape)
    vector_total = lax.dynamic_slice_in_dim(
        vector_total, frame_index * (model_width // 4), model_width // 4, 1
    )
    grad_query, grad_key, grad_value = jnp.split(totals["heads"], 3, axis=1)
    cross_grads = cross_grads.astype(jnp.float32)

    ordered = (
        vector_total[0],
        vector_total[1],
        grad_query,
        grad_key,
        grad_value,
        totals["output"],
        vector_total[2],
        vector_total[3],
        totals["cross_query"],
        cross_grads[:, :columns],
        cross_grads[:, columns:],
        totals["cross_output"],
        vector_total[4],
        vector_total[5],
        totals["expand"],
        totals["reduce"],
    )
    layer_outputs, input_grads = (a.astype(jnp.float32) for a in (layer_outputs, both_grads))
    return (layer_outputs[None], input_grads[None], text_grad) + tuple(g[None] for g in ordered)


def self_attention(query, key_rows, value_rows, masks):
    all_keys = lax.all_gather(key_rows, FRAME, axis=0, tiled=True)
    all_values = lax.all_gather(value_rows, FRAME, axis=0, tiled=True)
    return attend(query, all_keys, all_values, masks["own"]), (query, all_keys, all_values)


def self_attention_back(kept, grad_out, masks):
    query, keys, values = kept
    grad_q, grad_k_all, grad_v_all = attend_back(query, keys, values, masks["own"], grad_out)
    grad_k, grad_v = (
        lax.psum_scatter(g.astype(jnp.bfloat16), FRAME, scatter_dimension=0, tiled=True)
        for g in (grad_k_all, grad_v_all)
    )
    return grad_q.astype(jnp.bfloat16), grad_k, grad_v


def forward(entering, vectors, weights, cross_keys, cross_values, masks):
    first_gain, first_shift, second_gain, second_shift, third_gain, third_shift = vectors
    (
        query_weight,
        key_weight,
        value_weight,
        output_weight,
        cross_query,
        cross_output,
        expand_weight,
        reduce_weight,
    ) = weights
    signal = entering.astype(jnp.float32)
    first_normed = layer_norm(signal, first_gain, first_shift).astype(jnp.bfloat16)
    query = matmul(first_normed, query_weight).astype(jnp.bfloat16)
    key_rows = matmul(first_normed, key_weight).astype(jnp.bfloat16)
    value_rows = matmul(first_normed, value_weight).astype(jnp.bfloat16)
    attended, heads_kept = self_attention(query, key_rows, value_rows, masks)
    middle = signal + head_total(matmul(attended, output_weight))
    second_normed = layer_norm(middle, second_gain, second_shift).astype(jnp.bfloat16)
    cross_queries = matmul(second_normed, cross_query).astype(jnp.bfloat16)
    cross_att = attend(cross_queries, cross_keys, cross_values, masks["cross"])
    latter = middle + head_total(matmul(cross_att, cross_output))
    third_normed = layer_norm(latter, third_gain, third_shift).astype(jnp.bfloat16)
    hidden_pre = matmul(third_normed, expand_weight)
    hidden_act = jax.nn.gelu(hidden_pre, approximate=False).astype(jnp.bfloat16)
    result = latter + head_total(matmul(hidden_act, reduce_weight))
    saved = (
        signal,
        first_normed,
        heads_kept,
        attended,
        middle,
        second_normed,
        cross_queries,
        cross_att,
        latter,
        third_normed,
        hidden_pre,
        hidden_act,
    )
    return (result, saved)


def backward(saved, upstream, vectors, weights, cross_keys, cross_values, masks):
    first_gain, first_shift, second_gain, second_shift, third_gain, third_shift = vectors
    (
        query_weight,
        key_weight,
        value_weight,
        output_weight,
        cross_query,
        cross_output,
        expand_weight,
        reduce_weight,
    ) = weights
    (
        signal,
        first_normed,
        heads_kept,
        attended,
        middle,
        second_normed,
        cross_queries,
        cross_att,
        latter,
        third_normed,
        hidden_pre,
        hidden_act,
    ) = saved
    grad_out = upstream.astype(jnp.bfloat16)
    grad_reduce = matmul_tn(hidden_act, grad_out)
    grad_act = matmul_nt(grad_out, reduce_weight)
    slope = (
        0.5 * (1.0 + lax.erf(hidden_pre * inv_sqrt_two))
        + hidden_pre * jnp.exp(-0.5 * hidden_pre * hidden_pre) * inv_sqrt_tau
    )
    grad_pre = (grad_act * slope).astype(jnp.bfloat16)
    grad_expand = matmul_tn(third_normed, grad_pre)
    grad_third = head_total(matmul_nt(grad_pre, expand_weight))
    grad_latter, grad_third_gain, grad_third_shift = norm_back(latter, third_gain, grad_third)
    grad_latter = grad_latter + upstream
    grad_cross = grad_latter.astype(jnp.bfloat16)
    grad_cross_output = matmul_tn(cross_att, grad_cross)
    grad_cross_att = matmul_nt(grad_cross, cross_output).astype(jnp.bfloat16)
    grad_cq, grad_ck, grad_cv = attend_back(
        cross_queries, cross_keys, cross_values, masks["cross"], grad_cross_att
    )
    grad_text_rows = jnp.concatenate([grad_ck, grad_cv], axis=1).astype(jnp.bfloat16)
    grad_text_rows = lax.psum_scatter(
        grad_text_rows.reshape(ITEMS, TEXT, -1), FRAME, scatter_dimension=1, tiled=True
    )
    grad_cquery = grad_cq.astype(jnp.bfloat16)
    grad_cross_query = matmul_tn(second_normed, grad_cquery)
    grad_second = head_total(matmul_nt(grad_cquery, cross_query))
    grad_middle, grad_second_gain, grad_second_shift = norm_back(middle, second_gain, grad_second)
    grad_middle = grad_middle + grad_latter
    grad_self = grad_middle.astype(jnp.bfloat16)
    grad_output = matmul_tn(attended, grad_self)
    grad_att = matmul_nt(grad_self, output_weight).astype(jnp.bfloat16)
    grad_query_low, grad_key_low, grad_value_low = self_attention_back(heads_kept, grad_att, masks)
    grad_query = matmul_tn(first_normed, grad_query_low)
    grad_key = matmul_tn(first_normed, grad_key_low)
    grad_value = matmul_tn(first_normed, grad_value_low)
    grad_first = head_total(
        matmul_nt(grad_query_low, query_weight)
        + matmul_nt(grad_key_low, key_weight)
        + matmul_nt(grad_value_low, value_weight)
    )
    grad_signal, grad_first_gain, grad_first_shift = norm_back(signal, first_gain, grad_first)
    grad_signal = grad_signal + grad_middle
    vector_grads = (
        grad_first_gain,
        grad_first_shift,
        grad_second_gain,
        grad_second_shift,
        grad_third_gain,
        grad_third_shift,
    )
    matrix_grads = (
        grad_query,
        grad_key,
        grad_value,
        grad_output,
        grad_cross_query,
        grad_cross_output,
        grad_expand,
        grad_reduce,
    )
    matrix_grads = tuple(
        lax.psum_scatter(g.astype(jnp.bfloat16), FRAME, scatter_dimension=0, tiled=True)
        for g in matrix_grads
    )
    return grad_signal, vector_grads, matrix_grads, grad_text_rows


def per_device(
    inputs,
    lengths,
    text,
    cotangent,
    first_gain,
    first_shift,
    query_weight,
    key_weight,
    value_weight,
    output_weight,
    second_gain,
    second_shift,
    cross_query,
    cross_key,
    cross_value,
    cross_output,
    third_gain,
    third_shift,
    expand_weight,
    reduce_weight,
):
    head_count, frame_count = lax.axis_size(LINE), lax.axis_size(FRAME)
    local_heads = query_weight.shape[2] // HEAD
    if head_count == 4 and frame_count == 4 and local_heads == 4:
        return on_four_frames(
            inputs,
            lengths,
            text,
            cotangent,
            (first_gain, first_shift, second_gain, second_shift, third_gain, third_shift),
            (
                query_weight,
                key_weight,
                value_weight,
                output_weight,
                cross_query,
                cross_key,
                cross_value,
                cross_output,
                expand_weight,
                reduce_weight,
            ),
        )
    section = lax.axis_index(SECTION)
    at_zero = section == 0
    frame_index = lax.axis_index(FRAME)
    micro_count, rows_dev, model_width = inputs.shape
    rows_all = rows_dev * frame_count
    text_rows_dev = text.shape[2]

    def keep(pair):
        return jnp.where(at_zero, pair[0], pair[1])

    def give(pair):
        return jnp.where(at_zero, pair[1], pair[0])

    vector_args = jnp.concatenate(
        [first_gain, first_shift, second_gain, second_shift, third_gain, third_shift], axis=0
    )
    vectors = lax.all_gather(vector_args, SECTION)
    matrix_args = (
        query_weight,
        key_weight,
        value_weight,
        output_weight,
        cross_query,
        cross_output,
        expand_weight,
        reduce_weight,
    )
    matrices = [lax.all_gather(w[0], SECTION) for w in matrix_args]
    weights = [tuple(w[layer] for w in matrices) for layer in range(2)]

    text_full = lax.all_gather(text, FRAME, axis=2, tiled=True)
    text_flat = text_full.reshape(micro_count * ITEMS * TEXT, model_width)
    text_heads = jnp.concatenate(
        [matmul(text_flat, cross_key[0]), matmul(text_flat, cross_value[0])], axis=1
    ).astype(jnp.bfloat16)
    text_heads = text_heads.reshape(micro_count, ITEMS * TEXT, -1)
    own_text = keep(text_heads)
    other_text = swapped(give(text_heads))
    columns = cross_key.shape[2]
    cross_states = [
        jnp.where(at_zero, own_text, other_text),
        jnp.where(at_zero, other_text, own_text),
    ]
    cross_keys = [c[:, :columns] for c in cross_states]
    cross_values = [c[:, columns:] for c in cross_states]

    item_ends = jnp.cumsum(lax.dynamic_index_in_dim(lengths, section, 0, keepdims=False))
    all_positions = jnp.arange(rows_all, dtype=jnp.int32)
    seg_all = jnp.sum((all_positions[:, None] >= item_ends[None, :]).astype(jnp.int32), axis=1)
    own_start = frame_index * rows_dev
    own_positions = own_start + jnp.arange(rows_dev, dtype=jnp.int32)
    seg_own = lax.dynamic_slice_in_dim(seg_all, own_start, rows_dev)
    text_item = jnp.arange(ITEMS * TEXT, dtype=jnp.int32) // TEXT
    masks = {
        "own": (all_positions[None, :] <= own_positions[:, None])
        & (seg_own[:, None] == seg_all[None, :]),
        "cross": seg_own[:, None] == text_item[None, :],
    }

    signal = lax.dynamic_index_in_dim(inputs, section, 0, keepdims=False)
    results, saves = [], []
    for layer in range(2):
        result, saved = forward(
            signal, vectors[layer], weights[layer], cross_keys[layer], cross_values[layer], masks
        )
        results.append(result)
        saves.append(saved)
        signal = result.astype(jnp.bfloat16)

    upstream = lax.dynamic_index_in_dim(cotangent, section, 0, keepdims=False)
    in_grads, vector_grads, matrix_grads, text_grads = [None] * 2, [None] * 2, [None] * 2, [None] * 2
    for layer in (1, 0):
        grad_signal, vector_grads[layer], matrix_grads[layer], text_grads[layer] = backward(
            saves[layer],
            upstream,
            vectors[layer],
            weights[layer],
            cross_keys[layer],
            cross_values[layer],
            masks,
        )
        in_grads[layer] = grad_signal
        upstream = grad_signal.astype(jnp.bfloat16).astype(jnp.float32)

    def both_micros(pair):
        own = keep(pair)
        other = swapped(give([p.astype(jnp.bfloat16) for p in pair])).astype(own.dtype)
        return jnp.stack([jnp.where(at_zero, own, other), jnp.where(at_zero, other, own)])

    layer_outputs = both_micros(results)
    input_grads = both_micros(in_grads)
    totals = [
        keep(pair).astype(jnp.float32) + swapped(give(pair)).astype(jnp.float32)
        for pair in zip(*matrix_grads)
    ]
    text_rows = both_micros(text_grads)
    text_rows = text_rows.reshape(micro_count * ITEMS * text_rows_dev, -1)
    key_part, value_part = text_rows[:, :columns], text_rows[:, columns:]
    text_local = text.reshape(-1, model_width)
    grad_cross_key, grad_cross_value = (
        lax.psum_scatter(
            matmul_tn(text_local, part).astype(jnp.bfloat16),
            FRAME,
            scatter_dimension=0,
            tiled=True,
        ).astype(jnp.float32)
        for part in (key_part, value_part)
    )
    text_part = matmul_nt(key_part, cross_key[0]) + matmul_nt(value_part, cross_value[0])
    text_grad = lax.psum(text_part.astype(jnp.bfloat16), (SECTION, LINE)).astype(jnp.float32)
    text_grad = text_grad.reshape(text.shape)

    stacked = jnp.stack([jnp.stack(v) for v in vector_grads])
    stacked = lax.psum_scatter(
        stacked.astype(jnp.bfloat16), FRAME, scatter_dimension=2, tiled=True
    )
    vector_total = keep(stacked).astype(jnp.float32) + swapped(give(stacked)).astype(jnp.float32)

    grad_q, grad_k, grad_v, grad_o, grad_cq, grad_co, grad_e, grad_r = totals
    ordered = (
        vector_total[0],
        vector_total[1],
        grad_q,
        grad_k,
        grad_v,
        grad_o,
        vector_total[2],
        vector_total[3],
        grad_cq,
        grad_cross_key,
        grad_cross_value,
        grad_co,
        vector_total[4],
        vector_total[5],
        grad_e,
        grad_r,
    )
    return (layer_outputs[None], input_grads[None], text_grad) + tuple(g[None] for g in ordered)


def solution(mesh):
    return jax.shard_map(
        per_device,
        mesh=mesh,
        in_specs=(
            P(None, FRAME, None),
            P(),
            P(None, None, FRAME, None),
            P(None, FRAME, None),
            P(SECTION, None),
            P(SECTION, None),
            P(SECTION, None, LINE),
            P(SECTION, None, LINE),
            P(SECTION, None, LINE),
            P(SECTION, LINE, None),
            P(SECTION, None),
            P(SECTION, None),
            P(SECTION, None, LINE),
            P(SECTION, None, LINE),
            P(SECTION, None, LINE),
            P(SECTION, LINE, None),
            P(SECTION, None),
            P(SECTION, None),
            P(SECTION, None, LINE),
            P(SECTION, LINE, None),
        ),
        out_specs=(
            P(SECTION, None, FRAME, None),
            P(SECTION, None, FRAME, None),
            P(None, None, FRAME, None),
            P(SECTION, FRAME),
            P(SECTION, FRAME),
            P(SECTION, FRAME, LINE),
            P(SECTION, FRAME, LINE),
            P(SECTION, FRAME, LINE),
            P(SECTION, (LINE, FRAME), None),
            P(SECTION, FRAME),
            P(SECTION, FRAME),
            P(SECTION, FRAME, LINE),
            P(SECTION, FRAME, LINE),
            P(SECTION, FRAME, LINE),
            P(SECTION, (LINE, FRAME), None),
            P(SECTION, FRAME),
            P(SECTION, FRAME),
            P(SECTION, FRAME, LINE),
            P(SECTION, (LINE, FRAME), None),
        ),
        check_vma=False,
    )
```

```python
import jax
import jax.numpy as jnp
from jax import lax
from jax.experimental import pallas as pl
from jax.experimental.pallas import tpu as pltpu
from jax.sharding import PartitionSpec as P

HEAD = 64
TEXT = 64
ITEMS = 4

masked_score = -1e30
inv_sqrt_two = 0.7071067811865476
inv_sqrt_tau = 0.3989422804014327

MESH_IDS = pl.DeviceIdType.MESH
BUSY = pl.CostEstimate(flops=30_000_000_000, bytes_accessed=8_000_000, transcendentals=0)
LAG = 3
BLOCK = 128
VMEM_BYTES = 60 * 1024 * 1024
EPS = 1e-05
SECTION, LINE, FRAME = "section", "head", "frame"
BOTH, LINE_ONLY, BY_SECTION = "both", "line", "one"
NORM, NEXT, END = range(3)


class Task:
    operands = ()
    outs = ()
    out_in_vmem = True
    scratch = ()
    greets = ()
    late = False
    hooked = 0

    def middle(self):
        pass

    def bind(self, ins, outs, scratch):
        self.ins, self.out, self.room = ins, outs, scratch
        self.far_ins = ins


def remote(source, landing, send_sem, recv_sem, target):
    return pltpu.make_async_remote_copy(
        src_ref=source,
        dst_ref=landing,
        send_sem=send_sem,
        recv_sem=recv_sem,
        device_id=target,
        device_id_type=MESH_IDS,
    )


def frame_partners():
    me = lax.axis_index(FRAME)
    return (me + 1 - 2 * lax.rem(me, 2), lax.rem(me + 2, 4), 3 - me)


def span(index, size):
    return pl.ds(pl.multiple_of(index * size, size), size)


class WeightTask(Task):
    out_in_vmem = False
    greets = (SECTION, FRAME)

    def __init__(self, weight, layer=None, quarter=None):
        self.layer = layer
        self.operands = (weight,) if quarter is None else (weight, quarter)
        self.outs = (jax.ShapeDtypeStruct(weight.shape, weight.dtype),)
        self.scratch = (pltpu.SemaphoreType.DMA((10,)),)
        if layer is not None:
            self.scratch += (pltpu.VMEM((2,) + weight.shape, weight.dtype),)
        self.quarter = weight.shape[0] // 4

    @property
    def ref(self):
        other = jnp.where(lax.axis_index(SECTION) == self.layer, 0, 1)
        return self.room[1].at[other]

    def arrived(self, at):
        return self.out[0].at[at] if self.layer is None else self.room[1].at[1, at]

    def over(self):
        sems, at = self.room[0], span(lax.axis_index(FRAME), self.quarter)
        target = {SECTION: 1 - lax.axis_index(SECTION)}
        return remote(self.ins[0].at[at], self.arrived(at), sems.at[0], sems.at[1], target)

    def along(self):
        sems, at = self.room[0], span(lax.axis_index(FRAME), self.quarter)
        target = {FRAME: frame_partners()[1]}
        source = self.ins[1] if len(self.ins) > 1 else self.arrived(at)
        return remote(source, self.arrived(at), sems.at[2], sems.at[3], target)

    def settle(self):
        at = span(lax.axis_index(FRAME), self.quarter)
        return pltpu.make_async_copy(self.ins[1], self.arrived(at), self.room[0].at[0])

    def within(self):
        sems, partners = self.room[0], frame_partners()
        copies = []
        for k, whose in enumerate((lax.axis_index(FRAME), partners[1])):
            at = span(whose, self.quarter)
            copies.append(
                remote(
                    self.arrived(at),
                    self.arrived(at),
                    sems.at[4 + 2 * k],
                    sems.at[5 + 2 * k],
                    {FRAME: partners[0]},
                )
            )
        return copies

    def begin(self):
        if len(self.ins) > 1:
            self.settle().start()
            self.along().start()
        else:
            self.over().start()
        if self.layer is not None:
            pltpu.make_async_copy(self.ins[0], self.room[1].at[0], self.room[0].at[8]).start()

    def first_hop(self):
        self.over().wait_recv()
        self.along().start()

    def second_hop(self):
        if len(self.ins) > 1:
            self.settle().wait()
        self.along().wait_recv()
        for copy in self.within():
            copy.start()

    def arrive(self):
        for copy in self.within():
            copy.wait_recv()
        if self.layer is not None:
            sems = self.room[0]
            pltpu.make_async_copy(self.ins[0], self.room[1].at[0], sems.at[8]).wait()
            pltpu.make_async_copy(self.room[1].at[1], self.out[0], sems.at[9]).start()

    def sent(self):
        over = [] if len(self.ins) > 1 else [self.over()]
        for copy in over + [self.along()] + self.within():
            copy.wait_send()
        if self.layer is not None:
            pltpu.make_async_copy(self.room[1].at[1], self.out[0], self.room[0].at[9]).wait()

    def steps(self):
        if self.layer is not None:
            return [self.sent]
        return [self.first_hop, self.second_hop][self.hooked :] + [self.arrive, self.sent]


class QuarterTask(Task):
    out_in_vmem = False
    greets = (SECTION,)

    def __init__(self, weight):
        self.quarter = weight.shape[0] // 4
        self.operands = (weight,)
        self.outs = (jax.ShapeDtypeStruct((self.quarter, weight.shape[1]), weight.dtype),)
        self.scratch = (pltpu.SemaphoreType.DMA((2,)),)

    def over(self):
        sems, at = self.room[0], span(lax.axis_index(FRAME), self.quarter)
        target = {SECTION: 1 - lax.axis_index(SECTION)}
        return remote(self.ins[0].at[at], self.out[0], sems.at[0], sems.at[1], target)

    def begin(self):
        self.over().start()

    def steps(self):
        return [lambda: self.over().wait()]


class ShareTask(Task):
    greets = (FRAME,)

    def __init__(self, grad):
        rows, width = grad.shape
        self.share = rows // 4
        self.far = isinstance(grad, jax.Array)
        self.operands = (grad,) if self.far else ()
        piece = (self.share, width)
        self.outs = (jax.ShapeDtypeStruct(piece, jnp.bfloat16),)
        self.scratch = (
            pltpu.VMEM((2,) + piece, jnp.bfloat16),
            pltpu.VMEM((2,) + piece, jnp.bfloat16),
            pltpu.SemaphoreType.DMA((3,)),
            pltpu.SemaphoreType.DMA((3,)),
        )
        if self.far:
            self.scratch += (pltpu.VMEM((2,) + piece, jnp.bfloat16), pltpu.SemaphoreType.DMA((2,)))

    def within(self):
        landing, _, send_sems, recv_sems, *here = self.room
        me = lax.axis_index(FRAME)
        other = frame_partners()[0]
        side = lax.div(me, 2)
        copies = []
        for k, to_side in enumerate((1 - side, side)):
            given = 2 * to_side + lax.rem(other, 2)
            kept = 2 * to_side + lax.rem(me, 2)
            copies.append(
                remote(
                    self.ins[0].at[span(given, self.share)],
                    landing.at[k],
                    send_sems.at[k],
                    recv_sems.at[k],
                    {FRAME: other},
                )
            )
            if self.far:
                own, sems = here[:2]
                source = self.ins[0].at[span(kept, self.share)]
                copies.append(pltpu.make_async_copy(source, own.at[k], sems.at[k]))
        return copies

    def over(self):
        crossing, send_sems, recv_sems = self.room[1:4]
        target = {FRAME: frame_partners()[1]}
        return remote(crossing.at[0], crossing.at[1], send_sems.at[2], recv_sems.at[2], target)

    def chip_sum(self, k):
        me = lax.axis_index(FRAME)
        if self.far:
            own = self.room[4][k]
        else:
            side = lax.div(me, 2) if k else 1 - lax.div(me, 2)
            own = self.ins[0][span(2 * side + lax.rem(me, 2), self.share), :]
        return own.astype(jnp.float32) + self.room[0][k].astype(jnp.float32)

    def begin(self):
        for copy in self.within():
            copy.start()

    def middle(self):
        for copy in self.within():
            copy.wait()
        self.room[1][0] = self.chip_sum(0).astype(jnp.bfloat16)
        self.over().start()

    def steps(self):
        def end():
            self.over().wait()
            total = self.chip_sum(1) + self.room[1][1].astype(jnp.float32)
            self.out[0][...] = total.astype(jnp.bfloat16)

        return [end]


class ShareCrossTask(ShareTask):
    greets = (FRAME, SECTION)
    late = True

    def __init__(self, grad, later):
        super().__init__(grad)
        self.operands = (later,)
        self.base = len(self.scratch)
        self.outs = (jax.ShapeDtypeStruct(later.shape, jnp.float32),)
        self.scratch += (pltpu.VMEM((3,) + later.shape, jnp.bfloat16), pltpu.SemaphoreType.DMA((3,)))

    def crossing(self, which):
        parts, sems = self.room[self.base :]
        target = {SECTION: 1 - lax.axis_index(SECTION)}
        later = self.far_ins[0]
        over = remote(parts.at[0] if which else later, parts.at[1], sems.at[0], sems.at[1], target)
        return over, pltpu.make_async_copy(later, parts.at[2], sems.at[2])

    def steps(self):
        parts = self.room[self.base]
        section = lax.axis_index(SECTION)

        def send():
            self.over().wait()
            total = self.chip_sum(1) + self.room[1][1].astype(jnp.float32)
            parts[0] = total.astype(jnp.bfloat16)
            for which in (0, 1):

                @pl.when(section == which)
                def _():
                    over, stay = self.crossing(which)
                    over.start()
                    if which:
                        stay.start()

        def end():
            over, stay = self.crossing(1)
            over.wait()
            came = parts[1].astype(jnp.float32)

            @pl.when(section == 0)
            def _():
                self.out[0][...] = parts[0].astype(jnp.float32) + came

            @pl.when(section == 1)
            def _():
                stay.wait()
                self.out[0][...] = parts[2].astype(jnp.float32) + came

        return [send, lambda: None, lambda: None, end]


class StatesTask(ShareTask):
    greets = (FRAME, SECTION)
    out_in_vmem = True

    def __init__(self, grad, later):
        super().__init__(grad)
        self.operands = (grad, later)
        self.base = len(self.scratch)
        self.outs = ()
        shape = (2,) + later.shape
        self.scratch += (pltpu.VMEM(shape, jnp.bfloat16), pltpu.VMEM(later.shape, jnp.bfloat16))
        self.scratch += (pltpu.SemaphoreType.DMA((3,)),)

    @property
    def both(self):
        return self.room[self.base]

    def crossing(self, which):
        both, total, sems = self.room[self.base :]
        later, place = self.ins[1], both.at[which]
        over = remote(total if which else later, place, sems.at[0], sems.at[1], {SECTION: 1 - which})
        return over, pltpu.make_async_copy(later, place, sems.at[2])

    def cross(self):
        self.over().wait()
        both, total, _ = self.room[self.base :]
        total[...] = (self.chip_sum(1) + self.room[1][1].astype(jnp.float32)).astype(jnp.bfloat16)
        section = lax.axis_index(SECTION)
        for which in (0, 1):

            @pl.when(section == which)
            def _():
                over, stay = self.crossing(which)
                over.start()
                if which:
                    stay.start()
                else:
                    both[0] = total[...]

    def arrive(self):
        section = lax.axis_index(SECTION)
        for which in (0, 1):

            @pl.when(section == which)
            def _():
                over, stay = self.crossing(which)
                over.wait()
                if which:
                    stay.wait()

    def steps(self):
        return []


class BothTask(Task):
    out_in_vmem = False
    greets = (SECTION,)

    def __init__(self, first, second):
        self.operands = (first, second)
        self.outs = (jax.ShapeDtypeStruct((2,) + first.shape, first.dtype),)
        self.scratch = (pltpu.SemaphoreType.DMA((3,)),)

    def copies(self, given, kept):
        (sems,) = self.room
        section = lax.axis_index(SECTION)
        place = self.out[0].at[section]
        over = remote(self.ins[given], place, sems.at[0], sems.at[1], {SECTION: 1 - section})
        return over, pltpu.make_async_copy(self.ins[kept], place, sems.at[2])

    def begin(self):
        section = lax.axis_index(SECTION)
        for which in (0, 1):

            @pl.when(section == which)
            def _():
                for copy in self.copies(1 - which, which):
                    copy.start()

    def steps(self):
        def end():
            for copy in self.copies(0, 1):
                copy.wait()

        return [end]


class CrossTask(Task):
    greets = (SECTION,)

    def __init__(self, first, second, added):
        self.operands = (first, second)
        self.added = added
        self.out_in_vmem = added
        shape = first.shape
        if added:
            self.outs = (jax.ShapeDtypeStruct(shape, jnp.float32),)
            self.scratch = (pltpu.VMEM(shape, jnp.bfloat16),) * 2 + (pltpu.SemaphoreType.DMA((3,)),)
        else:
            self.outs = (jax.ShapeDtypeStruct(shape, first.dtype),)
            self.scratch = (pltpu.SemaphoreType.DMA((2,)),)

    def copies(self, given, kept):
        sems = self.room[-1]
        landing = self.room[0] if self.added else self.out[0]
        target = {SECTION: 1 - lax.axis_index(SECTION)}
        copies = [remote(self.ins[given], landing, sems.at[0], sems.at[1], target)]
        if self.added:
            copies.append(pltpu.make_async_copy(self.ins[kept], self.room[1], sems.at[2]))
        return copies

    def begin(self):
        section = lax.axis_index(SECTION)
        for which in (0, 1):

            @pl.when(section == which)
            def _():
                for copy in self.copies(1 - which, which):
                    copy.start()

    def steps(self):
        def end():
            for copy in self.copies(0, 1):
                copy.wait()
            if self.added:
                self.out[0][...] = self.room[0][...].astype(jnp.float32) + self.room[1][...].astype(
                    jnp.float32
                )

        return [lambda: None, lambda: None, end]


class TextTask(Task):
    out_in_vmem = False
    greets = (SECTION, FRAME)
    late = True

    def __init__(self, states):
        micros, rows, width = states.shape
        self.outs = (jax.ShapeDtypeStruct((2, 4, rows, width), states.dtype),)
        self.scratch = (pltpu.SemaphoreType.DMA((3,)),) + (pltpu.SemaphoreType.DMA((2, 3)),) * 2

    def place(self, layer):
        return self.out[0].at[layer, lax.axis_index(FRAME)]

    def over(self):
        sems, section = self.room[0], lax.axis_index(SECTION)
        source = self.ins[0].at[1 - section]
        return remote(source, self.place(section), sems.at[0], sems.at[1], {SECTION: 1 - section})

    def stay(self):
        section = lax.axis_index(SECTION)
        return pltpu.make_async_copy(self.ins[0].at[section], self.place(section), self.room[0].at[2])

    def spread(self, far):
        section = lax.axis_index(SECTION)
        layer = 1 - section if far else section
        source = self.place(layer) if far else self.ins[0].at[section]
        pair = self.room[1 + far]
        return [
            remote(source, self.place(layer), pair.at[0, k], pair.at[1, k], {FRAME: other})
            for k, other in enumerate(frame_partners())
        ]

    def begin(self):
        for copy in [self.over(), self.stay()] + self.spread(0):
            copy.start()

    def steps(self):
        def first():
            self.over().wait_recv()
            for copy in self.spread(1):
                copy.start()

        def second():
            self.over().wait_send()
            self.stay().wait()
            for copy in self.spread(0) + self.spread(1):
                copy.wait()

        return [first, second]


class TotalTask(Task):
    greets = (SECTION, LINE)

    late = True

    def __init__(self, part):
        rows, width = part.shape
        self.share = rows // 4
        self.outs = (jax.ShapeDtypeStruct((rows, width), jnp.bfloat16),)
        piece = (self.share, width)
        self.scratch = (
            pltpu.VMEM((4,) + piece, jnp.bfloat16),
            pltpu.VMEM((2,) + piece, jnp.bfloat16),
            pltpu.SemaphoreType.DMA((4,)),
            pltpu.SemaphoreType.DMA((4,)),
            pltpu.SemaphoreType.DMA((2,)),
            pltpu.SemaphoreType.DMA((4,)),
            pltpu.SemaphoreType.DMA((4,)),
        )

    def partners(self):
        me = lax.axis_index(LINE)
        return [lax.rem(me + by, 4) for by in (1, 2, 3)]

    def spread(self):
        landing, _, send_sems, recv_sems = self.room[:4]
        me = lax.axis_index(LINE)
        away = [
            remote(
                self.ins[0].at[span(partner, self.share)],
                landing.at[by],
                send_sems.at[by],
                recv_sems.at[by],
                {LINE: partner},
            )
            for by, partner in enumerate(self.partners(), 1)
        ]
        stay = pltpu.make_async_copy(self.ins[0].at[span(me, self.share)], landing.at[0], send_sems.at[0])
        return away + [stay]

    def over(self):
        sums, sems = self.room[1], self.room[4]
        target = {SECTION: 1 - lax.axis_index(SECTION)}
        return remote(sums.at[0], sums.at[1], sems.at[0], sems.at[1], target)

    def gather(self):
        send_sems, recv_sems = self.room[5:]
        mine = self.out[0].at[span(lax.axis_index(LINE), self.share)]
        return [
            remote(mine, mine, send_sems.at[by], recv_sems.at[by], {LINE: partner})
            for by, partner in enumerate(self.partners(), 1)
        ]

    def begin(self):
        for copy in self.spread():
            copy.start()

    def sum_first(self):
        landing, sums = self.room[:2]
        for copy in self.spread():
            copy.wait()
        total = landing[0].astype(jnp.float32)
        for by in (1, 2, 3):
            total = total + landing[by].astype(jnp.float32)
        sums[0] = total.astype(jnp.bfloat16)
        self.over().start()

    def steps(self):
        sums = self.room[1]

        def second():
            self.over().wait()
            total = sums[0].astype(jnp.float32) + sums[1].astype(jnp.float32)
            self.out[0][span(lax.axis_index(LINE), self.share), :] = total.astype(jnp.bfloat16)
            for copy in self.gather():
                copy.start()

        def third():
            for copy in self.gather():
                copy.wait()

        return [second, third]


class VectorTask(Task):
    greets = (SECTION, FRAME)
    late = True

    def __init__(self, grads):
        shape = grads.shape[1:]
        self.outs = (jax.ShapeDtypeStruct(shape, jnp.float32),)
        self.scratch = (
            pltpu.VMEM((4,) + grads.shape, jnp.float32),
            pltpu.VMEM((3,) + shape, jnp.float32),
            pltpu.SemaphoreType.DMA((4,)),
            pltpu.SemaphoreType.DMA((4,)),
            pltpu.SemaphoreType.DMA((2,)),
        )

    def spread(self):
        landing, _, send_sems, recv_sems, _ = self.room
        away = [
            remote(self.ins[0], landing.at[k], send_sems.at[k], recv_sems.at[k], {FRAME: partner})
            for k, partner in enumerate(frame_partners(), 1)
        ]
        return away + [pltpu.make_async_copy(self.ins[0], landing.at[0], send_sems.at[0])]

    def over(self):
        sums, sems = self.room[1], self.room[4]
        target = {SECTION: 1 - lax.axis_index(SECTION)}
        return remote(sums.at[0], sums.at[1], sems.at[0], sems.at[1], target)

    def begin(self):
        for copy in self.spread():
            copy.start()

    def steps(self):
        landing, sums = self.room[:2]
        section = lax.axis_index(SECTION)

        def first():
            for copy in self.spread():
                copy.wait()
            total = [
                (landing[0, layer] + landing[1, layer]) + (landing[2, layer] + landing[3, layer])
                for layer in (0, 1)
            ]
            for which in (0, 1):

                @pl.when(section == which)
                def _():
                    sums[0] = total[1 - which]
                    sums[2] = total[which]

            self.over().start()

        def second():
            self.over().wait()
            self.out[0][...] = sums[2] + sums[1]

        return [first, second]


def greet(kinds):
    barrier = pltpu.get_barrier_semaphore()
    section, head, frame = (lax.axis_index(a) for a in (SECTION, LINE, FRAME))
    targets = []
    if FRAME in kinds:
        targets += [{FRAME: other} for other in frame_partners()]
    if SECTION in kinds:
        targets.append({SECTION: 1 - section})
    if BOTH in kinds:
        targets += [{SECTION: 1 - section, FRAME: other} for other in frame_partners()]
    if LINE in kinds:
        targets += [{LINE: lax.rem(head + by, 4)} for by in (1, 2, 3)]
    for target in targets:
        pl.semaphore_signal(barrier, 1, device_id=target, device_id_type=MESH_IDS)
    if LINE_ONLY not in kinds or LINE in kinds:
        return lambda: pl.semaphore_wait(barrier, len(targets))

    for way in (-1, 1):
        other = head + way

        @pl.when((other >= 0) & (other < 4))
        def _():
            pl.semaphore_signal(barrier, 1, device_id={LINE: other}, device_id_type=MESH_IDS)

    is_end = (head == 0) | (head == 3)

    def wait():
        @pl.when(is_end)
        def _():
            pl.semaphore_wait(barrier, len(targets) + 1)

        @pl.when(jnp.logical_not(is_end))
        def _():
            pl.semaphore_wait(barrier, len(targets) + 2)

    return wait


def call(body, operands, outs, scratch, kinds, collective_id, tasks=(), in_vmem=True, end=None):
    whole, anywhere = pl.BlockSpec(memory_space=pltpu.VMEM), pl.BlockSpec(memory_space=pl.ANY)
    place = whole if in_vmem else anywhere
    in_specs, out_specs = [place] * len(operands), [place] * len(outs)
    operands, all_outs, scratch = list(operands), list(outs), list(scratch)
    counts = [(len(operands), len(outs), len(scratch))]
    kinds = set(kinds)
    for task in tasks:
        kinds |= set(task.greets)
        in_specs += [anywhere] * len(task.operands)
        out_specs += [whole if task.out_in_vmem else anywhere] * len(task.outs)
        operands += task.operands
        all_outs += task.outs
        scratch += task.scratch
        counts.append((len(task.operands), len(task.outs), len(task.scratch)))
    n_in, n_out = len(operands), len(all_outs)

    def kernel(*refs):
        groups = [list(refs[:n_in]), list(refs[n_in : n_in + n_out]), list(refs[n_in + n_out :])]
        bound = []
        for sizes in counts:
            bound.append([])
            for group, size in zip(groups, sizes):
                bound[-1].append(group[:size])
                del group[:size]
        for task, parts in zip(tasks, bound[1:]):
            task.bind(*parts)

        meet = greet(kinds)

        def ride():
            for task in tasks:
                if not task.late:
                    task.begin()

        def middle():
            for task in tasks:
                if not task.late:
                    task.middle()

        if body is None:
            meet()
            ride()
            middle()
        else:
            body(*bound[0], meet, ride, middle)
        queues = [task.steps() for task in tasks]
        while any(queues):
            for queue in queues:
                if queue:
                    queue.pop(0)()
        if end is not None:
            end()

    results = pl.pallas_call(
        kernel,
        out_shape=all_outs,
        in_specs=in_specs,
        out_specs=out_specs,
        scratch_shapes=scratch,
        compiler_params=pltpu.CompilerParams(
            collective_id=collective_id, has_side_effects=True, vmem_limit_bytes=VMEM_BYTES
        ),
    )(*operands)
    results = list(results)
    main, results = results[: len(outs)], results[len(outs) :]
    return main, results


def chunking(rows):
    return max(1, min(16, rows // 16))


def nt_product(left, right):
    return lax.dot_general(left, right, (((1,), (1,)), ((), ())), preferred_element_type=jnp.float32)


def plain_product(left, right):
    return jnp.dot(left, right, preferred_element_type=jnp.float32)


def norm_parts(v):
    average = jnp.mean(v, axis=-1, keepdims=True)
    centered = v - average
    inverse = lax.rsqrt(jnp.mean(centered * centered, axis=-1, keepdims=True) + EPS)
    return centered * inverse, inverse


class Held:
    def __init__(self, shape, dtype, sources=(), choose=None, stage=0, kept=False):
        self.shape, self.dtype = tuple(shape), dtype
        self.sources, self.choose, self.stage, self.kept = sources, choose, stage, kept
        self.ref = self.far = self.sem = None

    def copy_in(self, index=0):
        source = self.far[index]
        if self.choose == BY_SECTION:
            source = source.at[lax.axis_index(SECTION)]
        return pltpu.make_async_copy(source, self.ref, self.sem)

    def start_in(self):
        if not isinstance(self.choose, int):
            self.copy_in().start()
            return
        section = lax.axis_index(SECTION)

        @pl.when(section == self.choose)
        def _():
            self.copy_in(0).start()

        @pl.when(section != self.choose)
        def _():
            self.copy_in(1).start()

    def write(self, at, value):
        self.ref[at, :] = value
        if self.kept:
            pltpu.make_async_copy(self.ref.at[at], self.far[0].at[at], self.sem).start()

    def flush(self):
        pltpu.make_async_copy(self.ref, self.far[0], self.sem).start()

    def drain(self):
        pltpu.make_async_copy(self.ref, self.far[0], self.sem).wait()


class Build:
    def __init__(self):
        self.helds, self.extras, self.starts, self.finals = [], [], [], []

    def add(self, held):
        self.helds.append(held)
        return held

    def arg(self, array, stage, choose=None):
        shape = array.shape[1:] if choose == BY_SECTION else array.shape
        return self.add(Held(shape, array.dtype, (array,), choose, stage))

    def pick(self, pair, layer, stage):
        return self.add(Held(pair[0].shape, pair[0].dtype, tuple(pair), layer, stage))

    def out(self, shape, dtype):
        return self.add(Held(shape, dtype, kept=True))

    def temp(self, shape, dtype):
        return self.add(Held(shape, dtype))

    def extra(self, scratch):
        self.extras.append(scratch)
        return len(self.extras) - 1


class Stage:
    def __init__(self, rows, width):
        self.rows, self.width = rows, width
        self.begin = self.prepare = self.finish = self.after = None
        self.ends = []


class Chore:
    def __init__(self, build, stage, piece, each, left, right, flipped=False, later=None, wait=5):
        self.start, self.each, self.wait = (stage, piece), each, wait
        self.left, self.right, self.flipped = left, right, flipped
        columns = left.shape[0] if flipped else left.shape[1]
        self.units = columns // BLOCK
        self.product = build.temp((columns, right.shape[1]), jnp.bfloat16)
        self.task = ShareTask(self.product) if later is None else ShareCrossTask(self.product, later)
        self.task.late = True

    def unit(self, number):
        at = span(number, BLOCK)
        right = self.right.ref[...].astype(jnp.bfloat16)
        if self.flipped:
            product = plain_product(self.left.ref[at, :], right)
        else:
            product = lax.dot_general(
                self.left.ref[:, at], right, (((0,), (0,)), ((), ())), preferred_element_type=jnp.float32
            )
        self.product.ref[at, :] = product.astype(jnp.bfloat16)

    def run(self, stage, pieces, piece):
        shift = (stage - self.start[0]) * pieces - self.start[1]
        steps = -(-self.units // self.each)

        def at_step(first, last, what):
            if shift >= last or shift + pieces <= first:
                return
            now = piece + shift

            @pl.when((now >= first) & (now < last))
            def _():
                what(now)

        def make(now):
            for more in range(self.each):
                self.unit(now * self.each + more)

        def begin(now):
            self.task.ins = [self.product.ref]
            self.task.begin()

        at_step(0, steps, make)
        at_step(steps, steps + 1, begin)
        at_step(steps + self.wait, steps + self.wait + 1, lambda now: self.task.middle())


def line_chain(stages, need, part, set_out, middle, chores, hooks):
    place = lax.axis_index(LINE)
    rows = stages[0].rows
    pieces = chunking(rows)
    step = rows // pieces
    per_block = max(1, min(BLOCK, rows) // step)
    lag = max(0, min(LAG, pieces - per_block))
    is_end = (place == 0) | (place == 3)
    inner = {LINE: jnp.where(place == 0, 1, 2)}
    outer = {LINE: jnp.where(place == 1, 0, 3)}
    peer = {LINE: 3 - place}

    def inwards(stage, piece):
        send, held, _, send_sems, recv_sems = stage.room[:5]
        at = span(piece, step)
        return remote(send.at[at], held.at[at], send_sems.at[piece], recv_sems.at[piece], inner)

    def crossing(stage, piece):
        send, _, across = stage.room[:3]
        send_sems, recv_sems = stage.room[5:7]
        at = span(piece, step)
        return remote(send.at[at], across.at[at], send_sems.at[piece], recv_sems.at[piece], peer)

    def outwards(stage, piece):
        held = stage.room[1]
        send_sems, recv_sems = stage.room[7:]
        at = span(piece, step)
        return remote(held.at[at], held.at[at], send_sems.at[piece], recv_sems.at[piece], outer)

    def hook(stage, piece, at_end):
        for run, *spots in hooks:
            index, when = spots[0 if at_end else 1]
            if stages[index] is stage:

                @pl.when(piece == when)
                def _():
                    run()

    def finish(stage, piece):
        stage.finish(span(piece, step), piece)
        if stage.after is not None:

            @pl.when(lax.rem(piece, per_block) == per_block - 1)
            def _():
                stage.after(lax.div(piece, per_block))

    def open_stage(index):
        need(index)
        if stages[index].begin is not None:
            stages[index].begin()

    def loop(first, last, step_of):
        def one(piece, carry):
            step_of(piece)
            return carry

        lax.fori_loop(first, last, one, 0)

    def chore(stage, piece):
        for one in chores:
            one.run(stages.index(stage), pieces, piece)

    @pl.when(is_end)
    def _():
        def beside(stage, piece):
            chore(stage, piece)
            hook(stage, piece, True)

        def take(stage, piece):
            outwards(stage, piece).wait_recv()
            finish(stage, piece)

        for index, stage in enumerate(stages):
            open_stage(index)

            def block_step(block):
                low, high = block * per_block, (block + 1) * per_block
                if index:
                    loop(low, high, lambda piece: take(stages[index - 1], piece))
                stage.room[0][span(block, per_block * step), :] = stage.prepare(block).astype(jnp.bfloat16)
                if index == 0:
                    pl.when(block == 0)(set_out)
                loop(low, high, lambda piece: inwards(stage, piece).start())
                loop(low, high, lambda piece: beside(stage, piece))
                if index == 0:

                    @pl.when(block == 1)
                    def _():
                        middle()

            loop(0, pieces // per_block, block_step)
        loop(0, pieces, lambda piece: take(stages[-1], piece))
        for stage in stages:
            loop(0, pieces, lambda piece: inwards(stage, piece).wait_send())

    @pl.when(jnp.logical_not(is_end))
    def _():
        def add(stage, piece):
            @pl.when(lax.rem(piece, per_block) == 0)
            def _():
                part[...] = stage.prepare(lax.div(piece, per_block))

            if stage is stages[0]:
                pl.when(piece == 0)(set_out)
            at = span(piece, step)
            send, held = stage.room[:2]
            inwards(stage, piece).wait_recv()
            own = part[span(lax.rem(piece, per_block), step), :]
            send[at, :] = (own + held[at, :].astype(jnp.float32)).astype(jnp.bfloat16)
            crossing(stage, piece).start()
            chore(stage, piece)
            hook(stage, piece, False)
            if stage is stages[0]:

                @pl.when(piece == 2 * per_block - 1)
                def _():
                    middle()

        def settle(stage, piece):
            at = span(piece, step)
            send, held, across = stage.room[:3]
            crossing(stage, piece).wait_recv()
            total = send[at, :].astype(jnp.float32) + across[at, :].astype(jnp.float32)
            held[at, :] = total.astype(jnp.bfloat16)
            outwards(stage, piece).start()
            finish(stage, piece)

        for index, stage in enumerate(stages):
            open_stage(index)

            def both(piece):
                add(stage, piece)

                @pl.when(piece >= lag)
                def _():
                    settle(stage, piece - lag)

                if index and lag:

                    @pl.when(piece < lag)
                    def _():
                        settle(stages[index - 1], pieces - lag + piece)

            loop(0, pieces, both)
        loop(pieces - lag, pieces, lambda piece: settle(stages[-1], piece))

        def drain(stage, piece):
            crossing(stage, piece).wait_send()
            outwards(stage, piece).wait_send()

        for stage in stages:
            loop(0, pieces, lambda piece: drain(stage, piece))

    for stage in stages:
        for end in stage.ends:
            end()


def run_build(build, body, kinds, collective_id, tasks):
    operands, outs, scratch = [], [], []
    for held in build.helds:
        operands += held.sources
        if held.kept:
            outs.append(jax.ShapeDtypeStruct(held.shape, held.dtype))
        scratch.append(pltpu.VMEM(held.shape, held.dtype))
    n_held = len(scratch)
    scratch += build.extras
    scratch.append(pltpu.SemaphoreType.DMA((n_held,)))
    reads = sorted((held for held in build.helds if held.sources), key=lambda held: held.stage)

    def need(stage):
        for held in reads:
            if held.stage == stage:
                held.copy_in().wait()

    def run(ins, outs, scratch, meet, ride, middle):
        ins, outs = list(ins), list(outs)
        sems = scratch[-1]
        for index, held in enumerate(build.helds):
            held.ref, held.sem = scratch[index], sems.at[index]
            held.far = [ins.pop(0) for _ in held.sources]
            if held.kept:
                held.far = [outs.pop(0)]
        build.bound = scratch[n_held:-1]
        for held in reads:
            held.start_in()
        for start in build.starts:
            start()
        body(need, meet, ride, middle)

    def end():
        for final in build.finals:
            final()
        for held in build.helds:
            if held.kept:
                held.drain()

    return call(run, operands, outs, scratch, kinds, collective_id, tasks, in_vmem=False, end=end)


def run_chain(
    build, stages, collective_id, tasks, kinds=(LINE_ONLY,), chores=(), hooks=(), then=None, first=None, ahead=0, last=()
):
    slots = []
    for stage in stages:
        pieces = chunking(stage.rows)
        room = [pltpu.VMEM((stage.rows, stage.width), jnp.bfloat16)] * 3
        room += [pltpu.SemaphoreType.DMA((pieces,))] * 6
        slots.append([build.extra(scratch) for scratch in room])
    part = build.extra(pltpu.VMEM((min(BLOCK, stages[0].rows), stages[0].width), jnp.float32))

    def body(need, meet, ride, middle):
        for stage, places in zip(stages, slots):
            stage.room = [build.bound[place] for place in places]
        def set_out():
            meet()
            ride()

        def nothing():
            pass

        go_on = middle
        if first is not None:
            first(need, meet, ride, middle)
            set_out = go_on = nothing
        line_chain(
            stages, lambda index: need(index + ahead), build.bound[part], set_out, go_on, chores, hooks
        )
        if then is not None:
            then(need)

    tasks = list(tasks) + [one.task for one in chores] + list(last)
    return run_build(build, body, kinds, collective_id, tasks)


def scaled_rows(standard, gains, row):
    return (standard * gains.ref[row : row + 1] + gains.ref[row + 1 : row + 2]).astype(jnp.bfloat16)


def residual_norm(build, stage, base, gains, row, mode):
    shape = (stage.rows, stage.width)
    result = build.temp(shape, jnp.float32) if mode == NORM else None
    normed = build.out(shape, jnp.bfloat16) if mode != END else None
    low = build.out(shape, jnp.bfloat16)

    def finish(at, piece):
        value = base.ref[at, :].astype(jnp.float32) + stage.room[1][at, :].astype(jnp.float32)
        rounded = value.astype(jnp.bfloat16)
        low.write(at, rounded)
        if mode == NORM:
            result.write(at, value)
        if mode == NEXT:
            value = rounded.astype(jnp.float32)
        if mode != END:
            standard, _ = norm_parts(value)
            normed.write(at, scaled_rows(standard, gains, row))

    stage.finish = finish
    return result, normed


def gain_rows(build, vectors, layer, index):
    if isinstance(vectors, tuple):
        return build.pick(vectors, layer, index)
    return build.arg(vectors, index)


def vector_rows(build, width):
    grads = build.out((8, width), jnp.float32)

    def clear():
        grads.ref[...] = jnp.zeros(grads.shape, jnp.float32)

    build.starts.append(clear)
    build.finals.append(grads.flush)
    return grads


def self_out_stage(build, index, layer, attended_t, weight, base):
    rows, width = base.shape
    stage = Stage(rows, width)
    flipped, matrix = build.arg(attended_t, index), build.pick(weight, layer, index)
    left = build.temp(attended_t.shape[::-1], jnp.bfloat16)

    def begin():
        left.ref[...] = flipped.ref[...].T

    def prepare(number):
        return plain_product(left.ref[span(number, min(BLOCK, rows)), :], matrix.ref[...])

    stage.begin, stage.prepare = begin, prepare
    return stage


def text_mask(states, seg):
    item = lax.rem(lax.div(lax.broadcasted_iota(jnp.int32, (states, 1), 0), TEXT // 4), ITEMS)
    return item == seg


def cross_stage(build, index, layer, normed, states, seg, into, out_of):
    rows, width = normed.shape
    stage = Stage(rows, width)
    states, seg = build.arg(states, index), build.arg(seg, index)
    columns, block = states.shape[1] // 2, min(BLOCK, rows)
    if not isinstance(into, WeightTask):
        into, out_of = build.pick(into, layer, index), build.pick(out_of, layer, index)
    queries = build.out((rows, columns), jnp.bfloat16)
    left = build.out((rows, columns), jnp.bfloat16)
    values_t = build.temp((columns, states.shape[0]), jnp.bfloat16)

    def begin():
        values_t.ref[...] = states.ref[:, columns:].T

    def prepare(number):
        at = span(number, block)
        query = plain_product(normed.ref[at, :], into.ref[...]).astype(jnp.bfloat16)
        queries.write(at, query)
        query_t = query.T
        allowed = text_mask(states.shape[0], seg.ref[:, at])
        mixed = []
        for head in range(columns // HEAD):
            cols = slice(head * HEAD, (head + 1) * HEAD)
            scores = plain_product(states.ref[:, cols], query_t[cols, :]) * HEAD ** (-0.5)
            scores = jnp.where(allowed, scores, masked_score)
            e = jnp.exp(scores - jnp.max(scores, axis=0, keepdims=True))
            total = jnp.sum(e, axis=0, keepdims=True)
            value = plain_product(values_t.ref[cols, :], e.astype(jnp.bfloat16))
            mixed.append((value * (1.0 / total)).astype(jnp.bfloat16))
        mixed = jnp.concatenate(mixed, axis=0).T
        left.write(at, mixed)
        return plain_product(mixed, out_of.ref[...])

    stage.begin, stage.prepare = begin, prepare
    return stage


def feed_stage(build, index, layer, normed, into, out_of):
    rows, width = normed.shape
    stage = Stage(rows, width)
    block = min(BLOCK, rows)
    if isinstance(into, WeightTask):
        hidden = into.operands[0].shape[1]
    else:
        hidden = into[0].shape[1]
        into, out_of = build.pick(into, layer, index), build.pick(out_of, layer, index)
    before = build.out((rows, hidden), jnp.bfloat16)
    left = build.out((rows, hidden), jnp.bfloat16)

    def prepare(number):
        at = span(number, block)
        u = plain_product(normed.ref[at, :], into.ref[...])
        before.write(at, u.astype(jnp.bfloat16))
        active = (0.5 * u * (1.0 + lax.erf(u * inv_sqrt_two))).astype(jnp.bfloat16)
        left.write(at, active)
        return plain_product(active, out_of.ref[...])

    stage.prepare = prepare
    return stage


def norm_backward(build, index, stage, value, gains, row, grads, upstream, feeds, spare=None):
    shape = (stage.rows, stage.width)
    pieces = chunking(stage.rows)
    value = build.arg(value, index, BY_SECTION if value.ndim == 3 else None)
    result = build.temp(shape, jnp.float32) if feeds else None
    low = build.out(shape, jnp.bfloat16)
    parts = build.extra(pltpu.VMEM((2, pieces, 1, stage.width), jnp.float32))
    if spare is not None:
        spare = build.arg(spare, index)
        both = build.out((2,) + shape, jnp.bfloat16)
        sems = build.extra(pltpu.SemaphoreType.DMA((2, pieces)))

    def over(at, piece, source):
        target = {SECTION: 1 - lax.axis_index(SECTION)}
        pair = build.bound[sems]
        landing = both.ref.at[lax.axis_index(SECTION), at]
        return remote(source.ref.at[at], landing, pair.at[0, piece], pair.at[1, piece], target)

    def finish(at, piece):
        grad = stage.room[1][at, :].astype(jnp.float32)
        standard, inverse = norm_parts(value.ref[at, :].astype(jnp.float32))
        scaled = grad * gains.ref[row : row + 1]
        through = inverse * (
            scaled
            - jnp.mean(scaled, axis=-1, keepdims=True)
            - standard * jnp.mean(scaled * standard, axis=-1, keepdims=True)
        )
        total = through + upstream.ref[at, :].astype(jnp.float32)
        if feeds:
            result.write(at, total)
        low.write(at, total.astype(jnp.bfloat16))
        build.bound[parts][0, piece] = jnp.sum(grad * standard, axis=0, keepdims=True)
        build.bound[parts][1, piece] = jnp.sum(grad, axis=0, keepdims=True)
        if spare is not None:
            section = lax.axis_index(SECTION)

            @pl.when(section == 0)
            def _():
                both.ref[0, at, :] = low.ref[at, :]
                over(at, piece, spare).start()

            @pl.when(section == 1)
            def _():
                both.ref[1, at, :] = spare.ref[at, :]
                over(at, piece, low).start()

    def end():
        grads.ref[row : row + 1] = jnp.sum(build.bound[parts][0], axis=0)
        grads.ref[row + 1 : row + 2] = jnp.sum(build.bound[parts][1], axis=0)

    def settle():
        def one(piece, carry):
            over(span(piece, stage.rows // pieces), piece, low).wait()
            return carry

        lax.fori_loop(0, pieces, one, 0)
        both.flush()

    if spare is not None:
        build.finals.append(settle)
    stage.finish, stage.value = finish, value
    stage.ends.append(end)
    return result, low


def feed_back_stage(build, index, layer, grad_out, before, out_of, into):
    rows, width = grad_out.shape
    stage = Stage(rows, width)
    hidden, block = out_of[0].shape[0], min(BLOCK, rows)
    before = build.arg(before, index)
    out_of, into = build.pick(out_of, layer, index), build.pick(into, layer, index)
    left = build.out((rows, hidden), jnp.bfloat16)

    def prepare(number):
        at = span(number, block)
        grad = nt_product(grad_out.ref[at, :].astype(jnp.bfloat16), out_of.ref[...])
        u = before.ref[at, :].astype(jnp.float32)
        slope = 0.5 * (1.0 + lax.erf(u * inv_sqrt_two)) + u * jnp.exp(-0.5 * u * u) * inv_sqrt_tau
        grad = (grad * slope).astype(jnp.bfloat16)
        left.write(at, grad)
        return nt_product(grad, into.ref[...])

    stage.prepare, stage.left = prepare, left
    return stage


def cross_back_stage(build, index, layer, grad_low, queries, states, seg, out_of, into):
    rows, width = grad_low.shape
    stage = Stage(rows, width)
    columns, block = out_of[0].shape[0], min(BLOCK, rows)
    queries, states, seg = (build.arg(array, index) for array in (queries, states, seg))
    out_of, into = build.pick(out_of, layer, index), build.pick(into, layer, index)
    left = build.out((rows, columns), jnp.bfloat16)
    state_grads = build.out(states.shape, jnp.bfloat16)
    keys_t = build.temp((columns, states.shape[0]), jnp.bfloat16)
    sums = build.temp(states.shape, jnp.float32)
    scale = HEAD ** (-0.5)

    def begin():
        keys_t.ref[...] = states.ref[:, :columns].T
        sums.ref[...] = jnp.zeros(sums.shape, jnp.float32)

    def prepare(number):
        at = span(number, block)
        grad = nt_product(grad_low.ref[at, :], out_of.ref[...]).astype(jnp.bfloat16)
        query = queries.ref[at, :]
        grad_t, query_t = grad.T, query.T
        allowed = text_mask(states.shape[0], seg.ref[:, at])
        query_grads = []
        for head in range(columns // HEAD):
            cols = slice(head * HEAD, (head + 1) * HEAD)
            more = slice(columns + head * HEAD, columns + (head + 1) * HEAD)
            scores = plain_product(states.ref[:, cols], query_t[cols, :]) * scale
            scores = jnp.where(allowed, scores, masked_score)
            e = jnp.exp(scores - jnp.max(scores, axis=0, keepdims=True))
            p = e * (1.0 / jnp.sum(e, axis=0, keepdims=True))
            slope = plain_product(states.ref[:, more], grad_t[cols, :])
            weighted = p * slope
            ds = (weighted - p * jnp.sum(weighted, axis=0, keepdims=True)).astype(jnp.bfloat16)
            query_grads.append((plain_product(keys_t.ref[cols, :], ds) * scale).astype(jnp.bfloat16))
            sums.ref[:, cols] += plain_product(ds, query[:, cols]) * scale
            sums.ref[:, more] += plain_product(p.astype(jnp.bfloat16), grad[:, cols])
        query_grads = jnp.concatenate(query_grads, axis=0).T
        left.write(at, query_grads)
        return nt_product(query_grads, into.ref[...])

    def end():
        state_grads.write(slice(0, states.shape[0]), sums.ref[...].astype(jnp.bfloat16))

    stage.begin, stage.prepare, stage.state_grads = begin, prepare, state_grads
    stage.ends.append(end)
    return stage


def self_in_stage(build, index, layer, grads_t, weights, width):
    columns, rows = grads_t.shape
    stage = Stage(rows, width)
    part = columns // 3
    flipped = grads_t if isinstance(grads_t, Held) else build.arg(grads_t, index)
    matrices = [build.pick(weight, layer, index) for weight in weights]
    left = build.temp((rows, columns), jnp.bfloat16)

    def begin():
        for number in range(3):
            heads = [
                flipped.ref[(3 * head + number) * HEAD : (3 * head + number + 1) * HEAD, :]
                for head in range(part // HEAD)
            ]
            left.ref[:, number * part : (number + 1) * part] = jnp.concatenate(heads, axis=0).T

    def prepare(number):
        at = span(number, min(BLOCK, rows))
        total = jnp.zeros((min(BLOCK, rows), width), jnp.float32)
        for number, matrix in enumerate(matrices):
            total = total + nt_product(left.ref[at, number * part : (number + 1) * part], matrix.ref[...])
        return total

    stage.begin, stage.prepare = begin, prepare
    stage.left = left
    return stage


def forward_chain(
    layer, attended_t, entering, states, seg, vectors, weights, collective_id, tasks=(), late=None, begins=None
):
    output, query, cross, expand, reduce = weights
    build = Build()
    gains = build.pick(vectors, layer, 0)
    base = build.arg(entering, 0, BY_SECTION if entering.ndim == 3 else None)
    first = self_out_stage(build, 0, layer, attended_t, output, base)
    middle, second_normed = residual_norm(build, first, base, gains, 2, NORM)
    second = cross_stage(build, 1, layer, second_normed, states, seg, query, cross)
    latter, third_normed = residual_norm(build, second, middle, gains, 4, NORM)
    third = feed_stage(build, 2, layer, third_normed, expand, reduce)
    after = None if late is None else build.pick(vectors, 1 - layer, 2)
    _, next_normed = residual_norm(build, third, latter, after, 0, END if late is None else NEXT)
    hooks, then, kinds = [], None, (LINE_ONLY,)
    if isinstance(expand, WeightTask):
        hooks = [
            (expand.first_hop, (1, 0), (0, 9)),
            (reduce.first_hop, (1, 5), (1, 0)),
            (expand.second_hop, (1, 9), (1, 2)),
            (reduce.second_hop, (1, 15), (1, 9)),
        ]
        for one in late:
            hooks += [(one.first_hop, (2, 0), (1, 8)), (one.second_hop, (2, 8), (2, 0))]
        start_second = second.begin

        def begin_second():
            query.second_hop()
            cross.second_hop()
            query.arrive()
            cross.arrive()
            start_second()

        def begin_third():
            expand.arrive()
            reduce.arrive()

        second.begin, third.begin = begin_second, begin_third
        attention = Attention(build, third.rows, begins, 2)
        sender = BlockSender(build, third.rows, 3 * HEAD, attention.heads_t)

        def project(block):
            @pl.when(block == 0)
            def _():
                for one in late:
                    one.arrive()

            lanes = span(block, BLOCK)
            turned_parts(next_normed.ref[lanes, :], late, sender.own, (), lanes)
            sender.send(block)

        def then(need):
            sender.wait()
            attention.run()

        third.after = project
        kinds = (LINE_ONLY, FRAME)
    return run_chain(build, [first, second, third], collective_id, tasks, kinds, hooks=hooks, then=then)


def add_backward(build, index, layer, arriving, saved, states, seg, vectors, weights):
    _, query, cross, expand, reduce = weights
    middle, latter, third_normed, queries, before, hidden = saved
    gains, grads = gain_rows(build, vectors, layer, index), vector_rows(build, arriving.shape[1])
    first = feed_back_stage(build, index, layer, arriving, before, reduce, expand)
    grad_latter, grad_cross = norm_backward(build, index, first, latter, gains, 4, grads, arriving, True)
    second = cross_back_stage(build, index + 1, layer, grad_cross, queries, states, seg, cross, query)
    _, grad_self = norm_backward(
        build, index + 1, second, middle, gains, 2, grads, grad_latter, False
    )
    first_piece, each, wait = (12, 4, 3) if index else (0, 1, 5)
    chores = [
        Chore(build, index, first_piece, each, build.arg(hidden, index), arriving, wait=wait),
        Chore(build, index + 1, 0, each, build.arg(third_normed, index + 1), first.left, wait=wait),
    ]
    return [first, second], chores, grad_self, second.state_grads


def add_last(
    build, index, layer, grads_t, entering, vectors, grads, residual, weights, spare, products, later=None
):
    stage = self_in_stage(build, index, layer, grads_t, weights, residual.shape[1])
    stage.gains = gain_rows(build, vectors, layer, index)
    _, low = norm_backward(build, index, stage, entering, stage.gains, 0, grads, residual, False, spare)
    chores = []
    for number, (left, right) in enumerate(products):
        flipped = left is not None and left.shape[0] != residual.shape[0]
        if right is None:
            right = stage.left
        elif right is not residual:
            right = build.arg(right, index)
        more = None if later is None else later[number]
        if left is None:
            stage.normed = build.temp(residual.shape, jnp.bfloat16)
            chores.append(Chore(build, 0, 3, 1, stage.normed, right, False, more, 4))
        else:
            chores.append(Chore(build, 0, 0, 1, build.arg(left, index), right, flipped, more))
    return stage, low, chores


def backward_chain(layer, upstream, saved, states, seg, vectors, weights, heads_t, begins, collective_id, tasks):
    build = Build()
    arriving = build.arg(upstream, 0, BY_SECTION)
    stages, chores, grad_self, grad_states = add_backward(
        build, 0, layer, arriving, saved, states, seg, vectors, weights
    )
    output = build.pick(weights[0], layer, 1)
    attention = AttentionBack(build, stages[1].rows, heads_t, begins, 1)
    sender = BlockSender(build, stages[1].rows, HEAD, attention.grad_t)
    share = ShareTask(grad_states)
    share.late = True

    def project(block):
        lanes = span(block, BLOCK)
        turned_grads(grad_self.ref[lanes, :], output, sender.own, lanes)
        sender.send(block)

    def then(need):
        share.ins = [grad_states.ref]
        share.begin()
        attention.begin()
        sender.wait()
        attention.run(share.middle)

    stages[1].after = project
    kinds = (LINE_ONLY, FRAME)
    return run_chain(build, stages, collective_id, tasks + [share], kinds, chores, then=then)


def between_chain(layer, grads_t, entering, vectors, upstream, weights, products, backward, collective_id, tasks):
    build = Build()
    residual = build.arg(upstream, 0)
    products = [(left, residual if right is upstream else right) for left, right in products]
    grads = vector_rows(build, residual.shape[1])
    stage, low, chores = add_last(
        build, 0, layer, grads_t, entering, vectors, grads, residual, weights, None, products
    )
    stages, more, _, _ = add_backward(build, 1, layer - 1, low, *backward)
    return run_chain(build, [stage] + stages, collective_id, tasks, chores=chores + more)


def last_kernel(
    heads_t,
    grad_self,
    output,
    begins,
    inputs,
    vectors,
    weights,
    spare,
    products,
    later,
    states,
    text_local,
    text_weights,
    vector_grads,
    collective_id,
    tasks,
):
    rows, width = grad_self.shape
    build = Build()
    attention = AttentionBack(build, rows, heads_t, begins, 1)
    grad_low, output = build.arg(grad_self, 0), build.pick(output, 0, 0)
    own = build.temp((4, HEAD, rows), jnp.bfloat16)
    sems = build.extra(pltpu.SemaphoreType.DMA((2, 3)))
    products = [(left, grad_low if right is grad_self else right) for left, right in products]
    vector_grads = [build.arg(grads, 2) for grads in vector_grads]
    stage, _, chores = add_last(
        build, 2, 0, attention.out, inputs, vectors, vector_grads[1], grad_low, weights, spare, products, later
    )
    text_local = build.arg(text_local, 2)
    text_weights = [build.arg(weight, 2) for weight in text_weights]
    columns = text_weights[0].shape[1]
    text_rows = build.temp((text_local.shape[0], 2 * columns), jnp.bfloat16)
    text_part = build.temp(text_local.shape, jnp.bfloat16)
    both_grads = build.temp((2, 8, width), jnp.float32)
    chores.append(Chore(build, 0, 10, 2, text_local, text_rows, wait=1))
    from_states, from_vectors, from_text = StatesTask(*states), VectorTask(both_grads), TotalTask(text_part)

    def make_normed():
        def one(number, carry):
            at = span(number, BLOCK)
            standard, _ = norm_parts(stage.value.ref[at, :].astype(jnp.float32))
            stage.normed.ref[at, :] = scaled_rows(standard, stage.gains, 0)
            return carry

        lax.fori_loop(0, rows // BLOCK, one, 0)

    def text_step():
        from_states.arrive()
        text_rows.ref[...] = jnp.concatenate([from_states.both[0], from_states.both[1]], axis=0)
        total = nt_product(text_rows.ref[:, :columns], text_weights[0].ref[...])
        total = total + nt_product(text_rows.ref[:, columns:], text_weights[1].ref[...])
        text_part.ref[...] = total.astype(jnp.bfloat16)
        from_text.ins = [text_part.ref]
        from_text.begin()

    def first(need, meet, ride, middle):
        me, grad_t = lax.axis_index(FRAME), attention.grad_t
        landing = grad_t.ref.at[:, span(me, rows)]
        arriving = to_frames(lambda g: own.ref.at[g], lambda f: landing, build.bound[sems])
        need(0)
        turned_grads(grad_low.ref[...], output, own, slice(0, rows))
        meet()
        for copy in arriving[::-1]:
            copy.start()
        ride()
        grad_t.ref[:, span(me, rows)] = own.ref[me]
        need(1)
        attention.begin()
        for copy in arriving:
            copy.wait()
        attention.run(middle)
        from_states.cross()

    def then(need):
        from_text.sum_first()
        both_grads.ref[0] = vector_grads[1].ref[...]
        both_grads.ref[1] = vector_grads[0].ref[...]
        from_vectors.ins = [both_grads.ref]
        from_vectors.begin()

    tasks = [from_states] + list(tasks)
    return run_chain(
        build,
        [stage],
        collective_id,
        tasks,
        (LINE_ONLY, SECTION),
        chores,
        [(make_normed, (0, 2), (0, 2)), (text_step, (0, 9), (0, 9))],
        then,
        first,
        2,
        [from_vectors, from_text],
    )


def masked_scores(keys, query_t, begins, start):
    reach, block = keys.shape[0], query_t.shape[1]
    scores = plain_product(keys, query_t)
    key_pos = lax.broadcasted_iota(jnp.int32, (reach, 1), 0)
    query_pos = start + lax.broadcasted_iota(jnp.int32, (1, block), 1)
    allowed = (key_pos <= query_pos) & (key_pos >= begins)
    return jnp.where(allowed, scores * HEAD ** (-0.5), masked_score)


def to_frames(source, landing, sems):
    me = lax.axis_index(FRAME)
    return [
        remote(source(other), landing(me), sems.at[0, k], sems.at[1, k], {FRAME: other})
        for k, other in enumerate(frame_partners())
    ]


def turned_parts(normed, matrices, own, at, lanes):
    for part, matrix in enumerate(matrices):
        turned = plain_product(normed, matrix.ref[...]).astype(jnp.bfloat16).T
        for head in range(4):
            rows = slice(part * HEAD, (part + 1) * HEAD)
            own.ref[at + (head, rows, lanes)] = turned[head * HEAD : (head + 1) * HEAD, :]


class Attention:
    def __init__(self, build, rows, begins, stage):
        frames, width = 4, 3 * HEAD
        self.rows = rows
        self.begins = build.arg(begins, stage)
        self.heads_t = build.out((width, rows * frames), jnp.bfloat16)
        self.out = build.out((frames * HEAD, rows), jnp.bfloat16)
        self.keys = build.temp((rows * frames, HEAD), jnp.bfloat16)
        self.mixed_t = build.temp((frames, HEAD, rows), jnp.bfloat16)
        self.sems = build.extra(pltpu.SemaphoreType.DMA((2, frames - 1)))
        self.build = build

    def run(self, early=()):
        me, partners, rows = lax.axis_index(FRAME), frame_partners(), self.rows
        heads_t, keys, mixed_t, out = self.heads_t, self.keys, self.mixed_t, self.out
        block = min(2 * BLOCK, rows)
        leaving = to_frames(
            lambda g: mixed_t.ref.at[g], lambda f: out.ref.at[span(f, HEAD), :], self.build.bound[self.sems]
        )
        heads_t.flush()
        keys.ref[...] = heads_t.ref[HEAD : 2 * HEAD, :].T
        for target in range(4):
            if target == 3:
                for task in early:
                    task.first_hop()
            for start in range(target * rows, (target + 1) * rows, block):
                reach = start + block
                scores = masked_scores(
                    keys.ref[:reach, :],
                    heads_t.ref[:HEAD, start:reach],
                    self.begins.ref[:, start:reach],
                    start,
                )
                e = jnp.exp(scores - jnp.max(scores, axis=0, keepdims=True))
                total = jnp.sum(e, axis=0, keepdims=True)
                mixed = plain_product(heads_t.ref[2 * HEAD :, :reach], e.astype(jnp.bfloat16))
                at = start - target * rows
                mixed_t.ref[target, :, at : at + block] = (mixed * (1.0 / total)).astype(jnp.bfloat16)

            for copy, other in zip(leaving, partners):

                @pl.when(other == target)
                def _():
                    copy.start()

        out.ref[span(me, HEAD), :] = mixed_t.ref[me]
        for copy in leaving:
            copy.wait()
        out.flush()


class BlockSender:
    def __init__(self, build, rows, height, landing):
        self.rows, self.landing = rows, landing
        self.blocks = rows // BLOCK
        self.own = build.temp((4, height, rows), jnp.bfloat16)
        self.sems = build.extra(pltpu.SemaphoreType.DMA((2, 3, self.blocks)))
        self.build = build

    def copies(self, block):
        lanes, me = span(block, BLOCK), lax.axis_index(FRAME)
        place = self.landing.ref.at[:, span(me * self.blocks + block, BLOCK)]
        sems = self.build.bound[self.sems]
        return [
            remote(
                self.own.ref.at[other, :, lanes], place, sems.at[0, k, block], sems.at[1, k, block], {FRAME: other}
            )
            for k, other in enumerate(frame_partners())
        ]

    def send(self, block):
        me = lax.axis_index(FRAME)
        for copy in self.copies(block)[::-1]:
            copy.start()
        lanes = span(block, BLOCK)
        self.landing.ref[:, span(me * self.blocks + block, BLOCK)] = self.own.ref[me, :, lanes]

    def wait(self):
        def one(block, carry):
            for copy in self.copies(block):
                copy.wait()
            return carry

        lax.fori_loop(0, self.blocks, one, 0)


def first_attention(inputs, vectors, weights, begins, text, text_weights, collective_id, tasks, early):
    micros, rows, model = inputs.shape
    frames, width = 4, 3 * HEAD
    build = Build()
    inputs, vectors = build.arg(inputs, 0), build.arg(vectors, 0)
    matrices = [build.arg(weight, 0) for weight in weights]
    attention = Attention(build, rows, begins, 1)
    text, text_weights = build.arg(text, 1), [build.arg(weight, 1) for weight in text_weights]
    heads_t = attention.heads_t
    normed = build.temp((rows, model), jnp.bfloat16)
    own = build.temp((2, frames, width, rows), jnp.bfloat16)
    columns = text_weights[0].shape[1]
    states = build.temp((micros, text.shape[0] // micros, 2 * columns), jnp.bfloat16)
    sems = build.extra(pltpu.SemaphoreType.DMA((2, frames - 1)))
    over_sems = build.extra(pltpu.SemaphoreType.DMA((2, frames)))
    from_text = TextTask(states)

    def project(micro):
        def one(number, carry):
            at = span(number, BLOCK)
            standard, _ = norm_parts(inputs.ref[micro, at, :].astype(jnp.float32))
            normed.ref[at, :] = scaled_rows(standard, vectors, 0)
            return carry

        lax.fori_loop(0, rows // BLOCK, one, 0)
        turned_parts(normed.ref[...], matrices, own, (micro,), slice(0, rows))

    def body(need, meet, ride, middle):
        me, section = lax.axis_index(FRAME), lax.axis_index(SECTION)
        landing = heads_t.ref.at[:, span(me, rows)]
        arriving = to_frames(lambda g: own.ref.at[0, g], lambda f: landing, build.bound[sems])
        pair = build.bound[over_sems]
        over = [
            remote(own.ref.at[1, g], landing, pair.at[0, k], pair.at[1, k], {SECTION: 1, FRAME: g})
            for k, g in enumerate((me,) + frame_partners())
        ]
        need(0)

        @pl.when(section == 0)
        def _():
            project(1)
            meet()
            for copy in over:
                copy.start()
            project(0)
            for copy in arriving[::-1]:
                copy.start()
            heads_t.ref[:, span(me, rows)] = own.ref[0, me]

        @pl.when(section == 1)
        def _():
            meet()

        need(1)
        for part, weight in enumerate(text_weights):
            made = plain_product(text.ref[...], weight.ref[...]).astype(jnp.bfloat16)
            for micro in range(micros):
                some = slice(micro * states.shape[1], (micro + 1) * states.shape[1])
                states.ref[micro, :, part * columns : (part + 1) * columns] = made[some, :]
        from_text.ins = [states.ref]
        from_text.begin()
        ride()

        @pl.when(section == 0)
        def _():
            for copy in arriving + over:
                copy.wait_send()
            for copy in arriving:
                copy.wait_recv()

        @pl.when(section == 1)
        def _():
            for copy in over:
                copy.wait_recv()

        attention.run(early)

    return run_build(build, body, (FRAME, SECTION, BOTH), collective_id, tasks + [from_text])


class AttentionBack:
    def __init__(self, build, rows, heads_t, begins, stage):
        frames, width = 4, 3 * HEAD
        all_rows = rows * frames
        self.build, self.rows = build, rows
        self.heads_t, self.begins = build.arg(heads_t, stage), build.arg(begins, stage)
        self.out = build.out((frames * width, rows), jnp.bfloat16)
        self.grad_t = build.temp((HEAD, all_rows), jnp.bfloat16)
        self.columns = build.temp((4, all_rows, HEAD), jnp.bfloat16)
        self.key_sum, self.value_sum = (build.temp((all_rows, HEAD), jnp.float32) for _ in range(2))
        self.grads_t = build.temp((frames, width, rows), jnp.bfloat16)
        self.sems = build.extra(pltpu.SemaphoreType.DMA((2, frames - 1)))

    def begin(self):
        key_sum, value_sum = self.key_sum, self.value_sum
        key_sum.ref[...] = jnp.zeros(key_sum.shape, jnp.float32)
        value_sum.ref[...] = jnp.zeros(key_sum.shape, jnp.float32)
        for part in range(3):
            self.columns.ref[part] = self.heads_t.ref[part * HEAD : (part + 1) * HEAD, :].T

    def run(self, middle):
        rows, width, scale = self.rows, 3 * HEAD, HEAD ** (-0.5)
        me, partners = lax.axis_index(FRAME), frame_partners()
        heads_t, begins, grad_t, columns = self.heads_t, self.begins, self.grad_t, self.columns
        key_sum, value_sum, grads_t, out = self.key_sum, self.value_sum, self.grads_t, self.out
        block = min(2 * BLOCK, rows)
        leaving = to_frames(
            lambda g: grads_t.ref.at[g], lambda f: out.ref.at[span(f, width), :], self.build.bound[self.sems]
        )
        columns.ref[3] = grad_t.ref[...].T
        middle()
        for target in reversed(range(4)):
            for start in reversed(range(target * rows, (target + 1) * rows, block)):
                reach = start + block
                scores = masked_scores(
                    columns.ref[1, :reach, :],
                    heads_t.ref[:HEAD, start:reach],
                    begins.ref[:, start:reach],
                    start,
                )
                e = jnp.exp(scores - jnp.max(scores, axis=0, keepdims=True))
                p = e * (1.0 / jnp.sum(e, axis=0, keepdims=True))
                slope = plain_product(columns.ref[2, :reach, :], grad_t.ref[:, start:reach])
                weighted = p * slope
                ds = (weighted - p * jnp.sum(weighted, axis=0, keepdims=True)).astype(jnp.bfloat16)
                value_sum.ref[:reach, :] += plain_product(
                    p.astype(jnp.bfloat16), columns.ref[3, start:reach, :]
                )
                key_sum.ref[:reach, :] += plain_product(ds, columns.ref[0, start:reach, :])
                here = slice(start - target * rows, reach - target * rows)
                query_grad = plain_product(heads_t.ref[HEAD : 2 * HEAD, :reach], ds) * scale
                grads_t.ref[target, :HEAD, here] = query_grad.astype(jnp.bfloat16)
                key_grad = key_sum.ref[start:reach, :] * scale
                grads_t.ref[target, HEAD : 2 * HEAD, here] = key_grad.T.astype(jnp.bfloat16)
                grads_t.ref[target, 2 * HEAD :, here] = value_sum.ref[start:reach, :].T.astype(jnp.bfloat16)

            for copy, other in zip(leaving, partners):

                @pl.when(other == target)
                def _():
                    copy.start()

        out.ref[span(me, width), :] = grads_t.ref[me]
        for copy in leaving:
            copy.wait()
        out.flush()


def turned_grads(grad, weight, own, lanes):
    turned = nt_product(weight.ref[...], grad).astype(jnp.bfloat16)
    for head in range(4):
        own.ref[head, :, lanes] = turned[head * HEAD : (head + 1) * HEAD, :]


def matmul(left_side, right_side):
    return jnp.dot(left_side, right_side, preferred_element_type=jnp.float32)


def matmul_tn(left_side, right_side):
    return lax.dot_general(
        left_side, right_side, (((0,), (0,)), ((), ())), preferred_element_type=jnp.float32
    )


def matmul_nt(left_side, right_side):
    return lax.dot_general(
        left_side, right_side, (((1,), (1,)), ((), ())), preferred_element_type=jnp.float32
    )


def layer_norm(signal, gain_vec, shift_vec):
    average = jnp.mean(signal, axis=-1, keepdims=True)
    centered = signal - average
    variance = jnp.mean(centered * centered, axis=-1, keepdims=True)
    return centered * lax.rsqrt(variance + 1e-05) * gain_vec + shift_vec


def norm_back(signal, gain_vec, upstream):
    average = jnp.mean(signal, axis=-1, keepdims=True)
    centered = signal - average
    inverse = lax.rsqrt(jnp.mean(centered * centered, axis=-1, keepdims=True) + 1e-05)
    standard = centered * inverse
    scaled = upstream * gain_vec
    through = inverse * (
        scaled
        - jnp.mean(scaled, axis=-1, keepdims=True)
        - standard * jnp.mean(scaled * standard, axis=-1, keepdims=True)
    )
    return (through, jnp.sum(upstream * standard, axis=0), jnp.sum(upstream, axis=0))


def head_total(partial_sum):
    return lax.psum(partial_sum.astype(jnp.bfloat16), LINE).astype(jnp.float32)


def swapped(x):
    return lax.ppermute(x, SECTION, [(0, 1), (1, 0)])


def split_heads(matrix):
    return matrix.reshape(matrix.shape[0], matrix.shape[1] // HEAD, HEAD)


def softmax_rows(query, key_rows, allowed):
    logits = jnp.einsum(
        "qhd,khd->hqk",
        split_heads(query),
        split_heads(key_rows),
        preferred_element_type=jnp.float32,
    ) * HEAD ** (-0.5)
    logits = jnp.where(allowed[None], logits, masked_score)
    exponent = jnp.exp(logits - jnp.max(logits, axis=-1, keepdims=True))
    return exponent / jnp.sum(exponent, axis=-1, keepdims=True)


def attend(query, key_rows, value_rows, allowed):
    weights_low = softmax_rows(query, key_rows, allowed).astype(jnp.bfloat16)
    result = jnp.einsum(
        "hqk,khd->qhd", weights_low, split_heads(value_rows), preferred_element_type=jnp.float32
    )
    return result.reshape(query.shape).astype(jnp.bfloat16)


def attend_back(query, key_rows, value_rows, allowed, grad_out):
    probabilities = softmax_rows(query, key_rows, allowed)
    weights_low = probabilities.astype(jnp.bfloat16)
    grad_heads = split_heads(grad_out)
    grad_prob = jnp.einsum(
        "qhd,khd->hqk", grad_heads, split_heads(value_rows), preferred_element_type=jnp.float32
    )
    centre = jnp.sum(probabilities * grad_prob, axis=-1, keepdims=True)
    grad_logit = (probabilities * (grad_prob - centre)).astype(jnp.bfloat16)
    scale = HEAD ** (-0.5)
    grad_query = (
        jnp.einsum(
            "hqk,khd->qhd", grad_logit, split_heads(key_rows), preferred_element_type=jnp.float32
        )
        * scale
    )
    grad_keys = (
        jnp.einsum(
            "hqk,qhd->khd", grad_logit, split_heads(query), preferred_element_type=jnp.float32
        )
        * scale
    )
    grad_values = jnp.einsum(
        "hqk,qhd->khd", weights_low, grad_heads, preferred_element_type=jnp.float32
    )
    return (
        grad_query.reshape(query.shape),
        grad_keys.reshape(key_rows.shape),
        grad_values.reshape(value_rows.shape),
    )


def on_four_frames(inputs, lengths, text, cotangent, vector_args, matrix_args):
    section = lax.axis_index(SECTION)
    at_zero = section == 0
    frame_index = lax.axis_index(FRAME)
    micro_count, rows_dev, model_width = inputs.shape
    rows_all = rows_dev * 4
    (
        query_weight,
        key_weight,
        value_weight,
        output_weight,
        cross_query,
        cross_key,
        cross_value,
        cross_output,
        expand_weight,
        reduce_weight,
    ) = (w[0] for w in matrix_args)
    columns = query_weight.shape[1]

    def by_section(first, second):
        return jnp.where(at_zero, first, second)

    own_vectors = jnp.pad(jnp.concatenate(vector_args, axis=0), ((0, 2), (0, 0)))
    self_weights = (query_weight, key_weight, value_weight)
    text_local = text.reshape(-1, model_width)

    item_ends = jnp.cumsum(lax.dynamic_index_in_dim(lengths, section, 0, keepdims=False))
    passed = jnp.arange(rows_all, dtype=jnp.int32)[None, :] >= item_ends[:, None]
    begins = jnp.max(jnp.where(passed, item_ends[:, None], 0), axis=0, keepdims=True).astype(jnp.int32)
    seg = jnp.sum(passed.astype(jnp.int32), axis=0, keepdims=True)
    seg = lax.dynamic_slice_in_dim(seg, frame_index * rows_dev, rows_dev, 1)

    early = WeightTask(output_weight)
    early.hooked = 1
    others = (cross_query, cross_output, expand_weight, reduce_weight)
    (heads_t, attended_t), carried = first_attention(
        inputs,
        own_vectors,
        self_weights,
        begins,
        text_local,
        (cross_key, cross_value),
        1,
        [early, CrossTask(own_vectors, own_vectors, False)] + [QuarterTask(w) for w in others[:2]],
        [early],
    )
    vectors = (own_vectors, carried[1])
    selected = [by_section(*vectors), by_section(*vectors[::-1])]
    states = carried[4].reshape(2, -1, 2 * columns)
    coming = [WeightTask(w, 0, quarter) for w, quarter in zip(others, carried[2:4] + [None] * 2)]
    late = [WeightTask(w, 1) for w in self_weights]
    weights = [(output_weight, carried[0])]
    outs, carried = forward_chain(
        0,
        attended_t,
        inputs,
        states[0],
        seg,
        vectors,
        weights + coming,
        2,
        coming + late,
        late,
        begins,
    )
    weights += list(zip(others, carried))
    self_pairs = list(zip(self_weights, carried[4:]))
    def keep(entering, normed, heads_t, attended_t, outs):
        second_normed, middle, queries, cross_att, third_normed, latter, before, hidden = outs[:8]
        return (
            entering,
            normed,
            heads_t,
            attended_t,
            middle,
            second_normed,
            latter,
            third_normed,
            queries,
            cross_att,
            before,
            hidden,
        )

    saved = [keep(inputs, None, heads_t, attended_t, outs)]
    normed, entering, heads_t, attended_t = outs[8:]
    outs, _ = forward_chain(
        1, attended_t, entering, states[1], seg, vectors, weights, 3
    )
    saved.append(keep(entering, normed, heads_t, attended_t, outs))
    result_low = outs[8]

    shares = [{}, {}]

    def crossing(*names):
        return [CrossTask(shares[0][name], shares[1][name], True) for name in names]

    def unpack(outs):
        names = ("vectors", "grad_pre", "grad_cross", "queries", "states", "grad_self")
        return dict(zip(names, outs))

    def for_backward(layer):
        return saved[layer][4], *saved[layer][6:9], *saved[layer][10:]

    def products(layer, outs):
        attended_t, second_normed, cross_att = saved[layer][3], saved[layer][5], saved[layer][9]
        return [
            (cross_att, outs["grad_cross"]),
            (attended_t, outs["grad_self"]),
            (second_normed, outs["queries"]),
            (saved[layer][1], None),
        ]

    names = ("cross_output", "output", "cross_query", "heads")
    outs, carried = backward_chain(
        1,
        cotangent,
        for_backward(1),
        states[1],
        seg,
        vectors,
        weights,
        saved[1][2],
        begins,
        8,
        [BothTask(saved[1][0], result_low)],
    )
    later, grad_heads_t = unpack(outs), outs[6]
    layer_outputs, shares[1]["states"], shares[1]["reduce"], shares[1]["expand"] = carried
    outs, carried = between_chain(
        1,
        grad_heads_t,
        saved[1][0],
        selected[1],
        later["grad_self"],
        self_pairs,
        products(1, later),
        (for_backward(0), states[0], seg, selected[0], weights),
        10,
        [],
    )
    last_vectors, later_low = outs[:2]
    sooner = unpack(outs[2:])
    shares[1].update(zip(names, carried))
    shares[0]["reduce"], shares[0]["expand"] = carried[4:]
    outs, carried = last_kernel(
        saved[0][2],
        sooner["grad_self"],
        weights[0],
        begins,
        inputs,
        vectors,
        self_pairs,
        later_low,
        products(0, sooner),
        [shares[1][name] for name in names],
        (sooner["states"], shares[1]["states"]),
        text_local,
        (cross_key, cross_value),
        (later["vectors"] + last_vectors, sooner["vectors"]),
        11,
        crossing("reduce", "expand"),
    )
    both_grads = outs[-1]
    totals = dict(zip(("reduce", "expand") + names + ("text",), carried))
    cross_grads, (vector_total, text_grad) = totals["text"], carried[7:]
    kernel_outs = widen(
        [layer_outputs, both_grads, text_grad, cross_grads],
        [totals[name] for name in ("reduce", "expand", "cross_output", "output", "cross_query", "heads")],
        vector_total,
    )
    layer_outputs, input_grads, text_grad, cross_key_grad, cross_value_grad = kernel_outs[:5]
    reduce_grad, expand_grad, cross_output_grad, output_grad, cross_query_grad = kernel_outs[5:10]
    query_grad, key_grad, value_grad = kernel_outs[10:13]
    rows = kernel_outs[13:]
    ordered = (
        rows[0],
        rows[1],
        query_grad,
        key_grad,
        value_grad,
        output_grad,
        rows[2],
        rows[3],
        cross_query_grad,
        cross_key_grad,
        cross_value_grad,
        cross_output_grad,
        rows[4],
        rows[5],
        expand_grad,
        reduce_grad,
    )
    vector_places = (0, 1, 6, 7, 12, 13)
    ordered = tuple(
        g if place in vector_places else g[None] for place, g in enumerate(ordered)
    )
    return (layer_outputs[None], input_grads[None], text_grad.reshape(text.shape)) + ordered


def widen(lows, wides, vectors):
    *lows, pair = lows
    *wides, triple = wides
    wide = jnp.float32
    half, third = pair.shape[1] // 2, triple.shape[1] // 3
    quarter = vectors.shape[1] // 4
    outs = [jax.ShapeDtypeStruct(low.shape, wide) for low in lows]
    outs += [jax.ShapeDtypeStruct((pair.shape[0], half), wide)] * 2
    outs += [jax.ShapeDtypeStruct(one.shape, wide) for one in wides]
    outs += [jax.ShapeDtypeStruct((triple.shape[0], third), wide)] * 3
    outs += [jax.ShapeDtypeStruct((1, quarter), wide)] * 6
    widened = [*lows, pair]
    n_in, n_out, n_low = len(widened) + len(wides) + 2, len(outs), len(widened)

    def kernel(*refs):
        ins, outs = refs[:n_in], refs[n_in : n_in + n_out]
        narrow = refs[n_in + n_out : n_in + n_out + n_low]
        broad = refs[n_in + n_out + n_low : n_in + n_out + 2 * n_low]
        *held, rows, in_sems, out_sems = refs[n_in + n_out + 2 * n_low :]
        lane = span(lax.axis_index(FRAME), quarter)
        started = []

        def copy(source, landing):
            one = pltpu.make_async_copy(source, landing, out_sems.at[len(started)])
            one.start()
            started.append(one)

        loads = [pltpu.make_async_copy(ins[i], narrow[i], in_sems.at[i]) for i in range(n_low)]
        copied = [
            pltpu.make_async_copy(source, room, in_sems.at[n_low + i])
            for i, (source, room) in enumerate(zip(ins[n_low:], held + [rows]))
        ]
        for load in copied + loads:
            load.start()
        for i in range(len(wides)):
            copied[i].wait()
            copy(held[i], outs[n_low + 1 + i])
        place = n_low + 1 + len(wides)
        copied[-2].wait()
        for part in range(3):
            copy(held[-1].at[:, part * third : (part + 1) * third], outs[place + part])
        copied[-1].wait()
        for row in range(6):
            copy(rows.at[row : row + 1, lane], outs[place + 3 + row])
        for i in range(n_low):
            loads[i].wait()
            broad[i][...] = narrow[i][...].astype(wide)
            if i + 1 < n_low:
                copy(broad[i], outs[i])
            else:
                copy(broad[i].at[:, :half], outs[i])
                copy(broad[i].at[:, half:], outs[i + 1])
        for one in started:
            one.wait()

    anywhere = pl.BlockSpec(memory_space=pl.ANY)
    scratch = [pltpu.VMEM(low.shape, jnp.bfloat16) for low in widened]
    scratch += [pltpu.VMEM(low.shape, wide) for low in widened]
    scratch += [pltpu.VMEM(one.shape, wide) for one in (*wides, triple, vectors)]
    scratch += [pltpu.SemaphoreType.DMA((n_in,)), pltpu.SemaphoreType.DMA((n_out,))]
    return pl.pallas_call(
        kernel,
        out_shape=outs,
        in_specs=[anywhere] * n_in,
        out_specs=[anywhere] * n_out,
        scratch_shapes=scratch,
        compiler_params=pltpu.CompilerParams(vmem_limit_bytes=VMEM_BYTES),
    )(*widened, *wides, triple, vectors)


def self_attention(query, key_rows, value_rows, masks):
    all_keys = lax.all_gather(key_rows, FRAME, axis=0, tiled=True)
    all_values = lax.all_gather(value_rows, FRAME, axis=0, tiled=True)
    return attend(query, all_keys, all_values, masks["own"]), (query, all_keys, all_values)


def self_attention_back(kept, grad_out, masks):
    query, keys, values = kept
    grad_q, grad_k_all, grad_v_all = attend_back(query, keys, values, masks["own"], grad_out)
    grad_k, grad_v = (
        lax.psum_scatter(g.astype(jnp.bfloat16), FRAME, scatter_dimension=0, tiled=True)
        for g in (grad_k_all, grad_v_all)
    )
    return grad_q.astype(jnp.bfloat16), grad_k, grad_v


def forward(entering, vectors, weights, cross_keys, cross_values, masks):
    first_gain, first_shift, second_gain, second_shift, third_gain, third_shift = vectors
    (
        query_weight,
        key_weight,
        value_weight,
        output_weight,
        cross_query,
        cross_output,
        expand_weight,
        reduce_weight,
    ) = weights
    signal = entering.astype(jnp.float32)
    first_normed = layer_norm(signal, first_gain, first_shift).astype(jnp.bfloat16)
    query = matmul(first_normed, query_weight).astype(jnp.bfloat16)
    key_rows = matmul(first_normed, key_weight).astype(jnp.bfloat16)
    value_rows = matmul(first_normed, value_weight).astype(jnp.bfloat16)
    attended, heads_kept = self_attention(query, key_rows, value_rows, masks)
    middle = signal + head_total(matmul(attended, output_weight))
    second_normed = layer_norm(middle, second_gain, second_shift).astype(jnp.bfloat16)
    cross_queries = matmul(second_normed, cross_query).astype(jnp.bfloat16)
    cross_att = attend(cross_queries, cross_keys, cross_values, masks["cross"])
    latter = middle + head_total(matmul(cross_att, cross_output))
    third_normed = layer_norm(latter, third_gain, third_shift).astype(jnp.bfloat16)
    hidden_pre = matmul(third_normed, expand_weight)
    hidden_act = jax.nn.gelu(hidden_pre, approximate=False).astype(jnp.bfloat16)
    result = latter + head_total(matmul(hidden_act, reduce_weight))
    saved = (
        signal,
        first_normed,
        heads_kept,
        attended,
        middle,
        second_normed,
        cross_queries,
        cross_att,
        latter,
        third_normed,
        hidden_pre,
        hidden_act,
    )
    return (result, saved)


def backward(saved, upstream, vectors, weights, cross_keys, cross_values, masks):
    first_gain, first_shift, second_gain, second_shift, third_gain, third_shift = vectors
    (
        query_weight,
        key_weight,
        value_weight,
        output_weight,
        cross_query,
        cross_output,
        expand_weight,
        reduce_weight,
    ) = weights
    (
        signal,
        first_normed,
        heads_kept,
        attended,
        middle,
        second_normed,
        cross_queries,
        cross_att,
        latter,
        third_normed,
        hidden_pre,
        hidden_act,
    ) = saved
    grad_out = upstream.astype(jnp.bfloat16)
    grad_reduce = matmul_tn(hidden_act, grad_out)
    grad_act = matmul_nt(grad_out, reduce_weight)
    slope = (
        0.5 * (1.0 + lax.erf(hidden_pre * inv_sqrt_two))
        + hidden_pre * jnp.exp(-0.5 * hidden_pre * hidden_pre) * inv_sqrt_tau
    )
    grad_pre = (grad_act * slope).astype(jnp.bfloat16)
    grad_expand = matmul_tn(third_normed, grad_pre)
    grad_third = head_total(matmul_nt(grad_pre, expand_weight))
    grad_latter, grad_third_gain, grad_third_shift = norm_back(latter, third_gain, grad_third)
    grad_latter = grad_latter + upstream
    grad_cross = grad_latter.astype(jnp.bfloat16)
    grad_cross_output = matmul_tn(cross_att, grad_cross)
    grad_cross_att = matmul_nt(grad_cross, cross_output).astype(jnp.bfloat16)
    grad_cq, grad_ck, grad_cv = attend_back(
        cross_queries, cross_keys, cross_values, masks["cross"], grad_cross_att
    )
    grad_text_rows = jnp.concatenate([grad_ck, grad_cv], axis=1).astype(jnp.bfloat16)
    grad_text_rows = lax.psum_scatter(
        grad_text_rows.reshape(ITEMS, TEXT, -1), FRAME, scatter_dimension=1, tiled=True
    )
    grad_cquery = grad_cq.astype(jnp.bfloat16)
    grad_cross_query = matmul_tn(second_normed, grad_cquery)
    grad_second = head_total(matmul_nt(grad_cquery, cross_query))
    grad_middle, grad_second_gain, grad_second_shift = norm_back(middle, second_gain, grad_second)
    grad_middle = grad_middle + grad_latter
    grad_self = grad_middle.astype(jnp.bfloat16)
    grad_output = matmul_tn(attended, grad_self)
    grad_att = matmul_nt(grad_self, output_weight).astype(jnp.bfloat16)
    grad_query_low, grad_key_low, grad_value_low = self_attention_back(heads_kept, grad_att, masks)
    grad_query = matmul_tn(first_normed, grad_query_low)
    grad_key = matmul_tn(first_normed, grad_key_low)
    grad_value = matmul_tn(first_normed, grad_value_low)
    grad_first = head_total(
        matmul_nt(grad_query_low, query_weight)
        + matmul_nt(grad_key_low, key_weight)
        + matmul_nt(grad_value_low, value_weight)
    )
    grad_signal, grad_first_gain, grad_first_shift = norm_back(signal, first_gain, grad_first)
    grad_signal = grad_signal + grad_middle
    vector_grads = (
        grad_first_gain,
        grad_first_shift,
        grad_second_gain,
        grad_second_shift,
        grad_third_gain,
        grad_third_shift,
    )
    matrix_grads = (
        grad_query,
        grad_key,
        grad_value,
        grad_output,
        grad_cross_query,
        grad_cross_output,
        grad_expand,
        grad_reduce,
    )
    matrix_grads = tuple(
        lax.psum_scatter(g.astype(jnp.bfloat16), FRAME, scatter_dimension=0, tiled=True)
        for g in matrix_grads
    )
    return grad_signal, vector_grads, matrix_grads, grad_text_rows


def per_device(
    inputs,
    lengths,
    text,
    cotangent,
    first_gain,
    first_shift,
    query_weight,
    key_weight,
    value_weight,
    output_weight,
    second_gain,
    second_shift,
    cross_query,
    cross_key,
    cross_value,
    cross_output,
    third_gain,
    third_shift,
    expand_weight,
    reduce_weight,
):
    head_count, frame_count = lax.axis_size(LINE), lax.axis_size(FRAME)
    local_heads = query_weight.shape[2] // HEAD
    if head_count == 4 and frame_count == 4 and local_heads == 4:
        return on_four_frames(
            inputs,
            lengths,
            text,
            cotangent,
            (first_gain, first_shift, second_gain, second_shift, third_gain, third_shift),
            (
                query_weight,
                key_weight,
                value_weight,
                output_weight,
                cross_query,
                cross_key,
                cross_value,
                cross_output,
                expand_weight,
                reduce_weight,
            ),
        )
    section = lax.axis_index(SECTION)
    at_zero = section == 0
    frame_index = lax.axis_index(FRAME)
    micro_count, rows_dev, model_width = inputs.shape
    rows_all = rows_dev * frame_count
    text_rows_dev = text.shape[2]

    def keep(pair):
        return jnp.where(at_zero, pair[0], pair[1])

    def give(pair):
        return jnp.where(at_zero, pair[1], pair[0])

    vector_args = jnp.concatenate(
        [first_gain, first_shift, second_gain, second_shift, third_gain, third_shift], axis=0
    )
    vectors = lax.all_gather(vector_args, SECTION)
    matrix_args = (
        query_weight,
        key_weight,
        value_weight,
        output_weight,
        cross_query,
        cross_output,
        expand_weight,
        reduce_weight,
    )
    matrices = [lax.all_gather(w[0], SECTION) for w in matrix_args]
    weights = [tuple(w[layer] for w in matrices) for layer in range(2)]

    text_full = lax.all_gather(text, FRAME, axis=2, tiled=True)
    text_flat = text_full.reshape(micro_count * ITEMS * TEXT, model_width)
    text_heads = jnp.concatenate(
        [matmul(text_flat, cross_key[0]), matmul(text_flat, cross_value[0])], axis=1
    ).astype(jnp.bfloat16)
    text_heads = text_heads.reshape(micro_count, ITEMS * TEXT, -1)
    own_text = keep(text_heads)
    other_text = swapped(give(text_heads))
    columns = cross_key.shape[2]
    cross_states = [
        jnp.where(at_zero, own_text, other_text),
        jnp.where(at_zero, other_text, own_text),
    ]
    cross_keys = [c[:, :columns] for c in cross_states]
    cross_values = [c[:, columns:] for c in cross_states]

    item_ends = jnp.cumsum(lax.dynamic_index_in_dim(lengths, section, 0, keepdims=False))
    all_positions = jnp.arange(rows_all, dtype=jnp.int32)
    seg_all = jnp.sum((all_positions[:, None] >= item_ends[None, :]).astype(jnp.int32), axis=1)
    own_start = frame_index * rows_dev
    own_positions = own_start + jnp.arange(rows_dev, dtype=jnp.int32)
    seg_own = lax.dynamic_slice_in_dim(seg_all, own_start, rows_dev)
    text_item = jnp.arange(ITEMS * TEXT, dtype=jnp.int32) // TEXT
    masks = {
        "own": (all_positions[None, :] <= own_positions[:, None])
        & (seg_own[:, None] == seg_all[None, :]),
        "cross": seg_own[:, None] == text_item[None, :],
    }

    signal = lax.dynamic_index_in_dim(inputs, section, 0, keepdims=False)
    results, saves = [], []
    for layer in range(2):
        result, saved = forward(
            signal, vectors[layer], weights[layer], cross_keys[layer], cross_values[layer], masks
        )
        results.append(result)
        saves.append(saved)
        signal = result.astype(jnp.bfloat16)

    upstream = lax.dynamic_index_in_dim(cotangent, section, 0, keepdims=False)
    in_grads, vector_grads, matrix_grads, text_grads = [None] * 2, [None] * 2, [None] * 2, [None] * 2
    for layer in (1, 0):
        grad_signal, vector_grads[layer], matrix_grads[layer], text_grads[layer] = backward(
            saves[layer],
            upstream,
            vectors[layer],
            weights[layer],
            cross_keys[layer],
            cross_values[layer],
            masks,
        )
        in_grads[layer] = grad_signal
        upstream = grad_signal.astype(jnp.bfloat16).astype(jnp.float32)

    def both_micros(pair):
        own = keep(pair)
        other = swapped(give([p.astype(jnp.bfloat16) for p in pair])).astype(own.dtype)
        return jnp.stack([jnp.where(at_zero, own, other), jnp.where(at_zero, other, own)])

    layer_outputs = both_micros(results)
    input_grads = both_micros(in_grads)
    totals = [
        keep(pair).astype(jnp.float32) + swapped(give(pair)).astype(jnp.float32)
        for pair in zip(*matrix_grads)
    ]
    text_rows = both_micros(text_grads)
    text_rows = text_rows.reshape(micro_count * ITEMS * text_rows_dev, -1)
    key_part, value_part = text_rows[:, :columns], text_rows[:, columns:]
    text_local = text.reshape(-1, model_width)
    grad_cross_key, grad_cross_value = (
        lax.psum_scatter(
            matmul_tn(text_local, part).astype(jnp.bfloat16),
            FRAME,
            scatter_dimension=0,
            tiled=True,
        ).astype(jnp.float32)
        for part in (key_part, value_part)
    )
    text_part = matmul_nt(key_part, cross_key[0]) + matmul_nt(value_part, cross_value[0])
    text_grad = lax.psum(text_part.astype(jnp.bfloat16), (SECTION, LINE)).astype(jnp.float32)
    text_grad = text_grad.reshape(text.shape)

    stacked = jnp.stack([jnp.stack(v) for v in vector_grads])
    stacked = lax.psum_scatter(
        stacked.astype(jnp.bfloat16), FRAME, scatter_dimension=2, tiled=True
    )
    vector_total = keep(stacked).astype(jnp.float32) + swapped(give(stacked)).astype(jnp.float32)

    grad_q, grad_k, grad_v, grad_o, grad_cq, grad_co, grad_e, grad_r = totals
    ordered = (
        vector_total[0],
        vector_total[1],
        grad_q,
        grad_k,
        grad_v,
        grad_o,
        vector_total[2],
        vector_total[3],
        grad_cq,
        grad_cross_key,
        grad_cross_value,
        grad_co,
        vector_total[4],
        vector_total[5],
        grad_e,
        grad_r,
    )
    return (layer_outputs[None], input_grads[None], text_grad) + tuple(g[None] for g in ordered)


def solution(mesh):
    return jax.shard_map(
        per_device,
        mesh=mesh,
        in_specs=(
            P(None, FRAME, None),
            P(),
            P(None, None, FRAME, None),
            P(None, FRAME, None),
            P(SECTION, None),
            P(SECTION, None),
            P(SECTION, None, LINE),
            P(SECTION, None, LINE),
            P(SECTION, None, LINE),
            P(SECTION, LINE, None),
            P(SECTION, None),
            P(SECTION, None),
            P(SECTION, None, LINE),
            P(SECTION, None, LINE),
            P(SECTION, None, LINE),
            P(SECTION, LINE, None),
            P(SECTION, None),
            P(SECTION, None),
            P(SECTION, None, LINE),
            P(SECTION, LINE, None),
        ),
        out_specs=(
            P(SECTION, None, FRAME, None),
            P(SECTION, None, FRAME, None),
            P(None, None, FRAME, None),
            P(SECTION, FRAME),
            P(SECTION, FRAME),
            P(SECTION, FRAME, LINE),
            P(SECTION, FRAME, LINE),
            P(SECTION, FRAME, LINE),
            P(SECTION, (LINE, FRAME), None),
            P(SECTION, FRAME),
            P(SECTION, FRAME),
            P(SECTION, FRAME, LINE),
            P(SECTION, FRAME, LINE),
            P(SECTION, FRAME, LINE),
            P(SECTION, (LINE, FRAME), None),
            P(SECTION, FRAME),
            P(SECTION, FRAME),
            P(SECTION, FRAME, LINE),
            P(SECTION, (LINE, FRAME), None),
        ),
        check_vma=False,
    )
```

```python
import jax
import jax.numpy as jnp
from jax import lax
from jax.experimental import pallas as pl
from jax.experimental.pallas import tpu as pltpu
from jax.sharding import PartitionSpec as P

HEAD = 64
TEXT = 64
ITEMS = 4

masked_score = -1e30
inv_sqrt_two = 0.7071067811865476
inv_sqrt_tau = 0.3989422804014327

MESH_IDS = pl.DeviceIdType.MESH
BUSY = pl.CostEstimate(flops=30_000_000_000, bytes_accessed=8_000_000, transcendentals=0)
LAG = 3
BLOCK = 128
VMEM_BYTES = 60 * 1024 * 1024
EPS = 1e-05
SECTION, LINE, FRAME = "section", "head", "frame"
BOTH, LINE_ONLY, BY_SECTION = "both", "line", "one"
NORM, NEXT, END = range(3)


class Task:
    operands = ()
    outs = ()
    out_in_vmem = True
    scratch = ()
    greets = ()
    late = False
    hooked = 0

    def middle(self):
        pass

    def bind(self, ins, outs, scratch):
        self.ins, self.out, self.room = ins, outs, scratch
        self.far_ins = ins


def remote(source, landing, send_sem, recv_sem, target):
    return pltpu.make_async_remote_copy(
        src_ref=source,
        dst_ref=landing,
        send_sem=send_sem,
        recv_sem=recv_sem,
        device_id=target,
        device_id_type=MESH_IDS,
    )


def frame_partners():
    me = lax.axis_index(FRAME)
    return (me + 1 - 2 * lax.rem(me, 2), lax.rem(me + 2, 4), 3 - me)


def span(index, size):
    return pl.ds(pl.multiple_of(index * size, size), size)


class WeightTask(Task):
    out_in_vmem = False
    greets = (SECTION, FRAME)

    def __init__(self, weight, layer=None, quarter=None):
        self.layer = layer
        self.operands = (weight,) if quarter is None else (weight, quarter)
        self.outs = (jax.ShapeDtypeStruct(weight.shape, weight.dtype),)
        self.scratch = (pltpu.SemaphoreType.DMA((10,)),)
        if layer is not None:
            self.scratch += (pltpu.VMEM((2,) + weight.shape, weight.dtype),)
        self.quarter = weight.shape[0] // 4

    @property
    def ref(self):
        other = jnp.where(lax.axis_index(SECTION) == self.layer, 0, 1)
        return self.room[1].at[other]

    def arrived(self, at):
        return self.out[0].at[at] if self.layer is None else self.room[1].at[1, at]

    def over(self):
        sems, at = self.room[0], span(lax.axis_index(FRAME), self.quarter)
        target = {SECTION: 1 - lax.axis_index(SECTION)}
        return remote(self.ins[0].at[at], self.arrived(at), sems.at[0], sems.at[1], target)

    def along(self):
        sems, at = self.room[0], span(lax.axis_index(FRAME), self.quarter)
        target = {FRAME: frame_partners()[1]}
        source = self.ins[1] if len(self.ins) > 1 else self.arrived(at)
        return remote(source, self.arrived(at), sems.at[2], sems.at[3], target)

    def settle(self):
        at = span(lax.axis_index(FRAME), self.quarter)
        return pltpu.make_async_copy(self.ins[1], self.arrived(at), self.room[0].at[0])

    def within(self):
        sems, partners = self.room[0], frame_partners()
        copies = []
        for k, whose in enumerate((lax.axis_index(FRAME), partners[1])):
            at = span(whose, self.quarter)
            copies.append(
                remote(
                    self.arrived(at),
                    self.arrived(at),
                    sems.at[4 + 2 * k],
                    sems.at[5 + 2 * k],
                    {FRAME: partners[0]},
                )
            )
        return copies

    def begin(self):
        if len(self.ins) > 1:
            self.settle().start()
            self.along().start()
        else:
            self.over().start()
        if self.layer is not None:
            pltpu.make_async_copy(self.ins[0], self.room[1].at[0], self.room[0].at[8]).start()

    def first_hop(self):
        self.over().wait_recv()
        self.along().start()

    def second_hop(self):
        if len(self.ins) > 1:
            self.settle().wait()
        self.along().wait_recv()
        for copy in self.within():
            copy.start()

    def arrive(self):
        for copy in self.within():
            copy.wait_recv()
        if self.layer is not None:
            sems = self.room[0]
            pltpu.make_async_copy(self.ins[0], self.room[1].at[0], sems.at[8]).wait()
            pltpu.make_async_copy(self.room[1].at[1], self.out[0], sems.at[9]).start()

    def sent(self):
        over = [] if len(self.ins) > 1 else [self.over()]
        for copy in over + [self.along()] + self.within():
            copy.wait_send()
        if self.layer is not None:
            pltpu.make_async_copy(self.room[1].at[1], self.out[0], self.room[0].at[9]).wait()

    def steps(self):
        if self.layer is not None:
            return [self.sent]
        return [self.first_hop, self.second_hop][self.hooked :] + [self.arrive, self.sent]


class QuarterTask(Task):
    out_in_vmem = False
    greets = (SECTION,)

    def __init__(self, weight):
        self.quarter = weight.shape[0] // 4
        self.operands = (weight,)
        self.outs = (jax.ShapeDtypeStruct((self.quarter, weight.shape[1]), weight.dtype),)
        self.scratch = (pltpu.SemaphoreType.DMA((2,)),)

    def over(self):
        sems, at = self.room[0], span(lax.axis_index(FRAME), self.quarter)
        target = {SECTION: 1 - lax.axis_index(SECTION)}
        return remote(self.ins[0].at[at], self.out[0], sems.at[0], sems.at[1], target)

    def begin(self):
        self.over().start()

    def steps(self):
        return [lambda: self.over().wait()]


class ShareTask(Task):
    greets = (FRAME,)

    def __init__(self, grad):
        rows, width = grad.shape
        self.share = rows // 4
        self.far = isinstance(grad, jax.Array)
        self.operands = (grad,) if self.far else ()
        piece = (self.share, width)
        self.outs = (jax.ShapeDtypeStruct(piece, jnp.bfloat16),)
        self.scratch = (
            pltpu.VMEM((2,) + piece, jnp.bfloat16),
            pltpu.VMEM((2,) + piece, jnp.bfloat16),
            pltpu.SemaphoreType.DMA((3,)),
            pltpu.SemaphoreType.DMA((3,)),
        )
        if self.far:
            self.scratch += (pltpu.VMEM((2,) + piece, jnp.bfloat16), pltpu.SemaphoreType.DMA((2,)))

    def within(self):
        landing, _, send_sems, recv_sems, *here = self.room
        me = lax.axis_index(FRAME)
        other = frame_partners()[0]
        side = lax.div(me, 2)
        copies = []
        for k, to_side in enumerate((1 - side, side)):
            given = 2 * to_side + lax.rem(other, 2)
            kept = 2 * to_side + lax.rem(me, 2)
            copies.append(
                remote(
                    self.ins[0].at[span(given, self.share)],
                    landing.at[k],
                    send_sems.at[k],
                    recv_sems.at[k],
                    {FRAME: other},
                )
            )
            if self.far:
                own, sems = here[:2]
                source = self.ins[0].at[span(kept, self.share)]
                copies.append(pltpu.make_async_copy(source, own.at[k], sems.at[k]))
        return copies

    def over(self):
        crossing, send_sems, recv_sems = self.room[1:4]
        target = {FRAME: frame_partners()[1]}
        return remote(crossing.at[0], crossing.at[1], send_sems.at[2], recv_sems.at[2], target)

    def chip_sum(self, k):
        me = lax.axis_index(FRAME)
        if self.far:
            own = self.room[4][k]
        else:
            side = lax.div(me, 2) if k else 1 - lax.div(me, 2)
            own = self.ins[0][span(2 * side + lax.rem(me, 2), self.share), :]
        return own.astype(jnp.float32) + self.room[0][k].astype(jnp.float32)

    def begin(self):
        for copy in self.within():
            copy.start()

    def middle(self):
        for copy in self.within():
            copy.wait()
        self.room[1][0] = self.chip_sum(0).astype(jnp.bfloat16)
        self.over().start()

    def steps(self):
        def end():
            self.over().wait()
            total = self.chip_sum(1) + self.room[1][1].astype(jnp.float32)
            self.out[0][...] = total.astype(jnp.bfloat16)

        return [end]


class ShareCrossTask(ShareTask):
    greets = (FRAME, SECTION)
    late = True

    def __init__(self, grad, later):
        super().__init__(grad)
        self.operands = (later,)
        self.base = len(self.scratch)
        self.outs = (jax.ShapeDtypeStruct(later.shape, jnp.float32),)
        self.scratch += (pltpu.VMEM((3,) + later.shape, jnp.bfloat16), pltpu.SemaphoreType.DMA((3,)))

    def crossing(self, which):
        parts, sems = self.room[self.base :]
        target = {SECTION: 1 - lax.axis_index(SECTION)}
        later = self.far_ins[0]
        over = remote(parts.at[0] if which else later, parts.at[1], sems.at[0], sems.at[1], target)
        return over, pltpu.make_async_copy(later, parts.at[2], sems.at[2])

    def send(self):
        parts = self.room[self.base]
        section = lax.axis_index(SECTION)
        self.over().wait()
        total = self.chip_sum(1) + self.room[1][1].astype(jnp.float32)
        parts[0] = total.astype(jnp.bfloat16)
        for which in (0, 1):

            @pl.when(section == which)
            def _():
                over, stay = self.crossing(which)
                over.start()
                if which:
                    stay.start()

    def steps(self):
        parts = self.room[self.base]
        section = lax.axis_index(SECTION)

        def end():
            over, stay = self.crossing(1)
            over.wait()
            came = parts[1].astype(jnp.float32)

            @pl.when(section == 0)
            def _():
                self.out[0][...] = parts[0].astype(jnp.float32) + came

            @pl.when(section == 1)
            def _():
                stay.wait()
                self.out[0][...] = parts[2].astype(jnp.float32) + came

        first = (lambda: None) if self.hooked else self.send
        return [first, lambda: None, lambda: None, end]


class StatesTask(ShareTask):
    greets = (FRAME, SECTION)
    out_in_vmem = True

    def __init__(self, grad, later):
        super().__init__(grad)
        self.operands = (grad, later)
        self.base = len(self.scratch)
        self.outs = ()
        shape = (2,) + later.shape
        self.scratch += (pltpu.VMEM(shape, jnp.bfloat16), pltpu.VMEM(later.shape, jnp.bfloat16))
        self.scratch += (pltpu.SemaphoreType.DMA((3,)),)

    @property
    def both(self):
        return self.room[self.base]

    def crossing(self, which):
        both, total, sems = self.room[self.base :]
        later, place = self.ins[1], both.at[which]
        over = remote(total if which else later, place, sems.at[0], sems.at[1], {SECTION: 1 - which})
        return over, pltpu.make_async_copy(later, place, sems.at[2])

    def cross(self):
        self.over().wait()
        both, total, _ = self.room[self.base :]
        total[...] = (self.chip_sum(1) + self.room[1][1].astype(jnp.float32)).astype(jnp.bfloat16)
        section = lax.axis_index(SECTION)
        for which in (0, 1):

            @pl.when(section == which)
            def _():
                over, stay = self.crossing(which)
                over.start()
                if which:
                    stay.start()
                else:
                    both[0] = total[...]

    def arrive(self):
        section = lax.axis_index(SECTION)
        for which in (0, 1):

            @pl.when(section == which)
            def _():
                over, stay = self.crossing(which)
                over.wait()
                if which:
                    stay.wait()

    def steps(self):
        return []


class BothTask(Task):
    out_in_vmem = False
    greets = (SECTION,)

    def __init__(self, first, second):
        self.operands = (first, second)
        self.outs = (jax.ShapeDtypeStruct((2,) + first.shape, first.dtype),)
        self.scratch = (pltpu.SemaphoreType.DMA((3,)),)

    def copies(self, given, kept):
        (sems,) = self.room
        section = lax.axis_index(SECTION)
        place = self.out[0].at[section]
        over = remote(self.ins[given], place, sems.at[0], sems.at[1], {SECTION: 1 - section})
        return over, pltpu.make_async_copy(self.ins[kept], place, sems.at[2])

    def begin(self):
        section = lax.axis_index(SECTION)
        for which in (0, 1):

            @pl.when(section == which)
            def _():
                for copy in self.copies(1 - which, which):
                    copy.start()

    def steps(self):
        def end():
            for copy in self.copies(0, 1):
                copy.wait()

        return [end]


class CrossTask(Task):
    greets = (SECTION,)

    def __init__(self, first, second, added):
        self.operands = (first, second)
        self.added = added
        self.out_in_vmem = added
        shape = first.shape
        if added:
            self.outs = (jax.ShapeDtypeStruct(shape, jnp.float32),)
            self.scratch = (pltpu.VMEM(shape, jnp.bfloat16),) * 2 + (pltpu.SemaphoreType.DMA((3,)),)
        else:
            self.outs = (jax.ShapeDtypeStruct(shape, first.dtype),)
            self.scratch = (pltpu.SemaphoreType.DMA((2,)),)

    def copies(self, given, kept):
        sems = self.room[-1]
        landing = self.room[0] if self.added else self.out[0]
        target = {SECTION: 1 - lax.axis_index(SECTION)}
        copies = [remote(self.ins[given], landing, sems.at[0], sems.at[1], target)]
        if self.added:
            copies.append(pltpu.make_async_copy(self.ins[kept], self.room[1], sems.at[2]))
        return copies

    def begin(self):
        section = lax.axis_index(SECTION)
        for which in (0, 1):

            @pl.when(section == which)
            def _():
                for copy in self.copies(1 - which, which):
                    copy.start()

    def steps(self):
        def end():
            for copy in self.copies(0, 1):
                copy.wait()
            if self.added:
                self.out[0][...] = self.room[0][...].astype(jnp.float32) + self.room[1][...].astype(
                    jnp.float32
                )

        return [lambda: None, lambda: None, end]


class TextTask(Task):
    out_in_vmem = False
    greets = (SECTION, FRAME)
    late = True

    def __init__(self, states):
        micros, rows, width = states.shape
        self.outs = (jax.ShapeDtypeStruct((2, 4, rows, width), states.dtype),)
        self.scratch = (pltpu.SemaphoreType.DMA((3,)),) + (pltpu.SemaphoreType.DMA((2, 3)),) * 2

    def place(self, layer):
        return self.out[0].at[layer, lax.axis_index(FRAME)]

    def over(self):
        sems, section = self.room[0], lax.axis_index(SECTION)
        source = self.ins[0].at[1 - section]
        return remote(source, self.place(section), sems.at[0], sems.at[1], {SECTION: 1 - section})

    def stay(self):
        section = lax.axis_index(SECTION)
        return pltpu.make_async_copy(self.ins[0].at[section], self.place(section), self.room[0].at[2])

    def spread(self, far):
        section = lax.axis_index(SECTION)
        layer = 1 - section if far else section
        source = self.place(layer) if far else self.ins[0].at[section]
        pair = self.room[1 + far]
        return [
            remote(source, self.place(layer), pair.at[0, k], pair.at[1, k], {FRAME: other})
            for k, other in enumerate(frame_partners())
        ]

    def begin(self):
        for copy in [self.over(), self.stay()] + self.spread(0):
            copy.start()

    def steps(self):
        def first():
            self.over().wait_recv()
            for copy in self.spread(1):
                copy.start()

        def second():
            self.over().wait_send()
            self.stay().wait()
            for copy in self.spread(0) + self.spread(1):
                copy.wait()

        return [first, second]


class TotalTask(Task):
    greets = (SECTION, LINE)

    late = True

    def __init__(self, part):
        rows, width = part.shape
        self.share = rows // 4
        self.outs = (jax.ShapeDtypeStruct((rows, width), jnp.bfloat16),)
        piece = (self.share, width)
        self.scratch = (
            pltpu.VMEM((4,) + piece, jnp.bfloat16),
            pltpu.VMEM((2,) + piece, jnp.bfloat16),
            pltpu.SemaphoreType.DMA((4,)),
            pltpu.SemaphoreType.DMA((4,)),
            pltpu.SemaphoreType.DMA((2,)),
            pltpu.SemaphoreType.DMA((4,)),
            pltpu.SemaphoreType.DMA((4,)),
        )

    def partners(self):
        me = lax.axis_index(LINE)
        return [lax.rem(me + by, 4) for by in (1, 2, 3)]

    def spread(self):
        landing, _, send_sems, recv_sems = self.room[:4]
        me = lax.axis_index(LINE)
        away = [
            remote(
                self.ins[0].at[span(partner, self.share)],
                landing.at[by],
                send_sems.at[by],
                recv_sems.at[by],
                {LINE: partner},
            )
            for by, partner in enumerate(self.partners(), 1)
        ]
        stay = pltpu.make_async_copy(self.ins[0].at[span(me, self.share)], landing.at[0], send_sems.at[0])
        return away + [stay]

    def over(self):
        sums, sems = self.room[1], self.room[4]
        target = {SECTION: 1 - lax.axis_index(SECTION)}
        return remote(sums.at[0], sums.at[1], sems.at[0], sems.at[1], target)

    def gather(self):
        send_sems, recv_sems = self.room[5:]
        mine = self.out[0].at[span(lax.axis_index(LINE), self.share)]
        return [
            remote(mine, mine, send_sems.at[by], recv_sems.at[by], {LINE: partner})
            for by, partner in enumerate(self.partners(), 1)
        ]

    def begin(self):
        for copy in self.spread():
            copy.start()

    def sum_first(self):
        landing, sums = self.room[:2]
        for copy in self.spread():
            copy.wait()
        total = landing[0].astype(jnp.float32)
        for by in (1, 2, 3):
            total = total + landing[by].astype(jnp.float32)
        sums[0] = total.astype(jnp.bfloat16)
        self.over().start()

    def steps(self):
        sums = self.room[1]

        def second():
            self.over().wait()
            total = sums[0].astype(jnp.float32) + sums[1].astype(jnp.float32)
            self.out[0][span(lax.axis_index(LINE), self.share), :] = total.astype(jnp.bfloat16)
            for copy in self.gather():
                copy.start()

        def third():
            for copy in self.gather():
                copy.wait()

        return [second, third]


class VectorTask(Task):
    greets = (SECTION, FRAME)
    late = True

    def __init__(self, grads):
        shape = grads.shape[1:]
        self.outs = (jax.ShapeDtypeStruct(shape, jnp.float32),)
        self.scratch = (
            pltpu.VMEM((4,) + grads.shape, jnp.float32),
            pltpu.VMEM((3,) + shape, jnp.float32),
            pltpu.SemaphoreType.DMA((4,)),
            pltpu.SemaphoreType.DMA((4,)),
            pltpu.SemaphoreType.DMA((2,)),
        )

    def spread(self):
        landing, _, send_sems, recv_sems, _ = self.room
        away = [
            remote(self.ins[0], landing.at[k], send_sems.at[k], recv_sems.at[k], {FRAME: partner})
            for k, partner in enumerate(frame_partners(), 1)
        ]
        return away + [pltpu.make_async_copy(self.ins[0], landing.at[0], send_sems.at[0])]

    def over(self):
        sums, sems = self.room[1], self.room[4]
        target = {SECTION: 1 - lax.axis_index(SECTION)}
        return remote(sums.at[0], sums.at[1], sems.at[0], sems.at[1], target)

    def begin(self):
        for copy in self.spread():
            copy.start()

    def steps(self):
        landing, sums = self.room[:2]
        section = lax.axis_index(SECTION)

        def first():
            for copy in self.spread():
                copy.wait()
            total = [
                (landing[0, layer] + landing[1, layer]) + (landing[2, layer] + landing[3, layer])
                for layer in (0, 1)
            ]
            for which in (0, 1):

                @pl.when(section == which)
                def _():
                    sums[0] = total[1 - which]
                    sums[2] = total[which]

            self.over().start()

        def second():
            self.over().wait()
            self.out[0][...] = sums[2] + sums[1]

        return [first, second]


def greet(kinds):
    barrier = pltpu.get_barrier_semaphore()
    section, head, frame = (lax.axis_index(a) for a in (SECTION, LINE, FRAME))
    targets = []
    if FRAME in kinds:
        targets += [{FRAME: other} for other in frame_partners()]
    if SECTION in kinds:
        targets.append({SECTION: 1 - section})
    if BOTH in kinds:
        targets += [{SECTION: 1 - section, FRAME: other} for other in frame_partners()]
    if LINE in kinds:
        targets += [{LINE: lax.rem(head + by, 4)} for by in (1, 2, 3)]
    for target in targets:
        pl.semaphore_signal(barrier, 1, device_id=target, device_id_type=MESH_IDS)
    if LINE_ONLY not in kinds or LINE in kinds:
        return lambda: pl.semaphore_wait(barrier, len(targets))

    for way in (-1, 1):
        other = head + way

        @pl.when((other >= 0) & (other < 4))
        def _():
            pl.semaphore_signal(barrier, 1, device_id={LINE: other}, device_id_type=MESH_IDS)

    is_end = (head == 0) | (head == 3)

    def wait():
        @pl.when(is_end)
        def _():
            pl.semaphore_wait(barrier, len(targets) + 1)

        @pl.when(jnp.logical_not(is_end))
        def _():
            pl.semaphore_wait(barrier, len(targets) + 2)

    return wait


def call(body, operands, outs, scratch, kinds, collective_id, tasks=(), in_vmem=True, end=None):
    whole, anywhere = pl.BlockSpec(memory_space=pltpu.VMEM), pl.BlockSpec(memory_space=pl.ANY)
    place = whole if in_vmem else anywhere
    in_specs, out_specs = [place] * len(operands), [place] * len(outs)
    operands, all_outs, scratch = list(operands), list(outs), list(scratch)
    counts = [(len(operands), len(outs), len(scratch))]
    kinds = set(kinds)
    for task in tasks:
        kinds |= set(task.greets)
        in_specs += [anywhere] * len(task.operands)
        out_specs += [whole if task.out_in_vmem else anywhere] * len(task.outs)
        operands += task.operands
        all_outs += task.outs
        scratch += task.scratch
        counts.append((len(task.operands), len(task.outs), len(task.scratch)))
    n_in, n_out = len(operands), len(all_outs)

    def kernel(*refs):
        groups = [list(refs[:n_in]), list(refs[n_in : n_in + n_out]), list(refs[n_in + n_out :])]
        bound = []
        for sizes in counts:
            bound.append([])
            for group, size in zip(groups, sizes):
                bound[-1].append(group[:size])
                del group[:size]
        for task, parts in zip(tasks, bound[1:]):
            task.bind(*parts)

        meet = greet(kinds)

        def ride():
            for task in tasks:
                if not task.late:
                    task.begin()

        def middle():
            for task in tasks:
                if not task.late:
                    task.middle()

        if body is None:
            meet()
            ride()
            middle()
        else:
            body(*bound[0], meet, ride, middle)
        queues = [task.steps() for task in tasks]
        while any(queues):
            for queue in queues:
                if queue:
                    queue.pop(0)()
        if end is not None:
            end()

    results = pl.pallas_call(
        kernel,
        out_shape=all_outs,
        in_specs=in_specs,
        out_specs=out_specs,
        scratch_shapes=scratch,
        compiler_params=pltpu.CompilerParams(
            collective_id=collective_id, has_side_effects=True, vmem_limit_bytes=VMEM_BYTES
        ),
    )(*operands)
    results = list(results)
    main, results = results[: len(outs)], results[len(outs) :]
    return main, results


def chunking(rows):
    return max(1, min(16, rows // 16))


def nt_product(left, right):
    return lax.dot_general(left, right, (((1,), (1,)), ((), ())), preferred_element_type=jnp.float32)


def plain_product(left, right):
    return jnp.dot(left, right, preferred_element_type=jnp.float32)


def norm_parts(v):
    average = jnp.mean(v, axis=-1, keepdims=True)
    centered = v - average
    inverse = lax.rsqrt(jnp.mean(centered * centered, axis=-1, keepdims=True) + EPS)
    return centered * inverse, inverse


class Held:
    def __init__(self, shape, dtype, sources=(), choose=None, stage=0, kept=False):
        self.shape, self.dtype = tuple(shape), dtype
        self.sources, self.choose, self.stage, self.kept = sources, choose, stage, kept
        self.ref = self.far = self.sem = None

    def copy_in(self, index=0):
        source = self.far[index]
        if self.choose == BY_SECTION:
            source = source.at[lax.axis_index(SECTION)]
        return pltpu.make_async_copy(source, self.ref, self.sem)

    def start_in(self):
        if not isinstance(self.choose, int):
            self.copy_in().start()
            return
        section = lax.axis_index(SECTION)

        @pl.when(section == self.choose)
        def _():
            self.copy_in(0).start()

        @pl.when(section != self.choose)
        def _():
            self.copy_in(1).start()

    def write(self, at, value):
        self.ref[at, :] = value
        if self.kept:
            pltpu.make_async_copy(self.ref.at[at], self.far[0].at[at], self.sem).start()

    def flush(self):
        pltpu.make_async_copy(self.ref, self.far[0], self.sem).start()

    def drain(self):
        pltpu.make_async_copy(self.ref, self.far[0], self.sem).wait()


class Build:
    def __init__(self):
        self.helds, self.extras, self.starts, self.finals = [], [], [], []

    def add(self, held):
        self.helds.append(held)
        return held

    def arg(self, array, stage, choose=None):
        shape = array.shape[1:] if choose == BY_SECTION else array.shape
        return self.add(Held(shape, array.dtype, (array,), choose, stage))

    def pick(self, pair, layer, stage):
        return self.add(Held(pair[0].shape, pair[0].dtype, tuple(pair), layer, stage))

    def out(self, shape, dtype):
        return self.add(Held(shape, dtype, kept=True))

    def temp(self, shape, dtype):
        return self.add(Held(shape, dtype))

    def extra(self, scratch):
        self.extras.append(scratch)
        return len(self.extras) - 1


class Stage:
    def __init__(self, rows, width):
        self.rows, self.width = rows, width
        self.begin = self.prepare = self.finish = self.after = None
        self.ends = []


class Chore:
    def __init__(self, build, stage, piece, each, left, right, flipped=False, later=None, wait=5):
        self.start, self.each, self.wait = (stage, piece), each, wait
        self.left, self.right, self.flipped = left, right, flipped
        columns = left.shape[0] if flipped else left.shape[1]
        self.units = columns // BLOCK
        self.product = build.temp((columns, right.shape[1]), jnp.bfloat16)
        self.task = ShareTask(self.product) if later is None else ShareCrossTask(self.product, later)
        self.task.late = True

    def make_all(self):
        def one(number, carry):
            self.unit(number)
            return carry

        lax.fori_loop(0, self.units, one, 0)
        self.task.ins = [self.product.ref]
        self.task.begin()

    def unit(self, number):
        at = span(number, BLOCK)
        right = self.right.ref[...].astype(jnp.bfloat16)
        if self.flipped:
            product = plain_product(self.left.ref[at, :], right)
        else:
            product = lax.dot_general(
                self.left.ref[:, at], right, (((0,), (0,)), ((), ())), preferred_element_type=jnp.float32
            )
        self.product.ref[at, :] = product.astype(jnp.bfloat16)

    def run(self, stage, pieces, piece):
        shift = (stage - self.start[0]) * pieces - self.start[1]
        steps = -(-self.units // self.each)

        def at_step(first, last, what):
            if shift >= last or shift + pieces <= first:
                return
            now = piece + shift

            @pl.when((now >= first) & (now < last))
            def _():
                what(now)

        def make(now):
            for more in range(self.each):
                self.unit(now * self.each + more)

        def begin(now):
            self.task.ins = [self.product.ref]
            self.task.begin()

        at_step(0, steps, make)
        at_step(steps, steps + 1, begin)
        at_step(steps + self.wait, steps + self.wait + 1, lambda now: self.task.middle())


def line_chain(stages, need, part, set_out, middle, chores, hooks):
    place = lax.axis_index(LINE)
    rows = stages[0].rows
    pieces = chunking(rows)
    step = rows // pieces
    per_block = max(1, min(BLOCK, rows) // step)
    lag = max(0, min(LAG, pieces - per_block))
    is_end = (place == 0) | (place == 3)
    inner = {LINE: jnp.where(place == 0, 1, 2)}
    outer = {LINE: jnp.where(place == 1, 0, 3)}
    peer = {LINE: 3 - place}

    def inwards(stage, piece):
        send, held, _, send_sems, recv_sems = stage.room[:5]
        at = span(piece, step)
        return remote(send.at[at], held.at[at], send_sems.at[piece], recv_sems.at[piece], inner)

    def crossing(stage, piece):
        send, _, across = stage.room[:3]
        send_sems, recv_sems = stage.room[5:7]
        at = span(piece, step)
        return remote(send.at[at], across.at[at], send_sems.at[piece], recv_sems.at[piece], peer)

    def outwards(stage, piece):
        held = stage.room[1]
        send_sems, recv_sems = stage.room[7:]
        at = span(piece, step)
        return remote(held.at[at], held.at[at], send_sems.at[piece], recv_sems.at[piece], outer)

    def hook(stage, piece, at_end):
        for run, *spots in hooks:
            index, when = spots[0 if at_end else 1]
            if stages[index] is stage:

                @pl.when(piece == when)
                def _():
                    run()

    def finish(stage, piece):
        stage.finish(span(piece, step), piece)
        if stage.after is not None:

            @pl.when(lax.rem(piece, per_block) == per_block - 1)
            def _():
                stage.after(lax.div(piece, per_block))

    def open_stage(index):
        need(index)
        if stages[index].begin is not None:
            stages[index].begin()

    def loop(first, last, step_of):
        def one(piece, carry):
            step_of(piece)
            return carry

        lax.fori_loop(first, last, one, 0)

    def chore(stage, piece):
        for one in chores:
            one.run(stages.index(stage), pieces, piece)

    @pl.when(is_end)
    def _():
        def beside(stage, piece):
            chore(stage, piece)
            hook(stage, piece, True)

        def take(stage, piece):
            outwards(stage, piece).wait_recv()
            finish(stage, piece)

        for index, stage in enumerate(stages):
            open_stage(index)

            def block_step(block):
                low, high = block * per_block, (block + 1) * per_block
                if index:
                    loop(low, high, lambda piece: take(stages[index - 1], piece))
                stage.room[0][span(block, per_block * step), :] = stage.prepare(block).astype(jnp.bfloat16)
                if index == 0:
                    pl.when(block == 0)(set_out)
                loop(low, high, lambda piece: inwards(stage, piece).start())
                loop(low, high, lambda piece: beside(stage, piece))
                if index == 0:

                    @pl.when(block == 1)
                    def _():
                        middle()

            loop(0, pieces // per_block, block_step)
        loop(0, pieces, lambda piece: take(stages[-1], piece))
        for stage in stages:
            loop(0, pieces, lambda piece: inwards(stage, piece).wait_send())

    @pl.when(jnp.logical_not(is_end))
    def _():
        def add(stage, piece):
            @pl.when(lax.rem(piece, per_block) == 0)
            def _():
                part[...] = stage.prepare(lax.div(piece, per_block))

            if stage is stages[0]:
                pl.when(piece == 0)(set_out)
            at = span(piece, step)
            send, held = stage.room[:2]
            inwards(stage, piece).wait_recv()
            own = part[span(lax.rem(piece, per_block), step), :]
            send[at, :] = (own + held[at, :].astype(jnp.float32)).astype(jnp.bfloat16)
            crossing(stage, piece).start()
            chore(stage, piece)
            hook(stage, piece, False)
            if stage is stages[0]:

                @pl.when(piece == 2 * per_block - 1)
                def _():
                    middle()

        def settle(stage, piece):
            at = span(piece, step)
            send, held, across = stage.room[:3]
            crossing(stage, piece).wait_recv()
            total = send[at, :].astype(jnp.float32) + across[at, :].astype(jnp.float32)
            held[at, :] = total.astype(jnp.bfloat16)
            outwards(stage, piece).start()
            finish(stage, piece)

        for index, stage in enumerate(stages):
            open_stage(index)

            def both(piece):
                add(stage, piece)

                @pl.when(piece >= lag)
                def _():
                    settle(stage, piece - lag)

                if index and lag:

                    @pl.when(piece < lag)
                    def _():
                        settle(stages[index - 1], pieces - lag + piece)

            loop(0, pieces, both)
        loop(pieces - lag, pieces, lambda piece: settle(stages[-1], piece))

        def drain(stage, piece):
            crossing(stage, piece).wait_send()
            outwards(stage, piece).wait_send()

        for stage in stages:
            loop(0, pieces, lambda piece: drain(stage, piece))

    for stage in stages:
        for end in stage.ends:
            end()


def run_build(build, body, kinds, collective_id, tasks):
    operands, outs, scratch = [], [], []
    for held in build.helds:
        operands += held.sources
        if held.kept:
            outs.append(jax.ShapeDtypeStruct(held.shape, held.dtype))
        scratch.append(pltpu.VMEM(held.shape, held.dtype))
    n_held = len(scratch)
    scratch += build.extras
    scratch.append(pltpu.SemaphoreType.DMA((n_held,)))
    reads = sorted((held for held in build.helds if held.sources), key=lambda held: held.stage)

    def need(stage):
        for held in reads:
            if held.stage == stage:
                held.copy_in().wait()

    def run(ins, outs, scratch, meet, ride, middle):
        ins, outs = list(ins), list(outs)
        sems = scratch[-1]
        for index, held in enumerate(build.helds):
            held.ref, held.sem = scratch[index], sems.at[index]
            held.far = [ins.pop(0) for _ in held.sources]
            if held.kept:
                held.far = [outs.pop(0)]
        build.bound = scratch[n_held:-1]
        for held in reads:
            held.start_in()
        for start in build.starts:
            start()
        body(need, meet, ride, middle)

    def end():
        for final in build.finals:
            final()
        for held in build.helds:
            if held.kept:
                held.drain()

    return call(run, operands, outs, scratch, kinds, collective_id, tasks, in_vmem=False, end=end)


def run_chain(
    build, stages, collective_id, tasks, kinds=(LINE_ONLY,), chores=(), hooks=(), then=None, first=None, ahead=0, last=()
):
    slots = []
    for stage in stages:
        pieces = chunking(stage.rows)
        room = [pltpu.VMEM((stage.rows, stage.width), jnp.bfloat16)] * 3
        room += [pltpu.SemaphoreType.DMA((pieces,))] * 6
        slots.append([build.extra(scratch) for scratch in room])
    part = build.extra(pltpu.VMEM((min(BLOCK, stages[0].rows), stages[0].width), jnp.float32))

    def body(need, meet, ride, middle):
        for stage, places in zip(stages, slots):
            stage.room = [build.bound[place] for place in places]
        def set_out():
            meet()
            ride()

        def nothing():
            pass

        go_on = middle
        if first is not None:
            first(need, meet, ride, middle)
            set_out = go_on = nothing
        line_chain(
            stages, lambda index: need(index + ahead), build.bound[part], set_out, go_on, chores, hooks
        )
        if then is not None:
            then(need)

    tasks = list(tasks) + [one.task for one in chores] + list(last)
    return run_build(build, body, kinds, collective_id, tasks)


def scaled_rows(standard, gains, row):
    return (standard * gains.ref[row : row + 1] + gains.ref[row + 1 : row + 2]).astype(jnp.bfloat16)


def residual_norm(build, stage, base, gains, row, mode):
    shape = (stage.rows, stage.width)
    result = build.temp(shape, jnp.float32) if mode == NORM else None
    normed = build.out(shape, jnp.bfloat16) if mode != END else None
    low = build.out(shape, jnp.bfloat16)

    def finish(at, piece):
        value = base.ref[at, :].astype(jnp.float32) + stage.room[1][at, :].astype(jnp.float32)
        rounded = value.astype(jnp.bfloat16)
        low.write(at, rounded)
        if mode == NORM:
            result.write(at, value)
        if mode == NEXT:
            value = rounded.astype(jnp.float32)
        if mode != END:
            standard, _ = norm_parts(value)
            normed.write(at, scaled_rows(standard, gains, row))

    stage.finish = finish
    return result, normed


def gain_rows(build, vectors, layer, index):
    if isinstance(vectors, tuple):
        return build.pick(vectors, layer, index)
    return build.arg(vectors, index)


def vector_rows(build, width):
    grads = build.out((8, width), jnp.float32)

    def clear():
        grads.ref[...] = jnp.zeros(grads.shape, jnp.float32)

    build.starts.append(clear)
    build.finals.append(grads.flush)
    return grads


def self_out_stage(build, index, layer, attended_t, weight, base):
    rows, width = base.shape
    stage = Stage(rows, width)
    flipped, matrix = build.arg(attended_t, index), build.pick(weight, layer, index)
    left = build.temp(attended_t.shape[::-1], jnp.bfloat16)

    def begin():
        left.ref[...] = flipped.ref[...].T

    def prepare(number):
        return plain_product(left.ref[span(number, min(BLOCK, rows)), :], matrix.ref[...])

    stage.begin, stage.prepare = begin, prepare
    return stage


def text_mask(states, seg):
    item = lax.rem(lax.div(lax.broadcasted_iota(jnp.int32, (states, 1), 0), TEXT // 4), ITEMS)
    return item == seg


def cross_stage(build, index, layer, normed, states, seg, into, out_of):
    rows, width = normed.shape
    stage = Stage(rows, width)
    states, seg = build.arg(states, index), build.arg(seg, index)
    columns, block = states.shape[1] // 2, min(BLOCK, rows)
    if not isinstance(into, WeightTask):
        into, out_of = build.pick(into, layer, index), build.pick(out_of, layer, index)
    queries = build.out((rows, columns), jnp.bfloat16)
    left = build.out((rows, columns), jnp.bfloat16)
    values_t = build.temp((columns, states.shape[0]), jnp.bfloat16)

    def begin():
        values_t.ref[...] = states.ref[:, columns:].T

    def prepare(number):
        at = span(number, block)
        query = plain_product(normed.ref[at, :], into.ref[...]).astype(jnp.bfloat16)
        queries.write(at, query)
        query_t = query.T
        allowed = text_mask(states.shape[0], seg.ref[:, at])
        mixed = []
        for head in range(columns // HEAD):
            cols = slice(head * HEAD, (head + 1) * HEAD)
            scores = plain_product(states.ref[:, cols], query_t[cols, :]) * HEAD ** (-0.5)
            scores = jnp.where(allowed, scores, masked_score)
            e = jnp.exp(scores - jnp.max(scores, axis=0, keepdims=True))
            total = jnp.sum(e, axis=0, keepdims=True)
            value = plain_product(values_t.ref[cols, :], e.astype(jnp.bfloat16))
            mixed.append((value * (1.0 / total)).astype(jnp.bfloat16))
        mixed = jnp.concatenate(mixed, axis=0).T
        left.write(at, mixed)
        return plain_product(mixed, out_of.ref[...])

    stage.begin, stage.prepare = begin, prepare
    return stage


def feed_stage(build, index, layer, normed, into, out_of):
    rows, width = normed.shape
    stage = Stage(rows, width)
    block = min(BLOCK, rows)
    if isinstance(into, WeightTask):
        hidden = into.operands[0].shape[1]
    else:
        hidden = into[0].shape[1]
        into, out_of = build.pick(into, layer, index), build.pick(out_of, layer, index)
    before = build.out((rows, hidden), jnp.bfloat16)
    left = build.out((rows, hidden), jnp.bfloat16)

    def prepare(number):
        at = span(number, block)
        u = plain_product(normed.ref[at, :], into.ref[...])
        before.write(at, u.astype(jnp.bfloat16))
        active = (0.5 * u * (1.0 + lax.erf(u * inv_sqrt_two))).astype(jnp.bfloat16)
        left.write(at, active)
        return plain_product(active, out_of.ref[...])

    stage.prepare = prepare
    return stage


def norm_backward(build, index, stage, value, gains, row, grads, upstream, feeds, spare=None):
    shape = (stage.rows, stage.width)
    pieces = chunking(stage.rows)
    value = build.arg(value, index, BY_SECTION if value.ndim == 3 else None)
    result = build.temp(shape, jnp.float32) if feeds else None
    low = build.out(shape, jnp.bfloat16)
    parts = build.extra(pltpu.VMEM((2, pieces, 1, stage.width), jnp.float32))
    if spare is not None:
        spare = build.arg(spare, index)
        both = build.out((2,) + shape, jnp.bfloat16)
        sems = build.extra(pltpu.SemaphoreType.DMA((2, pieces)))

    def over(at, piece, source):
        target = {SECTION: 1 - lax.axis_index(SECTION)}
        pair = build.bound[sems]
        landing = both.ref.at[lax.axis_index(SECTION), at]
        return remote(source.ref.at[at], landing, pair.at[0, piece], pair.at[1, piece], target)

    def finish(at, piece):
        grad = stage.room[1][at, :].astype(jnp.float32)
        standard, inverse = norm_parts(value.ref[at, :].astype(jnp.float32))
        scaled = grad * gains.ref[row : row + 1]
        through = inverse * (
            scaled
            - jnp.mean(scaled, axis=-1, keepdims=True)
            - standard * jnp.mean(scaled * standard, axis=-1, keepdims=True)
        )
        total = through + upstream.ref[at, :].astype(jnp.float32)
        if feeds:
            result.write(at, total)
        low.write(at, total.astype(jnp.bfloat16))
        build.bound[parts][0, piece] = jnp.sum(grad * standard, axis=0, keepdims=True)
        build.bound[parts][1, piece] = jnp.sum(grad, axis=0, keepdims=True)
        if spare is not None:
            section = lax.axis_index(SECTION)

            @pl.when(section == 0)
            def _():
                both.ref[0, at, :] = low.ref[at, :]
                over(at, piece, spare).start()

            @pl.when(section == 1)
            def _():
                both.ref[1, at, :] = spare.ref[at, :]
                over(at, piece, low).start()

    def end():
        grads.ref[row : row + 1] = jnp.sum(build.bound[parts][0], axis=0)
        grads.ref[row + 1 : row + 2] = jnp.sum(build.bound[parts][1], axis=0)

    def settle():
        def one(piece, carry):
            over(span(piece, stage.rows // pieces), piece, low).wait()
            return carry

        lax.fori_loop(0, pieces, one, 0)
        both.flush()

    if spare is not None:
        build.finals.append(settle)
    stage.finish, stage.value = finish, value
    stage.ends.append(end)
    return result, low


def feed_back_stage(build, index, layer, grad_out, before, out_of, into):
    rows, width = grad_out.shape
    stage = Stage(rows, width)
    hidden, block = out_of[0].shape[0], min(BLOCK, rows)
    before = build.arg(before, index)
    out_of, into = build.pick(out_of, layer, index), build.pick(into, layer, index)
    left = build.out((rows, hidden), jnp.bfloat16)

    def prepare(number):
        at = span(number, block)
        grad = nt_product(grad_out.ref[at, :].astype(jnp.bfloat16), out_of.ref[...])
        u = before.ref[at, :].astype(jnp.float32)
        slope = 0.5 * (1.0 + lax.erf(u * inv_sqrt_two)) + u * jnp.exp(-0.5 * u * u) * inv_sqrt_tau
        grad = (grad * slope).astype(jnp.bfloat16)
        left.write(at, grad)
        return nt_product(grad, into.ref[...])

    stage.prepare, stage.left = prepare, left
    return stage


def cross_back_stage(build, index, layer, grad_low, queries, states, seg, out_of, into):
    rows, width = grad_low.shape
    stage = Stage(rows, width)
    columns, block = out_of[0].shape[0], min(BLOCK, rows)
    queries, states, seg = (build.arg(array, index) for array in (queries, states, seg))
    out_of, into = build.pick(out_of, layer, index), build.pick(into, layer, index)
    left = build.out((rows, columns), jnp.bfloat16)
    state_grads = build.out(states.shape, jnp.bfloat16)
    keys_t = build.temp((columns, states.shape[0]), jnp.bfloat16)
    sums = build.temp(states.shape, jnp.float32)
    scale = HEAD ** (-0.5)

    def begin():
        keys_t.ref[...] = states.ref[:, :columns].T
        sums.ref[...] = jnp.zeros(sums.shape, jnp.float32)

    def prepare(number):
        at = span(number, block)
        grad = nt_product(grad_low.ref[at, :], out_of.ref[...]).astype(jnp.bfloat16)
        query = queries.ref[at, :]
        grad_t, query_t = grad.T, query.T
        allowed = text_mask(states.shape[0], seg.ref[:, at])
        query_grads = []
        for head in range(columns // HEAD):
            cols = slice(head * HEAD, (head + 1) * HEAD)
            more = slice(columns + head * HEAD, columns + (head + 1) * HEAD)
            scores = plain_product(states.ref[:, cols], query_t[cols, :]) * scale
            scores = jnp.where(allowed, scores, masked_score)
            e = jnp.exp(scores - jnp.max(scores, axis=0, keepdims=True))
            p = e * (1.0 / jnp.sum(e, axis=0, keepdims=True))
            slope = plain_product(states.ref[:, more], grad_t[cols, :])
            weighted = p * slope
            ds = (weighted - p * jnp.sum(weighted, axis=0, keepdims=True)).astype(jnp.bfloat16)
            query_grads.append((plain_product(keys_t.ref[cols, :], ds) * scale).astype(jnp.bfloat16))
            sums.ref[:, cols] += plain_product(ds, query[:, cols]) * scale
            sums.ref[:, more] += plain_product(p.astype(jnp.bfloat16), grad[:, cols])
        query_grads = jnp.concatenate(query_grads, axis=0).T
        left.write(at, query_grads)
        return nt_product(query_grads, into.ref[...])

    def end():
        state_grads.write(slice(0, states.shape[0]), sums.ref[...].astype(jnp.bfloat16))

    stage.begin, stage.prepare, stage.state_grads = begin, prepare, state_grads
    stage.ends.append(end)
    return stage


def self_in_stage(build, index, layer, grads_t, weights, width):
    columns, rows = grads_t.shape
    stage = Stage(rows, width)
    part = columns // 3
    flipped = grads_t if isinstance(grads_t, Held) else build.arg(grads_t, index)
    matrices = [build.pick(weight, layer, index) for weight in weights]
    left = build.temp((rows, columns), jnp.bfloat16)

    def begin():
        for number in range(3):
            heads = [
                flipped.ref[(3 * head + number) * HEAD : (3 * head + number + 1) * HEAD, :]
                for head in range(part // HEAD)
            ]
            left.ref[:, number * part : (number + 1) * part] = jnp.concatenate(heads, axis=0).T

    def prepare(number):
        at = span(number, min(BLOCK, rows))
        total = jnp.zeros((min(BLOCK, rows), width), jnp.float32)
        for number, matrix in enumerate(matrices):
            total = total + nt_product(left.ref[at, number * part : (number + 1) * part], matrix.ref[...])
        return total

    stage.begin, stage.prepare = begin, prepare
    stage.left = left
    return stage


def forward_chain(
    layer, attended_t, entering, states, seg, vectors, weights, collective_id, tasks=(), late=None, begins=None
):
    output, query, cross, expand, reduce = weights
    build = Build()
    gains = build.pick(vectors, layer, 0)
    base = build.arg(entering, 0, BY_SECTION if entering.ndim == 3 else None)
    first = self_out_stage(build, 0, layer, attended_t, output, base)
    middle, second_normed = residual_norm(build, first, base, gains, 2, NORM)
    second = cross_stage(build, 1, layer, second_normed, states, seg, query, cross)
    latter, third_normed = residual_norm(build, second, middle, gains, 4, NORM)
    third = feed_stage(build, 2, layer, third_normed, expand, reduce)
    after = None if late is None else build.pick(vectors, 1 - layer, 2)
    _, next_normed = residual_norm(build, third, latter, after, 0, END if late is None else NEXT)
    hooks, then, kinds = [], None, (LINE_ONLY,)
    if isinstance(expand, WeightTask):
        hooks = [
            (expand.first_hop, (1, 0), (0, 9)),
            (reduce.first_hop, (1, 5), (1, 0)),
            (expand.second_hop, (1, 9), (1, 2)),
            (reduce.second_hop, (1, 15), (1, 9)),
        ]
        for one in late:
            hooks += [(one.first_hop, (2, 0), (1, 8)), (one.second_hop, (2, 8), (2, 0))]
        start_second = second.begin

        def begin_second():
            query.second_hop()
            cross.second_hop()
            query.arrive()
            cross.arrive()
            start_second()

        def begin_third():
            expand.arrive()
            reduce.arrive()

        second.begin, third.begin = begin_second, begin_third
        attention = Attention(build, third.rows, begins, 2)
        sender = BlockSender(build, third.rows, 3 * HEAD, attention.heads_t)

        def project(block):
            @pl.when(block == 0)
            def _():
                for one in late:
                    one.arrive()

            lanes = span(block, BLOCK)
            turned_parts(next_normed.ref[lanes, :], late, sender.own, (), lanes)
            sender.send(block)

        def then(need):
            sender.wait()
            attention.run()

        third.after = project
        kinds = (LINE_ONLY, FRAME)
    return run_chain(build, [first, second, third], collective_id, tasks, kinds, hooks=hooks, then=then)


def add_backward(build, index, layer, arriving, saved, states, seg, vectors, weights):
    _, query, cross, expand, reduce = weights
    middle, latter, third_normed, queries, before, hidden = saved
    gains, grads = gain_rows(build, vectors, layer, index), vector_rows(build, arriving.shape[1])
    first = feed_back_stage(build, index, layer, arriving, before, reduce, expand)
    grad_latter, grad_cross = norm_backward(build, index, first, latter, gains, 4, grads, arriving, True)
    second = cross_back_stage(build, index + 1, layer, grad_cross, queries, states, seg, cross, query)
    _, grad_self = norm_backward(
        build, index + 1, second, middle, gains, 2, grads, grad_latter, False
    )
    first_piece, each, wait = (12, 4, 3) if index else (0, 1, 5)
    chores = [
        Chore(build, index, first_piece, each, build.arg(hidden, index), arriving, wait=wait),
        Chore(build, index + 1, 0, each, build.arg(third_normed, index + 1), first.left, wait=wait),
    ]
    return [first, second], chores, grad_self, second.state_grads


def add_last(
    build, index, layer, grads_t, entering, vectors, grads, residual, weights, spare, products, later=None
):
    stage = self_in_stage(build, index, layer, grads_t, weights, residual.shape[1])
    stage.gains = gain_rows(build, vectors, layer, index)
    _, low = norm_backward(build, index, stage, entering, stage.gains, 0, grads, residual, False, spare)
    chores = []
    for number, (left, right) in enumerate(products):
        flipped = left is not None and left.shape[0] != residual.shape[0]
        if right is None:
            right = stage.left
        elif right is not residual:
            right = build.arg(right, index)
        more = None if later is None else later[number]
        if left is None:
            stage.normed = build.temp(residual.shape, jnp.bfloat16)
            chores.append(Chore(build, 0, 3, 1, stage.normed, right, False, more, 4))
        else:
            chores.append(Chore(build, 0, 0, 1, build.arg(left, index), right, flipped, more))
    return stage, low, chores


def backward_chain(layer, upstream, saved, states, seg, vectors, weights, heads_t, begins, collective_id, tasks):
    build = Build()
    arriving = build.arg(upstream, 0, BY_SECTION)
    stages, chores, grad_self, grad_states = add_backward(
        build, 0, layer, arriving, saved, states, seg, vectors, weights
    )
    output = build.pick(weights[0], layer, 1)
    attention = AttentionBack(build, stages[1].rows, heads_t, begins, 1)
    sender = BlockSender(build, stages[1].rows, HEAD, attention.grad_t)
    share = ShareTask(grad_states)
    share.late = True

    def project(block):
        lanes = span(block, BLOCK)
        turned_grads(grad_self.ref[lanes, :], output, sender.own, lanes)
        sender.send(block)

    def then(need):
        share.ins = [grad_states.ref]
        share.begin()
        attention.begin()
        sender.wait()
        attention.run(share.middle)

    stages[1].after = project
    kinds = (LINE_ONLY, FRAME)
    return run_chain(build, stages, collective_id, tasks + [share], kinds, chores, then=then)


def between_chain(layer, grads_t, entering, vectors, upstream, weights, products, backward, collective_id, tasks):
    build = Build()
    residual = build.arg(upstream, 0)
    products = [(left, residual if right is upstream else right) for left, right in products]
    grads = vector_rows(build, residual.shape[1])
    stage, low, chores = add_last(
        build, 0, layer, grads_t, entering, vectors, grads, residual, weights, None, products
    )
    stages, more, _, _ = add_backward(build, 1, layer - 1, low, *backward)
    return run_chain(build, [stage] + stages, collective_id, tasks, chores=chores + more)


def last_kernel(
    heads_t,
    grad_self,
    output,
    begins,
    inputs,
    vectors,
    weights,
    spare,
    products,
    later,
    states,
    text_local,
    text_weights,
    vector_grads,
    collective_id,
    tasks,
):
    rows, width = grad_self.shape
    build = Build()
    attention = AttentionBack(build, rows, heads_t, begins, 1)
    grad_low, output = build.arg(grad_self, 0), build.pick(output, 0, 0)
    own = build.temp((4, HEAD, rows), jnp.bfloat16)
    sems = build.extra(pltpu.SemaphoreType.DMA((2, 3)))
    products = [(left, grad_low if right is grad_self else right) for left, right in products]
    vector_grads = [build.arg(grads, 2) for grads in vector_grads]
    early = []
    for (left, right), share in zip(products[:3], later):
        flipped = left.shape[0] != rows
        right = right if right is grad_low else build.arg(right, 1)
        early.append(Chore(build, 0, 0, 1, build.arg(left, 1), right, flipped, share))
        early[-1].task.hooked = 1
    stage, _, chores = add_last(
        build, 2, 0, attention.out, inputs, vectors, vector_grads[1], grad_low, weights, spare, products[3:], later[3:]
    )
    text_local = build.arg(text_local, 2)
    text_weights = [build.arg(weight, 2) for weight in text_weights]
    columns = text_weights[0].shape[1]
    text_rows = build.temp((text_local.shape[0], 2 * columns), jnp.bfloat16)
    text_part = build.temp(text_local.shape, jnp.bfloat16)
    both_grads = build.temp((2, 8, width), jnp.float32)
    chores.append(Chore(build, 0, 10, 2, text_local, text_rows, wait=1))
    from_states, from_vectors, from_text = StatesTask(*states), VectorTask(both_grads), TotalTask(text_part)

    def make_normed():
        def one(number, carry):
            at = span(number, BLOCK)
            standard, _ = norm_parts(stage.value.ref[at, :].astype(jnp.float32))
            stage.normed.ref[at, :] = scaled_rows(standard, stage.gains, 0)
            return carry

        lax.fori_loop(0, rows // BLOCK, one, 0)

    def text_step():
        from_states.arrive()
        text_rows.ref[...] = jnp.concatenate([from_states.both[0], from_states.both[1]], axis=0)
        total = nt_product(text_rows.ref[:, :columns], text_weights[0].ref[...])
        total = total + nt_product(text_rows.ref[:, columns:], text_weights[1].ref[...])
        text_part.ref[...] = total.astype(jnp.bfloat16)
        from_text.ins = [text_part.ref]
        from_text.begin()

    def first(need, meet, ride, middle):
        me, grad_t = lax.axis_index(FRAME), attention.grad_t
        landing = grad_t.ref.at[:, span(me, rows)]
        arriving = to_frames(lambda g: own.ref.at[g], lambda f: landing, build.bound[sems])
        need(0)
        turned_grads(grad_low.ref[...], output, own, slice(0, rows))
        meet()
        for copy in arriving[::-1]:
            copy.start()
        ride()
        grad_t.ref[:, span(me, rows)] = own.ref[me]
        need(1)
        for one in early:
            one.make_all()
        attention.begin()
        for copy in arriving:
            copy.wait()

        def along():
            middle()
            for one in early:
                one.task.middle()

        attention.run(along)
        from_states.cross()
        for one in early:
            one.task.send()

    def then(need):
        from_text.sum_first()
        both_grads.ref[0] = vector_grads[1].ref[...]
        both_grads.ref[1] = vector_grads[0].ref[...]
        from_vectors.ins = [both_grads.ref]
        from_vectors.begin()

    tasks = [from_states] + list(tasks) + [one.task for one in early]
    return run_chain(
        build,
        [stage],
        collective_id,
        tasks,
        (LINE_ONLY, SECTION),
        chores,
        [(make_normed, (0, 2), (0, 2)), (text_step, (0, 9), (0, 9))],
        then,
        first,
        2,
        [from_vectors, from_text],
    )


def masked_scores(keys, query_t, begins, start):
    reach, block = keys.shape[0], query_t.shape[1]
    scores = plain_product(keys, query_t)
    key_pos = lax.broadcasted_iota(jnp.int32, (reach, 1), 0)
    query_pos = start + lax.broadcasted_iota(jnp.int32, (1, block), 1)
    allowed = (key_pos <= query_pos) & (key_pos >= begins)
    return jnp.where(allowed, scores * HEAD ** (-0.5), masked_score)


def to_frames(source, landing, sems):
    me = lax.axis_index(FRAME)
    return [
        remote(source(other), landing(me), sems.at[0, k], sems.at[1, k], {FRAME: other})
        for k, other in enumerate(frame_partners())
    ]


def turned_parts(normed, matrices, own, at, lanes):
    for part, matrix in enumerate(matrices):
        turned = plain_product(normed, matrix.ref[...]).astype(jnp.bfloat16).T
        for head in range(4):
            rows = slice(part * HEAD, (part + 1) * HEAD)
            own.ref[at + (head, rows, lanes)] = turned[head * HEAD : (head + 1) * HEAD, :]


class Attention:
    def __init__(self, build, rows, begins, stage):
        frames, width = 4, 3 * HEAD
        self.rows = rows
        self.begins = build.arg(begins, stage)
        self.heads_t = build.out((width, rows * frames), jnp.bfloat16)
        self.out = build.out((frames * HEAD, rows), jnp.bfloat16)
        self.keys = build.temp((rows * frames, HEAD), jnp.bfloat16)
        self.mixed_t = build.temp((frames, HEAD, rows), jnp.bfloat16)
        self.sems = build.extra(pltpu.SemaphoreType.DMA((2, frames - 1)))
        self.build = build

    def run(self, early=()):
        me, partners, rows = lax.axis_index(FRAME), frame_partners(), self.rows
        heads_t, keys, mixed_t, out = self.heads_t, self.keys, self.mixed_t, self.out
        block = min(2 * BLOCK, rows)
        leaving = to_frames(
            lambda g: mixed_t.ref.at[g], lambda f: out.ref.at[span(f, HEAD), :], self.build.bound[self.sems]
        )
        heads_t.flush()
        keys.ref[...] = heads_t.ref[HEAD : 2 * HEAD, :].T
        for target in range(4):
            if target == 3:
                for task in early:
                    task.first_hop()
            for start in range(target * rows, (target + 1) * rows, block):
                reach = start + block
                scores = masked_scores(
                    keys.ref[:reach, :],
                    heads_t.ref[:HEAD, start:reach],
                    self.begins.ref[:, start:reach],
                    start,
                )
                e = jnp.exp(scores - jnp.max(scores, axis=0, keepdims=True))
                total = jnp.sum(e, axis=0, keepdims=True)
                mixed = plain_product(heads_t.ref[2 * HEAD :, :reach], e.astype(jnp.bfloat16))
                at = start - target * rows
                mixed_t.ref[target, :, at : at + block] = (mixed * (1.0 / total)).astype(jnp.bfloat16)

            for copy, other in zip(leaving, partners):

                @pl.when(other == target)
                def _():
                    copy.start()

        out.ref[span(me, HEAD), :] = mixed_t.ref[me]
        for copy in leaving:
            copy.wait()
        out.flush()


class BlockSender:
    def __init__(self, build, rows, height, landing):
        self.rows, self.landing = rows, landing
        self.blocks = rows // BLOCK
        self.own = build.temp((4, height, rows), jnp.bfloat16)
        self.sems = build.extra(pltpu.SemaphoreType.DMA((2, 3, self.blocks)))
        self.build = build

    def copies(self, block):
        lanes, me = span(block, BLOCK), lax.axis_index(FRAME)
        place = self.landing.ref.at[:, span(me * self.blocks + block, BLOCK)]
        sems = self.build.bound[self.sems]
        return [
            remote(
                self.own.ref.at[other, :, lanes], place, sems.at[0, k, block], sems.at[1, k, block], {FRAME: other}
            )
            for k, other in enumerate(frame_partners())
        ]

    def send(self, block):
        me = lax.axis_index(FRAME)
        for copy in self.copies(block)[::-1]:
            copy.start()
        lanes = span(block, BLOCK)
        self.landing.ref[:, span(me * self.blocks + block, BLOCK)] = self.own.ref[me, :, lanes]

    def wait(self):
        def one(block, carry):
            for copy in self.copies(block):
                copy.wait()
            return carry

        lax.fori_loop(0, self.blocks, one, 0)


def first_attention(inputs, vectors, weights, begins, text, text_weights, collective_id, tasks, early):
    micros, rows, model = inputs.shape
    frames, width = 4, 3 * HEAD
    build = Build()
    inputs, vectors = build.arg(inputs, 0), build.arg(vectors, 0)
    matrices = [build.arg(weight, 0) for weight in weights]
    attention = Attention(build, rows, begins, 1)
    text, text_weights = build.arg(text, 1), [build.arg(weight, 1) for weight in text_weights]
    heads_t = attention.heads_t
    normed = build.temp((rows, model), jnp.bfloat16)
    own = build.temp((2, frames, width, rows), jnp.bfloat16)
    columns = text_weights[0].shape[1]
    states = build.temp((micros, text.shape[0] // micros, 2 * columns), jnp.bfloat16)
    sems = build.extra(pltpu.SemaphoreType.DMA((2, frames - 1)))
    over_sems = build.extra(pltpu.SemaphoreType.DMA((2, frames)))
    from_text = TextTask(states)

    def project(micro):
        def one(number, carry):
            at = span(number, BLOCK)
            standard, _ = norm_parts(inputs.ref[micro, at, :].astype(jnp.float32))
            normed.ref[at, :] = scaled_rows(standard, vectors, 0)
            return carry

        lax.fori_loop(0, rows // BLOCK, one, 0)
        turned_parts(normed.ref[...], matrices, own, (micro,), slice(0, rows))

    def body(need, meet, ride, middle):
        me, section = lax.axis_index(FRAME), lax.axis_index(SECTION)
        landing = heads_t.ref.at[:, span(me, rows)]
        arriving = to_frames(lambda g: own.ref.at[0, g], lambda f: landing, build.bound[sems])
        pair = build.bound[over_sems]
        over = [
            remote(own.ref.at[1, g], landing, pair.at[0, k], pair.at[1, k], {SECTION: 1, FRAME: g})
            for k, g in enumerate((me,) + frame_partners())
        ]
        need(0)

        @pl.when(section == 0)
        def _():
            project(1)
            meet()
            for copy in over:
                copy.start()
            project(0)
            for copy in arriving[::-1]:
                copy.start()
            heads_t.ref[:, span(me, rows)] = own.ref[0, me]

        @pl.when(section == 1)
        def _():
            meet()

        need(1)
        for part, weight in enumerate(text_weights):
            made = plain_product(text.ref[...], weight.ref[...]).astype(jnp.bfloat16)
            for micro in range(micros):
                some = slice(micro * states.shape[1], (micro + 1) * states.shape[1])
                states.ref[micro, :, part * columns : (part + 1) * columns] = made[some, :]
        from_text.ins = [states.ref]
        from_text.begin()
        ride()

        @pl.when(section == 0)
        def _():
            for copy in arriving + over:
                copy.wait_send()
            for copy in arriving:
                copy.wait_recv()

        @pl.when(section == 1)
        def _():
            for copy in over:
                copy.wait_recv()

        attention.run(early)

    return run_build(build, body, (FRAME, SECTION, BOTH), collective_id, tasks + [from_text])


class AttentionBack:
    def __init__(self, build, rows, heads_t, begins, stage):
        frames, width = 4, 3 * HEAD
        all_rows = rows * frames
        self.build, self.rows = build, rows
        self.heads_t, self.begins = build.arg(heads_t, stage), build.arg(begins, stage)
        self.out = build.out((frames * width, rows), jnp.bfloat16)
        self.grad_t = build.temp((HEAD, all_rows), jnp.bfloat16)
        self.columns = build.temp((4, all_rows, HEAD), jnp.bfloat16)
        self.key_sum, self.value_sum = (build.temp((all_rows, HEAD), jnp.float32) for _ in range(2))
        self.grads_t = build.temp((frames, width, rows), jnp.bfloat16)
        self.sems = build.extra(pltpu.SemaphoreType.DMA((2, frames - 1)))

    def begin(self):
        key_sum, value_sum = self.key_sum, self.value_sum
        key_sum.ref[...] = jnp.zeros(key_sum.shape, jnp.float32)
        value_sum.ref[...] = jnp.zeros(key_sum.shape, jnp.float32)
        for part in range(3):
            self.columns.ref[part] = self.heads_t.ref[part * HEAD : (part + 1) * HEAD, :].T

    def run(self, middle):
        rows, width, scale = self.rows, 3 * HEAD, HEAD ** (-0.5)
        me, partners = lax.axis_index(FRAME), frame_partners()
        heads_t, begins, grad_t, columns = self.heads_t, self.begins, self.grad_t, self.columns
        key_sum, value_sum, grads_t, out = self.key_sum, self.value_sum, self.grads_t, self.out
        block = min(2 * BLOCK, rows)
        leaving = to_frames(
            lambda g: grads_t.ref.at[g], lambda f: out.ref.at[span(f, width), :], self.build.bound[self.sems]
        )
        columns.ref[3] = grad_t.ref[...].T
        middle()
        for target in reversed(range(4)):
            for start in reversed(range(target * rows, (target + 1) * rows, block)):
                reach = start + block
                scores = masked_scores(
                    columns.ref[1, :reach, :],
                    heads_t.ref[:HEAD, start:reach],
                    begins.ref[:, start:reach],
                    start,
                )
                e = jnp.exp(scores - jnp.max(scores, axis=0, keepdims=True))
                p = e * (1.0 / jnp.sum(e, axis=0, keepdims=True))
                slope = plain_product(columns.ref[2, :reach, :], grad_t.ref[:, start:reach])
                weighted = p * slope
                ds = (weighted - p * jnp.sum(weighted, axis=0, keepdims=True)).astype(jnp.bfloat16)
                value_sum.ref[:reach, :] += plain_product(
                    p.astype(jnp.bfloat16), columns.ref[3, start:reach, :]
                )
                key_sum.ref[:reach, :] += plain_product(ds, columns.ref[0, start:reach, :])
                here = slice(start - target * rows, reach - target * rows)
                query_grad = plain_product(heads_t.ref[HEAD : 2 * HEAD, :reach], ds) * scale
                grads_t.ref[target, :HEAD, here] = query_grad.astype(jnp.bfloat16)
                key_grad = key_sum.ref[start:reach, :] * scale
                grads_t.ref[target, HEAD : 2 * HEAD, here] = key_grad.T.astype(jnp.bfloat16)
                grads_t.ref[target, 2 * HEAD :, here] = value_sum.ref[start:reach, :].T.astype(jnp.bfloat16)

            for copy, other in zip(leaving, partners):

                @pl.when(other == target)
                def _():
                    copy.start()

        out.ref[span(me, width), :] = grads_t.ref[me]
        for copy in leaving:
            copy.wait()
        out.flush()


def turned_grads(grad, weight, own, lanes):
    turned = nt_product(weight.ref[...], grad).astype(jnp.bfloat16)
    for head in range(4):
        own.ref[head, :, lanes] = turned[head * HEAD : (head + 1) * HEAD, :]


def matmul(left_side, right_side):
    return jnp.dot(left_side, right_side, preferred_element_type=jnp.float32)


def matmul_tn(left_side, right_side):
    return lax.dot_general(
        left_side, right_side, (((0,), (0,)), ((), ())), preferred_element_type=jnp.float32
    )


def matmul_nt(left_side, right_side):
    return lax.dot_general(
        left_side, right_side, (((1,), (1,)), ((), ())), preferred_element_type=jnp.float32
    )


def layer_norm(signal, gain_vec, shift_vec):
    average = jnp.mean(signal, axis=-1, keepdims=True)
    centered = signal - average
    variance = jnp.mean(centered * centered, axis=-1, keepdims=True)
    return centered * lax.rsqrt(variance + 1e-05) * gain_vec + shift_vec


def norm_back(signal, gain_vec, upstream):
    average = jnp.mean(signal, axis=-1, keepdims=True)
    centered = signal - average
    inverse = lax.rsqrt(jnp.mean(centered * centered, axis=-1, keepdims=True) + 1e-05)
    standard = centered * inverse
    scaled = upstream * gain_vec
    through = inverse * (
        scaled
        - jnp.mean(scaled, axis=-1, keepdims=True)
        - standard * jnp.mean(scaled * standard, axis=-1, keepdims=True)
    )
    return (through, jnp.sum(upstream * standard, axis=0), jnp.sum(upstream, axis=0))


def head_total(partial_sum):
    return lax.psum(partial_sum.astype(jnp.bfloat16), LINE).astype(jnp.float32)


def swapped(x):
    return lax.ppermute(x, SECTION, [(0, 1), (1, 0)])


def split_heads(matrix):
    return matrix.reshape(matrix.shape[0], matrix.shape[1] // HEAD, HEAD)


def softmax_rows(query, key_rows, allowed):
    logits = jnp.einsum(
        "qhd,khd->hqk",
        split_heads(query),
        split_heads(key_rows),
        preferred_element_type=jnp.float32,
    ) * HEAD ** (-0.5)
    logits = jnp.where(allowed[None], logits, masked_score)
    exponent = jnp.exp(logits - jnp.max(logits, axis=-1, keepdims=True))
    return exponent / jnp.sum(exponent, axis=-1, keepdims=True)


def attend(query, key_rows, value_rows, allowed):
    weights_low = softmax_rows(query, key_rows, allowed).astype(jnp.bfloat16)
    result = jnp.einsum(
        "hqk,khd->qhd", weights_low, split_heads(value_rows), preferred_element_type=jnp.float32
    )
    return result.reshape(query.shape).astype(jnp.bfloat16)


def attend_back(query, key_rows, value_rows, allowed, grad_out):
    probabilities = softmax_rows(query, key_rows, allowed)
    weights_low = probabilities.astype(jnp.bfloat16)
    grad_heads = split_heads(grad_out)
    grad_prob = jnp.einsum(
        "qhd,khd->hqk", grad_heads, split_heads(value_rows), preferred_element_type=jnp.float32
    )
    centre = jnp.sum(probabilities * grad_prob, axis=-1, keepdims=True)
    grad_logit = (probabilities * (grad_prob - centre)).astype(jnp.bfloat16)
    scale = HEAD ** (-0.5)
    grad_query = (
        jnp.einsum(
            "hqk,khd->qhd", grad_logit, split_heads(key_rows), preferred_element_type=jnp.float32
        )
        * scale
    )
    grad_keys = (
        jnp.einsum(
            "hqk,qhd->khd", grad_logit, split_heads(query), preferred_element_type=jnp.float32
        )
        * scale
    )
    grad_values = jnp.einsum(
        "hqk,qhd->khd", weights_low, grad_heads, preferred_element_type=jnp.float32
    )
    return (
        grad_query.reshape(query.shape),
        grad_keys.reshape(key_rows.shape),
        grad_values.reshape(value_rows.shape),
    )


def on_four_frames(inputs, lengths, text, cotangent, vector_args, matrix_args):
    section = lax.axis_index(SECTION)
    at_zero = section == 0
    frame_index = lax.axis_index(FRAME)
    micro_count, rows_dev, model_width = inputs.shape
    rows_all = rows_dev * 4
    (
        query_weight,
        key_weight,
        value_weight,
        output_weight,
        cross_query,
        cross_key,
        cross_value,
        cross_output,
        expand_weight,
        reduce_weight,
    ) = (w[0] for w in matrix_args)
    columns = query_weight.shape[1]

    def by_section(first, second):
        return jnp.where(at_zero, first, second)

    own_vectors = jnp.concatenate([*vector_args, jnp.zeros((2, model_width), jnp.float32)], axis=0)
    self_weights = (query_weight, key_weight, value_weight)
    text_local = text.reshape(-1, model_width)

    item_ends = jnp.cumsum(lax.dynamic_index_in_dim(lengths, section, 0, keepdims=False))
    passed = jnp.arange(rows_all, dtype=jnp.int32)[None, :] >= item_ends[:, None]
    begins = jnp.max(jnp.where(passed, item_ends[:, None], 0), axis=0, keepdims=True).astype(jnp.int32)
    seg = jnp.sum(passed.astype(jnp.int32), axis=0, keepdims=True)
    seg = lax.dynamic_slice_in_dim(seg, frame_index * rows_dev, rows_dev, 1)

    early = WeightTask(output_weight)
    early.hooked = 1
    others = (cross_query, cross_output, expand_weight, reduce_weight)
    (heads_t, attended_t), carried = first_attention(
        inputs,
        own_vectors,
        self_weights,
        begins,
        text_local,
        (cross_key, cross_value),
        1,
        [early, CrossTask(own_vectors, own_vectors, False)] + [QuarterTask(w) for w in others[:2]],
        [early],
    )
    vectors = (own_vectors, carried[1])
    selected = [by_section(*vectors), by_section(*vectors[::-1])]
    states = carried[4].reshape(2, -1, 2 * columns)
    coming = [WeightTask(w, 0, quarter) for w, quarter in zip(others, carried[2:4] + [None] * 2)]
    late = [WeightTask(w, 1) for w in self_weights]
    weights = [(output_weight, carried[0])]
    outs, carried = forward_chain(
        0,
        attended_t,
        inputs,
        states[0],
        seg,
        vectors,
        weights + coming,
        2,
        coming + late,
        late,
        begins,
    )
    weights += list(zip(others, carried))
    self_pairs = list(zip(self_weights, carried[4:]))
    def keep(entering, normed, heads_t, attended_t, outs):
        second_normed, middle, queries, cross_att, third_normed, latter, before, hidden = outs[:8]
        return (
            entering,
            normed,
            heads_t,
            attended_t,
            middle,
            second_normed,
            latter,
            third_normed,
            queries,
            cross_att,
            before,
            hidden,
        )

    saved = [keep(inputs, None, heads_t, attended_t, outs)]
    normed, entering, heads_t, attended_t = outs[8:]
    outs, _ = forward_chain(
        1, attended_t, entering, states[1], seg, vectors, weights, 3
    )
    saved.append(keep(entering, normed, heads_t, attended_t, outs))
    result_low = outs[8]

    shares = [{}, {}]

    def crossing(*names):
        return [CrossTask(shares[0][name], shares[1][name], True) for name in names]

    def unpack(outs):
        names = ("vectors", "grad_pre", "grad_cross", "queries", "states", "grad_self")
        return dict(zip(names, outs))

    def for_backward(layer):
        return saved[layer][4], *saved[layer][6:9], *saved[layer][10:]

    def products(layer, outs):
        attended_t, second_normed, cross_att = saved[layer][3], saved[layer][5], saved[layer][9]
        return [
            (cross_att, outs["grad_cross"]),
            (attended_t, outs["grad_self"]),
            (second_normed, outs["queries"]),
            (saved[layer][1], None),
        ]

    names = ("cross_output", "output", "cross_query", "heads")
    outs, carried = backward_chain(
        1,
        cotangent,
        for_backward(1),
        states[1],
        seg,
        vectors,
        weights,
        saved[1][2],
        begins,
        8,
        [BothTask(saved[1][0], result_low)],
    )
    later, grad_heads_t = unpack(outs), outs[6]
    layer_outputs, shares[1]["states"], shares[1]["reduce"], shares[1]["expand"] = carried
    outs, carried = between_chain(
        1,
        grad_heads_t,
        saved[1][0],
        selected[1],
        later["grad_self"],
        self_pairs,
        products(1, later),
        (for_backward(0), states[0], seg, selected[0], weights),
        10,
        [],
    )
    last_vectors, later_low = outs[:2]
    sooner = unpack(outs[2:])
    shares[1].update(zip(names, carried))
    shares[0]["reduce"], shares[0]["expand"] = carried[4:]
    outs, carried = last_kernel(
        saved[0][2],
        sooner["grad_self"],
        weights[0],
        begins,
        inputs,
        vectors,
        self_pairs,
        later_low,
        products(0, sooner),
        [shares[1][name] for name in names],
        (sooner["states"], shares[1]["states"]),
        text_local,
        (cross_key, cross_value),
        (later["vectors"] + last_vectors, sooner["vectors"]),
        11,
        crossing("reduce", "expand"),
    )
    both_grads = outs[-1]
    totals = dict(zip(("reduce", "expand") + names + ("text",), carried))
    cross_grads, (vector_total, text_grad) = totals["text"], carried[7:]
    kernel_outs = widen(
        [layer_outputs, both_grads, text_grad, cross_grads],
        [totals[name] for name in ("reduce", "expand", "cross_output", "output", "cross_query", "heads")],
        vector_total,
    )
    layer_outputs, input_grads, text_grad, cross_key_grad, cross_value_grad = kernel_outs[:5]
    reduce_grad, expand_grad, cross_output_grad, output_grad, cross_query_grad = kernel_outs[5:10]
    query_grad, key_grad, value_grad = kernel_outs[10:13]
    rows = kernel_outs[13:]
    ordered = (
        rows[0],
        rows[1],
        query_grad,
        key_grad,
        value_grad,
        output_grad,
        rows[2],
        rows[3],
        cross_query_grad,
        cross_key_grad,
        cross_value_grad,
        cross_output_grad,
        rows[4],
        rows[5],
        expand_grad,
        reduce_grad,
    )
    vector_places = (0, 1, 6, 7, 12, 13)
    ordered = tuple(
        g if place in vector_places else g[None] for place, g in enumerate(ordered)
    )
    return (layer_outputs[None], input_grads[None], text_grad.reshape(text.shape)) + ordered


def widen(lows, wides, vectors):
    *lows, pair = lows
    *wides, triple = wides
    wide = jnp.float32
    half, third = pair.shape[1] // 2, triple.shape[1] // 3
    quarter = vectors.shape[1] // 4
    outs = [jax.ShapeDtypeStruct(low.shape, wide) for low in lows]
    outs += [jax.ShapeDtypeStruct((pair.shape[0], half), wide)] * 2
    outs += [jax.ShapeDtypeStruct(one.shape, wide) for one in wides]
    outs += [jax.ShapeDtypeStruct((triple.shape[0], third), wide)] * 3
    outs += [jax.ShapeDtypeStruct((1, quarter), wide)] * 6
    widened = [*lows, pair]
    n_in, n_out, n_low = len(widened) + len(wides) + 2, len(outs), len(widened)

    def kernel(*refs):
        ins, outs = refs[:n_in], refs[n_in : n_in + n_out]
        narrow = refs[n_in + n_out : n_in + n_out + n_low]
        broad = refs[n_in + n_out + n_low : n_in + n_out + 2 * n_low]
        *held, rows, in_sems, out_sems = refs[n_in + n_out + 2 * n_low :]
        lane = span(lax.axis_index(FRAME), quarter)
        started = []

        def copy(source, landing):
            one = pltpu.make_async_copy(source, landing, out_sems.at[len(started)])
            one.start()
            started.append(one)

        loads = [pltpu.make_async_copy(ins[i], narrow[i], in_sems.at[i]) for i in range(n_low)]
        copied = [
            pltpu.make_async_copy(source, room, in_sems.at[n_low + i])
            for i, (source, room) in enumerate(zip(ins[n_low:], held + [rows]))
        ]
        for load in copied + loads:
            load.start()
        for i in range(len(wides)):
            copied[i].wait()
            copy(held[i], outs[n_low + 1 + i])
        place = n_low + 1 + len(wides)
        copied[-2].wait()
        for part in range(3):
            copy(held[-1].at[:, part * third : (part + 1) * third], outs[place + part])
        copied[-1].wait()
        for row in range(6):
            copy(rows.at[row : row + 1, lane], outs[place + 3 + row])
        for i in range(n_low):
            loads[i].wait()
            broad[i][...] = narrow[i][...].astype(wide)
            if i + 1 < n_low:
                copy(broad[i], outs[i])
            else:
                copy(broad[i].at[:, :half], outs[i])
                copy(broad[i].at[:, half:], outs[i + 1])
        for one in started:
            one.wait()

    anywhere = pl.BlockSpec(memory_space=pl.ANY)
    scratch = [pltpu.VMEM(low.shape, jnp.bfloat16) for low in widened]
    scratch += [pltpu.VMEM(low.shape, wide) for low in widened]
    scratch += [pltpu.VMEM(one.shape, wide) for one in (*wides, triple, vectors)]
    scratch += [pltpu.SemaphoreType.DMA((n_in,)), pltpu.SemaphoreType.DMA((n_out,))]
    return pl.pallas_call(
        kernel,
        out_shape=outs,
        in_specs=[anywhere] * n_in,
        out_specs=[anywhere] * n_out,
        scratch_shapes=scratch,
        compiler_params=pltpu.CompilerParams(vmem_limit_bytes=VMEM_BYTES),
    )(*widened, *wides, triple, vectors)


def self_attention(query, key_rows, value_rows, masks):
    all_keys = lax.all_gather(key_rows, FRAME, axis=0, tiled=True)
    all_values = lax.all_gather(value_rows, FRAME, axis=0, tiled=True)
    return attend(query, all_keys, all_values, masks["own"]), (query, all_keys, all_values)


def self_attention_back(kept, grad_out, masks):
    query, keys, values = kept
    grad_q, grad_k_all, grad_v_all = attend_back(query, keys, values, masks["own"], grad_out)
    grad_k, grad_v = (
        lax.psum_scatter(g.astype(jnp.bfloat16), FRAME, scatter_dimension=0, tiled=True)
        for g in (grad_k_all, grad_v_all)
    )
    return grad_q.astype(jnp.bfloat16), grad_k, grad_v


def forward(entering, vectors, weights, cross_keys, cross_values, masks):
    first_gain, first_shift, second_gain, second_shift, third_gain, third_shift = vectors
    (
        query_weight,
        key_weight,
        value_weight,
        output_weight,
        cross_query,
        cross_output,
        expand_weight,
        reduce_weight,
    ) = weights
    signal = entering.astype(jnp.float32)
    first_normed = layer_norm(signal, first_gain, first_shift).astype(jnp.bfloat16)
    query = matmul(first_normed, query_weight).astype(jnp.bfloat16)
    key_rows = matmul(first_normed, key_weight).astype(jnp.bfloat16)
    value_rows = matmul(first_normed, value_weight).astype(jnp.bfloat16)
    attended, heads_kept = self_attention(query, key_rows, value_rows, masks)
    middle = signal + head_total(matmul(attended, output_weight))
    second_normed = layer_norm(middle, second_gain, second_shift).astype(jnp.bfloat16)
    cross_queries = matmul(second_normed, cross_query).astype(jnp.bfloat16)
    cross_att = attend(cross_queries, cross_keys, cross_values, masks["cross"])
    latter = middle + head_total(matmul(cross_att, cross_output))
    third_normed = layer_norm(latter, third_gain, third_shift).astype(jnp.bfloat16)
    hidden_pre = matmul(third_normed, expand_weight)
    hidden_act = jax.nn.gelu(hidden_pre, approximate=False).astype(jnp.bfloat16)
    result = latter + head_total(matmul(hidden_act, reduce_weight))
    saved = (
        signal,
        first_normed,
        heads_kept,
        attended,
        middle,
        second_normed,
        cross_queries,
        cross_att,
        latter,
        third_normed,
        hidden_pre,
        hidden_act,
    )
    return (result, saved)


def backward(saved, upstream, vectors, weights, cross_keys, cross_values, masks):
    first_gain, first_shift, second_gain, second_shift, third_gain, third_shift = vectors
    (
        query_weight,
        key_weight,
        value_weight,
        output_weight,
        cross_query,
        cross_output,
        expand_weight,
        reduce_weight,
    ) = weights
    (
        signal,
        first_normed,
        heads_kept,
        attended,
        middle,
        second_normed,
        cross_queries,
        cross_att,
        latter,
        third_normed,
        hidden_pre,
        hidden_act,
    ) = saved
    grad_out = upstream.astype(jnp.bfloat16)
    grad_reduce = matmul_tn(hidden_act, grad_out)
    grad_act = matmul_nt(grad_out, reduce_weight)
    slope = (
        0.5 * (1.0 + lax.erf(hidden_pre * inv_sqrt_two))
        + hidden_pre * jnp.exp(-0.5 * hidden_pre * hidden_pre) * inv_sqrt_tau
    )
    grad_pre = (grad_act * slope).astype(jnp.bfloat16)
    grad_expand = matmul_tn(third_normed, grad_pre)
    grad_third = head_total(matmul_nt(grad_pre, expand_weight))
    grad_latter, grad_third_gain, grad_third_shift = norm_back(latter, third_gain, grad_third)
    grad_latter = grad_latter + upstream
    grad_cross = grad_latter.astype(jnp.bfloat16)
    grad_cross_output = matmul_tn(cross_att, grad_cross)
    grad_cross_att = matmul_nt(grad_cross, cross_output).astype(jnp.bfloat16)
    grad_cq, grad_ck, grad_cv = attend_back(
        cross_queries, cross_keys, cross_values, masks["cross"], grad_cross_att
    )
    grad_text_rows = jnp.concatenate([grad_ck, grad_cv], axis=1).astype(jnp.bfloat16)
    grad_text_rows = lax.psum_scatter(
        grad_text_rows.reshape(ITEMS, TEXT, -1), FRAME, scatter_dimension=1, tiled=True
    )
    grad_cquery = grad_cq.astype(jnp.bfloat16)
    grad_cross_query = matmul_tn(second_normed, grad_cquery)
    grad_second = head_total(matmul_nt(grad_cquery, cross_query))
    grad_middle, grad_second_gain, grad_second_shift = norm_back(middle, second_gain, grad_second)
    grad_middle = grad_middle + grad_latter
    grad_self = grad_middle.astype(jnp.bfloat16)
    grad_output = matmul_tn(attended, grad_self)
    grad_att = matmul_nt(grad_self, output_weight).astype(jnp.bfloat16)
    grad_query_low, grad_key_low, grad_value_low = self_attention_back(heads_kept, grad_att, masks)
    grad_query = matmul_tn(first_normed, grad_query_low)
    grad_key = matmul_tn(first_normed, grad_key_low)
    grad_value = matmul_tn(first_normed, grad_value_low)
    grad_first = head_total(
        matmul_nt(grad_query_low, query_weight)
        + matmul_nt(grad_key_low, key_weight)
        + matmul_nt(grad_value_low, value_weight)
    )
    grad_signal, grad_first_gain, grad_first_shift = norm_back(signal, first_gain, grad_first)
    grad_signal = grad_signal + grad_middle
    vector_grads = (
        grad_first_gain,
        grad_first_shift,
        grad_second_gain,
        grad_second_shift,
        grad_third_gain,
        grad_third_shift,
    )
    matrix_grads = (
        grad_query,
        grad_key,
        grad_value,
        grad_output,
        grad_cross_query,
        grad_cross_output,
        grad_expand,
        grad_reduce,
    )
    matrix_grads = tuple(
        lax.psum_scatter(g.astype(jnp.bfloat16), FRAME, scatter_dimension=0, tiled=True)
        for g in matrix_grads
    )
    return grad_signal, vector_grads, matrix_grads, grad_text_rows


def per_device(
    inputs,
    lengths,
    text,
    cotangent,
    first_gain,
    first_shift,
    query_weight,
    key_weight,
    value_weight,
    output_weight,
    second_gain,
    second_shift,
    cross_query,
    cross_key,
    cross_value,
    cross_output,
    third_gain,
    third_shift,
    expand_weight,
    reduce_weight,
):
    head_count, frame_count = lax.axis_size(LINE), lax.axis_size(FRAME)
    local_heads = query_weight.shape[2] // HEAD
    if head_count == 4 and frame_count == 4 and local_heads == 4:
        return on_four_frames(
            inputs,
            lengths,
            text,
            cotangent,
            (first_gain, first_shift, second_gain, second_shift, third_gain, third_shift),
            (
                query_weight,
                key_weight,
                value_weight,
                output_weight,
                cross_query,
                cross_key,
                cross_value,
                cross_output,
                expand_weight,
                reduce_weight,
            ),
        )
    section = lax.axis_index(SECTION)
    at_zero = section == 0
    frame_index = lax.axis_index(FRAME)
    micro_count, rows_dev, model_width = inputs.shape
    rows_all = rows_dev * frame_count
    text_rows_dev = text.shape[2]

    def keep(pair):
        return jnp.where(at_zero, pair[0], pair[1])

    def give(pair):
        return jnp.where(at_zero, pair[1], pair[0])

    vector_args = jnp.concatenate(
        [first_gain, first_shift, second_gain, second_shift, third_gain, third_shift], axis=0
    )
    vectors = lax.all_gather(vector_args, SECTION)
    matrix_args = (
        query_weight,
        key_weight,
        value_weight,
        output_weight,
        cross_query,
        cross_output,
        expand_weight,
        reduce_weight,
    )
    matrices = [lax.all_gather(w[0], SECTION) for w in matrix_args]
    weights = [tuple(w[layer] for w in matrices) for layer in range(2)]

    text_full = lax.all_gather(text, FRAME, axis=2, tiled=True)
    text_flat = text_full.reshape(micro_count * ITEMS * TEXT, model_width)
    text_heads = jnp.concatenate(
        [matmul(text_flat, cross_key[0]), matmul(text_flat, cross_value[0])], axis=1
    ).astype(jnp.bfloat16)
    text_heads = text_heads.reshape(micro_count, ITEMS * TEXT, -1)
    own_text = keep(text_heads)
    other_text = swapped(give(text_heads))
    columns = cross_key.shape[2]
    cross_states = [
        jnp.where(at_zero, own_text, other_text),
        jnp.where(at_zero, other_text, own_text),
    ]
    cross_keys = [c[:, :columns] for c in cross_states]
    cross_values = [c[:, columns:] for c in cross_states]

    item_ends = jnp.cumsum(lax.dynamic_index_in_dim(lengths, section, 0, keepdims=False))
    all_positions = jnp.arange(rows_all, dtype=jnp.int32)
    seg_all = jnp.sum((all_positions[:, None] >= item_ends[None, :]).astype(jnp.int32), axis=1)
    own_start = frame_index * rows_dev
    own_positions = own_start + jnp.arange(rows_dev, dtype=jnp.int32)
    seg_own = lax.dynamic_slice_in_dim(seg_all, own_start, rows_dev)
    text_item = jnp.arange(ITEMS * TEXT, dtype=jnp.int32) // TEXT
    masks = {
        "own": (all_positions[None, :] <= own_positions[:, None])
        & (seg_own[:, None] == seg_all[None, :]),
        "cross": seg_own[:, None] == text_item[None, :],
    }

    signal = lax.dynamic_index_in_dim(inputs, section, 0, keepdims=False)
    results, saves = [], []
    for layer in range(2):
        result, saved = forward(
            signal, vectors[layer], weights[layer], cross_keys[layer], cross_values[layer], masks
        )
        results.append(result)
        saves.append(saved)
        signal = result.astype(jnp.bfloat16)

    upstream = lax.dynamic_index_in_dim(cotangent, section, 0, keepdims=False)
    in_grads, vector_grads, matrix_grads, text_grads = [None] * 2, [None] * 2, [None] * 2, [None] * 2
    for layer in (1, 0):
        grad_signal, vector_grads[layer], matrix_grads[layer], text_grads[layer] = backward(
            saves[layer],
            upstream,
            vectors[layer],
            weights[layer],
            cross_keys[layer],
            cross_values[layer],
            masks,
        )
        in_grads[layer] = grad_signal
        upstream = grad_signal.astype(jnp.bfloat16).astype(jnp.float32)

    def both_micros(pair):
        own = keep(pair)
        other = swapped(give([p.astype(jnp.bfloat16) for p in pair])).astype(own.dtype)
        return jnp.stack([jnp.where(at_zero, own, other), jnp.where(at_zero, other, own)])

    layer_outputs = both_micros(results)
    input_grads = both_micros(in_grads)
    totals = [
        keep(pair).astype(jnp.float32) + swapped(give(pair)).astype(jnp.float32)
        for pair in zip(*matrix_grads)
    ]
    text_rows = both_micros(text_grads)
    text_rows = text_rows.reshape(micro_count * ITEMS * text_rows_dev, -1)
    key_part, value_part = text_rows[:, :columns], text_rows[:, columns:]
    text_local = text.reshape(-1, model_width)
    grad_cross_key, grad_cross_value = (
        lax.psum_scatter(
            matmul_tn(text_local, part).astype(jnp.bfloat16),
            FRAME,
            scatter_dimension=0,
            tiled=True,
        ).astype(jnp.float32)
        for part in (key_part, value_part)
    )
    text_part = matmul_nt(key_part, cross_key[0]) + matmul_nt(value_part, cross_value[0])
    text_grad = lax.psum(text_part.astype(jnp.bfloat16), (SECTION, LINE)).astype(jnp.float32)
    text_grad = text_grad.reshape(text.shape)

    stacked = jnp.stack([jnp.stack(v) for v in vector_grads])
    stacked = lax.psum_scatter(
        stacked.astype(jnp.bfloat16), FRAME, scatter_dimension=2, tiled=True
    )
    vector_total = keep(stacked).astype(jnp.float32) + swapped(give(stacked)).astype(jnp.float32)

    grad_q, grad_k, grad_v, grad_o, grad_cq, grad_co, grad_e, grad_r = totals
    ordered = (
        vector_total[0],
        vector_total[1],
        grad_q,
        grad_k,
        grad_v,
        grad_o,
        vector_total[2],
        vector_total[3],
        grad_cq,
        grad_cross_key,
        grad_cross_value,
        grad_co,
        vector_total[4],
        vector_total[5],
        grad_e,
        grad_r,
    )
    return (layer_outputs[None], input_grads[None], text_grad) + tuple(g[None] for g in ordered)


def solution(mesh):
    return jax.shard_map(
        per_device,
        mesh=mesh,
        in_specs=(
            P(None, FRAME, None),
            P(),
            P(None, None, FRAME, None),
            P(None, FRAME, None),
            P(SECTION, None),
            P(SECTION, None),
            P(SECTION, None, LINE),
            P(SECTION, None, LINE),
            P(SECTION, None, LINE),
            P(SECTION, LINE, None),
            P(SECTION, None),
            P(SECTION, None),
            P(SECTION, None, LINE),
            P(SECTION, None, LINE),
            P(SECTION, None, LINE),
            P(SECTION, LINE, None),
            P(SECTION, None),
            P(SECTION, None),
            P(SECTION, None, LINE),
            P(SECTION, LINE, None),
        ),
        out_specs=(
            P(SECTION, None, FRAME, None),
            P(SECTION, None, FRAME, None),
            P(None, None, FRAME, None),
            P(SECTION, FRAME),
            P(SECTION, FRAME),
            P(SECTION, FRAME, LINE),
            P(SECTION, FRAME, LINE),
            P(SECTION, FRAME, LINE),
            P(SECTION, (LINE, FRAME), None),
            P(SECTION, FRAME),
            P(SECTION, FRAME),
            P(SECTION, FRAME, LINE),
            P(SECTION, FRAME, LINE),
            P(SECTION, FRAME, LINE),
            P(SECTION, (LINE, FRAME), None),
            P(SECTION, FRAME),
            P(SECTION, FRAME),
            P(SECTION, FRAME, LINE),
            P(SECTION, (LINE, FRAME), None),
        ),
        check_vma=False,
    )
```

```python
import jax
import jax.numpy as jnp
from jax import lax
from jax.experimental import pallas as pl
from jax.experimental.pallas import tpu as pltpu
from jax.sharding import PartitionSpec as P

HEAD = 64
TEXT = 64
ITEMS = 4

masked_score = -1e30
inv_sqrt_two = 0.7071067811865476
inv_sqrt_tau = 0.3989422804014327

MESH_IDS = pl.DeviceIdType.MESH
BUSY = pl.CostEstimate(flops=30_000_000_000, bytes_accessed=8_000_000, transcendentals=0)
LAG = 3
BLOCK = 128
VMEM_BYTES = 60 * 1024 * 1024
EPS = 1e-05
SECTION, LINE, FRAME = "section", "head", "frame"
BOTH, LINE_ONLY, BY_SECTION = "both", "line", "one"
NORM, NEXT, END = range(3)


class Task:
    operands = ()
    outs = ()
    out_in_vmem = True
    scratch = ()
    greets = ()
    late = False
    hooked = 0

    def middle(self):
        pass

    def bind(self, ins, outs, scratch):
        self.ins, self.out, self.room = ins, outs, scratch
        self.far_ins = ins


def remote(source, landing, send_sem, recv_sem, target):
    return pltpu.make_async_remote_copy(
        src_ref=source,
        dst_ref=landing,
        send_sem=send_sem,
        recv_sem=recv_sem,
        device_id=target,
        device_id_type=MESH_IDS,
    )


def frame_partners():
    me = lax.axis_index(FRAME)
    return (me + 1 - 2 * lax.rem(me, 2), lax.rem(me + 2, 4), 3 - me)


def span(index, size):
    return pl.ds(pl.multiple_of(index * size, size), size)


class WeightTask(Task):
    out_in_vmem = False
    greets = (SECTION, FRAME)

    def __init__(self, weight, layer=None, quarter=None):
        self.layer = layer
        self.operands = (weight,) if quarter is None else (weight, quarter)
        self.outs = (jax.ShapeDtypeStruct(weight.shape, weight.dtype),)
        self.scratch = (pltpu.SemaphoreType.DMA((10,)),)
        if layer is not None:
            self.scratch += (pltpu.VMEM((2,) + weight.shape, weight.dtype),)
        self.quarter = weight.shape[0] // 4

    @property
    def ref(self):
        other = jnp.where(lax.axis_index(SECTION) == self.layer, 0, 1)
        return self.room[1].at[other]

    def arrived(self, at):
        return self.out[0].at[at] if self.layer is None else self.room[1].at[1, at]

    def over(self):
        sems, at = self.room[0], span(lax.axis_index(FRAME), self.quarter)
        target = {SECTION: 1 - lax.axis_index(SECTION)}
        return remote(self.ins[0].at[at], self.arrived(at), sems.at[0], sems.at[1], target)

    def along(self):
        sems, at = self.room[0], span(lax.axis_index(FRAME), self.quarter)
        target = {FRAME: frame_partners()[1]}
        source = self.ins[1] if len(self.ins) > 1 else self.arrived(at)
        return remote(source, self.arrived(at), sems.at[2], sems.at[3], target)

    def settle(self):
        at = span(lax.axis_index(FRAME), self.quarter)
        return pltpu.make_async_copy(self.ins[1], self.arrived(at), self.room[0].at[0])

    def within(self):
        sems, partners = self.room[0], frame_partners()
        copies = []
        for k, whose in enumerate((lax.axis_index(FRAME), partners[1])):
            at = span(whose, self.quarter)
            copies.append(
                remote(
                    self.arrived(at),
                    self.arrived(at),
                    sems.at[4 + 2 * k],
                    sems.at[5 + 2 * k],
                    {FRAME: partners[0]},
                )
            )
        return copies

    def begin(self):
        if len(self.ins) > 1:
            self.settle().start()
            self.along().start()
        else:
            self.over().start()
        if self.layer is not None:
            pltpu.make_async_copy(self.ins[0], self.room[1].at[0], self.room[0].at[8]).start()

    def first_hop(self):
        self.over().wait_recv()
        self.along().start()

    def second_hop(self):
        if len(self.ins) > 1:
            self.settle().wait()
        self.along().wait_recv()
        for copy in self.within():
            copy.start()

    def arrive(self):
        for copy in self.within():
            copy.wait_recv()
        if self.layer is not None:
            sems = self.room[0]
            pltpu.make_async_copy(self.ins[0], self.room[1].at[0], sems.at[8]).wait()
            pltpu.make_async_copy(self.room[1].at[1], self.out[0], sems.at[9]).start()

    def sent(self):
        over = [] if len(self.ins) > 1 else [self.over()]
        for copy in over + [self.along()] + self.within():
            copy.wait_send()
        if self.layer is not None:
            pltpu.make_async_copy(self.room[1].at[1], self.out[0], self.room[0].at[9]).wait()

    def steps(self):
        if self.layer is not None:
            return [self.sent]
        return [self.first_hop, self.second_hop][self.hooked :] + [self.arrive, self.sent]


class QuarterTask(Task):
    out_in_vmem = False
    greets = (SECTION,)

    def __init__(self, weight):
        self.quarter = weight.shape[0] // 4
        self.operands = (weight,)
        self.outs = (jax.ShapeDtypeStruct((self.quarter, weight.shape[1]), weight.dtype),)
        self.scratch = (pltpu.SemaphoreType.DMA((2,)),)

    def over(self):
        sems, at = self.room[0], span(lax.axis_index(FRAME), self.quarter)
        target = {SECTION: 1 - lax.axis_index(SECTION)}
        return remote(self.ins[0].at[at], self.out[0], sems.at[0], sems.at[1], target)

    def begin(self):
        self.over().start()

    def steps(self):
        return [lambda: self.over().wait()]


class ShareTask(Task):
    greets = (FRAME,)

    def __init__(self, grad):
        rows, width = grad.shape
        self.share = rows // 4
        self.far = isinstance(grad, jax.Array)
        self.operands = (grad,) if self.far else ()
        piece = (self.share, width)
        self.outs = (jax.ShapeDtypeStruct(piece, jnp.bfloat16),)
        self.scratch = (
            pltpu.VMEM((2,) + piece, jnp.bfloat16),
            pltpu.VMEM((2,) + piece, jnp.bfloat16),
            pltpu.SemaphoreType.DMA((3,)),
            pltpu.SemaphoreType.DMA((3,)),
        )
        if self.far:
            self.scratch += (pltpu.VMEM((2,) + piece, jnp.bfloat16), pltpu.SemaphoreType.DMA((2,)))

    def within(self):
        landing, _, send_sems, recv_sems, *here = self.room
        me = lax.axis_index(FRAME)
        other = frame_partners()[0]
        side = lax.div(me, 2)
        copies = []
        for k, to_side in enumerate((1 - side, side)):
            given = 2 * to_side + lax.rem(other, 2)
            kept = 2 * to_side + lax.rem(me, 2)
            copies.append(
                remote(
                    self.ins[0].at[span(given, self.share)],
                    landing.at[k],
                    send_sems.at[k],
                    recv_sems.at[k],
                    {FRAME: other},
                )
            )
            if self.far:
                own, sems = here[:2]
                source = self.ins[0].at[span(kept, self.share)]
                copies.append(pltpu.make_async_copy(source, own.at[k], sems.at[k]))
        return copies

    def over(self):
        crossing, send_sems, recv_sems = self.room[1:4]
        target = {FRAME: frame_partners()[1]}
        return remote(crossing.at[0], crossing.at[1], send_sems.at[2], recv_sems.at[2], target)

    def chip_sum(self, k):
        me = lax.axis_index(FRAME)
        if self.far:
            own = self.room[4][k]
        else:
            side = lax.div(me, 2) if k else 1 - lax.div(me, 2)
            own = self.ins[0][span(2 * side + lax.rem(me, 2), self.share), :]
        return own.astype(jnp.float32) + self.room[0][k].astype(jnp.float32)

    def begin(self):
        for copy in self.within():
            copy.start()

    def middle(self):
        for copy in self.within():
            copy.wait()
        self.room[1][0] = self.chip_sum(0).astype(jnp.bfloat16)
        self.over().start()

    def steps(self):
        def end():
            self.over().wait()
            total = self.chip_sum(1) + self.room[1][1].astype(jnp.float32)
            self.out[0][...] = total.astype(jnp.bfloat16)

        return [end]


class ShareCrossTask(ShareTask):
    greets = (FRAME, SECTION)
    late = True

    def __init__(self, grad, later):
        super().__init__(grad)
        self.operands = (later,)
        self.base = len(self.scratch)
        self.outs = (jax.ShapeDtypeStruct(later.shape, jnp.float32),)
        self.scratch += (pltpu.VMEM((3,) + later.shape, jnp.bfloat16), pltpu.SemaphoreType.DMA((3,)))

    def crossing(self, which):
        parts, sems = self.room[self.base :]
        target = {SECTION: 1 - lax.axis_index(SECTION)}
        later = self.far_ins[0]
        over = remote(parts.at[0] if which else later, parts.at[1], sems.at[0], sems.at[1], target)
        return over, pltpu.make_async_copy(later, parts.at[2], sems.at[2])

    def send(self):
        parts = self.room[self.base]
        section = lax.axis_index(SECTION)
        self.over().wait()
        total = self.chip_sum(1) + self.room[1][1].astype(jnp.float32)
        parts[0] = total.astype(jnp.bfloat16)
        for which in (0, 1):

            @pl.when(section == which)
            def _():
                over, stay = self.crossing(which)
                over.start()
                if which:
                    stay.start()

    def steps(self):
        parts = self.room[self.base]
        section = lax.axis_index(SECTION)

        def end():
            over, stay = self.crossing(1)
            over.wait()
            came = parts[1].astype(jnp.float32)

            @pl.when(section == 0)
            def _():
                self.out[0][...] = parts[0].astype(jnp.float32) + came

            @pl.when(section == 1)
            def _():
                stay.wait()
                self.out[0][...] = parts[2].astype(jnp.float32) + came

        first = (lambda: None) if self.hooked else self.send
        return [first, lambda: None, lambda: None, end]


class StatesTask(ShareTask):
    greets = (FRAME, SECTION)
    out_in_vmem = True

    def __init__(self, grad, later):
        super().__init__(grad)
        self.operands = (grad, later)
        self.base = len(self.scratch)
        self.outs = ()
        shape = (2,) + later.shape
        self.scratch += (pltpu.VMEM(shape, jnp.bfloat16), pltpu.VMEM(later.shape, jnp.bfloat16))
        self.scratch += (pltpu.SemaphoreType.DMA((3,)),)

    @property
    def both(self):
        return self.room[self.base]

    def crossing(self, which):
        both, total, sems = self.room[self.base :]
        later, place = self.ins[1], both.at[which]
        over = remote(total if which else later, place, sems.at[0], sems.at[1], {SECTION: 1 - which})
        return over, pltpu.make_async_copy(later, place, sems.at[2])

    def cross(self):
        self.over().wait()
        both, total, _ = self.room[self.base :]
        total[...] = (self.chip_sum(1) + self.room[1][1].astype(jnp.float32)).astype(jnp.bfloat16)
        section = lax.axis_index(SECTION)
        for which in (0, 1):

            @pl.when(section == which)
            def _():
                over, stay = self.crossing(which)
                over.start()
                if which:
                    stay.start()
                else:
                    both[0] = total[...]

    def arrive(self):
        section = lax.axis_index(SECTION)
        for which in (0, 1):

            @pl.when(section == which)
            def _():
                over, stay = self.crossing(which)
                over.wait()
                if which:
                    stay.wait()

    def steps(self):
        return []


class BothTask(Task):
    out_in_vmem = False
    greets = (SECTION,)

    def __init__(self, first, second):
        self.operands = (first, second)
        self.outs = (jax.ShapeDtypeStruct((2,) + first.shape, first.dtype),)
        self.scratch = (pltpu.SemaphoreType.DMA((3,)),)

    def copies(self, given, kept):
        (sems,) = self.room
        section = lax.axis_index(SECTION)
        place = self.out[0].at[section]
        over = remote(self.ins[given], place, sems.at[0], sems.at[1], {SECTION: 1 - section})
        return over, pltpu.make_async_copy(self.ins[kept], place, sems.at[2])

    def begin(self):
        section = lax.axis_index(SECTION)
        for which in (0, 1):

            @pl.when(section == which)
            def _():
                for copy in self.copies(1 - which, which):
                    copy.start()

    def steps(self):
        def end():
            for copy in self.copies(0, 1):
                copy.wait()

        return [end]


class CrossTask(Task):
    greets = (SECTION,)

    def __init__(self, first, second, added):
        self.operands = (first, second)
        self.added = added
        self.out_in_vmem = added
        shape = first.shape
        if added:
            self.outs = (jax.ShapeDtypeStruct(shape, jnp.float32),)
            self.scratch = (pltpu.VMEM(shape, jnp.bfloat16),) * 2 + (pltpu.SemaphoreType.DMA((3,)),)
        else:
            self.outs = (jax.ShapeDtypeStruct(shape, first.dtype),)
            self.scratch = (pltpu.SemaphoreType.DMA((2,)),)

    def copies(self, given, kept):
        sems = self.room[-1]
        landing = self.room[0] if self.added else self.out[0]
        target = {SECTION: 1 - lax.axis_index(SECTION)}
        copies = [remote(self.ins[given], landing, sems.at[0], sems.at[1], target)]
        if self.added:
            copies.append(pltpu.make_async_copy(self.ins[kept], self.room[1], sems.at[2]))
        return copies

    def begin(self):
        section = lax.axis_index(SECTION)
        for which in (0, 1):

            @pl.when(section == which)
            def _():
                for copy in self.copies(1 - which, which):
                    copy.start()

    def steps(self):
        def end():
            for copy in self.copies(0, 1):
                copy.wait()
            if self.added:
                self.out[0][...] = self.room[0][...].astype(jnp.float32) + self.room[1][...].astype(
                    jnp.float32
                )

        return [lambda: None, lambda: None, end]


class TextTask(Task):
    out_in_vmem = False
    greets = (SECTION, FRAME)
    late = True

    def __init__(self, states):
        micros, rows, width = states.shape
        self.outs = (jax.ShapeDtypeStruct((2, 4, rows, width), states.dtype),)
        self.scratch = (pltpu.SemaphoreType.DMA((3,)),) + (pltpu.SemaphoreType.DMA((2, 3)),) * 2

    def place(self, layer):
        return self.out[0].at[layer, lax.axis_index(FRAME)]

    def over(self):
        sems, section = self.room[0], lax.axis_index(SECTION)
        source = self.ins[0].at[1 - section]
        return remote(source, self.place(section), sems.at[0], sems.at[1], {SECTION: 1 - section})

    def stay(self):
        section = lax.axis_index(SECTION)
        return pltpu.make_async_copy(self.ins[0].at[section], self.place(section), self.room[0].at[2])

    def spread(self, far):
        section = lax.axis_index(SECTION)
        layer = 1 - section if far else section
        source = self.place(layer) if far else self.ins[0].at[section]
        pair = self.room[1 + far]
        return [
            remote(source, self.place(layer), pair.at[0, k], pair.at[1, k], {FRAME: other})
            for k, other in enumerate(frame_partners())
        ]

    def begin(self):
        for copy in [self.over(), self.stay()] + self.spread(0):
            copy.start()

    def steps(self):
        def first():
            self.over().wait_recv()
            for copy in self.spread(1):
                copy.start()

        def second():
            self.over().wait_send()
            self.stay().wait()
            for copy in self.spread(0) + self.spread(1):
                copy.wait()

        return [first, second]


class TotalTask(Task):
    greets = (SECTION, LINE)

    late = True

    def __init__(self, part):
        rows, width = part.shape
        self.share = rows // 4
        self.outs = (jax.ShapeDtypeStruct((rows, width), jnp.bfloat16),)
        piece = (self.share, width)
        self.scratch = (
            pltpu.VMEM((4,) + piece, jnp.bfloat16),
            pltpu.VMEM((2,) + piece, jnp.bfloat16),
            pltpu.SemaphoreType.DMA((4,)),
            pltpu.SemaphoreType.DMA((4,)),
            pltpu.SemaphoreType.DMA((2,)),
            pltpu.SemaphoreType.DMA((4,)),
            pltpu.SemaphoreType.DMA((4,)),
        )

    def partners(self):
        me = lax.axis_index(LINE)
        return [lax.rem(me + by, 4) for by in (1, 2, 3)]

    def spread(self):
        landing, _, send_sems, recv_sems = self.room[:4]
        me = lax.axis_index(LINE)
        away = [
            remote(
                self.ins[0].at[span(partner, self.share)],
                landing.at[by],
                send_sems.at[by],
                recv_sems.at[by],
                {LINE: partner},
            )
            for by, partner in enumerate(self.partners(), 1)
        ]
        stay = pltpu.make_async_copy(self.ins[0].at[span(me, self.share)], landing.at[0], send_sems.at[0])
        return away + [stay]

    def over(self):
        sums, sems = self.room[1], self.room[4]
        target = {SECTION: 1 - lax.axis_index(SECTION)}
        return remote(sums.at[0], sums.at[1], sems.at[0], sems.at[1], target)

    def gather(self):
        send_sems, recv_sems = self.room[5:]
        mine = self.out[0].at[span(lax.axis_index(LINE), self.share)]
        return [
            remote(mine, mine, send_sems.at[by], recv_sems.at[by], {LINE: partner})
            for by, partner in enumerate(self.partners(), 1)
        ]

    def begin(self):
        for copy in self.spread():
            copy.start()

    def sum_first(self):
        landing, sums = self.room[:2]
        for copy in self.spread():
            copy.wait()
        total = landing[0].astype(jnp.float32)
        for by in (1, 2, 3):
            total = total + landing[by].astype(jnp.float32)
        sums[0] = total.astype(jnp.bfloat16)
        self.over().start()

    def steps(self):
        sums = self.room[1]

        def second():
            self.over().wait()
            total = sums[0].astype(jnp.float32) + sums[1].astype(jnp.float32)
            self.out[0][span(lax.axis_index(LINE), self.share), :] = total.astype(jnp.bfloat16)
            for copy in self.gather():
                copy.start()

        def third():
            for copy in self.gather():
                copy.wait()

        return [second, third]


class VectorTask(Task):
    greets = (SECTION, FRAME)
    late = True

    def __init__(self, grads):
        shape = grads.shape[1:]
        self.outs = (jax.ShapeDtypeStruct(shape, jnp.float32),)
        self.scratch = (
            pltpu.VMEM((4,) + grads.shape, jnp.float32),
            pltpu.VMEM((3,) + shape, jnp.float32),
            pltpu.SemaphoreType.DMA((4,)),
            pltpu.SemaphoreType.DMA((4,)),
            pltpu.SemaphoreType.DMA((2,)),
        )

    def spread(self):
        landing, _, send_sems, recv_sems, _ = self.room
        away = [
            remote(self.ins[0], landing.at[k], send_sems.at[k], recv_sems.at[k], {FRAME: partner})
            for k, partner in enumerate(frame_partners(), 1)
        ]
        return away + [pltpu.make_async_copy(self.ins[0], landing.at[0], send_sems.at[0])]

    def over(self):
        sums, sems = self.room[1], self.room[4]
        target = {SECTION: 1 - lax.axis_index(SECTION)}
        return remote(sums.at[0], sums.at[1], sems.at[0], sems.at[1], target)

    def begin(self):
        for copy in self.spread():
            copy.start()

    def steps(self):
        landing, sums = self.room[:2]
        section = lax.axis_index(SECTION)

        def first():
            for copy in self.spread():
                copy.wait()
            total = [
                (landing[0, layer] + landing[1, layer]) + (landing[2, layer] + landing[3, layer])
                for layer in (0, 1)
            ]
            for which in (0, 1):

                @pl.when(section == which)
                def _():
                    sums[0] = total[1 - which]
                    sums[2] = total[which]

            self.over().start()

        def second():
            self.over().wait()
            self.out[0][...] = sums[2] + sums[1]

        return [first, second]


def greet(kinds):
    barrier = pltpu.get_barrier_semaphore()
    section, head, frame = (lax.axis_index(a) for a in (SECTION, LINE, FRAME))
    targets = []
    if FRAME in kinds:
        targets += [{FRAME: other} for other in frame_partners()]
    if SECTION in kinds:
        targets.append({SECTION: 1 - section})
    if BOTH in kinds:
        targets += [{SECTION: 1 - section, FRAME: other} for other in frame_partners()]
    if LINE in kinds:
        targets += [{LINE: lax.rem(head + by, 4)} for by in (1, 2, 3)]
    for target in targets:
        pl.semaphore_signal(barrier, 1, device_id=target, device_id_type=MESH_IDS)
    if LINE_ONLY not in kinds or LINE in kinds:
        return lambda: pl.semaphore_wait(barrier, len(targets))

    for way in (-1, 1):
        other = head + way

        @pl.when((other >= 0) & (other < 4))
        def _():
            pl.semaphore_signal(barrier, 1, device_id={LINE: other}, device_id_type=MESH_IDS)

    is_end = (head == 0) | (head == 3)

    def wait():
        @pl.when(is_end)
        def _():
            pl.semaphore_wait(barrier, len(targets) + 1)

        @pl.when(jnp.logical_not(is_end))
        def _():
            pl.semaphore_wait(barrier, len(targets) + 2)

    return wait


def call(body, operands, outs, scratch, kinds, collective_id, tasks=(), in_vmem=True, end=None):
    whole, anywhere = pl.BlockSpec(memory_space=pltpu.VMEM), pl.BlockSpec(memory_space=pl.ANY)
    place = whole if in_vmem else anywhere
    in_specs, out_specs = [place] * len(operands), [place] * len(outs)
    operands, all_outs, scratch = list(operands), list(outs), list(scratch)
    counts = [(len(operands), len(outs), len(scratch))]
    kinds = set(kinds)
    for task in tasks:
        kinds |= set(task.greets)
        in_specs += [anywhere] * len(task.operands)
        out_specs += [whole if task.out_in_vmem else anywhere] * len(task.outs)
        operands += task.operands
        all_outs += task.outs
        scratch += task.scratch
        counts.append((len(task.operands), len(task.outs), len(task.scratch)))
    n_in, n_out = len(operands), len(all_outs)

    def kernel(*refs):
        groups = [list(refs[:n_in]), list(refs[n_in : n_in + n_out]), list(refs[n_in + n_out :])]
        bound = []
        for sizes in counts:
            bound.append([])
            for group, size in zip(groups, sizes):
                bound[-1].append(group[:size])
                del group[:size]
        for task, parts in zip(tasks, bound[1:]):
            task.bind(*parts)

        meet = greet(kinds)

        def ride():
            for task in tasks:
                if not task.late:
                    task.begin()

        def middle():
            for task in tasks:
                if not task.late:
                    task.middle()

        if body is None:
            meet()
            ride()
            middle()
        else:
            body(*bound[0], meet, ride, middle)
        queues = [task.steps() for task in tasks]
        while any(queues):
            for queue in queues:
                if queue:
                    queue.pop(0)()
        if end is not None:
            end()

    results = pl.pallas_call(
        kernel,
        out_shape=all_outs,
        in_specs=in_specs,
        out_specs=out_specs,
        scratch_shapes=scratch,
        compiler_params=pltpu.CompilerParams(
            collective_id=collective_id, has_side_effects=True, vmem_limit_bytes=VMEM_BYTES
        ),
    )(*operands)
    results = list(results)
    main, results = results[: len(outs)], results[len(outs) :]
    return main, results


def chunking(rows):
    return max(1, min(16, rows // 16))


def nt_product(left, right):
    return lax.dot_general(left, right, (((1,), (1,)), ((), ())), preferred_element_type=jnp.float32)


def plain_product(left, right):
    return jnp.dot(left, right, preferred_element_type=jnp.float32)


def norm_parts(v):
    average = jnp.mean(v, axis=-1, keepdims=True)
    centered = v - average
    inverse = lax.rsqrt(jnp.mean(centered * centered, axis=-1, keepdims=True) + EPS)
    return centered * inverse, inverse


class Held:
    def __init__(self, shape, dtype, sources=(), choose=None, stage=0, kept=False):
        self.shape, self.dtype = tuple(shape), dtype
        self.sources, self.choose, self.stage, self.kept = sources, choose, stage, kept
        self.ref = self.far = self.sem = None

    def copy_in(self, index=0):
        source = self.far[index]
        if self.choose == BY_SECTION:
            source = source.at[lax.axis_index(SECTION)]
        return pltpu.make_async_copy(source, self.ref, self.sem)

    def start_in(self):
        if not isinstance(self.choose, int):
            self.copy_in().start()
            return
        section = lax.axis_index(SECTION)

        @pl.when(section == self.choose)
        def _():
            self.copy_in(0).start()

        @pl.when(section != self.choose)
        def _():
            self.copy_in(1).start()

    def write(self, at, value):
        self.ref[at, :] = value
        if self.kept:
            pltpu.make_async_copy(self.ref.at[at], self.far[0].at[at], self.sem).start()

    def flush(self):
        pltpu.make_async_copy(self.ref, self.far[0], self.sem).start()

    def drain(self):
        pltpu.make_async_copy(self.ref, self.far[0], self.sem).wait()


class Build:
    def __init__(self):
        self.helds, self.extras, self.starts, self.finals = [], [], [], []

    def add(self, held):
        self.helds.append(held)
        return held

    def arg(self, array, stage, choose=None):
        shape = array.shape[1:] if choose == BY_SECTION else array.shape
        return self.add(Held(shape, array.dtype, (array,), choose, stage))

    def pick(self, pair, layer, stage):
        return self.add(Held(pair[0].shape, pair[0].dtype, tuple(pair), layer, stage))

    def out(self, shape, dtype):
        return self.add(Held(shape, dtype, kept=True))

    def temp(self, shape, dtype):
        return self.add(Held(shape, dtype))

    def extra(self, scratch):
        self.extras.append(scratch)
        return len(self.extras) - 1


class Stage:
    def __init__(self, rows, width):
        self.rows, self.width = rows, width
        self.begin = self.prepare = self.finish = self.after = None
        self.ends = []


class Chore:
    def __init__(self, build, stage, piece, each, left, right, flipped=False, later=None, wait=5):
        self.start, self.each, self.wait = (stage, piece), each, wait
        self.left, self.right, self.flipped = left, right, flipped
        columns = left.shape[0] if flipped else left.shape[1]
        self.units = columns // BLOCK
        self.product = build.temp((columns, right.shape[1]), jnp.bfloat16)
        self.task = ShareTask(self.product) if later is None else ShareCrossTask(self.product, later)
        self.task.late = True

    def make_all(self):
        def one(number, carry):
            self.unit(number)
            return carry

        lax.fori_loop(0, self.units, one, 0)
        self.task.ins = [self.product.ref]
        self.task.begin()

    def unit(self, number):
        at = span(number, BLOCK)
        right = self.right.ref[...].astype(jnp.bfloat16)
        if self.flipped:
            product = plain_product(self.left.ref[at, :], right)
        else:
            product = lax.dot_general(
                self.left.ref[:, at], right, (((0,), (0,)), ((), ())), preferred_element_type=jnp.float32
            )
        self.product.ref[at, :] = product.astype(jnp.bfloat16)

    def run(self, stage, pieces, piece):
        shift = (stage - self.start[0]) * pieces - self.start[1]
        steps = -(-self.units // self.each)

        def at_step(first, last, what):
            if shift >= last or shift + pieces <= first:
                return
            now = piece + shift

            @pl.when((now >= first) & (now < last))
            def _():
                what(now)

        def make(now):
            for more in range(self.each):
                self.unit(now * self.each + more)

        def begin(now):
            self.task.ins = [self.product.ref]
            self.task.begin()

        at_step(0, steps, make)
        at_step(steps, steps + 1, begin)
        at_step(steps + self.wait, steps + self.wait + 1, lambda now: self.task.middle())


def line_chain(stages, need, part, set_out, middle, chores, hooks):
    place = lax.axis_index(LINE)
    rows = stages[0].rows
    pieces = chunking(rows)
    step = rows // pieces
    per_block = max(1, min(BLOCK, rows) // step)
    lag = max(0, min(LAG, pieces - per_block))
    is_end = (place == 0) | (place == 3)
    inner = {LINE: jnp.where(place == 0, 1, 2)}
    outer = {LINE: jnp.where(place == 1, 0, 3)}
    peer = {LINE: 3 - place}

    def inwards(stage, piece):
        send, held, _, send_sems, recv_sems = stage.room[:5]
        at = span(piece, step)
        return remote(send.at[at], held.at[at], send_sems.at[piece], recv_sems.at[piece], inner)

    def crossing(stage, piece):
        send, _, across = stage.room[:3]
        send_sems, recv_sems = stage.room[5:7]
        at = span(piece, step)
        return remote(send.at[at], across.at[at], send_sems.at[piece], recv_sems.at[piece], peer)

    def outwards(stage, piece):
        held = stage.room[1]
        send_sems, recv_sems = stage.room[7:]
        at = span(piece, step)
        return remote(held.at[at], held.at[at], send_sems.at[piece], recv_sems.at[piece], outer)

    def hook(stage, piece, at_end):
        for run, *spots in hooks:
            index, when = spots[0 if at_end else 1]
            if stages[index] is stage:

                @pl.when(piece == when)
                def _():
                    run()

    def finish(stage, piece):
        stage.finish(span(piece, step), piece)
        if stage.after is not None:

            @pl.when(lax.rem(piece, per_block) == per_block - 1)
            def _():
                stage.after(lax.div(piece, per_block))

    def open_stage(index):
        need(index)
        if stages[index].begin is not None:
            stages[index].begin()

    def loop(first, last, step_of):
        def one(piece, carry):
            step_of(piece)
            return carry

        lax.fori_loop(first, last, one, 0)

    def chore(stage, piece):
        for one in chores:
            one.run(stages.index(stage), pieces, piece)

    @pl.when(is_end)
    def _():
        def beside(stage, piece):
            chore(stage, piece)
            hook(stage, piece, True)

        def take(stage, piece):
            outwards(stage, piece).wait_recv()
            finish(stage, piece)

        for index, stage in enumerate(stages):
            open_stage(index)

            def block_step(block):
                low, high = block * per_block, (block + 1) * per_block
                if index:
                    loop(low, high, lambda piece: take(stages[index - 1], piece))
                stage.room[0][span(block, per_block * step), :] = stage.prepare(block).astype(jnp.bfloat16)
                if index == 0:
                    pl.when(block == 0)(set_out)
                loop(low, high, lambda piece: inwards(stage, piece).start())
                loop(low, high, lambda piece: beside(stage, piece))
                if index == 0:

                    @pl.when(block == 1)
                    def _():
                        middle()

            loop(0, pieces // per_block, block_step)
        loop(0, pieces, lambda piece: take(stages[-1], piece))
        for stage in stages:
            loop(0, pieces, lambda piece: inwards(stage, piece).wait_send())

    @pl.when(jnp.logical_not(is_end))
    def _():
        def add(stage, piece):
            @pl.when(lax.rem(piece, per_block) == 0)
            def _():
                part[...] = stage.prepare(lax.div(piece, per_block))

            if stage is stages[0]:
                pl.when(piece == 0)(set_out)
            at = span(piece, step)
            send, held = stage.room[:2]
            inwards(stage, piece).wait_recv()
            own = part[span(lax.rem(piece, per_block), step), :]
            send[at, :] = (own + held[at, :].astype(jnp.float32)).astype(jnp.bfloat16)
            crossing(stage, piece).start()
            chore(stage, piece)
            hook(stage, piece, False)
            if stage is stages[0]:

                @pl.when(piece == 2 * per_block - 1)
                def _():
                    middle()

        def settle(stage, piece):
            at = span(piece, step)
            send, held, across = stage.room[:3]
            crossing(stage, piece).wait_recv()
            total = send[at, :].astype(jnp.float32) + across[at, :].astype(jnp.float32)
            held[at, :] = total.astype(jnp.bfloat16)
            outwards(stage, piece).start()
            finish(stage, piece)

        for index, stage in enumerate(stages):
            open_stage(index)

            def both(piece):
                add(stage, piece)

                @pl.when(piece >= lag)
                def _():
                    settle(stage, piece - lag)

                if index and lag:

                    @pl.when(piece < lag)
                    def _():
                        settle(stages[index - 1], pieces - lag + piece)

            loop(0, pieces, both)
        loop(pieces - lag, pieces, lambda piece: settle(stages[-1], piece))

        def drain(stage, piece):
            crossing(stage, piece).wait_send()
            outwards(stage, piece).wait_send()

        for stage in stages:
            loop(0, pieces, lambda piece: drain(stage, piece))

    for stage in stages:
        for end in stage.ends:
            end()


def run_build(build, body, kinds, collective_id, tasks):
    operands, outs, scratch = [], [], []
    for held in build.helds:
        operands += held.sources
        if held.kept:
            outs.append(jax.ShapeDtypeStruct(held.shape, held.dtype))
        scratch.append(pltpu.VMEM(held.shape, held.dtype))
    n_held = len(scratch)
    scratch += build.extras
    scratch.append(pltpu.SemaphoreType.DMA((n_held,)))
    reads = sorted((held for held in build.helds if held.sources), key=lambda held: held.stage)

    def need(stage):
        for held in reads:
            if held.stage == stage:
                held.copy_in().wait()

    def run(ins, outs, scratch, meet, ride, middle):
        ins, outs = list(ins), list(outs)
        sems = scratch[-1]
        for index, held in enumerate(build.helds):
            held.ref, held.sem = scratch[index], sems.at[index]
            held.far = [ins.pop(0) for _ in held.sources]
            if held.kept:
                held.far = [outs.pop(0)]
        build.bound = scratch[n_held:-1]
        for held in reads:
            held.start_in()
        for start in build.starts:
            start()
        body(need, meet, ride, middle)

    def end():
        for final in build.finals:
            final()
        for held in build.helds:
            if held.kept:
                held.drain()

    return call(run, operands, outs, scratch, kinds, collective_id, tasks, in_vmem=False, end=end)


def run_chain(
    build, stages, collective_id, tasks, kinds=(LINE_ONLY,), chores=(), hooks=(), then=None, first=None, ahead=0, last=()
):
    slots = []
    for stage in stages:
        pieces = chunking(stage.rows)
        room = [pltpu.VMEM((stage.rows, stage.width), jnp.bfloat16)] * 3
        room += [pltpu.SemaphoreType.DMA((pieces,))] * 6
        slots.append([build.extra(scratch) for scratch in room])
    part = build.extra(pltpu.VMEM((min(BLOCK, stages[0].rows), stages[0].width), jnp.float32))

    def body(need, meet, ride, middle):
        for stage, places in zip(stages, slots):
            stage.room = [build.bound[place] for place in places]
        def set_out():
            meet()
            ride()

        def nothing():
            pass

        go_on = middle
        if first is not None:
            first(need, meet, ride, middle)
            set_out = go_on = nothing
        line_chain(
            stages, lambda index: need(index + ahead), build.bound[part], set_out, go_on, chores, hooks
        )
        if then is not None:
            then(need)

    tasks = list(tasks) + [one.task for one in chores] + list(last)
    return run_build(build, body, kinds, collective_id, tasks)


def scaled_rows(standard, gains, row):
    return (standard * gains.ref[row : row + 1] + gains.ref[row + 1 : row + 2]).astype(jnp.bfloat16)


def residual_norm(build, stage, base, gains, row, mode):
    shape = (stage.rows, stage.width)
    result = build.temp(shape, jnp.float32) if mode == NORM else None
    normed = build.out(shape, jnp.bfloat16) if mode != END else None
    low = build.out(shape, jnp.bfloat16)

    def finish(at, piece):
        value = base.ref[at, :].astype(jnp.float32) + stage.room[1][at, :].astype(jnp.float32)
        rounded = value.astype(jnp.bfloat16)
        low.write(at, rounded)
        if mode == NORM:
            result.write(at, value)
        if mode == NEXT:
            value = rounded.astype(jnp.float32)
        if mode != END:
            standard, _ = norm_parts(value)
            normed.write(at, scaled_rows(standard, gains, row))

    stage.finish = finish
    return result, normed


def gain_rows(build, vectors, layer, index):
    if isinstance(vectors, tuple):
        return build.pick(vectors, layer, index)
    return build.arg(vectors, index)


def vector_rows(build, width):
    grads = build.out((8, width), jnp.float32)

    def clear():
        grads.ref[...] = jnp.zeros(grads.shape, jnp.float32)

    build.starts.append(clear)
    build.finals.append(grads.flush)
    return grads


def self_out_stage(build, index, layer, attended_t, weight, base):
    rows, width = base.shape
    stage = Stage(rows, width)
    flipped, matrix = build.arg(attended_t, index), build.pick(weight, layer, index)
    left = build.temp(attended_t.shape[::-1], jnp.bfloat16)

    def begin():
        left.ref[...] = flipped.ref[...].T

    def prepare(number):
        return plain_product(left.ref[span(number, min(BLOCK, rows)), :], matrix.ref[...])

    stage.begin, stage.prepare = begin, prepare
    return stage


def text_mask(states, seg):
    item = lax.rem(lax.div(lax.broadcasted_iota(jnp.int32, (states, 1), 0), TEXT // 4), ITEMS)
    return item == seg


def cross_stage(build, index, layer, normed, states, seg, into, out_of):
    rows, width = normed.shape
    stage = Stage(rows, width)
    states, seg = build.arg(states, index), build.arg(seg, index)
    columns, block = states.shape[1] // 2, min(BLOCK, rows)
    if not isinstance(into, WeightTask):
        into, out_of = build.pick(into, layer, index), build.pick(out_of, layer, index)
    queries = build.out((rows, columns), jnp.bfloat16)
    left = build.out((rows, columns), jnp.bfloat16)
    values_t = build.temp((columns, states.shape[0]), jnp.bfloat16)

    def begin():
        values_t.ref[...] = states.ref[:, columns:].T

    def prepare(number):
        at = span(number, block)
        query = plain_product(normed.ref[at, :], into.ref[...]).astype(jnp.bfloat16)
        queries.write(at, query)
        query_t = query.T
        allowed = text_mask(states.shape[0], seg.ref[:, at])
        mixed = []
        for head in range(columns // HEAD):
            cols = slice(head * HEAD, (head + 1) * HEAD)
            scores = plain_product(states.ref[:, cols], query_t[cols, :]) * HEAD ** (-0.5)
            scores = jnp.where(allowed, scores, masked_score)
            e = jnp.exp(scores - jnp.max(scores, axis=0, keepdims=True))
            total = jnp.sum(e, axis=0, keepdims=True)
            value = plain_product(values_t.ref[cols, :], e.astype(jnp.bfloat16))
            mixed.append((value * (1.0 / total)).astype(jnp.bfloat16))
        mixed = jnp.concatenate(mixed, axis=0).T
        left.write(at, mixed)
        return plain_product(mixed, out_of.ref[...])

    stage.begin, stage.prepare = begin, prepare
    return stage


def feed_stage(build, index, layer, normed, into, out_of):
    rows, width = normed.shape
    stage = Stage(rows, width)
    block = min(BLOCK, rows)
    if isinstance(into, WeightTask):
        hidden = into.operands[0].shape[1]
    else:
        hidden = into[0].shape[1]
        into, out_of = build.pick(into, layer, index), build.pick(out_of, layer, index)
    before = build.out((rows, hidden), jnp.bfloat16)
    left = build.out((rows, hidden), jnp.bfloat16)

    def prepare(number):
        at = span(number, block)
        u = plain_product(normed.ref[at, :], into.ref[...])
        before.write(at, u.astype(jnp.bfloat16))
        active = (0.5 * u * (1.0 + lax.erf(u * inv_sqrt_two))).astype(jnp.bfloat16)
        left.write(at, active)
        return plain_product(active, out_of.ref[...])

    stage.prepare = prepare
    return stage


def norm_backward(build, index, stage, value, gains, row, grads, upstream, feeds, spare=None):
    shape = (stage.rows, stage.width)
    pieces = chunking(stage.rows)
    value = build.arg(value, index, BY_SECTION if value.ndim == 3 else None)
    result = build.temp(shape, jnp.float32) if feeds else None
    low = build.out(shape, jnp.bfloat16)
    parts = build.extra(pltpu.VMEM((2, pieces, 1, stage.width), jnp.float32))
    if spare is not None:
        spare = build.arg(spare, index)
        both = build.out((2,) + shape, jnp.bfloat16)
        sems = build.extra(pltpu.SemaphoreType.DMA((2, pieces)))

    def over(at, piece, source):
        target = {SECTION: 1 - lax.axis_index(SECTION)}
        pair = build.bound[sems]
        landing = both.ref.at[lax.axis_index(SECTION), at]
        return remote(source.ref.at[at], landing, pair.at[0, piece], pair.at[1, piece], target)

    def finish(at, piece):
        grad = stage.room[1][at, :].astype(jnp.float32)
        standard, inverse = norm_parts(value.ref[at, :].astype(jnp.float32))
        scaled = grad * gains.ref[row : row + 1]
        through = inverse * (
            scaled
            - jnp.mean(scaled, axis=-1, keepdims=True)
            - standard * jnp.mean(scaled * standard, axis=-1, keepdims=True)
        )
        total = through + upstream.ref[at, :].astype(jnp.float32)
        if feeds:
            result.write(at, total)
        low.write(at, total.astype(jnp.bfloat16))
        build.bound[parts][0, piece] = jnp.sum(grad * standard, axis=0, keepdims=True)
        build.bound[parts][1, piece] = jnp.sum(grad, axis=0, keepdims=True)
        if spare is not None:
            section = lax.axis_index(SECTION)

            @pl.when(section == 0)
            def _():
                both.ref[0, at, :] = low.ref[at, :]
                over(at, piece, spare).start()

            @pl.when(section == 1)
            def _():
                both.ref[1, at, :] = spare.ref[at, :]
                over(at, piece, low).start()

    def end():
        grads.ref[row : row + 1] = jnp.sum(build.bound[parts][0], axis=0)
        grads.ref[row + 1 : row + 2] = jnp.sum(build.bound[parts][1], axis=0)

    def settle():
        def one(piece, carry):
            over(span(piece, stage.rows // pieces), piece, low).wait()
            return carry

        lax.fori_loop(0, pieces, one, 0)
        both.flush()

    if spare is not None:
        build.finals.append(settle)
    stage.finish, stage.value = finish, value
    stage.ends.append(end)
    return result, low


def feed_back_stage(build, index, layer, grad_out, before, out_of, into):
    rows, width = grad_out.shape
    stage = Stage(rows, width)
    hidden, block = out_of[0].shape[0], min(BLOCK, rows)
    before = build.arg(before, index)
    out_of, into = build.pick(out_of, layer, index), build.pick(into, layer, index)
    left = build.out((rows, hidden), jnp.bfloat16)

    def prepare(number):
        at = span(number, block)
        grad = nt_product(grad_out.ref[at, :].astype(jnp.bfloat16), out_of.ref[...])
        u = before.ref[at, :].astype(jnp.float32)
        slope = 0.5 * (1.0 + lax.erf(u * inv_sqrt_two)) + u * jnp.exp(-0.5 * u * u) * inv_sqrt_tau
        grad = (grad * slope).astype(jnp.bfloat16)
        left.write(at, grad)
        return nt_product(grad, into.ref[...])

    stage.prepare, stage.left = prepare, left
    return stage


def cross_back_stage(build, index, layer, grad_low, queries, states, seg, out_of, into):
    rows, width = grad_low.shape
    stage = Stage(rows, width)
    columns, block = out_of[0].shape[0], min(BLOCK, rows)
    queries, states, seg = (build.arg(array, index) for array in (queries, states, seg))
    out_of, into = build.pick(out_of, layer, index), build.pick(into, layer, index)
    left = build.out((rows, columns), jnp.bfloat16)
    state_grads = build.out(states.shape, jnp.bfloat16)
    keys_t = build.temp((columns, states.shape[0]), jnp.bfloat16)
    sums = build.temp(states.shape, jnp.float32)
    scale = HEAD ** (-0.5)

    def begin():
        keys_t.ref[...] = states.ref[:, :columns].T
        sums.ref[...] = jnp.zeros(sums.shape, jnp.float32)

    def prepare(number):
        at = span(number, block)
        grad = nt_product(grad_low.ref[at, :], out_of.ref[...]).astype(jnp.bfloat16)
        query = queries.ref[at, :]
        grad_t, query_t = grad.T, query.T
        allowed = text_mask(states.shape[0], seg.ref[:, at])
        query_grads = []
        for head in range(columns // HEAD):
            cols = slice(head * HEAD, (head + 1) * HEAD)
            more = slice(columns + head * HEAD, columns + (head + 1) * HEAD)
            scores = plain_product(states.ref[:, cols], query_t[cols, :]) * scale
            scores = jnp.where(allowed, scores, masked_score)
            e = jnp.exp(scores - jnp.max(scores, axis=0, keepdims=True))
            p = e * (1.0 / jnp.sum(e, axis=0, keepdims=True))
            slope = plain_product(states.ref[:, more], grad_t[cols, :])
            weighted = p * slope
            ds = (weighted - p * jnp.sum(weighted, axis=0, keepdims=True)).astype(jnp.bfloat16)
            query_grads.append((plain_product(keys_t.ref[cols, :], ds) * scale).astype(jnp.bfloat16))
            sums.ref[:, cols] += plain_product(ds, query[:, cols]) * scale
            sums.ref[:, more] += plain_product(p.astype(jnp.bfloat16), grad[:, cols])
        query_grads = jnp.concatenate(query_grads, axis=0).T
        left.write(at, query_grads)
        return nt_product(query_grads, into.ref[...])

    def end():
        state_grads.write(slice(0, states.shape[0]), sums.ref[...].astype(jnp.bfloat16))

    stage.begin, stage.prepare, stage.state_grads = begin, prepare, state_grads
    stage.ends.append(end)
    return stage


def self_in_stage(build, index, layer, grads_t, weights, width):
    columns, rows = grads_t.shape
    stage = Stage(rows, width)
    part = columns // 3
    flipped = grads_t if isinstance(grads_t, Held) else build.arg(grads_t, index)
    matrices = [build.pick(weight, layer, index) for weight in weights]
    left = build.temp((rows, columns), jnp.bfloat16)

    def begin():
        for number in range(3):
            heads = [
                flipped.ref[(3 * head + number) * HEAD : (3 * head + number + 1) * HEAD, :]
                for head in range(part // HEAD)
            ]
            left.ref[:, number * part : (number + 1) * part] = jnp.concatenate(heads, axis=0).T

    def prepare(number):
        at = span(number, min(BLOCK, rows))
        total = jnp.zeros((min(BLOCK, rows), width), jnp.float32)
        for number, matrix in enumerate(matrices):
            total = total + nt_product(left.ref[at, number * part : (number + 1) * part], matrix.ref[...])
        return total

    stage.begin, stage.prepare = begin, prepare
    stage.left = left
    return stage


def forward_chain(
    layer, attended_t, entering, states, seg, vectors, weights, collective_id, tasks=(), late=None, begins=None
):
    output, query, cross, expand, reduce = weights
    build = Build()
    gains = build.pick(vectors, layer, 0)
    base = build.arg(entering, 0, BY_SECTION if entering.ndim == 3 else None)
    first = self_out_stage(build, 0, layer, attended_t, output, base)
    middle, second_normed = residual_norm(build, first, base, gains, 2, NORM)
    second = cross_stage(build, 1, layer, second_normed, states, seg, query, cross)
    latter, third_normed = residual_norm(build, second, middle, gains, 4, NORM)
    third = feed_stage(build, 2, layer, third_normed, expand, reduce)
    after = None if late is None else build.pick(vectors, 1 - layer, 2)
    _, next_normed = residual_norm(build, third, latter, after, 0, END if late is None else NEXT)
    hooks, then, kinds = [], None, (LINE_ONLY,)
    if isinstance(expand, WeightTask):
        hooks = [
            (expand.first_hop, (1, 0), (0, 9)),
            (reduce.first_hop, (1, 5), (1, 0)),
            (expand.second_hop, (1, 9), (1, 2)),
            (reduce.second_hop, (1, 15), (1, 9)),
        ]
        for one in late:
            hooks += [(one.first_hop, (2, 0), (1, 8)), (one.second_hop, (2, 8), (2, 0))]
        start_second = second.begin

        def begin_second():
            query.second_hop()
            cross.second_hop()
            query.arrive()
            cross.arrive()
            start_second()

        def begin_third():
            expand.arrive()
            reduce.arrive()

        second.begin, third.begin = begin_second, begin_third
        attention = Attention(build, third.rows, begins, 2)
        sender = BlockSender(build, third.rows, 3 * HEAD, attention.heads_t)

        def project(block):
            @pl.when(block == 0)
            def _():
                for one in late:
                    one.arrive()

            lanes = span(block, BLOCK)
            turned_parts(next_normed.ref[lanes, :], late, sender.own, (), lanes)
            sender.send(block)

        def then(need):
            sender.wait()
            attention.run()

        third.after = project
        kinds = (LINE_ONLY, FRAME)
    return run_chain(build, [first, second, third], collective_id, tasks, kinds, hooks=hooks, then=then)


def add_backward(build, index, layer, arriving, saved, states, seg, vectors, weights):
    _, query, cross, expand, reduce = weights
    middle, latter, third_normed, queries, before, hidden = saved
    gains, grads = gain_rows(build, vectors, layer, index), vector_rows(build, arriving.shape[1])
    first = feed_back_stage(build, index, layer, arriving, before, reduce, expand)
    grad_latter, grad_cross = norm_backward(build, index, first, latter, gains, 4, grads, arriving, True)
    second = cross_back_stage(build, index + 1, layer, grad_cross, queries, states, seg, cross, query)
    _, grad_self = norm_backward(
        build, index + 1, second, middle, gains, 2, grads, grad_latter, False
    )
    first_piece, each, wait = (12, 4, 3) if index else (0, 1, 5)
    chores = [
        Chore(build, index, first_piece, each, build.arg(hidden, index), arriving, wait=wait),
        Chore(build, index + 1, 0, each, build.arg(third_normed, index + 1), first.left, wait=wait),
    ]
    return [first, second], chores, grad_self, second.state_grads


def add_last(
    build, index, layer, grads_t, entering, vectors, grads, residual, weights, spare, products, later=None
):
    stage = self_in_stage(build, index, layer, grads_t, weights, residual.shape[1])
    stage.gains = gain_rows(build, vectors, layer, index)
    _, low = norm_backward(build, index, stage, entering, stage.gains, 0, grads, residual, False, spare)
    chores = []
    for number, (left, right) in enumerate(products):
        flipped = left is not None and left.shape[0] != residual.shape[0]
        if right is None:
            right = stage.left
        elif right is not residual:
            right = build.arg(right, index)
        more = None if later is None else later[number]
        if left is None:
            stage.normed = build.temp(residual.shape, jnp.bfloat16)
            chores.append(Chore(build, 0, 3, 1, stage.normed, right, False, more, 4))
        else:
            chores.append(Chore(build, 0, 0, 1, build.arg(left, index), right, flipped, more))
    return stage, low, chores


def backward_chain(layer, upstream, saved, states, seg, vectors, weights, heads_t, begins, collective_id, tasks):
    build = Build()
    arriving = build.arg(upstream, 0, BY_SECTION)
    stages, chores, grad_self, grad_states = add_backward(
        build, 0, layer, arriving, saved, states, seg, vectors, weights
    )
    output = build.pick(weights[0], layer, 1)
    attention = AttentionBack(build, stages[1].rows, heads_t, begins, 1)
    sender = BlockSender(build, stages[1].rows, HEAD, attention.grad_t)
    share = ShareTask(grad_states)
    share.late = True

    def project(block):
        lanes = span(block, BLOCK)
        turned_grads(grad_self.ref[lanes, :], output, sender.own, lanes)
        sender.send(block)

    def then(need):
        share.ins = [grad_states.ref]
        share.begin()
        attention.begin()
        sender.wait()
        attention.run(share.middle)

    stages[1].after = project
    kinds = (LINE_ONLY, FRAME)
    return run_chain(build, stages, collective_id, tasks + [share], kinds, chores, then=then)


def between_chain(layer, grads_t, entering, vectors, upstream, weights, products, backward, collective_id, tasks):
    build = Build()
    residual = build.arg(upstream, 0)
    products = [(left, residual if right is upstream else right) for left, right in products]
    grads = vector_rows(build, residual.shape[1])
    stage, low, chores = add_last(
        build, 0, layer, grads_t, entering, vectors, grads, residual, weights, None, products
    )
    stages, more, _, _ = add_backward(build, 1, layer - 1, low, *backward)
    return run_chain(build, [stage] + stages, collective_id, tasks, chores=chores + more)


def last_kernel(
    heads_t,
    grad_self,
    output,
    begins,
    inputs,
    vectors,
    weights,
    spare,
    products,
    later,
    states,
    text_local,
    text_weights,
    vector_grads,
    collective_id,
    tasks,
):
    rows, width = grad_self.shape
    build = Build()
    attention = AttentionBack(build, rows, heads_t, begins, 1)
    grad_low, output = build.arg(grad_self, 0), build.pick(output, 0, 0)
    own = build.temp((4, HEAD, rows), jnp.bfloat16)
    sems = build.extra(pltpu.SemaphoreType.DMA((2, 3)))
    products = [(left, grad_low if right is grad_self else right) for left, right in products]
    vector_grads = [build.arg(grads, 2) for grads in vector_grads]
    early = []
    for (left, right), share in zip(products[:3], later):
        flipped = left.shape[0] != rows
        right = right if right is grad_low else build.arg(right, 1)
        early.append(Chore(build, 0, 0, 1, build.arg(left, 1), right, flipped, share))
        early[-1].task.hooked = 1
    stage, _, chores = add_last(
        build, 2, 0, attention.out, inputs, vectors, vector_grads[1], grad_low, weights, spare, products[3:], later[3:]
    )
    text_local = build.arg(text_local, 2)
    text_weights = [build.arg(weight, 2) for weight in text_weights]
    columns = text_weights[0].shape[1]
    text_rows = build.temp((text_local.shape[0], 2 * columns), jnp.bfloat16)
    text_part = build.temp(text_local.shape, jnp.bfloat16)
    both_grads = build.temp((2, 8, width), jnp.float32)
    chores.append(Chore(build, 0, 10, 2, text_local, text_rows, wait=1))
    from_states, from_vectors, from_text = StatesTask(*states), VectorTask(both_grads), TotalTask(text_part)

    def make_normed():
        def one(number, carry):
            at = span(number, BLOCK)
            standard, _ = norm_parts(stage.value.ref[at, :].astype(jnp.float32))
            stage.normed.ref[at, :] = scaled_rows(standard, stage.gains, 0)
            return carry

        lax.fori_loop(0, rows // BLOCK, one, 0)

    def text_step():
        from_states.arrive()
        text_rows.ref[...] = jnp.concatenate([from_states.both[0], from_states.both[1]], axis=0)
        total = nt_product(text_rows.ref[:, :columns], text_weights[0].ref[...])
        total = total + nt_product(text_rows.ref[:, columns:], text_weights[1].ref[...])
        text_part.ref[...] = total.astype(jnp.bfloat16)
        from_text.ins = [text_part.ref]
        from_text.begin()

    def first(need, meet, ride, middle):
        me, grad_t = lax.axis_index(FRAME), attention.grad_t
        landing = grad_t.ref.at[:, span(me, rows)]
        arriving = to_frames(lambda g: own.ref.at[g], lambda f: landing, build.bound[sems])
        need(0)
        turned_grads(grad_low.ref[...], output, own, slice(0, rows))
        meet()
        for copy in arriving[::-1]:
            copy.start()
        ride()
        grad_t.ref[:, span(me, rows)] = own.ref[me]
        need(1)
        for one in early:
            one.make_all()
        attention.begin()
        for copy in arriving:
            copy.wait()

        def along():
            middle()
            for one in early:
                one.task.middle()

        attention.run(along)
        from_states.cross()
        for one in early:
            one.task.send()

    def then(need):
        from_text.sum_first()
        both_grads.ref[0] = vector_grads[1].ref[...]
        both_grads.ref[1] = vector_grads[0].ref[...]
        from_vectors.ins = [both_grads.ref]
        from_vectors.begin()

    tasks = [from_states] + list(tasks) + [one.task for one in early]
    return run_chain(
        build,
        [stage],
        collective_id,
        tasks,
        (LINE_ONLY, SECTION),
        chores,
        [(make_normed, (0, 2), (0, 2)), (text_step, (0, 9), (0, 9))],
        then,
        first,
        2,
        [from_vectors, from_text],
    )


def masked_scores(keys, query_t, begins, start):
    reach, block = keys.shape[0], query_t.shape[1]
    scores = plain_product(keys, query_t)
    key_pos = lax.broadcasted_iota(jnp.int32, (reach, 1), 0)
    query_pos = start + lax.broadcasted_iota(jnp.int32, (1, block), 1)
    allowed = (key_pos <= query_pos) & (key_pos >= begins)
    return jnp.where(allowed, scores * HEAD ** (-0.5), masked_score)


def to_frames(source, landing, sems):
    me = lax.axis_index(FRAME)
    return [
        remote(source(other), landing(me), sems.at[0, k], sems.at[1, k], {FRAME: other})
        for k, other in enumerate(frame_partners())
    ]


def turned_parts(normed, matrices, own, at, lanes):
    for part, matrix in enumerate(matrices):
        turned = plain_product(normed, matrix.ref[...]).astype(jnp.bfloat16).T
        for head in range(4):
            rows = slice(part * HEAD, (part + 1) * HEAD)
            own.ref[at + (head, rows, lanes)] = turned[head * HEAD : (head + 1) * HEAD, :]


class Attention:
    def __init__(self, build, rows, begins, stage):
        frames, width = 4, 3 * HEAD
        self.rows = rows
        self.begins = build.arg(begins, stage)
        self.heads_t = build.out((width, rows * frames), jnp.bfloat16)
        self.out = build.out((frames * HEAD, rows), jnp.bfloat16)
        self.keys = build.temp((rows * frames, HEAD), jnp.bfloat16)
        self.mixed_t = build.temp((frames, HEAD, rows), jnp.bfloat16)
        self.sems = build.extra(pltpu.SemaphoreType.DMA((2, frames - 1)))
        self.build = build

    def run(self, early=()):
        me, partners, rows = lax.axis_index(FRAME), frame_partners(), self.rows
        heads_t, keys, mixed_t, out = self.heads_t, self.keys, self.mixed_t, self.out
        block = min(2 * BLOCK, rows)
        leaving = to_frames(
            lambda g: mixed_t.ref.at[g], lambda f: out.ref.at[span(f, HEAD), :], self.build.bound[self.sems]
        )
        heads_t.flush()
        keys.ref[...] = heads_t.ref[HEAD : 2 * HEAD, :].T
        for target in range(4):
            if target == 3:
                for task in early:
                    task.first_hop()
            for start in range(target * rows, (target + 1) * rows, block):
                reach = start + block
                scores = masked_scores(
                    keys.ref[:reach, :],
                    heads_t.ref[:HEAD, start:reach],
                    self.begins.ref[:, start:reach],
                    start,
                )
                e = jnp.exp(scores - jnp.max(scores, axis=0, keepdims=True))
                total = jnp.sum(e, axis=0, keepdims=True)
                mixed = plain_product(heads_t.ref[2 * HEAD :, :reach], e.astype(jnp.bfloat16))
                at = start - target * rows
                mixed_t.ref[target, :, at : at + block] = (mixed * (1.0 / total)).astype(jnp.bfloat16)

            for copy, other in zip(leaving, partners):

                @pl.when(other == target)
                def _():
                    copy.start()

        out.ref[span(me, HEAD), :] = mixed_t.ref[me]
        for copy in leaving:
            copy.wait()
        out.flush()


class BlockSender:
    def __init__(self, build, rows, height, landing):
        self.rows, self.landing = rows, landing
        self.blocks = rows // BLOCK
        self.own = build.temp((4, height, rows), jnp.bfloat16)
        self.sems = build.extra(pltpu.SemaphoreType.DMA((2, 3, self.blocks)))
        self.build = build

    def copies(self, block):
        lanes, me = span(block, BLOCK), lax.axis_index(FRAME)
        place = self.landing.ref.at[:, span(me * self.blocks + block, BLOCK)]
        sems = self.build.bound[self.sems]
        return [
            remote(
                self.own.ref.at[other, :, lanes], place, sems.at[0, k, block], sems.at[1, k, block], {FRAME: other}
            )
            for k, other in enumerate(frame_partners())
        ]

    def send(self, block):
        me = lax.axis_index(FRAME)
        for copy in self.copies(block)[::-1]:
            copy.start()
        lanes = span(block, BLOCK)
        self.landing.ref[:, span(me * self.blocks + block, BLOCK)] = self.own.ref[me, :, lanes]

    def wait(self):
        def one(block, carry):
            for copy in self.copies(block):
                copy.wait()
            return carry

        lax.fori_loop(0, self.blocks, one, 0)


def first_attention(inputs, vectors, weights, begins, text, text_weights, collective_id, tasks, early):
    micros, rows, model = inputs.shape
    frames, width = 4, 3 * HEAD
    build = Build()
    inputs, vectors = build.arg(inputs, 0), build.arg(vectors, 0)
    matrices = [build.arg(weight, 0) for weight in weights]
    attention = Attention(build, rows, begins, 1)
    text, text_weights = build.arg(text, 1), [build.arg(weight, 1) for weight in text_weights]
    heads_t = attention.heads_t
    own = build.temp((2, frames, width, rows), jnp.bfloat16)
    columns = text_weights[0].shape[1]
    states = build.temp((micros, text.shape[0] // micros, 2 * columns), jnp.bfloat16)
    sems = build.extra(pltpu.SemaphoreType.DMA((2, frames - 1)))
    blocks = rows // BLOCK
    over_sems = build.extra(pltpu.SemaphoreType.DMA((2, frames, blocks)))
    from_text = TextTask(states)

    def project(micro, then):
        def one(number, carry):
            at = span(number, BLOCK)
            standard, _ = norm_parts(inputs.ref[micro, at, :].astype(jnp.float32))
            turned_parts(scaled_rows(standard, vectors, 0), matrices, own, (micro,), at)
            then(number)
            return carry

        lax.fori_loop(0, blocks, one, 0)

    def body(need, meet, ride, middle):
        me, section = lax.axis_index(FRAME), lax.axis_index(SECTION)
        landing = heads_t.ref.at[:, span(me, rows)]
        arriving = to_frames(lambda g: own.ref.at[0, g], lambda f: landing, build.bound[sems])
        pair = build.bound[over_sems]
        def over(block):
            place = heads_t.ref.at[:, span(me * blocks + block, BLOCK)]
            return [
                remote(
                    own.ref.at[1, g, :, span(block, BLOCK)],
                    place,
                    pair.at[0, k, block],
                    pair.at[1, k, block],
                    {SECTION: 1, FRAME: g},
                )
                for k, g in enumerate((me,) + frame_partners())
            ]

        def each(what):
            def one(block, carry):
                for copy in over(block):
                    what(copy)
                return carry

            lax.fori_loop(0, blocks, one, 0)

        def send(block):
            pl.when(block == 0)(meet)
            for copy in over(block):
                copy.start()

        need(0)

        @pl.when(section == 0)
        def _():
            project(1, send)
            project(0, lambda block: None)
            for copy in arriving[::-1]:
                copy.start()
            heads_t.ref[:, span(me, rows)] = own.ref[0, me]

        @pl.when(section == 1)
        def _():
            meet()

        need(1)
        for part, weight in enumerate(text_weights):
            made = plain_product(text.ref[...], weight.ref[...]).astype(jnp.bfloat16)
            for micro in range(micros):
                some = slice(micro * states.shape[1], (micro + 1) * states.shape[1])
                states.ref[micro, :, part * columns : (part + 1) * columns] = made[some, :]
        from_text.ins = [states.ref]
        from_text.begin()
        ride()

        @pl.when(section == 0)
        def _():
            for copy in arriving:
                copy.wait()
            each(lambda copy: copy.wait_send())

        @pl.when(section == 1)
        def _():
            each(lambda copy: copy.wait_recv())

        attention.run(early)

    return run_build(build, body, (FRAME, SECTION, BOTH), collective_id, tasks + [from_text])


class AttentionBack:
    def __init__(self, build, rows, heads_t, begins, stage):
        frames, width = 4, 3 * HEAD
        all_rows = rows * frames
        self.build, self.rows = build, rows
        self.heads_t, self.begins = build.arg(heads_t, stage), build.arg(begins, stage)
        self.out = build.out((frames * width, rows), jnp.bfloat16)
        self.grad_t = build.temp((HEAD, all_rows), jnp.bfloat16)
        self.columns = build.temp((4, all_rows, HEAD), jnp.bfloat16)
        self.key_sum, self.value_sum = (build.temp((all_rows, HEAD), jnp.float32) for _ in range(2))
        self.grads_t = build.temp((frames, width, rows), jnp.bfloat16)
        self.sems = build.extra(pltpu.SemaphoreType.DMA((2, frames - 1)))

    def begin(self):
        key_sum, value_sum = self.key_sum, self.value_sum
        key_sum.ref[...] = jnp.zeros(key_sum.shape, jnp.float32)
        value_sum.ref[...] = jnp.zeros(key_sum.shape, jnp.float32)
        for part in range(3):
            self.columns.ref[part] = self.heads_t.ref[part * HEAD : (part + 1) * HEAD, :].T

    def run(self, middle):
        rows, width, scale = self.rows, 3 * HEAD, HEAD ** (-0.5)
        me, partners = lax.axis_index(FRAME), frame_partners()
        heads_t, begins, grad_t, columns = self.heads_t, self.begins, self.grad_t, self.columns
        key_sum, value_sum, grads_t, out = self.key_sum, self.value_sum, self.grads_t, self.out
        block = min(2 * BLOCK, rows)
        leaving = to_frames(
            lambda g: grads_t.ref.at[g], lambda f: out.ref.at[span(f, width), :], self.build.bound[self.sems]
        )
        columns.ref[3] = grad_t.ref[...].T
        middle()
        for target in reversed(range(4)):
            for start in reversed(range(target * rows, (target + 1) * rows, block)):
                reach = start + block
                scores = masked_scores(
                    columns.ref[1, :reach, :],
                    heads_t.ref[:HEAD, start:reach],
                    begins.ref[:, start:reach],
                    start,
                )
                e = jnp.exp(scores - jnp.max(scores, axis=0, keepdims=True))
                p = e * (1.0 / jnp.sum(e, axis=0, keepdims=True))
                slope = plain_product(columns.ref[2, :reach, :], grad_t.ref[:, start:reach])
                weighted = p * slope
                ds = (weighted - p * jnp.sum(weighted, axis=0, keepdims=True)).astype(jnp.bfloat16)
                value_sum.ref[:reach, :] += plain_product(
                    p.astype(jnp.bfloat16), columns.ref[3, start:reach, :]
                )
                key_sum.ref[:reach, :] += plain_product(ds, columns.ref[0, start:reach, :])
                here = slice(start - target * rows, reach - target * rows)
                query_grad = plain_product(heads_t.ref[HEAD : 2 * HEAD, :reach], ds) * scale
                grads_t.ref[target, :HEAD, here] = query_grad.astype(jnp.bfloat16)
                key_grad = key_sum.ref[start:reach, :] * scale
                grads_t.ref[target, HEAD : 2 * HEAD, here] = key_grad.T.astype(jnp.bfloat16)
                grads_t.ref[target, 2 * HEAD :, here] = value_sum.ref[start:reach, :].T.astype(jnp.bfloat16)

            for copy, other in zip(leaving, partners):

                @pl.when(other == target)
                def _():
                    copy.start()

        out.ref[span(me, width), :] = grads_t.ref[me]
        for copy in leaving:
            copy.wait()
        out.flush()


def turned_grads(grad, weight, own, lanes):
    turned = nt_product(weight.ref[...], grad).astype(jnp.bfloat16)
    for head in range(4):
        own.ref[head, :, lanes] = turned[head * HEAD : (head + 1) * HEAD, :]


def matmul(left_side, right_side):
    return jnp.dot(left_side, right_side, preferred_element_type=jnp.float32)


def matmul_tn(left_side, right_side):
    return lax.dot_general(
        left_side, right_side, (((0,), (0,)), ((), ())), preferred_element_type=jnp.float32
    )


def matmul_nt(left_side, right_side):
    return lax.dot_general(
        left_side, right_side, (((1,), (1,)), ((), ())), preferred_element_type=jnp.float32
    )


def layer_norm(signal, gain_vec, shift_vec):
    average = jnp.mean(signal, axis=-1, keepdims=True)
    centered = signal - average
    variance = jnp.mean(centered * centered, axis=-1, keepdims=True)
    return centered * lax.rsqrt(variance + 1e-05) * gain_vec + shift_vec


def norm_back(signal, gain_vec, upstream):
    average = jnp.mean(signal, axis=-1, keepdims=True)
    centered = signal - average
    inverse = lax.rsqrt(jnp.mean(centered * centered, axis=-1, keepdims=True) + 1e-05)
    standard = centered * inverse
    scaled = upstream * gain_vec
    through = inverse * (
        scaled
        - jnp.mean(scaled, axis=-1, keepdims=True)
        - standard * jnp.mean(scaled * standard, axis=-1, keepdims=True)
    )
    return (through, jnp.sum(upstream * standard, axis=0), jnp.sum(upstream, axis=0))


def head_total(partial_sum):
    return lax.psum(partial_sum.astype(jnp.bfloat16), LINE).astype(jnp.float32)


def swapped(x):
    return lax.ppermute(x, SECTION, [(0, 1), (1, 0)])


def split_heads(matrix):
    return matrix.reshape(matrix.shape[0], matrix.shape[1] // HEAD, HEAD)


def softmax_rows(query, key_rows, allowed):
    logits = jnp.einsum(
        "qhd,khd->hqk",
        split_heads(query),
        split_heads(key_rows),
        preferred_element_type=jnp.float32,
    ) * HEAD ** (-0.5)
    logits = jnp.where(allowed[None], logits, masked_score)
    exponent = jnp.exp(logits - jnp.max(logits, axis=-1, keepdims=True))
    return exponent / jnp.sum(exponent, axis=-1, keepdims=True)


def attend(query, key_rows, value_rows, allowed):
    weights_low = softmax_rows(query, key_rows, allowed).astype(jnp.bfloat16)
    result = jnp.einsum(
        "hqk,khd->qhd", weights_low, split_heads(value_rows), preferred_element_type=jnp.float32
    )
    return result.reshape(query.shape).astype(jnp.bfloat16)


def attend_back(query, key_rows, value_rows, allowed, grad_out):
    probabilities = softmax_rows(query, key_rows, allowed)
    weights_low = probabilities.astype(jnp.bfloat16)
    grad_heads = split_heads(grad_out)
    grad_prob = jnp.einsum(
        "qhd,khd->hqk", grad_heads, split_heads(value_rows), preferred_element_type=jnp.float32
    )
    centre = jnp.sum(probabilities * grad_prob, axis=-1, keepdims=True)
    grad_logit = (probabilities * (grad_prob - centre)).astype(jnp.bfloat16)
    scale = HEAD ** (-0.5)
    grad_query = (
        jnp.einsum(
            "hqk,khd->qhd", grad_logit, split_heads(key_rows), preferred_element_type=jnp.float32
        )
        * scale
    )
    grad_keys = (
        jnp.einsum(
            "hqk,qhd->khd", grad_logit, split_heads(query), preferred_element_type=jnp.float32
        )
        * scale
    )
    grad_values = jnp.einsum(
        "hqk,qhd->khd", weights_low, grad_heads, preferred_element_type=jnp.float32
    )
    return (
        grad_query.reshape(query.shape),
        grad_keys.reshape(key_rows.shape),
        grad_values.reshape(value_rows.shape),
    )


def on_four_frames(inputs, lengths, text, cotangent, vector_args, matrix_args):
    section = lax.axis_index(SECTION)
    at_zero = section == 0
    frame_index = lax.axis_index(FRAME)
    micro_count, rows_dev, model_width = inputs.shape
    rows_all = rows_dev * 4
    (
        query_weight,
        key_weight,
        value_weight,
        output_weight,
        cross_query,
        cross_key,
        cross_value,
        cross_output,
        expand_weight,
        reduce_weight,
    ) = (w[0] for w in matrix_args)
    columns = query_weight.shape[1]

    def by_section(first, second):
        return jnp.where(at_zero, first, second)

    own_vectors = jnp.concatenate([*vector_args, jnp.zeros((2, model_width), jnp.float32)], axis=0)
    self_weights = (query_weight, key_weight, value_weight)
    text_local = text.reshape(-1, model_width)

    item_ends = jnp.cumsum(lax.dynamic_index_in_dim(lengths, section, 0, keepdims=False))
    passed = jnp.arange(rows_all, dtype=jnp.int32)[None, :] >= item_ends[:, None]
    begins = jnp.max(jnp.where(passed, item_ends[:, None], 0), axis=0, keepdims=True).astype(jnp.int32)
    seg = jnp.sum(passed.astype(jnp.int32), axis=0, keepdims=True)
    seg = lax.dynamic_slice_in_dim(seg, frame_index * rows_dev, rows_dev, 1)

    early = WeightTask(output_weight)
    early.hooked = 1
    others = (cross_query, cross_output, expand_weight, reduce_weight)
    (heads_t, attended_t), carried = first_attention(
        inputs,
        own_vectors,
        self_weights,
        begins,
        text_local,
        (cross_key, cross_value),
        1,
        [early, CrossTask(own_vectors, own_vectors, False)] + [QuarterTask(w) for w in others[:2]],
        [early],
    )
    vectors = (own_vectors, carried[1])
    selected = [by_section(*vectors), by_section(*vectors[::-1])]
    states = carried[4].reshape(2, -1, 2 * columns)
    coming = [WeightTask(w, 0, quarter) for w, quarter in zip(others, carried[2:4] + [None] * 2)]
    late = [WeightTask(w, 1) for w in self_weights]
    weights = [(output_weight, carried[0])]
    outs, carried = forward_chain(
        0,
        attended_t,
        inputs,
        states[0],
        seg,
        vectors,
        weights + coming,
        2,
        coming + late,
        late,
        begins,
    )
    weights += list(zip(others, carried))
    self_pairs = list(zip(self_weights, carried[4:]))
    def keep(entering, normed, heads_t, attended_t, outs):
        second_normed, middle, queries, cross_att, third_normed, latter, before, hidden = outs[:8]
        return (
            entering,
            normed,
            heads_t,
            attended_t,
            middle,
            second_normed,
            latter,
            third_normed,
            queries,
            cross_att,
            before,
            hidden,
        )

    saved = [keep(inputs, None, heads_t, attended_t, outs)]
    normed, entering, heads_t, attended_t = outs[8:]
    outs, _ = forward_chain(
        1, attended_t, entering, states[1], seg, vectors, weights, 3
    )
    saved.append(keep(entering, normed, heads_t, attended_t, outs))
    result_low = outs[8]

    shares = [{}, {}]

    def crossing(*names):
        return [CrossTask(shares[0][name], shares[1][name], True) for name in names]

    def unpack(outs):
        names = ("vectors", "grad_pre", "grad_cross", "queries", "states", "grad_self")
        return dict(zip(names, outs))

    def for_backward(layer):
        return saved[layer][4], *saved[layer][6:9], *saved[layer][10:]

    def products(layer, outs):
        attended_t, second_normed, cross_att = saved[layer][3], saved[layer][5], saved[layer][9]
        return [
            (cross_att, outs["grad_cross"]),
            (attended_t, outs["grad_self"]),
            (second_normed, outs["queries"]),
            (saved[layer][1], None),
        ]

    names = ("cross_output", "output", "cross_query", "heads")
    outs, carried = backward_chain(
        1,
        cotangent,
        for_backward(1),
        states[1],
        seg,
        vectors,
        weights,
        saved[1][2],
        begins,
        8,
        [BothTask(saved[1][0], result_low)],
    )
    later, grad_heads_t = unpack(outs), outs[6]
    layer_outputs, shares[1]["states"], shares[1]["reduce"], shares[1]["expand"] = carried
    outs, carried = between_chain(
        1,
        grad_heads_t,
        saved[1][0],
        selected[1],
        later["grad_self"],
        self_pairs,
        products(1, later),
        (for_backward(0), states[0], seg, selected[0], weights),
        10,
        [],
    )
    last_vectors, later_low = outs[:2]
    sooner = unpack(outs[2:])
    shares[1].update(zip(names, carried))
    shares[0]["reduce"], shares[0]["expand"] = carried[4:]
    outs, carried = last_kernel(
        saved[0][2],
        sooner["grad_self"],
        weights[0],
        begins,
        inputs,
        vectors,
        self_pairs,
        later_low,
        products(0, sooner),
        [shares[1][name] for name in names],
        (sooner["states"], shares[1]["states"]),
        text_local,
        (cross_key, cross_value),
        (later["vectors"] + last_vectors, sooner["vectors"]),
        11,
        crossing("reduce", "expand"),
    )
    both_grads = outs[-1]
    totals = dict(zip(("reduce", "expand") + names + ("text",), carried))
    cross_grads, (vector_total, text_grad) = totals["text"], carried[7:]
    kernel_outs = widen(
        [layer_outputs, both_grads, text_grad, cross_grads],
        [totals[name] for name in ("reduce", "expand", "cross_output", "output", "cross_query", "heads")],
        vector_total,
    )
    layer_outputs, input_grads, text_grad, cross_key_grad, cross_value_grad = kernel_outs[:5]
    reduce_grad, expand_grad, cross_output_grad, output_grad, cross_query_grad = kernel_outs[5:10]
    query_grad, key_grad, value_grad = kernel_outs[10:13]
    rows = kernel_outs[13:]
    ordered = (
        rows[0],
        rows[1],
        query_grad,
        key_grad,
        value_grad,
        output_grad,
        rows[2],
        rows[3],
        cross_query_grad,
        cross_key_grad,
        cross_value_grad,
        cross_output_grad,
        rows[4],
        rows[5],
        expand_grad,
        reduce_grad,
    )
    vector_places = (0, 1, 6, 7, 12, 13)
    ordered = tuple(
        g if place in vector_places else g[None] for place, g in enumerate(ordered)
    )
    return (layer_outputs[None], input_grads[None], text_grad.reshape(text.shape)) + ordered


def widen(lows, wides, vectors):
    *lows, pair = lows
    *wides, triple = wides
    wide = jnp.float32
    half, third = pair.shape[1] // 2, triple.shape[1] // 3
    quarter = vectors.shape[1] // 4
    outs = [jax.ShapeDtypeStruct(low.shape, wide) for low in lows]
    outs += [jax.ShapeDtypeStruct((pair.shape[0], half), wide)] * 2
    outs += [jax.ShapeDtypeStruct(one.shape, wide) for one in wides]
    outs += [jax.ShapeDtypeStruct((triple.shape[0], third), wide)] * 3
    outs += [jax.ShapeDtypeStruct((1, quarter), wide)] * 6
    widened = [*lows, pair]
    n_in, n_out, n_low = len(widened) + len(wides) + 2, len(outs), len(widened)

    def kernel(*refs):
        ins, outs = refs[:n_in], refs[n_in : n_in + n_out]
        narrow = refs[n_in + n_out : n_in + n_out + n_low]
        broad = refs[n_in + n_out + n_low : n_in + n_out + 2 * n_low]
        *held, rows, in_sems, out_sems = refs[n_in + n_out + 2 * n_low :]
        lane = span(lax.axis_index(FRAME), quarter)
        started = []

        def copy(source, landing):
            one = pltpu.make_async_copy(source, landing, out_sems.at[len(started)])
            one.start()
            started.append(one)

        loads = [pltpu.make_async_copy(ins[i], narrow[i], in_sems.at[i]) for i in range(n_low)]
        copied = [
            pltpu.make_async_copy(source, room, in_sems.at[n_low + i])
            for i, (source, room) in enumerate(zip(ins[n_low:], held + [rows]))
        ]
        for load in copied + loads:
            load.start()
        for i in range(len(wides)):
            copied[i].wait()
            copy(held[i], outs[n_low + 1 + i])
        place = n_low + 1 + len(wides)
        copied[-2].wait()
        for part in range(3):
            copy(held[-1].at[:, part * third : (part + 1) * third], outs[place + part])
        copied[-1].wait()
        for row in range(6):
            copy(rows.at[row : row + 1, lane], outs[place + 3 + row])
        for i in range(n_low):
            loads[i].wait()
            broad[i][...] = narrow[i][...].astype(wide)
            if i + 1 < n_low:
                copy(broad[i], outs[i])
            else:
                copy(broad[i].at[:, :half], outs[i])
                copy(broad[i].at[:, half:], outs[i + 1])
        for one in started:
            one.wait()

    anywhere = pl.BlockSpec(memory_space=pl.ANY)
    scratch = [pltpu.VMEM(low.shape, jnp.bfloat16) for low in widened]
    scratch += [pltpu.VMEM(low.shape, wide) for low in widened]
    scratch += [pltpu.VMEM(one.shape, wide) for one in (*wides, triple, vectors)]
    scratch += [pltpu.SemaphoreType.DMA((n_in,)), pltpu.SemaphoreType.DMA((n_out,))]
    return pl.pallas_call(
        kernel,
        out_shape=outs,
        in_specs=[anywhere] * n_in,
        out_specs=[anywhere] * n_out,
        scratch_shapes=scratch,
        compiler_params=pltpu.CompilerParams(vmem_limit_bytes=VMEM_BYTES),
    )(*widened, *wides, triple, vectors)


def self_attention(query, key_rows, value_rows, masks):
    all_keys = lax.all_gather(key_rows, FRAME, axis=0, tiled=True)
    all_values = lax.all_gather(value_rows, FRAME, axis=0, tiled=True)
    return attend(query, all_keys, all_values, masks["own"]), (query, all_keys, all_values)


def self_attention_back(kept, grad_out, masks):
    query, keys, values = kept
    grad_q, grad_k_all, grad_v_all = attend_back(query, keys, values, masks["own"], grad_out)
    grad_k, grad_v = (
        lax.psum_scatter(g.astype(jnp.bfloat16), FRAME, scatter_dimension=0, tiled=True)
        for g in (grad_k_all, grad_v_all)
    )
    return grad_q.astype(jnp.bfloat16), grad_k, grad_v


def forward(entering, vectors, weights, cross_keys, cross_values, masks):
    first_gain, first_shift, second_gain, second_shift, third_gain, third_shift = vectors
    (
        query_weight,
        key_weight,
        value_weight,
        output_weight,
        cross_query,
        cross_output,
        expand_weight,
        reduce_weight,
    ) = weights
    signal = entering.astype(jnp.float32)
    first_normed = layer_norm(signal, first_gain, first_shift).astype(jnp.bfloat16)
    query = matmul(first_normed, query_weight).astype(jnp.bfloat16)
    key_rows = matmul(first_normed, key_weight).astype(jnp.bfloat16)
    value_rows = matmul(first_normed, value_weight).astype(jnp.bfloat16)
    attended, heads_kept = self_attention(query, key_rows, value_rows, masks)
    middle = signal + head_total(matmul(attended, output_weight))
    second_normed = layer_norm(middle, second_gain, second_shift).astype(jnp.bfloat16)
    cross_queries = matmul(second_normed, cross_query).astype(jnp.bfloat16)
    cross_att = attend(cross_queries, cross_keys, cross_values, masks["cross"])
    latter = middle + head_total(matmul(cross_att, cross_output))
    third_normed = layer_norm(latter, third_gain, third_shift).astype(jnp.bfloat16)
    hidden_pre = matmul(third_normed, expand_weight)
    hidden_act = jax.nn.gelu(hidden_pre, approximate=False).astype(jnp.bfloat16)
    result = latter + head_total(matmul(hidden_act, reduce_weight))
    saved = (
        signal,
        first_normed,
        heads_kept,
        attended,
        middle,
        second_normed,
        cross_queries,
        cross_att,
        latter,
        third_normed,
        hidden_pre,
        hidden_act,
    )
    return (result, saved)


def backward(saved, upstream, vectors, weights, cross_keys, cross_values, masks):
    first_gain, first_shift, second_gain, second_shift, third_gain, third_shift = vectors
    (
        query_weight,
        key_weight,
        value_weight,
        output_weight,
        cross_query,
        cross_output,
        expand_weight,
        reduce_weight,
    ) = weights
    (
        signal,
        first_normed,
        heads_kept,
        attended,
        middle,
        second_normed,
        cross_queries,
        cross_att,
        latter,
        third_normed,
        hidden_pre,
        hidden_act,
    ) = saved
    grad_out = upstream.astype(jnp.bfloat16)
    grad_reduce = matmul_tn(hidden_act, grad_out)
    grad_act = matmul_nt(grad_out, reduce_weight)
    slope = (
        0.5 * (1.0 + lax.erf(hidden_pre * inv_sqrt_two))
        + hidden_pre * jnp.exp(-0.5 * hidden_pre * hidden_pre) * inv_sqrt_tau
    )
    grad_pre = (grad_act * slope).astype(jnp.bfloat16)
    grad_expand = matmul_tn(third_normed, grad_pre)
    grad_third = head_total(matmul_nt(grad_pre, expand_weight))
    grad_latter, grad_third_gain, grad_third_shift = norm_back(latter, third_gain, grad_third)
    grad_latter = grad_latter + upstream
    grad_cross = grad_latter.astype(jnp.bfloat16)
    grad_cross_output = matmul_tn(cross_att, grad_cross)
    grad_cross_att = matmul_nt(grad_cross, cross_output).astype(jnp.bfloat16)
    grad_cq, grad_ck, grad_cv = attend_back(
        cross_queries, cross_keys, cross_values, masks["cross"], grad_cross_att
    )
    grad_text_rows = jnp.concatenate([grad_ck, grad_cv], axis=1).astype(jnp.bfloat16)
    grad_text_rows = lax.psum_scatter(
        grad_text_rows.reshape(ITEMS, TEXT, -1), FRAME, scatter_dimension=1, tiled=True
    )
    grad_cquery = grad_cq.astype(jnp.bfloat16)
    grad_cross_query = matmul_tn(second_normed, grad_cquery)
    grad_second = head_total(matmul_nt(grad_cquery, cross_query))
    grad_middle, grad_second_gain, grad_second_shift = norm_back(middle, second_gain, grad_second)
    grad_middle = grad_middle + grad_latter
    grad_self = grad_middle.astype(jnp.bfloat16)
    grad_output = matmul_tn(attended, grad_self)
    grad_att = matmul_nt(grad_self, output_weight).astype(jnp.bfloat16)
    grad_query_low, grad_key_low, grad_value_low = self_attention_back(heads_kept, grad_att, masks)
    grad_query = matmul_tn(first_normed, grad_query_low)
    grad_key = matmul_tn(first_normed, grad_key_low)
    grad_value = matmul_tn(first_normed, grad_value_low)
    grad_first = head_total(
        matmul_nt(grad_query_low, query_weight)
        + matmul_nt(grad_key_low, key_weight)
        + matmul_nt(grad_value_low, value_weight)
    )
    grad_signal, grad_first_gain, grad_first_shift = norm_back(signal, first_gain, grad_first)
    grad_signal = grad_signal + grad_middle
    vector_grads = (
        grad_first_gain,
        grad_first_shift,
        grad_second_gain,
        grad_second_shift,
        grad_third_gain,
        grad_third_shift,
    )
    matrix_grads = (
        grad_query,
        grad_key,
        grad_value,
        grad_output,
        grad_cross_query,
        grad_cross_output,
        grad_expand,
        grad_reduce,
    )
    matrix_grads = tuple(
        lax.psum_scatter(g.astype(jnp.bfloat16), FRAME, scatter_dimension=0, tiled=True)
        for g in matrix_grads
    )
    return grad_signal, vector_grads, matrix_grads, grad_text_rows


def per_device(
    inputs,
    lengths,
    text,
    cotangent,
    first_gain,
    first_shift,
    query_weight,
    key_weight,
    value_weight,
    output_weight,
    second_gain,
    second_shift,
    cross_query,
    cross_key,
    cross_value,
    cross_output,
    third_gain,
    third_shift,
    expand_weight,
    reduce_weight,
):
    head_count, frame_count = lax.axis_size(LINE), lax.axis_size(FRAME)
    local_heads = query_weight.shape[2] // HEAD
    if head_count == 4 and frame_count == 4 and local_heads == 4:
        return on_four_frames(
            inputs,
            lengths,
            text,
            cotangent,
            (first_gain, first_shift, second_gain, second_shift, third_gain, third_shift),
            (
                query_weight,
                key_weight,
                value_weight,
                output_weight,
                cross_query,
                cross_key,
                cross_value,
                cross_output,
                expand_weight,
                reduce_weight,
            ),
        )
    section = lax.axis_index(SECTION)
    at_zero = section == 0
    frame_index = lax.axis_index(FRAME)
    micro_count, rows_dev, model_width = inputs.shape
    rows_all = rows_dev * frame_count
    text_rows_dev = text.shape[2]

    def keep(pair):
        return jnp.where(at_zero, pair[0], pair[1])

    def give(pair):
        return jnp.where(at_zero, pair[1], pair[0])

    vector_args = jnp.concatenate(
        [first_gain, first_shift, second_gain, second_shift, third_gain, third_shift], axis=0
    )
    vectors = lax.all_gather(vector_args, SECTION)
    matrix_args = (
        query_weight,
        key_weight,
        value_weight,
        output_weight,
        cross_query,
        cross_output,
        expand_weight,
        reduce_weight,
    )
    matrices = [lax.all_gather(w[0], SECTION) for w in matrix_args]
    weights = [tuple(w[layer] for w in matrices) for layer in range(2)]

    text_full = lax.all_gather(text, FRAME, axis=2, tiled=True)
    text_flat = text_full.reshape(micro_count * ITEMS * TEXT, model_width)
    text_heads = jnp.concatenate(
        [matmul(text_flat, cross_key[0]), matmul(text_flat, cross_value[0])], axis=1
    ).astype(jnp.bfloat16)
    text_heads = text_heads.reshape(micro_count, ITEMS * TEXT, -1)
    own_text = keep(text_heads)
    other_text = swapped(give(text_heads))
    columns = cross_key.shape[2]
    cross_states = [
        jnp.where(at_zero, own_text, other_text),
        jnp.where(at_zero, other_text, own_text),
    ]
    cross_keys = [c[:, :columns] for c in cross_states]
    cross_values = [c[:, columns:] for c in cross_states]

    item_ends = jnp.cumsum(lax.dynamic_index_in_dim(lengths, section, 0, keepdims=False))
    all_positions = jnp.arange(rows_all, dtype=jnp.int32)
    seg_all = jnp.sum((all_positions[:, None] >= item_ends[None, :]).astype(jnp.int32), axis=1)
    own_start = frame_index * rows_dev
    own_positions = own_start + jnp.arange(rows_dev, dtype=jnp.int32)
    seg_own = lax.dynamic_slice_in_dim(seg_all, own_start, rows_dev)
    text_item = jnp.arange(ITEMS * TEXT, dtype=jnp.int32) // TEXT
    masks = {
        "own": (all_positions[None, :] <= own_positions[:, None])
        & (seg_own[:, None] == seg_all[None, :]),
        "cross": seg_own[:, None] == text_item[None, :],
    }

    signal = lax.dynamic_index_in_dim(inputs, section, 0, keepdims=False)
    results, saves = [], []
    for layer in range(2):
        result, saved = forward(
            signal, vectors[layer], weights[layer], cross_keys[layer], cross_values[layer], masks
        )
        results.append(result)
        saves.append(saved)
        signal = result.astype(jnp.bfloat16)

    upstream = lax.dynamic_index_in_dim(cotangent, section, 0, keepdims=False)
    in_grads, vector_grads, matrix_grads, text_grads = [None] * 2, [None] * 2, [None] * 2, [None] * 2
    for layer in (1, 0):
        grad_signal, vector_grads[layer], matrix_grads[layer], text_grads[layer] = backward(
            saves[layer],
            upstream,
            vectors[layer],
            weights[layer],
            cross_keys[layer],
            cross_values[layer],
            masks,
        )
        in_grads[layer] = grad_signal
        upstream = grad_signal.astype(jnp.bfloat16).astype(jnp.float32)

    def both_micros(pair):
        own = keep(pair)
        other = swapped(give([p.astype(jnp.bfloat16) for p in pair])).astype(own.dtype)
        return jnp.stack([jnp.where(at_zero, own, other), jnp.where(at_zero, other, own)])

    layer_outputs = both_micros(results)
    input_grads = both_micros(in_grads)
    totals = [
        keep(pair).astype(jnp.float32) + swapped(give(pair)).astype(jnp.float32)
        for pair in zip(*matrix_grads)
    ]
    text_rows = both_micros(text_grads)
    text_rows = text_rows.reshape(micro_count * ITEMS * text_rows_dev, -1)
    key_part, value_part = text_rows[:, :columns], text_rows[:, columns:]
    text_local = text.reshape(-1, model_width)
    grad_cross_key, grad_cross_value = (
        lax.psum_scatter(
            matmul_tn(text_local, part).astype(jnp.bfloat16),
            FRAME,
            scatter_dimension=0,
            tiled=True,
        ).astype(jnp.float32)
        for part in (key_part, value_part)
    )
    text_part = matmul_nt(key_part, cross_key[0]) + matmul_nt(value_part, cross_value[0])
    text_grad = lax.psum(text_part.astype(jnp.bfloat16), (SECTION, LINE)).astype(jnp.float32)
    text_grad = text_grad.reshape(text.shape)

    stacked = jnp.stack([jnp.stack(v) for v in vector_grads])
    stacked = lax.psum_scatter(
        stacked.astype(jnp.bfloat16), FRAME, scatter_dimension=2, tiled=True
    )
    vector_total = keep(stacked).astype(jnp.float32) + swapped(give(stacked)).astype(jnp.float32)

    grad_q, grad_k, grad_v, grad_o, grad_cq, grad_co, grad_e, grad_r = totals
    ordered = (
        vector_total[0],
        vector_total[1],
        grad_q,
        grad_k,
        grad_v,
        grad_o,
        vector_total[2],
        vector_total[3],
        grad_cq,
        grad_cross_key,
        grad_cross_value,
        grad_co,
        vector_total[4],
        vector_total[5],
        grad_e,
        grad_r,
    )
    return (layer_outputs[None], input_grads[None], text_grad) + tuple(g[None] for g in ordered)


def solution(mesh):
    return jax.shard_map(
        per_device,
        mesh=mesh,
        in_specs=(
            P(None, FRAME, None),
            P(),
            P(None, None, FRAME, None),
            P(None, FRAME, None),
            P(SECTION, None),
            P(SECTION, None),
            P(SECTION, None, LINE),
            P(SECTION, None, LINE),
            P(SECTION, None, LINE),
            P(SECTION, LINE, None),
            P(SECTION, None),
            P(SECTION, None),
            P(SECTION, None, LINE),
            P(SECTION, None, LINE),
            P(SECTION, None, LINE),
            P(SECTION, LINE, None),
            P(SECTION, None),
            P(SECTION, None),
            P(SECTION, None, LINE),
            P(SECTION, LINE, None),
        ),
        out_specs=(
            P(SECTION, None, FRAME, None),
            P(SECTION, None, FRAME, None),
            P(None, None, FRAME, None),
            P(SECTION, FRAME),
            P(SECTION, FRAME),
            P(SECTION, FRAME, LINE),
            P(SECTION, FRAME, LINE),
            P(SECTION, FRAME, LINE),
            P(SECTION, (LINE, FRAME), None),
            P(SECTION, FRAME),
            P(SECTION, FRAME),
            P(SECTION, FRAME, LINE),
            P(SECTION, FRAME, LINE),
            P(SECTION, FRAME, LINE),
            P(SECTION, (LINE, FRAME), None),
            P(SECTION, FRAME),
            P(SECTION, FRAME),
            P(SECTION, FRAME, LINE),
            P(SECTION, (LINE, FRAME), None),
        ),
        check_vma=False,
    )
```
